32 devices in a mesh: section: 2 (over x), wide: 16 (over z, y, core).
Axes of the slice: x: 2, y: 2, z: 4, core: 2. Of those that a mesh axis runs over, the one named last changes fastest.
Arguments:
- inputs: bfloat16 [2, 16, 512, 768], P(None, 'wide'), may hold values from -6 to 6
- cotangent: bfloat16 [2, 16, 512, 768], P(None, 'wide'), may hold values from -6 to 6
- token_size: int32 [2, 16, 512], P(None, 'wide'), may hold values from 1 to 16
- image_id: int32 [2, 16, 512], P(None, 'wide'), may hold values from 0 to 2, as said below
- w_in: bfloat16 [2, 768, 5376], P('section', 'wide'), may hold values from -0.21875 to 0.21875
- w_out: bfloat16 [2, 3840, 768], P('section', 'wide')
- ln_gain: bfloat16 [2, 768], P('section', 'wide'), may hold values from 0.099609375 to 1.8984375
- q_gain: bfloat16 [2, 64], P('section', 'wide'), may hold values from 0.099609375 to 1.8984375
- k_gain: bfloat16 [2, 64], P('section', 'wide'), may hold values from 0.099609375 to 1.8984375
Outputs:
- section_out: bfloat16 [2, 2, 16, 512, 768], P('section', None, 'wide')
- grad_in: float32 [2, 2, 16, 512, 768], P('section', None, 'wide')
- grad_w_in: float32 [2, 768, 5376], P('section', 'wide')
- grad_w_out: float32 [2, 3840, 768], P('section', 'wide')
- grad_ln_gain: float32 [2, 768], P('section', 'wide')
- grad_q_gain: float32 [2, 64], P('section', 'wide')
- grad_k_gain: float32 [2, 64], P('section', 'wide')
The draws below stay inside these ranges and needn't reach their ends.
Inputs may be any that keep to these rules, and one draw needn't show every extreme that they name: `image_id`: each row holds 2 images of 60 to 196 consecutive slots, numbered 0 to 1 from the row's start; one image of each row has exactly 196 slots; the remaining slots at the row's end, one or more, carry the number 2 and form one more group.
All inputs are finite; a program needn't handle non-finite values.
Results may differ from the reference program's by a relative error of at most 0.033.
Values may be sent and summed in bfloat16 or wider, within the bound.
A program may use at most 192 MiB of HBM per device.

```python
import jax
import jax.numpy as jnp
from jax import lax

HEADS = 12
HD = 64
FF = 3072
SLOTS = 512
PACK = 2
IMG_MIN = 60
IMG_MAX = 196
MB = 2
D = 768
ROWS = 16
LAYERS = 2


def draw_image_id(key, part):
    key = jax.random.fold_in(key, 11)
    key_len, key_star = jax.random.split(key)
    lengths = jax.random.randint(key_len, (MB, ROWS, PACK), IMG_MIN, IMG_MAX + 1)
    chosen = jax.random.randint(key_star, (MB, ROWS, 1), 0, PACK)
    lengths = jnp.where(jnp.arange(PACK)[None, None, :] == chosen, IMG_MAX, lengths)
    ends = jnp.cumsum(lengths, -1)
    slot_index = jnp.arange(SLOTS)
    passed = slot_index[None, None, :, None] >= ends[:, :, None, :]
    return jnp.sum(passed.astype(jnp.int32), -1).astype(jnp.int32)


def draw_w_out(key, part):
    key = jax.random.fold_in(key, 23)
    normal_draw = jax.random.normal(key, (LAYERS, D + FF, D), jnp.float32)
    row_index = jnp.arange(D + FF)
    scales = jnp.where(row_index < D, 0.25, 1.5 / FF ** 0.5)
    return (normal_draw * scales[None, :, None]).astype(jnp.bfloat16)


def place_ends(entries, rng, least, high):
    spot = [jax.random.randint(jax.random.fold_in(rng, axis), (), 0, length) for axis, length in enumerate(entries.shape)]
    longest = entries.shape.index(max(entries.shape))
    neighbour = spot[:longest] + [(spot[longest] + 1) % entries.shape[longest]] + spot[longest + 1:]
    return entries.at[tuple(spot)].set(least).at[tuple(neighbour)].set(high)


def steps_of(stream_key, dims, pieces, least, high):
    def one(dim, blocks):
        draws = jax.random.uniform(jax.random.fold_in(jax.random.fold_in(stream_key, 6), dim), (blocks,), jnp.float32, least / len(pieces), high / len(pieces))
        return jnp.repeat(jnp.exp(draws), dims[dim] // blocks).reshape((-1,) + (1,) * (len(dims) - dim - 1))

    factor_of = one(*pieces[0])
    for cut in pieces[1:]:
        factor_of = factor_of * one(*cut)
    return factor_of


def scatter_about(own_key, extent, scale, most, pieces=(), kind=jnp.bfloat16):
    gain = steps_of(own_key, extent, pieces, -0.22, 0.18) if pieces else 1.0
    array = jax.random.normal(own_key, extent, jnp.float32) * scale * gain
    return jnp.minimum(jnp.maximum(array, -most), most).astype(kind)


def setup_inputs(seed: int = 0) -> dict:
    arg_keys = jax.random.split(jax.random.key(seed), 10)
    inputs = scatter_about(arg_keys[0], (MB, ROWS, SLOTS, D), 1.0, 6.0, ((1, 16),))
    cotangent = scatter_about(arg_keys[1], (MB, ROWS, SLOTS, D), 1.0, 6.0, ((1, 16),))
    token_size = place_ends(jax.random.randint(arg_keys[2], (MB, ROWS, SLOTS), 1, 17), jax.random.fold_in(arg_keys[2], 1), 1, 16).astype(jnp.int32)
    image_id = draw_image_id(jax.random.fold_in(arg_keys[9], 71), 0)
    w_in = scatter_about(arg_keys[4], (LAYERS, D, 3 * D + FF), D ** -0.5, 0.21875, ((0, 2), (1, 16)))
    w_out = draw_w_out(jax.random.fold_in(arg_keys[9], 71), 0)
    ln_gain = jnp.clip(1.0 + 0.18 * jax.random.normal(arg_keys[6], (LAYERS, D), jnp.float32), 0.099609375, 1.8984375).astype(jnp.bfloat16)
    q_gain = jnp.clip(1.0 + 0.18 * jax.random.normal(arg_keys[7], (LAYERS, HD), jnp.float32), 0.099609375, 1.8984375).astype(jnp.bfloat16)
    k_gain = jnp.clip(1.0 + 0.18 * jax.random.normal(arg_keys[8], (LAYERS, HD), jnp.float32), 0.099609375, 1.8984375).astype(jnp.bfloat16)
    return {"inputs": inputs, "cotangent": cotangent, "token_size": token_size, "image_id": image_id, "w_in": w_in, "w_out": w_out, "ln_gain": ln_gain, "q_gain": q_gain, "k_gain": k_gain}


EPSILON = 1e-06
NEGATIVE = -1e+30
PRECISE = lax.Precision.HIGHEST

@jax.custom_vjp
def low(v):
    return lax.optimization_barrier(v.astype(jnp.bfloat16)).astype(jnp.float32)

@jax.custom_vjp
def low_back(v):
    return v

def low_keep(v):
    return (low(v), None)

def low_pass(kept, grad):
    return (grad,)

def back_keep(v):
    return (v, None)

def back_low(kept, grad):
    return (low(grad),)
low.defvjp(low_keep, low_pass)
low_back.defvjp(back_keep, back_low)

def layer_norm(values, gain_vec):
    average = lax.optimization_barrier(jnp.mean(values, -1, keepdims=True))
    centred = values - average
    variance = lax.optimization_barrier(jnp.mean(centred * centred, -1, keepdims=True))
    return centred * lax.rsqrt(variance + EPSILON) * gain_vec

def attend(row_block):
    queries, keys_in, values, image_ids, key_bias = row_block
    scores = jnp.einsum('qhd,khd->hqk', queries, keys_in, precision=PRECISE) * 0.125 + key_bias[None, None, :]
    scores = low_back(scores)
    same_image = image_ids[:, None] == image_ids[None, :]
    scores = jnp.where(same_image[None], scores, NEGATIVE)
    largest = lax.optimization_barrier(jnp.max(scores, -1, keepdims=True))
    exponent = jnp.exp(scores - largest)
    probabilities = exponent / lax.optimization_barrier(jnp.sum(exponent, -1, keepdims=True))
    return jnp.einsum('hqk,khd->qhd', low(probabilities), values, precision=PRECISE)

def layer(hidden, w_in, w_out, ln_gain, q_gain, k_gain, image_ids, key_bias):
    row_count, slot_count, model_width = hidden.shape
    normed = low(layer_norm(hidden, ln_gain))
    projected = low_back(jnp.einsum('rsd,df->rsf', normed, w_in, precision=PRECISE))
    head_shape = (row_count, slot_count, HEADS, HD)
    queries = low(layer_norm(projected[..., :model_width].reshape(head_shape), q_gain))
    keys_in = low(layer_norm(projected[..., model_width:2 * model_width].reshape(head_shape), k_gain))
    values = low(projected[..., 2 * model_width:3 * model_width].reshape(head_shape))
    attended = lax.map(jax.checkpoint(attend), (queries, keys_in, values, image_ids, key_bias))
    attended = low_back(attended.reshape(row_count, slot_count, model_width))
    activated = jax.nn.gelu(projected[..., 3 * model_width:], approximate=False)
    combined = low(jnp.concatenate([attended, activated], -1))
    return hidden + jnp.einsum('rsf,fd->rsd', combined, w_out, precision=PRECISE)

def reference(inputs, cotangent, token_size, image_id, w_in, w_out, ln_gain, q_gain, k_gain):
    key_bias = jnp.log(token_size.astype(jnp.float32))
    params = [tuple((weight[layer_index].astype(jnp.float32) for weight in (w_in, w_out, ln_gain, q_gain, k_gain))) for layer_index in range(2)]
    totals = [[jnp.zeros_like(piece) for piece in params[layer_index]] for layer_index in range(2)]
    first_out, second_out, first_grad, second_grad = ([], [], [], [])
    for micro_batch in range(MB):
        image_ids = image_id[micro_batch]
        row_bias = key_bias[micro_batch]

        def section_layer(hidden, w_one, w_two, gain_one, gain_two, gain_three):
            return layer(hidden, w_one, w_two, gain_one, gain_two, gain_three, image_ids, row_bias)
        first_value, first_back = jax.vjp(section_layer, inputs[micro_batch].astype(jnp.float32), *params[0])
        sent_value = low(first_value)
        second_value, second_back = jax.vjp(section_layer, sent_value, *params[1])
        grads_second = second_back(cotangent[micro_batch].astype(jnp.float32))
        grads_first = first_back(low(grads_second[0]))
        for position in range(5):
            totals[0][position] = totals[0][position] + grads_first[position + 1]
            totals[1][position] = totals[1][position] + grads_second[position + 1]
        first_out.append(first_value.astype(jnp.bfloat16))
        second_out.append(second_value.astype(jnp.bfloat16))
        first_grad.append(grads_first[0])
        second_grad.append(grads_second[0])
    section_out = jnp.stack([jnp.stack(first_out), jnp.stack(second_out)])
    grad_in = jnp.stack([jnp.stack(first_grad), jnp.stack(second_grad)])
    stacked = [jnp.stack([totals[0][position], totals[1][position]]) for position in range(5)]
    return (section_out, grad_in, stacked[0], stacked[1], stacked[2], stacked[3], stacked[4])
```

```python
import functools

import jax
import jax.numpy as jnp
from jax import lax
from jax.experimental import pallas as pl
from jax.experimental.pallas import tpu as pltpu
from jax.sharding import PartitionSpec as P

HEADS = 12
HD = 64


EPSILON = 1e-06
NEGATIVE = -1e30


def layer_norm(values, gain_vec):
    average = jnp.mean(values, -1, keepdims=True)
    centred = values - average
    variance = jnp.mean(centred * centred, -1, keepdims=True)
    return centred * lax.rsqrt(variance + EPSILON) * gain_vec


def exact_gelu(values):
    return jax.nn.gelu(values, approximate=False)


def head_norms(queries, keys_in, query_gain, key_gain):
    return (layer_norm(queries, query_gain), layer_norm(keys_in, key_gain))


def score_rows(queries, keys_in, image_ids, key_bias):
    scores = (
        jnp.einsum("qhd,khd->hqk", queries, keys_in, preferred_element_type=jnp.float32) * 0.125
        + key_bias[None, None, :]
    )
    same_image = image_ids[:, None] == image_ids[None, :]
    return jnp.where(same_image[None], scores, NEGATIVE)


def attend_forward(row_block):
    queries, keys_in, values, image_ids, key_bias = row_block
    scores = score_rows(queries, keys_in, image_ids, key_bias)
    largest = jnp.max(scores, -1, keepdims=True)
    exponent = jnp.exp(scores - largest)
    row_total = jnp.sum(exponent, -1, keepdims=True)
    weights = (exponent / row_total).astype(jnp.bfloat16)
    output = jnp.einsum("hqk,khd->qhd", weights, values, preferred_element_type=jnp.float32)
    return (output, largest + jnp.log(row_total))


def attend_backward(row_block):
    queries, keys_in, values, image_ids, key_bias, log_total, grad_out = row_block
    scores = score_rows(queries, keys_in, image_ids, key_bias)
    probabilities = jnp.exp(scores - log_total)
    grad_values = jnp.einsum(
        "hqk,qhd->khd",
        probabilities.astype(jnp.bfloat16),
        grad_out,
        preferred_element_type=jnp.float32,
    )
    grad_probs = jnp.einsum("qhd,khd->hqk", grad_out, values, preferred_element_type=jnp.float32)
    grad_scores = probabilities * (
        grad_probs - jnp.sum(probabilities * grad_probs, -1, keepdims=True)
    )
    grad_scores = grad_scores.astype(jnp.bfloat16)
    grad_queries = (
        jnp.einsum("hqk,khd->qhd", grad_scores, keys_in, preferred_element_type=jnp.float32) * 0.125
    )
    grad_keys = (
        jnp.einsum("hqk,qhd->khd", grad_scores, queries, preferred_element_type=jnp.float32) * 0.125
    )
    return (grad_queries, grad_keys, grad_values)


def layer_pieces(hidden, weights, image_ids, key_bias):
    w_in, w_out, ln_gain, q_gain, k_gain = weights
    row_count, slot_count, model_width = hidden.shape
    normed, norm_back = jax.vjp(layer_norm, hidden, ln_gain.astype(jnp.float32))
    normed_low = normed.astype(jnp.bfloat16).reshape(row_count * slot_count, model_width)
    projected = jnp.dot(normed_low, w_in, preferred_element_type=jnp.float32)
    head_shape = (row_count, slot_count, HEADS, HD)
    queries = projected[:, :model_width].reshape(head_shape)
    keys_in = projected[:, model_width : 2 * model_width].reshape(head_shape)
    values = (
        projected[:, 2 * model_width : 3 * model_width].reshape(head_shape).astype(jnp.bfloat16)
    )
    normed_heads, norms_back = jax.vjp(
        head_norms, queries, keys_in, q_gain.astype(jnp.float32), k_gain.astype(jnp.float32)
    )
    queries_low = normed_heads[0].astype(jnp.bfloat16)
    keys_low = normed_heads[1].astype(jnp.bfloat16)
    attended, log_total = lax.map(
        attend_forward, (queries_low, keys_low, values, image_ids, key_bias)
    )
    activated, gelu_back = jax.vjp(exact_gelu, projected[:, 3 * model_width :])
    combined = jnp.concatenate(
        [attended.reshape(row_count * slot_count, model_width), activated], 1
    ).astype(jnp.bfloat16)
    return (
        norm_back,
        normed_low,
        norms_back,
        queries_low,
        keys_low,
        values,
        log_total,
        gelu_back,
        combined,
    )


def layer_backward(hidden, grad_low, pieces, weights, image_ids, key_bias):
    (
        norm_back,
        normed_low,
        norms_back,
        queries_low,
        keys_low,
        values,
        log_total,
        gelu_back,
        combined,
    ) = pieces
    row_count, slot_count, model_width = hidden.shape
    flat_rows = row_count * slot_count
    grad_flat = grad_low.reshape(flat_rows, model_width)
    contract_last = (((1,), (1,)), ((), ()))
    grad_combined = lax.dot_general(
        grad_flat, weights[1], contract_last, preferred_element_type=jnp.float32
    )
    grad_attended = (
        grad_combined[:, :model_width]
        .astype(jnp.bfloat16)
        .reshape(row_count, slot_count, HEADS, HD)
    )
    grad_up = gelu_back(grad_combined[:, model_width:])[0]
    grad_q, grad_k, grad_v = lax.map(
        attend_backward,
        (queries_low, keys_low, values, image_ids, key_bias, log_total, grad_attended),
    )
    grad_queries, grad_keys, grad_qgain, grad_kgain = norms_back((grad_q, grad_k))
    grad_projected = jnp.concatenate(
        [
            grad_queries.reshape(flat_rows, model_width),
            grad_keys.reshape(flat_rows, model_width),
            grad_v.reshape(flat_rows, model_width),
            grad_up,
        ],
        1,
    ).astype(jnp.bfloat16)
    grad_normed = lax.dot_general(
        grad_projected, weights[0], contract_last, preferred_element_type=jnp.float32
    )
    grad_hidden, grad_lngain = norm_back(grad_normed.reshape(hidden.shape))
    return (
        grad_low.astype(jnp.float32) + grad_hidden,
        grad_lngain,
        grad_qgain,
        grad_kgain,
        normed_low,
        grad_projected,
        combined,
        grad_flat,
    )


MESH = pl.DeviceIdType.MESH
NZ = 4
BLOCK = ((48, 5376), (240, 768))
CUT_IN, CUT_OUT = 2176, 96
PART = ((48, CUT_IN), (CUT_OUT, 768))
REST = ((48, 5376 - 2 * CUT_IN), (240 - 2 * CUT_OUT, 768))


class Place:
    def __init__(self):
        self.x, self.wide = lax.axis_index("section"), lax.axis_index("wide")
        self.y, self.z, self.c = (self.wide // 2) % 2, self.wide // 4, self.wide % 2

    def at(self, x, y, z, c=None):
        return (x, z * 4 + y * 2 + (self.c if c is None else c))

    def along(self, colour, block_z, far_first, far_second):
        dx = jnp.where(colour == 0, far_first, far_second)
        dy = jnp.where(colour == 0, far_second, far_first)
        return self.flip(self.x, dx), self.flip(self.y, dy), block_z

    @staticmethod
    def flip(value, far):
        return value + far - 2 * value * far

    def first(self, colour):
        return self.at(*self.along(colour, self.z, 1, 0))

    def second(self, colour):
        return self.at(*self.along(colour, self.z, 0, 1))

    def sibling(self):
        return self.at(self.x, self.y, self.z, 1 - self.c)


def greet(place):
    barrier = pltpu.get_barrier_semaphore()
    x, y, z = place.x, place.y, place.z

    def signal(device):
        pl.semaphore_signal(barrier, inc=1, device_id=device, device_id_type=MESH)

    signal(place.at(1 - x, y, z))
    signal(place.at(x, 1 - y, z))
    signal(place.sibling())
    pl.when(z < NZ - 1)(lambda: signal(place.at(x, y, z + 1)))
    pl.when(z > 0)(lambda: signal(place.at(x, y, z - 1)))
    pl.semaphore_wait(barrier, 3 + (z < NZ - 1).astype(jnp.int32) + (z > 0).astype(jnp.int32))


def number_of(block):
    return block[0] * 8 + block[1] * 4 + block[2]


def cut(ref, array, colour):
    rows, cols = BLOCK[array]
    if array == 0:
        if colour is None:
            return ref.at[:, pl.ds(2 * CUT_IN, cols - 2 * CUT_IN)]
        return ref.at[:, pl.ds(pl.multiple_of(colour * CUT_IN, 128), CUT_IN)]
    if colour is None:
        return ref.at[pl.ds(2 * CUT_OUT, rows - 2 * CUT_OUT), :]
    return ref.at[pl.ds(pl.multiple_of(colour * CUT_OUT, 16), CUT_OUT), :]


def loop(count, body):
    def step(index, carry):
        body(index)
        return carry
    lax.fori_loop(0, count, step, 0)


class Gather:
    def __init__(self, place, array, own, full, send_sem, recv_sem, core_sem):
        self.place, self.array, self.own, self.full = place, array, own, full
        self.send_sem, self.recv_sem, self.core_sem = send_sem, recv_sem, core_sem

    def view(self, block, colour, plane=None):
        rows = BLOCK[self.array][0]
        place = self.place
        start = (block[2] * 4 + block[1] * 2 + (place.c if plane is None else plane)) * rows
        return cut(self.full.at[block[0], pl.ds(pl.multiple_of(start, 16), rows), :], self.array, colour)

    def copy(self, link, device, block, colour, own=False, other_plane=False):
        kind = 2 if colour is None else colour
        number = number_of(block)
        target = self.view(block, colour, 1 - self.place.c if other_plane else None)
        source = cut(self.own, self.array, colour) if own else target
        sems = self.core_sem if link == 4 else self.recv_sem
        return pltpu.make_async_remote_copy(
            src_ref=source, dst_ref=target, send_sem=self.send_sem.at[link, kind, number], recv_sem=sems.at[kind, number],
            device_id=device, device_id_type=MESH)

    def visit(self, block, colour, onward, first, second, drain, condition=None, own=False):
        place = self.place

        def body():
            if not drain and not own:
                self.copy(0, place.sibling(), block, colour).wait_recv()

            def send(link, device):
                copy = self.copy(link, device, block, colour, own)
                copy.wait_send() if drain else copy.start()

            for link, step in onward:
                target = place.z + step
                pl.when((target >= 0) & (target < NZ))(functools.partial(send, link, place.at(place.x, place.y, target)))
            if first is not None:
                send(2, first)
            if second is not None:
                if isinstance(second, tuple) and len(second) == 3:
                    pl.when(second[2])(functools.partial(send, 3, second[:2]))
                else:
                    send(3, second)
            send(4, place.sibling())
        if condition is None:
            body()
        else:
            pl.when(condition)(body)

    def begin(self, drain=False):
        place = self.place
        me = (place.x, place.y, place.z)
        everywhere = ((0, 1), (1, -1))
        self.visit(me, None, everywhere, place.at(1 - place.x, place.y, place.z), place.at(place.x, 1 - place.y, place.z), drain, own=True)

        def body(colour):
            self.visit(me, colour, everywhere, place.first(colour), place.second(colour), drain, own=True)
        loop(2, body)

    def square(self, drain=False):
        place = self.place

        def body(index):
            far_x, far_y = (index != 1).astype(jnp.int32), (index != 0).astype(jnp.int32)
            block = (place.flip(place.x, far_x), place.flip(place.y, far_y), place.z)
            self.visit(block, None, ((0, 1), (1, -1)), None, place.at(place.x, 1 - place.y, place.z) + (index == 0,), drain)
        loop(3, body)

    def sided(self, distance, body):
        place = self.place

        def side_body(side):
            step = 1 - 2 * side
            block_z = place.z - step * distance
            body(side, block_z, (block_z >= 0) & (block_z < NZ) & ((distance > 0) | (side == 0)))
        loop(2, side_body)

    def onward(self, side):
        return ((0, 1), (1, -1))[side]

    def z_step(self, distance, drain=False):
        place = self.place
        for side in (0, 1):
            step = 1 - 2 * side
            block_z = place.z - step * distance

            def body(colour):
                self.visit((place.x, place.y, block_z), colour, ((side, step),), place.first(colour), place.second(colour), drain)
            pl.when((block_z >= 0) & (block_z < NZ))(lambda: loop(2, body))

    def line(self, distance, drain=False):
        place = self.place
        for side in (0, 1):
            step = 1 - 2 * side
            block_z = place.z - step * distance

            def body(index):
                block = (place.flip(place.x, index % 2), place.flip(place.y, index // 2), block_z)
                self.visit(block, None, ((side, step),), None, None, drain)
            pl.when((block_z >= 0) & (block_z < NZ))(lambda: loop(4, body))

    def a_step(self, distance, drain=False):
        place = self.place

        def body(side, block_z, there):
            def inner(colour):
                self.visit(place.along(colour, block_z, 1, 0), colour, (), None, place.second(colour), drain)
            pl.when(there)(lambda: loop(2, inner))
        self.sided(distance, body)

    def b_step(self, distance, drain=False):
        place = self.place

        def body(side, block_z, there):
            def inner(index):
                colour = index // 2
                self.visit(place.along(colour, block_z, index % 2, 1), colour, (), None, None, drain)
            pl.when(there)(lambda: loop(4, inner))
        self.sided(distance, body)

    def from_core(self):
        place = self.place

        def body(number):
            block = (number // 8, (number // 4) % 2, number % 4)
            self.copy(4, place.sibling(), block, None, other_plane=True).wait_recv()
            for colour in (0, 1):
                self.copy(4, place.sibling(), block, colour, other_plane=True).wait_recv()
        loop(16, body)

    def drain(self):
        self.begin(True)
        self.square(True)

        def body(index):
            self.z_step(index + 1, True)
            self.line(index + 1, True)
            self.a_step(index, True)
            self.b_step(index, True)
        loop(NZ, body)


def gather_kernel(w_in, w_out, full_in, full_out, *sems):
    place = Place()
    greet(place)
    first = Gather(place, 0, w_in, full_in, *sems[:3])
    second = Gather(place, 1, w_out, full_out, *sems[3:6])
    copies = []
    for array, (own, full) in enumerate(((w_in, full_in), (w_out, full_out))):
        rows = BLOCK[array][0]
        copy = pltpu.make_async_copy(own, full.at[place.x, pl.ds(pl.multiple_of(place.wide * rows, 16), rows), :], sems[6].at[array])
        copy.start()
        copies.append(copy)
    first.begin()
    first.square()

    def early(index):
        first.z_step(index + 1)
        first.a_step(index)
        first.line(index + 1)
    loop(NZ, early)
    second.begin()
    second.square()

    def late(index):
        first.b_step(index)
        second.z_step(index + 1)
        second.a_step(index)
        second.line(index + 1)
    loop(NZ, late)
    loop(NZ, second.b_step)
    first.from_core()
    second.from_core()
    for copy in copies:
        copy.wait()
    first.drain()
    second.drain()


def gather_weights(w_in, w_out):
    any_space = pl.BlockSpec(memory_space=pl.ANY)
    dma = pltpu.SemaphoreType.DMA
    return pl.pallas_call(
        gather_kernel,
        out_shape=(jax.ShapeDtypeStruct((2, 768, 5376), jnp.bfloat16), jax.ShapeDtypeStruct((2, 3840, 768), jnp.bfloat16)),
        in_specs=[any_space] * 2, out_specs=(any_space,) * 2,
        scratch_shapes=[dma((5, 3, 16)), dma((3, 16)), dma((3, 16))] * 2 + [dma((2,))],
        compiler_params=pltpu.CompilerParams(collective_id=0, has_side_effects=True),
        name="gather_weights",
    )(w_in, w_out)


def gather_all(piece, axis):
    return lax.all_gather(lax.all_gather(piece, "wide", axis=axis, tiled=True), "section", axis=0, tiled=True)


def scatter_all(terms, axis):
    own = lax.psum_scatter(terms, "section", scatter_dimension=0, tiled=True)
    return lax.psum_scatter(own, "wide", scatter_dimension=axis, tiled=True)


def on_device(inputs, cotangent, token_size, image_id, w_in, w_out, ln_gain, q_gain, k_gain):
    section = lax.axis_index("section")
    wide = lax.axis_size("wide")
    model_width = inputs.shape[3]
    blocks_fit = wide == 16 and w_in.shape[1] == BLOCK[0][0] and w_out.shape[1] == BLOCK[1][0]
    if blocks_fit:
        full_in, full_out = gather_weights(w_in[0], w_out[0])
    else:
        full_in, full_out = gather_all(w_in, 1), gather_all(w_out, 1)
    cuts = (ln_gain.shape[1], ln_gain.shape[1] + q_gain.shape[1])
    gains = gather_all(jnp.concatenate([ln_gain, q_gain, k_gain], 1)[:, None], 1)
    full_ln, full_q, full_k = [
        part.reshape(2, -1) for part in (gains[:, :, : cuts[0]], gains[:, :, cuts[0] : cuts[1]], gains[:, :, cuts[1] :])
    ]
    weights = [(full_in[layer], full_out[layer], full_ln[layer], full_q[layer], full_k[layer]) for layer in range(2)]
    ids = image_id[section]
    bias = jnp.log(token_size[section].astype(jnp.float32))
    hidden = inputs[section]
    kept, outs = [], []
    for layer in range(2):
        hidden = hidden.astype(jnp.float32)
        pieces = layer_pieces(hidden, weights[layer], ids, bias)
        branch = jnp.dot(pieces[8], weights[layer][1], preferred_element_type=jnp.float32)
        kept.append((hidden, pieces))
        hidden = (hidden + branch.reshape(hidden.shape)).astype(jnp.bfloat16)
        outs.append(hidden)
    grad_low = cotangent[section]
    grads, gain_terms, terms_in, terms_out = [None, None], [None, None], [None, None], [None, None]
    contract_rows = (((0,), (0,)), ((), ()))
    for layer in (1, 0):
        results = layer_backward(kept[layer][0], grad_low, kept[layer][1], weights[layer], ids, bias)
        grads[layer] = results[0]
        gain_terms[layer] = results[1:4]
        terms_in[layer] = lax.dot_general(results[4], results[5], contract_rows, preferred_element_type=jnp.bfloat16)
        terms_out[layer] = lax.dot_general(results[6], results[7], contract_rows, preferred_element_type=jnp.bfloat16)
        grad_low = results[0].astype(jnp.bfloat16)
    terms_in, terms_out = jnp.stack(terms_in), jnp.stack(terms_out)
    own_in = scatter_all(terms_in, 1).astype(jnp.float32)
    own_out = scatter_all(terms_out, 1).astype(jnp.float32)
    gain_rows = [
        jnp.stack([gain_terms[layer][position] for layer in range(2)]).reshape(2, wide, -1) for position in range(3)
    ]
    own_gains = scatter_all(jnp.concatenate(gain_rows, 2), 1)[:, 0]
    swap = [(0, 1), (1, 0)]

    def both_micro(pair):
        mine = jnp.where(section == 0, pair[0], pair[1])
        other = lax.ppermute(jnp.where(section == 0, pair[1], pair[0]).astype(jnp.bfloat16), "section", swap)
        other = other.astype(mine.dtype)
        return jnp.where(section == 0, jnp.stack([mine, other]), jnp.stack([other, mine]))[None]

    return (
        both_micro(outs),
        both_micro(grads),
        own_in,
        own_out,
        own_gains[:, : cuts[0]],
        own_gains[:, cuts[0] : cuts[1]],
        own_gains[:, cuts[1] :],
    )


def solution(mesh):
    return jax.shard_map(
        on_device,
        mesh=mesh,
        in_specs=(
            P(None, "wide", None, None),
            P(None, "wide", None, None),
            P(None, "wide", None),
            P(None, "wide", None),
            P("section", "wide", None),
            P("section", "wide", None),
            P("section", "wide"),
            P("section", "wide"),
            P("section", "wide"),
        ),
        out_specs=(
            P("section", None, "wide", None, None),
            P("section", None, "wide", None, None),
            P("section", "wide", None),
            P("section", "wide", None),
            P("section", "wide"),
            P("section", "wide"),
            P("section", "wide"),
        ),
        check_vma=False,
    )
```

```python
import functools

import jax
import jax.numpy as jnp
from jax import lax
from jax.experimental import pallas as pl
from jax.experimental.pallas import tpu as pltpu
from jax.sharding import PartitionSpec as P

HEADS = 12
HD = 64


EPSILON = 1e-06
NEGATIVE = -1e30


def layer_norm(values, gain_vec):
    average = jnp.mean(values, -1, keepdims=True)
    centred = values - average
    variance = jnp.mean(centred * centred, -1, keepdims=True)
    return centred * lax.rsqrt(variance + EPSILON) * gain_vec


def exact_gelu(values):
    return jax.nn.gelu(values, approximate=False)


def head_norms(queries, keys_in, query_gain, key_gain):
    return (layer_norm(queries, query_gain), layer_norm(keys_in, key_gain))


def score_rows(queries, keys_in, image_ids, key_bias):
    scores = (
        jnp.einsum("qhd,khd->hqk", queries, keys_in, preferred_element_type=jnp.float32) * 0.125
        + key_bias[None, None, :]
    )
    same_image = image_ids[:, None] == image_ids[None, :]
    return jnp.where(same_image[None], scores, NEGATIVE)


def attend_forward(row_block):
    queries, keys_in, values, image_ids, key_bias = row_block
    scores = score_rows(queries, keys_in, image_ids, key_bias)
    largest = jnp.max(scores, -1, keepdims=True)
    exponent = jnp.exp(scores - largest)
    row_total = jnp.sum(exponent, -1, keepdims=True)
    weights = (exponent / row_total).astype(jnp.bfloat16)
    output = jnp.einsum("hqk,khd->qhd", weights, values, preferred_element_type=jnp.float32)
    return (output, largest + jnp.log(row_total))


def attend_backward(row_block):
    queries, keys_in, values, image_ids, key_bias, log_total, grad_out = row_block
    scores = score_rows(queries, keys_in, image_ids, key_bias)
    probabilities = jnp.exp(scores - log_total)
    grad_values = jnp.einsum(
        "hqk,qhd->khd",
        probabilities.astype(jnp.bfloat16),
        grad_out,
        preferred_element_type=jnp.float32,
    )
    grad_probs = jnp.einsum("qhd,khd->hqk", grad_out, values, preferred_element_type=jnp.float32)
    grad_scores = probabilities * (
        grad_probs - jnp.sum(probabilities * grad_probs, -1, keepdims=True)
    )
    grad_scores = grad_scores.astype(jnp.bfloat16)
    grad_queries = (
        jnp.einsum("hqk,khd->qhd", grad_scores, keys_in, preferred_element_type=jnp.float32) * 0.125
    )
    grad_keys = (
        jnp.einsum("hqk,qhd->khd", grad_scores, queries, preferred_element_type=jnp.float32) * 0.125
    )
    return (grad_queries, grad_keys, grad_values)


def layer_pieces(hidden, weights, image_ids, key_bias):
    w_in, w_out, ln_gain, q_gain, k_gain = weights
    row_count, slot_count, model_width = hidden.shape
    normed, norm_back = jax.vjp(layer_norm, hidden, ln_gain.astype(jnp.float32))
    normed_low = normed.astype(jnp.bfloat16).reshape(row_count * slot_count, model_width)
    projected = jnp.dot(normed_low, w_in, preferred_element_type=jnp.float32)
    head_shape = (row_count, slot_count, HEADS, HD)
    queries = projected[:, :model_width].reshape(head_shape)
    keys_in = projected[:, model_width : 2 * model_width].reshape(head_shape)
    values = (
        projected[:, 2 * model_width : 3 * model_width].reshape(head_shape).astype(jnp.bfloat16)
    )
    normed_heads, norms_back = jax.vjp(
        head_norms, queries, keys_in, q_gain.astype(jnp.float32), k_gain.astype(jnp.float32)
    )
    queries_low = normed_heads[0].astype(jnp.bfloat16)
    keys_low = normed_heads[1].astype(jnp.bfloat16)
    attended, log_total = lax.map(
        attend_forward, (queries_low, keys_low, values, image_ids, key_bias)
    )
    activated, gelu_back = jax.vjp(exact_gelu, projected[:, 3 * model_width :])
    combined = jnp.concatenate(
        [attended.reshape(row_count * slot_count, model_width), activated], 1
    ).astype(jnp.bfloat16)
    return (
        norm_back,
        normed_low,
        norms_back,
        queries_low,
        keys_low,
        values,
        log_total,
        gelu_back,
        combined,
    )


def layer_backward(hidden, grad_low, pieces, weights, image_ids, key_bias):
    (
        norm_back,
        normed_low,
        norms_back,
        queries_low,
        keys_low,
        values,
        log_total,
        gelu_back,
        combined,
    ) = pieces
    row_count, slot_count, model_width = hidden.shape
    flat_rows = row_count * slot_count
    grad_flat = grad_low.reshape(flat_rows, model_width)
    contract_last = (((1,), (1,)), ((), ()))
    grad_combined = lax.dot_general(
        grad_flat, weights[1], contract_last, preferred_element_type=jnp.float32
    )
    grad_attended = (
        grad_combined[:, :model_width]
        .astype(jnp.bfloat16)
        .reshape(row_count, slot_count, HEADS, HD)
    )
    grad_up = gelu_back(grad_combined[:, model_width:])[0]
    grad_q, grad_k, grad_v = lax.map(
        attend_backward,
        (queries_low, keys_low, values, image_ids, key_bias, log_total, grad_attended),
    )
    grad_queries, grad_keys, grad_qgain, grad_kgain = norms_back((grad_q, grad_k))
    grad_projected = jnp.concatenate(
        [
            grad_queries.reshape(flat_rows, model_width),
            grad_keys.reshape(flat_rows, model_width),
            grad_v.reshape(flat_rows, model_width),
            grad_up,
        ],
        1,
    ).astype(jnp.bfloat16)
    grad_normed = lax.dot_general(
        grad_projected, weights[0], contract_last, preferred_element_type=jnp.float32
    )
    grad_hidden, grad_lngain = norm_back(grad_normed.reshape(hidden.shape))
    return (
        grad_low.astype(jnp.float32) + grad_hidden,
        grad_lngain,
        grad_qgain,
        grad_kgain,
        normed_low,
        grad_projected,
        combined,
        grad_flat,
    )


MESH = pl.DeviceIdType.MESH
NZ = 4
BLOCK = ((48, 5376), (240, 768))
CUT_IN, CUT_OUT = 2176, 96
PART = ((48, CUT_IN), (CUT_OUT, 768))
REST = ((48, 5376 - 2 * CUT_IN), (240 - 2 * CUT_OUT, 768))


class Place:
    def __init__(self):
        self.x, self.wide = lax.axis_index("section"), lax.axis_index("wide")
        self.y, self.z, self.c = (self.wide // 2) % 2, self.wide // 4, self.wide % 2

    def at(self, x, y, z, c=None):
        return (x, z * 4 + y * 2 + (self.c if c is None else c))

    def along(self, colour, block_z, far_first, far_second):
        dx = jnp.where(colour == 0, far_first, far_second)
        dy = jnp.where(colour == 0, far_second, far_first)
        return self.flip(self.x, dx), self.flip(self.y, dy), block_z

    @staticmethod
    def flip(value, far):
        return value + far - 2 * value * far

    def first(self, colour):
        return self.at(*self.along(colour, self.z, 1, 0))

    def second(self, colour):
        return self.at(*self.along(colour, self.z, 0, 1))

    def sibling(self):
        return self.at(self.x, self.y, self.z, 1 - self.c)


def greet(place):
    barrier = pltpu.get_barrier_semaphore()
    x, y, z = place.x, place.y, place.z

    def signal(device):
        pl.semaphore_signal(barrier, inc=1, device_id=device, device_id_type=MESH)

    signal(place.at(1 - x, y, z))
    signal(place.at(x, 1 - y, z))
    signal(place.sibling())
    pl.when(z < NZ - 1)(lambda: signal(place.at(x, y, z + 1)))
    pl.when(z > 0)(lambda: signal(place.at(x, y, z - 1)))
    pl.semaphore_wait(barrier, 3 + (z < NZ - 1).astype(jnp.int32) + (z > 0).astype(jnp.int32))


def number_of(block):
    return block[0] * 8 + block[1] * 4 + block[2]


def cut(ref, array, colour):
    rows, cols = BLOCK[array]
    if array == 0:
        if colour is None:
            return ref.at[:, pl.ds(2 * CUT_IN, cols - 2 * CUT_IN)]
        return ref.at[:, pl.ds(pl.multiple_of(colour * CUT_IN, 128), CUT_IN)]
    if colour is None:
        return ref.at[pl.ds(2 * CUT_OUT, rows - 2 * CUT_OUT), :]
    return ref.at[pl.ds(pl.multiple_of(colour * CUT_OUT, 16), CUT_OUT), :]


def loop(count, body):
    def step(index, carry):
        body(index)
        return carry
    lax.fori_loop(0, count, step, 0)


class Gather:
    def __init__(self, place, array, own, full, send_sem, recv_sem, core_sem):
        self.place, self.array, self.own, self.full = place, array, own, full
        self.send_sem, self.recv_sem, self.core_sem = send_sem, recv_sem, core_sem

    def view(self, block, colour, plane=None):
        rows = BLOCK[self.array][0]
        place = self.place
        start = (block[2] * 4 + block[1] * 2 + (place.c if plane is None else plane)) * rows
        return cut(self.full.at[block[0], pl.ds(pl.multiple_of(start, 16), rows), :], self.array, colour)

    def copy(self, link, device, block, colour, own=False, other_plane=False):
        kind = 2 if colour is None else colour
        number = number_of(block)
        target = self.view(block, colour, 1 - self.place.c if other_plane else None)
        source = cut(self.own, self.array, colour) if own else target
        sems = self.core_sem if link == 4 else self.recv_sem
        return pltpu.make_async_remote_copy(
            src_ref=source, dst_ref=target, send_sem=self.send_sem.at[link, kind, number], recv_sem=sems.at[kind, number],
            device_id=device, device_id_type=MESH)

    def visit(self, block, colour, onward, first, second, drain, condition=None, own=False):
        place = self.place

        def body():
            if not drain and not own:
                self.copy(0, place.sibling(), block, colour).wait_recv()

            def send(link, device):
                copy = self.copy(link, device, block, colour, own)
                copy.wait_send() if drain else copy.start()

            for link, step in onward:
                target = place.z + step
                pl.when((target >= 0) & (target < NZ))(functools.partial(send, link, place.at(place.x, place.y, target)))
            if first is not None:
                send(2, first)
            if second is not None:
                if isinstance(second, tuple) and len(second) == 3:
                    pl.when(second[2])(functools.partial(send, 3, second[:2]))
                else:
                    send(3, second)
            send(4, place.sibling())
        if condition is None:
            body()
        else:
            pl.when(condition)(body)

    def begin(self, drain=False):
        place = self.place
        me = (place.x, place.y, place.z)
        everywhere = ((0, 1), (1, -1))
        self.visit(me, None, everywhere, place.at(1 - place.x, place.y, place.z), place.at(place.x, 1 - place.y, place.z), drain, own=True)

        def body(colour):
            self.visit(me, colour, everywhere, place.first(colour), place.second(colour), drain, own=True)
        loop(2, body)

    def square(self, drain=False):
        place = self.place

        def body(index):
            far_x, far_y = (index != 1).astype(jnp.int32), (index != 0).astype(jnp.int32)
            block = (place.flip(place.x, far_x), place.flip(place.y, far_y), place.z)
            self.visit(block, None, ((0, 1), (1, -1)), None, place.at(place.x, 1 - place.y, place.z) + (index == 0,), drain)
        loop(3, body)

    def sided(self, distance, body):
        place = self.place

        def side_body(side):
            step = 1 - 2 * side
            block_z = place.z - step * distance
            body(side, block_z, (block_z >= 0) & (block_z < NZ) & ((distance > 0) | (side == 0)))
        loop(2, side_body)

    def onward(self, side):
        return ((0, 1), (1, -1))[side]

    def z_step(self, distance, drain=False):
        place = self.place
        for side in (0, 1):
            step = 1 - 2 * side
            block_z = place.z - step * distance

            def body(colour):
                self.visit((place.x, place.y, block_z), colour, ((side, step),), place.first(colour), place.second(colour), drain)
            pl.when((block_z >= 0) & (block_z < NZ))(lambda: loop(2, body))

    def line(self, distance, drain=False):
        place = self.place
        for side in (0, 1):
            step = 1 - 2 * side
            block_z = place.z - step * distance

            def body(index):
                block = (place.flip(place.x, index % 2), place.flip(place.y, index // 2), block_z)
                self.visit(block, None, ((side, step),), None, None, drain)
            pl.when((block_z >= 0) & (block_z < NZ))(lambda: loop(4, body))

    def a_step(self, distance, drain=False):
        place = self.place

        def body(side, block_z, there):
            def inner(colour):
                self.visit(place.along(colour, block_z, 1, 0), colour, (), None, place.second(colour), drain)
            pl.when(there)(lambda: loop(2, inner))
        self.sided(distance, body)

    def b_step(self, distance, drain=False):
        place = self.place

        def body(side, block_z, there):
            def inner(index):
                colour = index // 2
                self.visit(place.along(colour, block_z, index % 2, 1), colour, (), None, None, drain)
            pl.when(there)(lambda: loop(4, inner))
        self.sided(distance, body)

    def from_core(self):
        place = self.place

        def body(number):
            block = (number // 8, (number // 4) % 2, number % 4)
            self.copy(4, place.sibling(), block, None, other_plane=True).wait_recv()
            for colour in (0, 1):
                self.copy(4, place.sibling(), block, colour, other_plane=True).wait_recv()
        loop(16, body)

    def drain(self):
        self.begin(True)
        self.square(True)

        def body(index):
            self.z_step(index + 1, True)
            self.line(index + 1, True)
            self.a_step(index, True)
            self.b_step(index, True)
        loop(NZ, body)


def gather_kernel(w_in, w_out, full_in, full_out, *sems):
    place = Place()
    greet(place)
    first = Gather(place, 0, w_in, full_in, *sems[:3])
    second = Gather(place, 1, w_out, full_out, *sems[3:6])
    copies = []
    for array, (own, full) in enumerate(((w_in, full_in), (w_out, full_out))):
        rows = BLOCK[array][0]
        copy = pltpu.make_async_copy(own, full.at[place.x, pl.ds(pl.multiple_of(place.wide * rows, 16), rows), :], sems[6].at[array])
        copy.start()
        copies.append(copy)
    first.begin()
    first.square()

    def early(index):
        first.z_step(index + 1)
        first.a_step(index)
        first.line(index + 1)
    loop(NZ, early)
    second.begin()
    second.square()

    def late(index):
        first.b_step(index)
        second.z_step(index + 1)
        second.a_step(index)
        second.line(index + 1)
    loop(NZ, late)
    loop(NZ, second.b_step)
    first.from_core()
    second.from_core()
    for copy in copies:
        copy.wait()
    first.drain()
    second.drain()


def gather_weights(w_in, w_out):
    any_space = pl.BlockSpec(memory_space=pl.ANY)
    dma = pltpu.SemaphoreType.DMA
    return pl.pallas_call(
        gather_kernel,
        out_shape=(jax.ShapeDtypeStruct((2, 768, 5376), jnp.bfloat16), jax.ShapeDtypeStruct((2, 3840, 768), jnp.bfloat16)),
        in_specs=[any_space] * 2, out_specs=(any_space,) * 2,
        scratch_shapes=[dma((5, 3, 16)), dma((3, 16)), dma((3, 16))] * 2 + [dma((2,))],
        compiler_params=pltpu.CompilerParams(collective_id=0, has_side_effects=True),
        name="gather_weights",
    )(w_in, w_out)


def add_into(target, source):
    rows = target.shape[0]

    def body(step):
        part = pl.ds(pl.multiple_of(step * 16, 16), 16)
        target[part, :] = (target[part, :].astype(jnp.float32) + source[part, :].astype(jnp.float32)).astype(jnp.bfloat16)
    loop(rows // 16, body)


class Scatter:
    def __init__(self, place, array, terms, held, core_land, land, rest_land, sems):
        self.place, self.array, self.terms, self.held, self.core_land = place, array, terms, held, core_land
        self.land, self.rest_land = land, rest_land
        self.send_sem, self.recv_sem, self.rest_send, self.rest_recv, self.core_send, self.core_recv, self.local_sem = sems

    def part(self, block, colour):
        return cut(self.held.at[number_of(block)], self.array, colour)

    def copy(self, device, block, colour, slot):
        if colour is None:
            target, send_sem, recv_sem = self.rest_land.at[slot], self.rest_send.at[slot], self.rest_recv.at[slot]
        else:
            target, send_sem, recv_sem = self.land.at[colour, slot], self.send_sem.at[colour, slot], self.recv_sem.at[colour, slot]
        return pltpu.make_async_remote_copy(
            src_ref=self.part(block, colour), dst_ref=target, send_sem=send_sem, recv_sem=recv_sem, device_id=device,
            device_id_type=MESH)

    def send(self, device, block, colour, slot, drain):
        copy = self.copy(device, block, colour, slot)
        copy.wait_send() if drain else copy.start()

    def arrive(self, block, colour, slot, drain):
        if not drain:
            self.copy(self.place.sibling(), block, colour, slot).wait_recv()
            add_into(self.part(block, colour), self.rest_land.at[slot] if colour is None else self.land.at[colour, slot])

    def core_copy(self, block, mine):
        rows = BLOCK[self.array][0]
        place = self.place
        number = number_of(block)
        start = (block[2] * 4 + block[1] * 2 + (place.c if mine else 1 - place.c)) * rows
        source = self.terms.at[block[0], pl.ds(pl.multiple_of(start, 16), rows), :]
        if mine:
            return pltpu.make_async_copy(source, self.held.at[number], self.local_sem.at[number])
        return pltpu.make_async_remote_copy(
            src_ref=source, dst_ref=self.core_land.at[number], send_sem=self.core_send.at[number],
            recv_sem=self.core_recv.at[number], device_id=place.sibling(), device_id_type=MESH)

    def sided(self, distance, body):
        place = self.place

        def side_body(side):
            block_z = place.z + (2 * side - 1) * distance
            there = (block_z >= 0) & (block_z < NZ) & (distance < NZ) & (distance >= 0) & ((distance > 0) | (side == 0))
            pl.when(there)(lambda: body(block_z))
        loop(2, side_body)

    def start(self, distance):
        place = self.place

        def body(block_z):
            def inner(index):
                block = (place.flip(place.x, 1 - index % 2), place.flip(place.y, 1 - index // 2), block_z)
                self.core_copy(block, False).start()
                self.core_copy(block, True).start()
            loop(4, inner)
        self.sided(distance, body)

    def k_step(self, distance, drain=False):
        place = self.place

        def body(block_z):
            def inner(index):
                far_x, far_y = 1 - index % 2, 1 - index // 2
                block = (place.flip(place.x, far_x), place.flip(place.y, far_y), block_z)
                if not drain:
                    self.core_copy(block, True).wait()
                    copy = self.core_copy(block, False)
                    copy.wait_recv()
                    add_into(self.held.at[number_of(block)], self.core_land.at[number_of(block)])
                    copy.wait_send()

                def out(colour):
                    far_first = jnp.where(colour == 0, far_x, far_y)
                    far_second = jnp.where(colour == 0, far_y, far_x)
                    pl.when(far_second == 1)(lambda: self.send(place.second(colour), block, colour, far_first * 4 + block_z, drain))
                loop(2, out)
            loop(4, inner)
        self.sided(distance, body)

    def a_step(self, distance, drain=False):
        place = self.place

        def body(block_z):
            def inner(index):
                colour, far_first = index % 2, 1 - index // 2
                block = place.along(colour, block_z, far_first, 0)
                self.arrive(block, colour, far_first * 4 + block_z, drain)
                pl.when(far_first == 1)(lambda: self.send(place.first(colour), block, colour, 8 + block_z, drain))
            loop(4, inner)
        self.sided(distance, body)

    def b_step(self, distance):
        place = self.place

        def body(block_z):
            loop(2, lambda colour: self.arrive((place.x, place.y, block_z), colour, 8 + block_z, False))
        self.sided(distance, body)

    def toward(self, distance, body):
        place = self.place
        for side, step in ((0, -1), (1, 1)):
            block_z, behind = place.z + step * distance, place.z - step
            there = (block_z >= 0) & (block_z < NZ) & (distance < NZ) & (distance >= 0)
            pl.when(there)(functools.partial(body, block_z, side, step, (behind >= 0) & (behind < NZ)))

    def z_step(self, distance, drain=False):
        place = self.place

        def body(block_z, side, step, more):
            block = (place.x, place.y, block_z)
            slot = 12 + 4 * side + block_z

            def inner(colour):
                pl.when(more)(lambda: self.arrive(block, colour, slot, drain))
                pl.when(distance > 0)(lambda: self.send(place.at(place.x, place.y, place.z + step), block, colour, slot, drain))
            loop(2, inner)
        self.toward(distance, body)

    def line(self, distance, drain=False):
        place = self.place

        def body(block_z, side, step, more):
            def inner(index):
                block = (place.flip(place.x, 1 - index % 2), place.flip(place.y, 1 - index // 2), block_z)
                slot = 16 * side + number_of(block)
                pl.when(more)(lambda: self.arrive(block, None, slot, drain))
                pl.when(distance > 0)(lambda: self.send(place.at(place.x, place.y, place.z + step), block, None, slot, drain))
            loop(4, inner)
        self.toward(distance, body)

    def square(self, drain=False):
        place = self.place
        over_x, over_y = place.at(1 - place.x, place.y, place.z), place.at(place.x, 1 - place.y, place.z)
        far = (1 - place.x, place.y, place.z)
        self.send(over_y, (1 - place.x, 1 - place.y, place.z), None, 33, drain)
        self.send(over_y, (place.x, 1 - place.y, place.z), None, 32, drain)
        self.arrive(far, None, 33, drain)
        self.send(over_x, far, None, 34, drain)
        self.arrive((place.x, place.y, place.z), None, 32, drain)
        self.arrive((place.x, place.y, place.z), None, 34, drain)

    def drain(self):
        def body(distance):
            self.k_step(distance, True)
            self.a_step(distance, True)
            self.z_step(distance, True)
            self.line(distance, True)
        loop(NZ, body)
        self.square(True)


def scatter_kernel(terms_in, terms_out, out_in, out_out, *rest):
    place = Place()
    greet(place)
    arrays = [Scatter(place, array, (terms_in, terms_out)[array], *rest[4 * array : 4 * array + 4], rest[8 + 7 * array : 15 + 7 * array])
              for array in range(2)]
    order = arrays[::-1]

    def begin(index):
        for array in order:
            array.start(NZ - 1 - index)
    loop(NZ, begin)

    def body(index):
        distance = NZ - 1 - index
        for array in order:
            array.k_step(distance)
        for array in order:
            array.line(distance + 1)
        for array in order:
            array.a_step(distance + 1)
        for array in order:
            array.b_step(distance + 2)
            array.z_step(distance + 2)
    loop(NZ + 2, body)
    for array in order:
        array.square()
    for array, out in zip(arrays, (out_in, out_out)):
        number = number_of((place.x, place.y, place.z))

        def last(step):
            part = pl.ds(pl.multiple_of(step * 16, 16), 16)
            out[part, :] = array.held[number, part, :].astype(jnp.float32)
        loop(out.shape[0] // 16, last)
    for array in order:
        array.drain()


def scatter_terms(terms_in, terms_out):
    any_space = pl.BlockSpec(memory_space=pl.ANY)
    vmem = pl.BlockSpec(memory_space=pltpu.VMEM)
    dma = pltpu.SemaphoreType.DMA
    buffers, sems = [], []
    for array in range(2):
        buffers += [pltpu.VMEM((16,) + BLOCK[array], jnp.bfloat16)] * 2
        buffers += [pltpu.VMEM((2, 20) + PART[array], jnp.bfloat16), pltpu.VMEM((35,) + REST[array], jnp.bfloat16)]
        sems += [dma((2, 20)), dma((2, 20)), dma((35,)), dma((35,)), dma((16,)), dma((16,)), dma((16,))]
    return pl.pallas_call(
        scatter_kernel,
        out_shape=tuple(jax.ShapeDtypeStruct(block, jnp.float32) for block in BLOCK),
        in_specs=[any_space] * 2, out_specs=(vmem,) * 2,
        scratch_shapes=buffers + sems,
        compiler_params=pltpu.CompilerParams(collective_id=1, has_side_effects=True, vmem_limit_bytes=58 * 2**20),
        name="scatter_terms",
    )(terms_in, terms_out)


def gather_all(piece, axis):
    return lax.all_gather(lax.all_gather(piece, "wide", axis=axis, tiled=True), "section", axis=0, tiled=True)


def scatter_all(terms, axis):
    own = lax.psum_scatter(terms, "section", scatter_dimension=0, tiled=True)
    return lax.psum_scatter(own, "wide", scatter_dimension=axis, tiled=True)


def on_device(inputs, cotangent, token_size, image_id, w_in, w_out, ln_gain, q_gain, k_gain):
    section = lax.axis_index("section")
    wide = lax.axis_size("wide")
    model_width = inputs.shape[3]
    blocks_fit = wide == 16 and w_in.shape[1] == BLOCK[0][0] and w_out.shape[1] == BLOCK[1][0]
    if blocks_fit:
        full_in, full_out = gather_weights(w_in[0], w_out[0])
    else:
        full_in, full_out = gather_all(w_in, 1), gather_all(w_out, 1)
    cuts = (ln_gain.shape[1], ln_gain.shape[1] + q_gain.shape[1])
    gains = gather_all(jnp.concatenate([ln_gain, q_gain, k_gain], 1)[:, None], 1)
    full_ln, full_q, full_k = [
        part.reshape(2, -1) for part in (gains[:, :, : cuts[0]], gains[:, :, cuts[0] : cuts[1]], gains[:, :, cuts[1] :])
    ]
    weights = [(full_in[layer], full_out[layer], full_ln[layer], full_q[layer], full_k[layer]) for layer in range(2)]
    ids = image_id[section]
    bias = jnp.log(token_size[section].astype(jnp.float32))
    hidden = inputs[section]
    kept, outs = [], []
    for layer in range(2):
        hidden = hidden.astype(jnp.float32)
        pieces = layer_pieces(hidden, weights[layer], ids, bias)
        branch = jnp.dot(pieces[8], weights[layer][1], preferred_element_type=jnp.float32)
        kept.append((hidden, pieces))
        hidden = (hidden + branch.reshape(hidden.shape)).astype(jnp.bfloat16)
        outs.append(hidden)
    grad_low = cotangent[section]
    grads, gain_terms, terms_in, terms_out = [None, None], [None, None], [None, None], [None, None]
    contract_rows = (((0,), (0,)), ((), ()))
    for layer in (1, 0):
        results = layer_backward(kept[layer][0], grad_low, kept[layer][1], weights[layer], ids, bias)
        grads[layer] = results[0]
        gain_terms[layer] = results[1:4]
        terms_in[layer] = lax.dot_general(results[4], results[5], contract_rows, preferred_element_type=jnp.bfloat16)
        terms_out[layer] = lax.dot_general(results[6], results[7], contract_rows, preferred_element_type=jnp.bfloat16)
        grad_low = results[0].astype(jnp.bfloat16)
    terms_in, terms_out = jnp.stack(terms_in), jnp.stack(terms_out)
    if blocks_fit:
        own_in, own_out = scatter_terms(terms_in, terms_out)
        own_in, own_out = own_in[None], own_out[None]
    else:
        own_in = scatter_all(terms_in, 1).astype(jnp.float32)
        own_out = scatter_all(terms_out, 1).astype(jnp.float32)
    gain_rows = [
        jnp.stack([gain_terms[layer][position] for layer in range(2)]).reshape(2, wide, -1) for position in range(3)
    ]
    own_gains = scatter_all(jnp.concatenate(gain_rows, 2), 1)[:, 0]
    swap = [(0, 1), (1, 0)]

    def both_micro(pair):
        mine = jnp.where(section == 0, pair[0], pair[1])
        other = lax.ppermute(jnp.where(section == 0, pair[1], pair[0]).astype(jnp.bfloat16), "section", swap)
        other = other.astype(mine.dtype)
        return jnp.where(section == 0, jnp.stack([mine, other]), jnp.stack([other, mine]))[None]

    return (
        both_micro(outs),
        both_micro(grads),
        own_in,
        own_out,
        own_gains[:, : cuts[0]],
        own_gains[:, cuts[0] : cuts[1]],
        own_gains[:, cuts[1] :],
    )


def solution(mesh):
    return jax.shard_map(
        on_device,
        mesh=mesh,
        in_specs=(
            P(None, "wide", None, None),
            P(None, "wide", None, None),
            P(None, "wide", None),
            P(None, "wide", None),
            P("section", "wide", None),
            P("section", "wide", None),
            P("section", "wide"),
            P("section", "wide"),
            P("section", "wide"),
        ),
        out_specs=(
            P("section", None, "wide", None, None),
            P("section", None, "wide", None, None),
            P("section", "wide", None),
            P("section", "wide", None),
            P("section", "wide"),
            P("section", "wide"),
            P("section", "wide"),
        ),
        check_vma=False,
    )
```

```python
import functools

import jax
import jax.numpy as jnp
import numpy as np
from jax import lax
from jax.experimental import pallas as pl
from jax.experimental.pallas import tpu as pltpu
from jax.sharding import PartitionSpec as P

MESH = pl.DeviceIdType.MESH
NZ = 4
BLOCK = ((48, 5376), (240, 768), (16, 128))
CUT_IN, CUT_OUT = 2176, 96
PART = ((48, CUT_IN), (CUT_OUT, 768))
REST = ((48, 5376 - 2 * CUT_IN), (240 - 2 * CUT_OUT, 768))


class Place:
    def __init__(self):
        self.x, self.wide = lax.axis_index("section"), lax.axis_index("wide")
        self.y, self.z, self.c = (self.wide // 2) % 2, self.wide // 4, self.wide % 2

    def at(self, x, y, z, c=None):
        return (x, z * 4 + y * 2 + (self.c if c is None else c))

    def along(self, colour, block_z, far_first, far_second):
        dx = jnp.where(colour == 0, far_first, far_second)
        dy = jnp.where(colour == 0, far_second, far_first)
        return self.flip(self.x, dx), self.flip(self.y, dy), block_z

    @staticmethod
    def flip(value, far):
        return value + far - 2 * value * far

    def first(self, colour):
        return self.at(*self.along(colour, self.z, 1, 0))

    def second(self, colour):
        return self.at(*self.along(colour, self.z, 0, 1))

    def sibling(self):
        return self.at(self.x, self.y, self.z, 1 - self.c)


def greet(place):
    barrier = pltpu.get_barrier_semaphore()
    x, y, z = place.x, place.y, place.z

    def signal(device):
        pl.semaphore_signal(barrier, inc=1, device_id=device, device_id_type=MESH)

    signal(place.at(1 - x, y, z))
    signal(place.at(x, 1 - y, z))
    signal(place.sibling())
    pl.when(z < NZ - 1)(lambda: signal(place.at(x, y, z + 1)))
    pl.when(z > 0)(lambda: signal(place.at(x, y, z - 1)))
    pl.semaphore_wait(barrier, 3 + (z < NZ - 1).astype(jnp.int32) + (z > 0).astype(jnp.int32))


def number_of(block):
    return block[0] * 8 + block[1] * 4 + block[2]


def cut(ref, array, colour):
    rows, cols = BLOCK[array]
    if array == 2:
        return ref
    if array == 0:
        if colour is None:
            return ref.at[:, pl.ds(2 * CUT_IN, cols - 2 * CUT_IN)]
        return ref.at[:, pl.ds(pl.multiple_of(colour * CUT_IN, 128), CUT_IN)]
    if colour is None:
        return ref.at[pl.ds(2 * CUT_OUT, rows - 2 * CUT_OUT), :]
    return ref.at[pl.ds(pl.multiple_of(colour * CUT_OUT, 16), CUT_OUT), :]


def loop(count, body):
    def step(index, carry):
        body(index)
        return carry
    lax.fori_loop(0, count, step, 0)


class Gather:
    def __init__(self, place, array, own, full, send_sem, recv_sem, core_sem):
        self.place, self.array, self.own, self.full = place, array, own, full
        self.send_sem, self.recv_sem, self.core_sem = send_sem, recv_sem, core_sem

    def view(self, block, colour, plane=None):
        rows = BLOCK[self.array][0]
        place = self.place
        start = (block[2] * 4 + block[1] * 2 + (place.c if plane is None else plane)) * rows
        return cut(self.full.at[block[0], pl.ds(pl.multiple_of(start, 16), rows), :], self.array, colour)

    def copy(self, link, device, block, colour, own=False, other_plane=False):
        kind = 2 if colour is None else colour
        number = number_of(block)
        target = self.view(block, colour, 1 - self.place.c if other_plane else None)
        source = cut(self.own, self.array, colour) if own else target
        sems = self.core_sem if link == 4 else self.recv_sem
        return pltpu.make_async_remote_copy(
            src_ref=source, dst_ref=target, send_sem=self.send_sem.at[link, kind, number], recv_sem=sems.at[kind, number],
            device_id=device, device_id_type=MESH)

    def visit(self, block, colour, onward, first, second, drain, condition=None, own=False):
        place = self.place

        def body():
            if not drain and not own:
                self.copy(0, place.sibling(), block, colour).wait_recv()

            def send(link, device):
                copy = self.copy(link, device, block, colour, own)
                copy.wait_send() if drain else copy.start()

            for link, step in onward:
                target = place.z + step
                pl.when((target >= 0) & (target < NZ))(functools.partial(send, link, place.at(place.x, place.y, target)))
            if first is not None:
                send(2, first)
            if second is not None:
                if isinstance(second, tuple) and len(second) == 3:
                    pl.when(second[2])(functools.partial(send, 3, second[:2]))
                else:
                    send(3, second)
            send(4, place.sibling())
        if condition is None:
            body()
        else:
            pl.when(condition)(body)

    def begin(self, drain=False):
        place = self.place
        me = (place.x, place.y, place.z)
        everywhere = ((0, 1), (1, -1))
        self.visit(me, None, everywhere, place.at(1 - place.x, place.y, place.z), place.at(place.x, 1 - place.y, place.z), drain, own=True)

        def body(colour):
            self.visit(me, colour, everywhere, place.first(colour), place.second(colour), drain, own=True)
        if self.array < 2:
            loop(2, body)

    def square(self, drain=False):
        place = self.place

        def body(index):
            far_x, far_y = (index != 1).astype(jnp.int32), (index != 0).astype(jnp.int32)
            block = (place.flip(place.x, far_x), place.flip(place.y, far_y), place.z)
            self.visit(block, None, ((0, 1), (1, -1)), None, place.at(place.x, 1 - place.y, place.z) + (index == 0,), drain)
        loop(3, body)

    def sided(self, distance, body):
        place = self.place

        def side_body(side):
            step = 1 - 2 * side
            block_z = place.z - step * distance
            body(side, block_z, (block_z >= 0) & (block_z < NZ) & ((distance > 0) | (side == 0)))
        loop(2, side_body)

    def onward(self, side):
        return ((0, 1), (1, -1))[side]

    def z_step(self, distance, drain=False):
        place = self.place
        for side in (0, 1):
            step = 1 - 2 * side
            block_z = place.z - step * distance

            def body(colour):
                self.visit((place.x, place.y, block_z), colour, ((side, step),), place.first(colour), place.second(colour), drain)
            pl.when((block_z >= 0) & (block_z < NZ))(lambda: loop(2, body))

    def line(self, distance, drain=False):
        place = self.place
        for side in (0, 1):
            step = 1 - 2 * side
            block_z = place.z - step * distance

            def body(index):
                block = (place.flip(place.x, index % 2), place.flip(place.y, index // 2), block_z)
                self.visit(block, None, ((side, step),), None, None, drain)
            pl.when((block_z >= 0) & (block_z < NZ))(lambda: loop(4, body))

    def a_step(self, distance, drain=False):
        place = self.place

        def body(side, block_z, there):
            def inner(colour):
                self.visit(place.along(colour, block_z, 1, 0), colour, (), None, place.second(colour), drain)
            pl.when(there)(lambda: loop(2, inner))
        self.sided(distance, body)

    def b_step(self, distance, drain=False):
        place = self.place

        def body(side, block_z, there):
            def inner(index):
                colour = index // 2
                self.visit(place.along(colour, block_z, index % 2, 1), colour, (), None, None, drain)
            pl.when(there)(lambda: loop(4, inner))
        self.sided(distance, body)

    def from_core(self):
        place = self.place

        def body(number):
            block = (number // 8, (number // 4) % 2, number % 4)
            self.copy(4, place.sibling(), block, None, other_plane=True).wait_recv()
            for colour in (0, 1) if self.array < 2 else ():
                self.copy(4, place.sibling(), block, colour, other_plane=True).wait_recv()
        loop(16, body)

    def drain(self):
        self.begin(True)
        self.square(True)

        def body(index):
            self.line(index + 1, True)
            if self.array < 2:
                self.z_step(index + 1, True)
                self.a_step(index, True)
                self.b_step(index, True)
        loop(NZ, body)


def gather_kernel(w_in, w_out, gains, full_in, full_out, full_gains, *sems):
    place = Place()
    greet(place)
    arrays = ((w_in, full_in), (w_out, full_out), (gains, full_gains))
    first, second, third = [Gather(place, array, *arrays[array], *sems[3 * array : 3 * array + 3]) for array in range(3)]
    copies = []
    for array, (own, full) in enumerate(arrays):
        rows = BLOCK[array][0]
        copy = pltpu.make_async_copy(own, full.at[place.x, pl.ds(pl.multiple_of(place.wide * rows, 16), rows), :], sems[9].at[array])
        copy.start()
        copies.append(copy)
    third.begin()
    first.begin()
    third.square()
    first.square()

    def early(index):
        first.z_step(index + 1)
        first.a_step(index)
        third.line(index + 1)
        first.line(index + 1)
    loop(NZ, early)
    second.begin()
    second.square()

    def late(index):
        first.b_step(index)
        second.z_step(index + 1)
        second.a_step(index)
        second.line(index + 1)
    loop(NZ, late)
    loop(NZ, second.b_step)
    for array in (third, first, second):
        array.from_core()
    for copy in copies:
        copy.wait()
    for array in (third, first, second):
        array.drain()


def gather_weights(w_in, w_out, gains):
    any_space = pl.BlockSpec(memory_space=pl.ANY)
    dma = pltpu.SemaphoreType.DMA
    return pl.pallas_call(
        gather_kernel,
        out_shape=tuple(jax.ShapeDtypeStruct(dims, jnp.bfloat16) for dims in ((2, 768, 5376), (2, 3840, 768), (2, 256, 128))),
        in_specs=[any_space] * 3, out_specs=(any_space,) * 3,
        scratch_shapes=[dma((5, 3, 16)), dma((3, 16)), dma((3, 16))] * 3 + [dma((3,))],
        compiler_params=pltpu.CompilerParams(collective_id=0, has_side_effects=True),
        name="gather_weights",
    )(w_in, w_out, gains)


def add_into(target, source):
    rows = target.shape[0]

    def body(step):
        part = pl.ds(pl.multiple_of(step * 16, 16), 16)
        target[part, :] = (target[part, :].astype(jnp.float32) + source[part, :].astype(jnp.float32)).astype(jnp.bfloat16)
    loop(rows // 16, body)


class Scatter:
    def __init__(self, place, array, terms, held, core_land, land, rest_land, sems):
        self.place, self.array, self.terms, self.held, self.core_land = place, array, terms, held, core_land
        self.land, self.rest_land = land, rest_land
        self.send_sem, self.recv_sem, self.rest_send, self.rest_recv, self.core_send, self.core_recv, self.local_sem = sems

    def part(self, block, colour):
        return cut(self.held.at[number_of(block)], self.array, colour)

    def copy(self, device, block, colour, slot):
        if colour is None:
            target, send_sem, recv_sem = self.rest_land.at[slot], self.rest_send.at[slot], self.rest_recv.at[slot]
        else:
            target, send_sem, recv_sem = self.land.at[colour, slot], self.send_sem.at[colour, slot], self.recv_sem.at[colour, slot]
        return pltpu.make_async_remote_copy(
            src_ref=self.part(block, colour), dst_ref=target, send_sem=send_sem, recv_sem=recv_sem, device_id=device,
            device_id_type=MESH)

    def send(self, device, block, colour, slot, drain):
        copy = self.copy(device, block, colour, slot)
        copy.wait_send() if drain else copy.start()

    def arrive(self, block, colour, slot, drain):
        if not drain:
            self.copy(self.place.sibling(), block, colour, slot).wait_recv()
            add_into(self.part(block, colour), self.rest_land.at[slot] if colour is None else self.land.at[colour, slot])

    def core_copy(self, block, mine):
        rows = BLOCK[self.array][0]
        place = self.place
        number = number_of(block)
        start = (block[2] * 4 + block[1] * 2 + (place.c if mine else 1 - place.c)) * rows
        source = self.terms.at[block[0], pl.ds(pl.multiple_of(start, 16), rows), :]
        if mine:
            return pltpu.make_async_copy(source, self.held.at[number], self.local_sem.at[number])
        return pltpu.make_async_remote_copy(
            src_ref=source, dst_ref=self.core_land.at[number], send_sem=self.core_send.at[number],
            recv_sem=self.core_recv.at[number], device_id=place.sibling(), device_id_type=MESH)

    def sided(self, distance, body):
        place = self.place

        def side_body(side):
            block_z = place.z + (2 * side - 1) * distance
            there = (block_z >= 0) & (block_z < NZ) & (distance < NZ) & (distance >= 0) & ((distance > 0) | (side == 0))
            pl.when(there)(lambda: body(block_z))
        loop(2, side_body)

    def start(self, distance):
        place = self.place

        def body(block_z):
            def inner(index):
                block = (place.flip(place.x, 1 - index % 2), place.flip(place.y, 1 - index // 2), block_z)
                self.core_copy(block, False).start()
                self.core_copy(block, True).start()
            loop(4, inner)
        self.sided(distance, body)

    def k_step(self, distance, drain=False):
        place = self.place

        def body(block_z):
            def inner(index):
                far_x, far_y = 1 - index % 2, 1 - index // 2
                block = (place.flip(place.x, far_x), place.flip(place.y, far_y), block_z)
                if not drain:
                    self.core_copy(block, True).wait()
                    copy = self.core_copy(block, False)
                    copy.wait_recv()
                    add_into(self.held.at[number_of(block)], self.core_land.at[number_of(block)])
                    copy.wait_send()

                def out(colour):
                    far_first = jnp.where(colour == 0, far_x, far_y)
                    far_second = jnp.where(colour == 0, far_y, far_x)
                    pl.when(far_second == 1)(lambda: self.send(place.second(colour), block, colour, far_first * 4 + block_z, drain))
                loop(2, out)
            loop(4, inner)
        self.sided(distance, body)

    def a_step(self, distance, drain=False):
        place = self.place

        def body(block_z):
            def inner(index):
                colour, far_first = index % 2, 1 - index // 2
                block = place.along(colour, block_z, far_first, 0)
                self.arrive(block, colour, far_first * 4 + block_z, drain)
                pl.when(far_first == 1)(lambda: self.send(place.first(colour), block, colour, 8 + block_z, drain))
            loop(4, inner)
        self.sided(distance, body)

    def b_step(self, distance):
        place = self.place

        def body(block_z):
            loop(2, lambda colour: self.arrive((place.x, place.y, block_z), colour, 8 + block_z, False))
        self.sided(distance, body)

    def toward(self, distance, body):
        place = self.place
        for side, step in ((0, -1), (1, 1)):
            block_z, behind = place.z + step * distance, place.z - step
            there = (block_z >= 0) & (block_z < NZ) & (distance < NZ) & (distance >= 0)
            pl.when(there)(functools.partial(body, block_z, side, step, (behind >= 0) & (behind < NZ)))

    def z_step(self, distance, drain=False):
        place = self.place

        def body(block_z, side, step, more):
            block = (place.x, place.y, block_z)
            slot = 12 + 4 * side + block_z

            def inner(colour):
                pl.when(more)(lambda: self.arrive(block, colour, slot, drain))
                pl.when(distance > 0)(lambda: self.send(place.at(place.x, place.y, place.z + step), block, colour, slot, drain))
            loop(2, inner)
        self.toward(distance, body)

    def line(self, distance, drain=False):
        place = self.place

        def body(block_z, side, step, more):
            def inner(index):
                block = (place.flip(place.x, 1 - index % 2), place.flip(place.y, 1 - index // 2), block_z)
                slot = 16 * side + number_of(block)
                pl.when(more)(lambda: self.arrive(block, None, slot, drain))
                pl.when(distance > 0)(lambda: self.send(place.at(place.x, place.y, place.z + step), block, None, slot, drain))
            loop(4, inner)
        self.toward(distance, body)

    def square(self, drain=False):
        place = self.place
        over_x, over_y = place.at(1 - place.x, place.y, place.z), place.at(place.x, 1 - place.y, place.z)
        far = (1 - place.x, place.y, place.z)
        self.send(over_y, (1 - place.x, 1 - place.y, place.z), None, 33, drain)
        self.send(over_y, (place.x, 1 - place.y, place.z), None, 32, drain)
        self.arrive(far, None, 33, drain)
        self.send(over_x, far, None, 34, drain)
        self.arrive((place.x, place.y, place.z), None, 32, drain)
        self.arrive((place.x, place.y, place.z), None, 34, drain)

    def drain(self):
        def body(distance):
            self.k_step(distance, True)
            self.a_step(distance, True)
            self.z_step(distance, True)
            self.line(distance, True)
        loop(NZ, body)
        self.square(True)


class Total:
    def __init__(self, place, own, out, run, land, send_sem, recv_sem):
        self.place, self.own, self.out, self.run, self.land = place, own, out, run, land
        self.send_sem, self.recv_sem = send_sem, recv_sem
        x, y, z = place.x, place.y, place.z
        self.routes = (place.sibling(), place.at(x, 1 - y, z), place.at(1 - x, y, z), place.at(x, y, z + 1), place.at(x, y, z - 1))
        self.sends = (None, None, None, z < NZ - 1, z > 0)
        self.gets = (None, None, None, z > 0, z < NZ - 1)

    def copy(self, link):
        source = self.own if link == 0 else self.run.at[link]
        return pltpu.make_async_remote_copy(
            src_ref=source, dst_ref=self.land.at[link], send_sem=self.send_sem.at[link], recv_sem=self.recv_sem.at[link],
            device_id=self.routes[link], device_id_type=MESH)

    def step(self, index):
        def chain(link, base):
            self.run[link] = base[...]

            def get():
                self.copy(link).wait_recv()
                self.run[link] += self.land[link]
            pl.when(self.gets[link])(get)
            pl.when(self.sends[link])(lambda: self.copy(link).start())

        def swap(link):
            if link:
                self.copy(link - 1).wait_recv()
                self.run[link] = (self.own[...] if link == 1 else self.run[link - 1]) + self.land[link - 1]
            if link < 3:
                self.copy(link).start()

        for link in range(3):
            pl.when(index == link)(functools.partial(swap, link))

        @pl.when(index == 3)
        def _():
            self.copy(2).wait_recv()
            self.out[...] = self.run[2] + self.land[2]
            chain(3, self.out)
            chain(4, self.out)
            self.out[...] = self.run[3]

            def add():
                self.out[...] += self.land[4]
            pl.when(self.gets[4])(add)

    def drain(self):
        for link, sent in enumerate(self.sends):
            if sent is None:
                self.copy(link).wait_send()
            else:
                pl.when(sent)(lambda: self.copy(link).wait_send())


def scatter_kernel(terms_in, terms_out, gains, out_in, out_out, out_gains, *rest):
    place = Place()
    greet(place)
    total = Total(place, gains, out_gains, *rest[22:26])
    arrays = [Scatter(place, array, (terms_in, terms_out)[array], *rest[4 * array : 4 * array + 4], rest[8 + 7 * array : 15 + 7 * array])
              for array in range(2)]
    order = arrays[::-1]

    def begin(index):
        for array in order:
            array.start(NZ - 1 - index)
    loop(NZ, begin)

    def body(index):
        distance = NZ - 1 - index
        for array in order:
            array.k_step(distance)
        total.step(index)
        for array in order:
            array.line(distance + 1)
        for array in order:
            array.a_step(distance + 1)
        for array in order:
            array.b_step(distance + 2)
            array.z_step(distance + 2)
    loop(NZ + 2, body)
    for array in order:
        array.square()
    for array, out in zip(arrays, (out_in, out_out)):
        number = number_of((place.x, place.y, place.z))

        def last(step):
            part = pl.ds(pl.multiple_of(step * 16, 16), 16)
            out[part, :] = array.held[number, part, :].astype(jnp.float32)
        loop(out.shape[0] // 16, last)
    for array in order:
        array.drain()
    total.drain()


def scatter_terms(terms_in, terms_out, gains):
    any_space = pl.BlockSpec(memory_space=pl.ANY)
    vmem = pl.BlockSpec(memory_space=pltpu.VMEM)
    dma = pltpu.SemaphoreType.DMA
    buffers, sems = [], []
    for array in range(2):
        buffers += [pltpu.VMEM((16,) + BLOCK[array], jnp.bfloat16)] * 2
        buffers += [pltpu.VMEM((2, 20) + PART[array], jnp.bfloat16), pltpu.VMEM((35,) + REST[array], jnp.bfloat16)]
        sems += [dma((2, 20)), dma((2, 20)), dma((35,)), dma((35,)), dma((16,)), dma((16,)), dma((16,))]
    small = [pltpu.VMEM((5,) + BLOCK[2], jnp.float32)] * 2 + [dma((5,))] * 2
    return pl.pallas_call(
        scatter_kernel,
        out_shape=tuple(jax.ShapeDtypeStruct(block, jnp.float32) for block in BLOCK),
        in_specs=[any_space] * 2 + [vmem], out_specs=(vmem,) * 3,
        scratch_shapes=buffers + sems + small,
        compiler_params=pltpu.CompilerParams(collective_id=1, has_side_effects=True, vmem_limit_bytes=58 * 2**20),
        name="scatter_terms",
    )(terms_in, terms_out, gains)


SLOTS, D, HD, PAIRS = 512, 768, 64, 6
WIDE_PAIRS = 3
TILES_IN, TILES_OUT = 7, 5
EPSILON = 1e-06
LOG2E = 1.4426950408889634
SCALE = 0.125 * LOG2E
APART = 256.0
F32, BF16 = jnp.float32, jnp.bfloat16
ACROSS, DOWN = ((1,), (1,)), ((0,), (0,))


def dot(a, b, dims=((1,), (0,))):
    return lax.dot_general(a, b, (dims, ((), ())), preferred_element_type=F32)


def split(value):
    high = value.astype(BF16)
    return high, (value - high.astype(F32)).astype(BF16)


def head_means(value, spread, exact=True):
    high, low = split(value)
    means = dot(high, spread)
    return means + dot(low, spread) if exact else means


def gelu_and_slope(x):
    t = 1.0 / (1.0 + (0.3275911 * 0.7071067811865476) * jnp.abs(x))
    bell = jnp.exp2((-0.5 * LOG2E) * (x * x))
    poly = t * (0.127414796 + t * (-0.142248368 + t * (0.7107068705 + t * (-0.7265760135 + t * 0.5307027145))))
    tail = poly * bell
    phi = jnp.where(x >= 0, 1.0 - tail, tail)
    return x * phi, phi + (0.3989422804014327 * x) * bell


def lanes(index, width):
    return pl.ds(pl.multiple_of(index * width, width), width)


PROJECT, OUTPUT, OUTPUT_BACK, BACK, PROJECT_BACK = range(5)
IN_ORDER = (3, 4, 5, 6, 0, 1, 2)


def plan():
    steps = [(PROJECT, 0, tile) for tile in range(TILES_IN)] + [(OUTPUT, 0, tile) for tile in range(TILES_OUT)]
    steps += [(PROJECT, 1, tile) for tile in range(TILES_IN)] + [(OUTPUT_BACK, 1, tile) for tile in range(TILES_OUT)]
    steps += [(PROJECT_BACK, 1, tile) for tile in IN_ORDER]
    steps += [(BACK, 0, tile) for tile in range(TILES_OUT)] + [(PROJECT_BACK, 0, tile) for tile in IN_ORDER]
    uses_in = [kind in (PROJECT, PROJECT_BACK) for kind, _, _ in steps]
    gives_in = [kind == PROJECT_BACK for kind, _, _ in steps]
    gives_out = [kind in (OUTPUT_BACK, BACK) for kind, _, _ in steps]

    def coming(used):
        table, now = [], None
        for step, use in zip(reversed(steps), reversed(used)):
            now = step[1:] if use else now
            table.append(now)
        table = table[::-1]
        last = [step[1:] for step, use in zip(steps, used) if use][-1]
        return [last if entry is None else entry for entry in table]

    def given(made):
        table, now = [], [step[1:] for step, use in zip(steps, made) if use][0]
        for step, use in zip(steps, made):
            now = step[1:] if use else now
            table.append(now)
        return table

    tables = [coming(uses_in), coming([not use for use in uses_in]), given(gives_in), given(gives_out)]
    columns = [[step[part] for step in steps] for part in range(3)]
    columns += [[entry[part] for entry in table] for table in tables for part in range(2)]
    return np.array(columns, np.int32)


def compute_kernel(plan_ref, h_ref, cot_ref, w_in_ref, w_out_ref, ln_ref, qg_ref, kg_ref, augq_ref, augk_ref, spread_ref,
                   out_ref, grad_ref, gain_ref, terms_in_ref, terms_out_ref,
                   hidden, normed, scale, q, k, v, rq, rk, linv, slope, combined, dy, dproj, acc, dq, dk, do, dhigh, dlow):
    t = pl.program_id(0)
    kind, layer, tile = plan_ref[0, t], plan_ref[1, t], plan_ref[2, t]
    spread = spread_ref[...]

    def halves(width=256):
        def run(body):
            def step(index):
                body(pl.ds(pl.multiple_of((index % 2) * 256, 256), 256), lanes(index // 2, width))
            loop(2 * D // width, step)
        return run

    def by_rows(body):
        loop(SLOTS // 128, lambda index: body(pl.ds(pl.multiple_of(index * 128, 128), 128)))

    @pl.when(t == 0)
    def _():
        hidden[0] = h_ref[...]
        gain_ref[...] = jnp.zeros_like(gain_ref)

    def low_lanes():
        return lax.broadcasted_iota(jnp.int32, (SLOTS, 128), 1) < HD

    @pl.when((kind == PROJECT) & (tile == 0))
    def _():
        def body(rows):
            h = hidden[layer, rows, :].astype(F32)
            centred = h - jnp.mean(h, -1, keepdims=True)
            root = lax.rsqrt(jnp.mean(centred * centred, -1, keepdims=True) + EPSILON)
            scale[layer, rows, :] = jnp.broadcast_to(root, (128, 128))
            normed[layer, rows, :] = (centred * root * ln_ref[layer]).astype(BF16)
        by_rows(body)

    @pl.when(kind == PROJECT)
    def _():
        acc[...] = dot(normed[layer], w_in_ref[...])

        def heads(low_ref, root_ref, gain, factor):
            @halves()
            def _(rows, columns):
                x = acc[rows, columns]
                centred = x - head_means(x, spread)
                root = lax.rsqrt(head_means(centred * centred, spread, False) + EPSILON)
                root_ref[layer, rows, columns] = root.astype(BF16)
                low_ref[layer, rows, columns] = (centred * root * (gain * factor)).astype(BF16)

        pl.when(tile == 0)(lambda: heads(q, rq, qg_ref[layer], SCALE))
        pl.when(tile == 1)(lambda: heads(k, rk, kg_ref[layer], 1.0))

        @pl.when(tile == 2)
        def _():
            v[layer] = acc[...].astype(BF16)
            low = low_lanes()
            augq, augk = augq_ref[...], augk_ref[...]
            ones = jnp.ones((SLOTS, 128), BF16)

            def pair(index):
                part = lanes(index, 128)
                qp, kp, vp = q[layer, :, part], k[layer, :, part], v[layer, :, part]
                results = []
                for head in (0, 1):
                    mine = low if head == 0 else ~low
                    scores = dot(jnp.where(mine, qp, augq), jnp.where(mine, kp, augk), ACROSS)
                    results.append(dot(jnp.exp2(scores).astype(BF16), jnp.where(mine, vp, ones)))
                inverse = 1.0 / pltpu.roll(jnp.where(low, results[1], results[0]), HD, 1)
                linv[layer, :, part] = inverse
                combined[layer, 0, :, part] = (jnp.where(low, results[0], results[1]) * inverse).astype(BF16)
            loop(PAIRS, pair)

        @pl.when(tile > 2)
        def _():
            @halves()
            def _(rows, columns):
                value, rise = gelu_and_slope(acc[rows, columns])
                slope[layer, tile - 3, rows, columns] = rise.astype(BF16)
                combined[layer, tile - 2, rows, columns] = value.astype(BF16)

    @pl.when((kind == OUTPUT) | (kind == OUTPUT_BACK))
    def _():
        product = dot(combined[layer, tile], w_out_ref[...])
        pl.when(tile == 0)(lambda: dq.__setitem__(..., hidden[layer].astype(F32) + product))
        pl.when(tile > 0)(lambda: dq.__setitem__(..., dq[...] + product))

        @pl.when(tile == TILES_OUT - 1)
        def _():
            result = dq[...].astype(BF16)
            out_ref[layer] = result
            pl.when(layer == 0)(lambda: hidden.__setitem__(1, result))

    @pl.when((kind == OUTPUT_BACK) & (tile == 0))
    def _():
        dy[...] = cot_ref[...]

    @pl.when((kind == OUTPUT_BACK) | (kind == BACK))
    def _():
        acc[...] = dot(dy[...], w_out_ref[...], ACROSS)
        terms_out_ref[...] = dot(combined[layer, tile], dy[...], DOWN).astype(BF16)

        @pl.when(tile == 0)
        def _():
            @halves()
            def _(rows, columns):
                grad, inverse = acc[rows, columns], linv[layer, rows, columns]
                do[rows, columns] = (grad * inverse).astype(BF16)
                total = head_means(grad * combined[layer, 0, rows, columns].astype(F32), spread) * (inverse * -HD)
                for half in (0, 128):
                    part = pl.ds(pl.multiple_of(columns.start + half, 128), 128)
                    high, low = split(pltpu.roll(total[:, half : half + 128], HD, 1))
                    dhigh[rows, part] = high
                    dlow[rows, part] = low

        @pl.when(tile > 0)
        def _():
            @halves()
            def _(rows, columns):
                dproj[tile + 2, rows, columns] = (acc[rows, columns] * slope[layer, tile - 1, rows, columns].astype(F32)).astype(BF16)

    @pl.when((kind == PROJECT_BACK) & (tile == 0))
    def _():
        low = low_lanes()
        spot = lax.broadcasted_iota(jnp.int32, (SLOTS, 128), 1) % HD
        first = spot == 0
        augv = jnp.where(spot < 2, 1.0, 0.0).astype(BF16)
        augq, augk = augq_ref[...], augk_ref[...]
        none = jnp.zeros((SLOTS, 128), BF16)

        def pair(index):
            part = lanes(index, 128)
            qp, kp, vp, dop = q[layer, :, part], k[layer, :, part], v[layer, :, part], do[:, part]
            augd = jnp.where(first, dhigh[:, part], dlow[:, part])
            sums = [None, None, None]
            for head in (0, 1):
                mine = low if head == 0 else ~low
                e = jnp.exp2(dot(jnp.where(mine, kp, augk), jnp.where(mine, qp, augq), ACROSS))
                dp = dot(jnp.where(mine, vp, augv), jnp.where(mine, dop, augd), ACROSS)
                ds = (e * dp).astype(BF16)
                parts = (dot(ds, jnp.where(mine, kp, none), DOWN), dot(ds, jnp.where(mine, qp, none)),
                         dot(e.astype(BF16), jnp.where(mine, dop, none)))
                sums = [part_sum if total is None else total + part_sum for total, part_sum in zip(sums, parts)]
            dq[:, part] = sums[0] * 0.125
            dk[:, part] = sums[1] * (1.0 / LOG2E)
            dproj[2, :, part] = sums[2].astype(BF16)
        loop(PAIRS, pair)
        for which, grads, low_ref, root_ref, gain, factor in ((0, dq, q, rq, qg_ref, SCALE), (1, dk, k, rk, kg_ref, 1.0)):
            @halves()
            def _(rows, columns):
                grad, gains = grads[rows, columns], gain[layer]
                xhat = low_ref[layer, rows, columns].astype(F32) * (1.0 / (gains * factor))
                scaled = grad * gains
                mean = head_means(scaled, spread, False)
                along = head_means(scaled * xhat, spread, False)
                dproj[which, rows, columns] = (root_ref[layer, rows, columns].astype(F32) * (scaled - mean - xhat * along)).astype(BF16)
                gain_ref[layer, which + 1 : which + 2, columns] += jnp.sum(grad * xhat, 0, keepdims=True)

    @pl.when(kind == PROJECT_BACK)
    def _():
        product = dot(dproj[tile], w_in_ref[...], ACROSS)
        pl.when(tile == IN_ORDER[0])(lambda: acc.__setitem__(..., product))
        pl.when(tile != IN_ORDER[0])(lambda: acc.__setitem__(..., acc[...] + product))
        terms_in_ref[...] = dot(normed[layer], dproj[tile], DOWN).astype(BF16)

        @pl.when(tile == IN_ORDER[-1])
        def _():
            gains = ln_ref[layer]

            def body(rows):
                grad = acc[rows, :]
                xhat = normed[layer, rows, :].astype(F32) * (1.0 / gains)
                scaled = grad * gains
                mean = jnp.mean(scaled, -1, keepdims=True)
                along = jnp.mean(scaled * xhat, -1, keepdims=True)
                total = dy[rows, :].astype(F32) + scale[layer, rows, :1] * (scaled - mean - xhat * along)
                grad_ref[layer, rows, :] = total
                dy[rows, :] = total.astype(BF16)
                gain_ref[layer, 0:1, :] += jnp.sum(grad * xhat, 0, keepdims=True)
            by_rows(body)


def both_layers(h, cot, full_in, full_out, ln, qg, kg, augq, augk, spread):
    table = plan()
    square = (SLOTS, D)

    def whole(*dims):
        return pl.BlockSpec(dims, lambda t, p: (0,) * len(dims))

    def tiled(row, by_rows):
        if by_rows:
            return pl.BlockSpec((None, D, D), lambda t, p: (p[row, t], p[row + 1, t], 0))
        return pl.BlockSpec((None, D, D), lambda t, p: (p[row, t], 0, p[row + 1, t]))

    low, wide = (lambda *dims: pltpu.VMEM(dims, BF16)), (lambda *dims: pltpu.VMEM(dims, F32))
    return pl.pallas_call(
        compute_kernel,
        grid_spec=pltpu.PrefetchScalarGridSpec(
            num_scalar_prefetch=1,
            grid=(table.shape[1],),
            in_specs=[
                whole(*square), whole(*square), tiled(3, False), tiled(5, True), whole(2, 1, D), whole(2, 1, 256), whole(2, 1, 256),
                whole(SLOTS, 128), whole(SLOTS, 128), whole(256, 256),
            ],
            out_specs=[whole(2, *square), whole(2, *square), whole(2, 8, D), tiled(7, False), tiled(9, True)],
            scratch_shapes=[
                low(2, *square), low(2, *square), wide(2, SLOTS, 128), low(2, *square), low(2, *square), low(2, *square), low(2, *square),
                low(2, *square), wide(2, *square), low(2, 4, *square), low(2, 5, *square), low(*square), low(7, *square), wide(*square),
                wide(*square), wide(*square), low(*square), low(*square), low(*square),
            ],
        ),
        out_shape=[
            jax.ShapeDtypeStruct((2,) + square, BF16), jax.ShapeDtypeStruct((2,) + square, F32), jax.ShapeDtypeStruct((2, 8, D), F32),
            jax.ShapeDtypeStruct(full_in.shape, BF16), jax.ShapeDtypeStruct(full_out.shape, BF16),
        ],
        compiler_params=pltpu.CompilerParams(vmem_limit_bytes=62 * 2**20),
        name="both_layers",
    )(jnp.asarray(table), h, cot, full_in, full_out, ln, qg, kg, augq, augk, spread)


def augment(image_id, token_size):
    high, low = split(jnp.log2(token_size.astype(F32)))
    same = (image_id[:, None] == jnp.arange(3)[None, :]).astype(BF16)
    one = jnp.ones_like(high)
    q = jnp.concatenate([one[:, None], one[:, None], same, one[:, None]], 1)
    k = jnp.concatenate([high[:, None], low[:, None], same * APART, one[:, None] * -APART], 1)
    return [jnp.tile(jnp.pad(part, ((0, 0), (0, HD - 6))), (1, 2)) for part in (q, k)]


def spread_matrix():
    head = jnp.arange(256) // HD
    return ((head[:, None] == head[None, :]) / HD).astype(BF16)


def gather_all(piece, axis):
    return lax.all_gather(lax.all_gather(piece, "wide", axis=axis, tiled=True), "section", axis=0, tiled=True)


def scatter_all(terms, axis):
    own = lax.psum_scatter(terms, "section", scatter_dimension=0, tiled=True)
    return lax.psum_scatter(own, "wide", scatter_dimension=axis, tiled=True)


def on_device(inputs, cotangent, token_size, image_id, w_in, w_out, ln_gain, q_gain, k_gain):
    section, wide = lax.axis_index("section"), lax.axis_index("wide")
    width = lax.axis_size("wide")
    blocks_fit = width == 16 and w_in.shape[1:] == BLOCK[0] and w_out.shape[1:] == BLOCK[1]
    ends = [0]
    for gain in (ln_gain, q_gain, k_gain):
        ends.append(ends[-1] + gain.shape[1])
    own_gains = jnp.concatenate([ln_gain, q_gain, k_gain], 1)
    if blocks_fit:
        padded = jnp.pad(own_gains, ((0, BLOCK[2][0] - 1), (0, BLOCK[2][1] - ends[3])))
        full_in, full_out, full_gains = gather_weights(w_in[0], w_out[0], padded)
        full_gains = full_gains.reshape((2, width) + BLOCK[2])[:, :, 0]
    else:
        full_in, full_out = gather_all(w_in, 1), gather_all(w_out, 1)
        full_gains = gather_all(own_gains[:, None], 1)
    ln, qg, kg = [full_gains[:, :, low:high].reshape(2, 1, -1).astype(F32) for low, high in zip(ends, ends[1:])]
    augq, augk = augment(image_id[section, 0], token_size[section, 0])
    outs, grads, gain_terms, terms_in, terms_out = both_layers(
        inputs[section, 0], cotangent[section, 0], full_in, full_out, ln, jnp.tile(qg, (1, 1, 4)), jnp.tile(kg, (1, 1, 4)),
        augq, augk, spread_matrix())
    swap = [(0, 1), (1, 0)]

    def both_micro(pair):
        mine = lax.dynamic_index_in_dim(pair, section, 0, False)
        other = lax.dynamic_index_in_dim(pair, 1 - section, 0, False).astype(BF16)
        other = lax.ppermute(other, "section", swap).astype(mine.dtype)
        return jnp.where(section == 0, jnp.stack([mine, other]), jnp.stack([other, mine]))[None, :, None]

    heads = gain_terms[:, 1:3].reshape(2, 2, -1, HD).sum(2).reshape(2, -1)
    totals = jnp.concatenate([gain_terms[:, 0], heads], 1)
    places = (0, D, D + HD, D + 2 * HD)
    if blocks_fit:
        totals = jnp.pad(totals, ((0, 0), (0, 1024 - places[3]))).reshape(BLOCK[2])
        own_in, own_out, totals = scatter_terms(terms_in, terms_out, totals)
        own_in, own_out = own_in[None], own_out[None]
        totals = totals.reshape(2, 1024)
    else:
        own_in = scatter_all(terms_in, 1).astype(F32)
        own_out = scatter_all(terms_out, 1).astype(F32)
        totals = lax.psum(totals, ("section", "wide"))
    mine = lax.dynamic_index_in_dim(totals, section, 0, False)
    gain_grads = [
        lax.dynamic_slice_in_dim(mine[low:high], wide * gain.shape[1], gain.shape[1])[None]
        for low, high, gain in zip(places, places[1:], (ln_gain, q_gain, k_gain))
    ]
    return (both_micro(outs), both_micro(grads), own_in, own_out, *gain_grads)


def solution(mesh):
    return jax.shard_map(
        on_device,
        mesh=mesh,
        in_specs=(
            P(None, "wide", None, None),
            P(None, "wide", None, None),
            P(None, "wide", None),
            P(None, "wide", None),
            P("section", "wide", None),
            P("section", "wide", None),
            P("section", "wide"),
            P("section", "wide"),
            P("section", "wide"),
        ),
        out_specs=(
            P("section", None, "wide", None, None),
            P("section", None, "wide", None, None),
            P("section", "wide", None),
            P("section", "wide", None),
            P("section", "wide"),
            P("section", "wide"),
            P("section", "wide"),
        ),
        check_vma=False,
    )
```

```python
import functools

import jax
import jax.numpy as jnp
from jax import lax
from jax.experimental import pallas as pl
from jax.experimental.pallas import tpu as pltpu
from jax.sharding import PartitionSpec as P

MESH = pl.DeviceIdType.MESH
NZ = 4
BLOCK = ((48, 5376), (240, 768), (16, 128))
GATHER_CUTS = (2176, 96)
SCATTER_CUTS = (2176, 96)


class Place:
    def __init__(self):
        self.x, self.wide = lax.axis_index("section"), lax.axis_index("wide")
        self.y, self.z, self.c = (self.wide // 2) % 2, self.wide // 4, self.wide % 2

    def at(self, x, y, z, c=None):
        return (x, z * 4 + y * 2 + (self.c if c is None else c))

    def along(self, colour, block_z, far_first, far_second):
        dx = jnp.where(colour == 0, far_first, far_second)
        dy = jnp.where(colour == 0, far_second, far_first)
        return self.flip(self.x, dx), self.flip(self.y, dy), block_z

    @staticmethod
    def flip(value, far):
        return value + far - 2 * value * far

    def first(self, colour):
        return self.at(*self.along(colour, self.z, 1, 0))

    def second(self, colour):
        return self.at(*self.along(colour, self.z, 0, 1))

    def sibling(self):
        return self.at(self.x, self.y, self.z, 1 - self.c)


def greet(place):
    barrier = pltpu.get_barrier_semaphore()
    x, y, z = place.x, place.y, place.z

    def signal(device):
        pl.semaphore_signal(barrier, inc=1, device_id=device, device_id_type=MESH)

    signal(place.at(1 - x, y, z))
    signal(place.at(x, 1 - y, z))
    signal(place.sibling())
    pl.when(z < NZ - 1)(lambda: signal(place.at(x, y, z + 1)))
    pl.when(z > 0)(lambda: signal(place.at(x, y, z - 1)))
    pl.semaphore_wait(barrier, 3 + (z < NZ - 1).astype(jnp.int32) + (z > 0).astype(jnp.int32))


def number_of(block):
    return block[0] * 8 + block[1] * 4 + block[2]


def part_shape(cuts, array, colour):
    rows, cols = BLOCK[array]
    size = cuts[array]
    if array == 0:
        return rows, cols - 2 * size if colour is None else size
    return rows - 2 * size if colour is None else size, cols


def cut(ref, cuts, array, colour):
    if array == 2:
        return ref
    rows, cols = part_shape(cuts, array, colour)
    size = cuts[array]
    if array == 0:
        return ref.at[:, pl.ds(2 * size if colour is None else pl.multiple_of(colour * size, 128), cols)]
    return ref.at[pl.ds(2 * size if colour is None else pl.multiple_of(colour * size, 16), rows), :]


def loop(count, body):
    def step(index, carry):
        body(index)
        return carry
    lax.fori_loop(0, count, step, 0)


class Gather:
    def __init__(self, place, array, own, full, send_sem, recv_sem, core_sem):
        self.place, self.array, self.own, self.full = place, array, own, full
        self.send_sem, self.recv_sem, self.core_sem = send_sem, recv_sem, core_sem

    def view(self, block, colour, plane=None):
        rows = BLOCK[self.array][0]
        place = self.place
        start = (block[2] * 4 + block[1] * 2 + (place.c if plane is None else plane)) * rows
        return cut(self.full.at[block[0], pl.ds(pl.multiple_of(start, 16), rows), :], GATHER_CUTS, self.array, colour)

    def copy(self, link, device, block, colour, own=False, other_plane=False):
        kind = 2 if colour is None else colour
        number = number_of(block)
        target = self.view(block, colour, 1 - self.place.c if other_plane else None)
        source = cut(self.own, GATHER_CUTS, self.array, colour) if own else target
        sems = self.core_sem if link == 4 else self.recv_sem
        return pltpu.make_async_remote_copy(
            src_ref=source, dst_ref=target, send_sem=self.send_sem.at[link, kind, number], recv_sem=sems.at[kind, number],
            device_id=device, device_id_type=MESH)

    def visit(self, block, colour, onward, first, second, drain, condition=None, own=False):
        place = self.place

        def body():
            if not drain and not own:
                self.copy(0, place.sibling(), block, colour).wait_recv()

            def send(link, device):
                copy = self.copy(link, device, block, colour, own)
                copy.wait_send() if drain else copy.start()

            for link, step in onward:
                target = place.z + step
                pl.when((target >= 0) & (target < NZ))(functools.partial(send, link, place.at(place.x, place.y, target)))
            if first is not None:
                send(2, first)
            if second is not None:
                if isinstance(second, tuple) and len(second) == 3:
                    pl.when(second[2])(functools.partial(send, 3, second[:2]))
                else:
                    send(3, second)
            send(4, place.sibling())
        if condition is None:
            body()
        else:
            pl.when(condition)(body)

    def begin(self, drain=False):
        place = self.place
        me = (place.x, place.y, place.z)
        everywhere = ((0, 1), (1, -1))
        self.visit(me, None, everywhere, place.at(1 - place.x, place.y, place.z), place.at(place.x, 1 - place.y, place.z), drain, own=True)

        def body(colour):
            self.visit(me, colour, everywhere, place.first(colour), place.second(colour), drain, own=True)
        if self.array < 2:
            loop(2, body)

    def square(self, drain=False):
        place = self.place

        def body(index):
            far_x, far_y = (index != 1).astype(jnp.int32), (index != 0).astype(jnp.int32)
            block = (place.flip(place.x, far_x), place.flip(place.y, far_y), place.z)
            self.visit(block, None, ((0, 1), (1, -1)), None, place.at(place.x, 1 - place.y, place.z) + (index == 0,), drain)
        loop(3, body)

    def sided(self, distance, body):
        place = self.place

        def side_body(side):
            step = 1 - 2 * side
            block_z = place.z - step * distance
            body(side, block_z, (block_z >= 0) & (block_z < NZ) & ((distance > 0) | (side == 0)))
        loop(2, side_body)

    def onward(self, side):
        return ((0, 1), (1, -1))[side]

    def z_step(self, distance, drain=False):
        place = self.place
        for side in (0, 1):
            step = 1 - 2 * side
            block_z = place.z - step * distance

            def body(colour):
                self.visit((place.x, place.y, block_z), colour, ((side, step),), place.first(colour), place.second(colour), drain)
            pl.when((block_z >= 0) & (block_z < NZ))(lambda: loop(2, body))

    def line(self, distance, drain=False):
        place = self.place
        for side in (0, 1):
            step = 1 - 2 * side
            block_z = place.z - step * distance

            def body(index):
                block = (place.flip(place.x, index % 2), place.flip(place.y, index // 2), block_z)
                self.visit(block, None, ((side, step),), None, None, drain)
            pl.when((block_z >= 0) & (block_z < NZ))(lambda: loop(4, body))

    def a_step(self, distance, drain=False):
        place = self.place

        def body(side, block_z, there):
            def inner(colour):
                self.visit(place.along(colour, block_z, 1, 0), colour, (), None, place.second(colour), drain)
            pl.when(there)(lambda: loop(2, inner))
        self.sided(distance, body)

    def b_step(self, distance, drain=False):
        place = self.place

        def body(side, block_z, there):
            def inner(index):
                colour = index // 2
                self.visit(place.along(colour, block_z, index % 2, 1), colour, (), None, None, drain)
            pl.when(there)(lambda: loop(4, inner))
        self.sided(distance, body)

    def from_core(self):
        place = self.place

        def body(number):
            block = (number // 8, (number // 4) % 2, number % 4)
            self.copy(4, place.sibling(), block, None, other_plane=True).wait_recv()
            for colour in (0, 1) if self.array < 2 else ():
                self.copy(4, place.sibling(), block, colour, other_plane=True).wait_recv()
        loop(16, body)

    def drain(self):
        self.begin(True)
        self.square(True)

        def body(index):
            self.line(index + 1, True)
            if self.array < 2:
                self.z_step(index + 1, True)
                self.a_step(index, True)
                self.b_step(index, True)
        loop(NZ, body)


def gather_kernel(w_in, w_out, gains, full_in, full_out, full_gains, *sems):
    place = Place()
    greet(place)
    arrays = ((w_in, full_in), (w_out, full_out), (gains, full_gains))
    first, second, third = [Gather(place, array, *arrays[array], *sems[3 * array : 3 * array + 3]) for array in range(3)]
    copies = []
    for array, (own, full) in enumerate(arrays):
        rows = BLOCK[array][0]
        copy = pltpu.make_async_copy(own, full.at[place.x, pl.ds(pl.multiple_of(place.wide * rows, 16), rows), :], sems[9].at[array])
        copy.start()
        copies.append(copy)
    third.begin()
    first.begin()
    third.square()
    first.square()

    def early(index):
        first.z_step(index + 1)
        first.a_step(index)
        third.line(index + 1)
        first.line(index + 1)
    loop(NZ, early)
    second.begin()
    second.square()

    def late(index):
        first.b_step(index)
        second.z_step(index + 1)
        second.a_step(index)
        second.line(index + 1)
    loop(NZ, late)
    loop(NZ, second.b_step)
    for array in (third, first, second):
        array.from_core()
    for copy in copies:
        copy.wait()
    for array in (third, first, second):
        array.drain()


def gather_weights(w_in, w_out, gains):
    any_space = pl.BlockSpec(memory_space=pl.ANY)
    dma = pltpu.SemaphoreType.DMA
    return pl.pallas_call(
        gather_kernel,
        out_shape=tuple(jax.ShapeDtypeStruct(dims, jnp.bfloat16) for dims in ((2, 768, 5376), (2, 3840, 768), (2, 256, 128))),
        in_specs=[any_space] * 3, out_specs=(any_space,) * 3,
        scratch_shapes=[dma((5, 3, 16)), dma((3, 16)), dma((3, 16))] * 3 + [dma((3,))],
        compiler_params=pltpu.CompilerParams(collective_id=0, has_side_effects=True),
        name="gather_weights",
    )(w_in, w_out, gains)


def add_into(target, source):
    rows = target.shape[0]

    def body(step):
        part = pl.ds(pl.multiple_of(step * 16, 16), 16)
        target[part, :] = (target[part, :].astype(jnp.float32) + source[part, :].astype(jnp.float32)).astype(jnp.bfloat16)
    loop(rows // 16, body)


class Scatter:
    def __init__(self, place, array, terms, held, core_land, land, rest_land, sems):
        self.place, self.array, self.terms, self.held, self.core_land = place, array, terms, held, core_land
        self.land, self.rest_land = land, rest_land
        self.send_sem, self.recv_sem, self.rest_send, self.rest_recv, self.core_send, self.core_recv, self.local_sem = sems

    def part(self, block, colour):
        return cut(self.held.at[number_of(block)], SCATTER_CUTS, self.array, colour)

    def copy(self, device, block, colour, slot):
        if colour is None:
            target, send_sem, recv_sem = self.rest_land.at[slot], self.rest_send.at[slot], self.rest_recv.at[slot]
        else:
            target, send_sem, recv_sem = self.land.at[colour * 20 + slot], self.send_sem.at[colour, slot], self.recv_sem.at[colour, slot]
        return pltpu.make_async_remote_copy(
            src_ref=self.part(block, colour), dst_ref=target, send_sem=send_sem, recv_sem=recv_sem, device_id=device,
            device_id_type=MESH)

    def send(self, device, block, colour, slot, drain):
        copy = self.copy(device, block, colour, slot)
        copy.wait_send() if drain else copy.start()

    def arrive(self, block, colour, slot, drain):
        if not drain:
            self.copy(self.place.sibling(), block, colour, slot).wait_recv()
            add_into(self.part(block, colour), self.rest_land.at[slot] if colour is None else self.land.at[colour * 20 + slot])

    def core_copy(self, block, mine):
        rows = BLOCK[self.array][0]
        place = self.place
        number = number_of(block)
        start = (block[2] * 4 + block[1] * 2 + (place.c if mine else 1 - place.c)) * rows
        source = self.terms.at[block[0], pl.ds(pl.multiple_of(start, 16), rows), :]
        if mine:
            return pltpu.make_async_copy(source, self.held.at[number], self.local_sem.at[number])
        return pltpu.make_async_remote_copy(
            src_ref=source, dst_ref=self.core_land.at[number], send_sem=self.core_send.at[number],
            recv_sem=self.core_recv.at[number], device_id=place.sibling(), device_id_type=MESH)

    def sided(self, distance, body):
        place = self.place

        def side_body(side):
            block_z = place.z + (2 * side - 1) * distance
            there = (block_z >= 0) & (block_z < NZ) & (distance < NZ) & (distance >= 0) & ((distance > 0) | (side == 0))
            pl.when(there)(lambda: body(block_z))
        loop(2, side_body)

    def start(self, distance):
        place = self.place

        def body(block_z):
            def inner(index):
                block = (place.flip(place.x, 1 - index % 2), place.flip(place.y, 1 - index // 2), block_z)
                self.core_copy(block, False).start()
                self.core_copy(block, True).start()
            loop(4, inner)
        self.sided(distance, body)

    def k_step(self, distance, drain=False):
        place = self.place

        def body(block_z):
            def inner(index):
                far_x, far_y = 1 - index % 2, 1 - index // 2
                block = (place.flip(place.x, far_x), place.flip(place.y, far_y), block_z)
                if not drain:
                    self.core_copy(block, True).wait()
                    copy = self.core_copy(block, False)
                    copy.wait_recv()
                    add_into(self.held.at[number_of(block)], self.core_land.at[number_of(block)])
                    copy.wait_send()

                def out(colour):
                    far_first = jnp.where(colour == 0, far_x, far_y)
                    far_second = jnp.where(colour == 0, far_y, far_x)
                    pl.when(far_second == 1)(lambda: self.send(place.second(colour), block, colour, far_first * 4 + block_z, drain))
                loop(2, out)
            loop(4, inner)
        self.sided(distance, body)

    def a_step(self, distance, drain=False):
        place = self.place

        def body(block_z):
            def inner(index):
                colour, far_first = index % 2, 1 - index // 2
                block = place.along(colour, block_z, far_first, 0)
                self.arrive(block, colour, far_first * 4 + block_z, drain)
                pl.when(far_first == 1)(lambda: self.send(place.first(colour), block, colour, 8 + block_z, drain))
            loop(4, inner)
        self.sided(distance, body)

    def b_step(self, distance):
        place = self.place

        def body(block_z):
            loop(2, lambda colour: self.arrive((place.x, place.y, block_z), colour, 8 + block_z, False))
        self.sided(distance, body)

    def toward(self, distance, body):
        place = self.place
        for side, step in ((0, -1), (1, 1)):
            block_z, behind = place.z + step * distance, place.z - step
            there = (block_z >= 0) & (block_z < NZ) & (distance < NZ) & (distance >= 0)
            pl.when(there)(functools.partial(body, block_z, side, step, (behind >= 0) & (behind < NZ)))

    def z_step(self, distance, drain=False):
        place = self.place

        def body(block_z, side, step, more):
            block = (place.x, place.y, block_z)
            slot = 12 + 4 * side + block_z

            def inner(colour):
                pl.when(more)(lambda: self.arrive(block, colour, slot, drain))
                pl.when(distance > 0)(lambda: self.send(place.at(place.x, place.y, place.z + step), block, colour, slot, drain))
            loop(2, inner)
        self.toward(distance, body)

    def line(self, distance, drain=False):
        place = self.place

        def body(block_z, side, step, more):
            def inner(index):
                block = (place.flip(place.x, 1 - index % 2), place.flip(place.y, 1 - index // 2), block_z)
                slot = 16 * side + number_of(block)
                pl.when(more)(lambda: self.arrive(block, None, slot, drain))
                pl.when(distance > 0)(lambda: self.send(place.at(place.x, place.y, place.z + step), block, None, slot, drain))
            loop(4, inner)
        self.toward(distance, body)

    def square(self, drain=False):
        place = self.place
        over_x, over_y = place.at(1 - place.x, place.y, place.z), place.at(place.x, 1 - place.y, place.z)
        far = (1 - place.x, place.y, place.z)
        self.send(over_y, (1 - place.x, 1 - place.y, place.z), None, 33, drain)
        self.send(over_y, (place.x, 1 - place.y, place.z), None, 32, drain)
        self.arrive(far, None, 33, drain)
        self.send(over_x, far, None, 34, drain)
        self.arrive((place.x, place.y, place.z), None, 32, drain)
        self.arrive((place.x, place.y, place.z), None, 34, drain)

    def drain(self):
        def body(distance):
            self.k_step(distance, True)
            self.a_step(distance, True)
            self.z_step(distance, True)
            self.line(distance, True)
        loop(NZ, body)
        self.square(True)


class Total:
    def __init__(self, place, own, out, run, land, send_sem, recv_sem):
        self.place, self.own, self.out, self.run, self.land = place, own, out, run, land
        self.send_sem, self.recv_sem = send_sem, recv_sem
        x, y, z = place.x, place.y, place.z
        self.routes = (place.sibling(), place.at(x, 1 - y, z), place.at(1 - x, y, z), place.at(x, y, z + 1), place.at(x, y, z - 1))
        self.sends = (None, None, None, z < NZ - 1, z > 0)
        self.gets = (None, None, None, z > 0, z < NZ - 1)

    def copy(self, link):
        source = self.own if link == 0 else self.run.at[link]
        return pltpu.make_async_remote_copy(
            src_ref=source, dst_ref=self.land.at[link], send_sem=self.send_sem.at[link], recv_sem=self.recv_sem.at[link],
            device_id=self.routes[link], device_id_type=MESH)

    def step(self, index):
        def chain(link, base):
            self.run[link] = base[...]

            def get():
                self.copy(link).wait_recv()
                self.run[link] += self.land[link]
            pl.when(self.gets[link])(get)
            pl.when(self.sends[link])(lambda: self.copy(link).start())

        def swap(link):
            if link:
                self.copy(link - 1).wait_recv()
                self.run[link] = (self.own[...] if link == 1 else self.run[link - 1]) + self.land[link - 1]
            if link < 3:
                self.copy(link).start()

        for link in range(3):
            pl.when(index == link)(functools.partial(swap, link))

        @pl.when(index == 3)
        def _():
            self.copy(2).wait_recv()
            self.out[...] = self.run[2] + self.land[2]
            chain(3, self.out)
            chain(4, self.out)
            self.out[...] = self.run[3]

            def add():
                self.out[...] += self.land[4]
            pl.when(self.gets[4])(add)

    def drain(self):
        for link, sent in enumerate(self.sends):
            if sent is None:
                self.copy(link).wait_send()
            else:
                pl.when(sent)(lambda: self.copy(link).wait_send())


def scatter_kernel(terms_in, terms_out, gains, grad, out_in, out_out, out_gains, grad_land, *rest):
    place = Place()
    greet(place)
    grad_copy = pltpu.make_async_remote_copy(
        src_ref=grad, dst_ref=grad_land, send_sem=rest[26].at[0], recv_sem=rest[26].at[1],
        device_id=place.at(1 - place.x, place.y, place.z), device_id_type=MESH)
    pl.when(place.x == 1)(lambda: grad_copy.start())
    total = Total(place, gains, out_gains, *rest[22:26])
    arrays = [Scatter(place, array, (terms_in, terms_out)[array], *rest[4 * array : 4 * array + 4], rest[8 + 7 * array : 15 + 7 * array])
              for array in range(2)]
    order = arrays[::-1]

    def begin(index):
        for array in order:
            array.start(NZ - 1 - index)
    loop(NZ, begin)

    def body(index):
        distance = NZ - 1 - index
        for array in order:
            array.k_step(distance)
        total.step(index)
        for array in order:
            array.line(distance + 1)
        for array in order:
            array.a_step(distance + 1)
        for array in order:
            array.b_step(distance + 2)
            array.z_step(distance + 2)
    loop(NZ + 2, body)
    for array in order:
        array.square()
    for array, out in zip(arrays, (out_in, out_out)):
        number = number_of((place.x, place.y, place.z))

        def last(step):
            part = pl.ds(pl.multiple_of(step * 16, 16), 16)
            out[part, :] = array.held[number, part, :].astype(jnp.float32)
        loop(out.shape[0] // 16, last)
    for array in order:
        array.drain()
    total.drain()
    pl.when(place.x == 1)(lambda: grad_copy.wait_send())
    pl.when(place.x == 0)(lambda: grad_copy.wait_recv())


def scatter_terms(terms_in, terms_out, gains, grad):
    any_space = pl.BlockSpec(memory_space=pl.ANY)
    vmem = pl.BlockSpec(memory_space=pltpu.VMEM)
    dma = pltpu.SemaphoreType.DMA
    buffers, sems = [], []
    for array in range(2):
        buffers += [pltpu.VMEM((16,) + BLOCK[array], jnp.bfloat16)] * 2
        buffers += [
            pltpu.VMEM((count,) + part_shape(SCATTER_CUTS, array, colour), jnp.bfloat16) for count, colour in ((40, 0), (35, None))]
        sems += [dma((2, 20)), dma((2, 20)), dma((35,)), dma((35,)), dma((16,)), dma((16,)), dma((16,))]
    small = [pltpu.VMEM((5,) + BLOCK[2], jnp.float32)] * 2 + [dma((5,))] * 2 + [dma((2,))]
    return pl.pallas_call(
        scatter_kernel,
        out_shape=tuple(jax.ShapeDtypeStruct(block, jnp.float32) for block in BLOCK) + (jax.ShapeDtypeStruct(grad.shape, grad.dtype),),
        in_specs=[any_space] * 2 + [vmem, any_space], out_specs=(vmem,) * 3 + (any_space,),
        scratch_shapes=buffers + sems + small,
        compiler_params=pltpu.CompilerParams(collective_id=1, has_side_effects=True, vmem_limit_bytes=58 * 2**20),
        name="scatter_terms",
    )(terms_in, terms_out, gains, grad)


SLOTS, D, HD, PAIRS = 512, 768, 64, 6
WIDE_PAIRS = 3
TILES_IN, TILES_OUT = 7, 5
EPSILON = 1e-06
LOG2E = 1.4426950408889634
SCALE = 0.125 * LOG2E
APART = 256.0
F32, BF16 = jnp.float32, jnp.bfloat16
ACROSS, DOWN = ((1,), (1,)), ((0,), (0,))


def dot(a, b, dims=((1,), (0,))):
    return lax.dot_general(a, b, (dims, ((), ())), preferred_element_type=F32)


def split(value):
    high = value.astype(BF16)
    return high, (value - high.astype(F32)).astype(BF16)


def head_means(value, spread, exact=True):
    high, low = split(value)
    means = dot(high, spread)
    return means + dot(low, spread) if exact else means


def gelu_and_slope(x):
    t = 1.0 / (1.0 + (0.3275911 * 0.7071067811865476) * jnp.abs(x))
    bell = jnp.exp2((-0.5 * LOG2E) * (x * x))
    poly = t * (0.127414796 + t * (-0.142248368 + t * (0.7107068705 + t * (-0.7265760135 + t * 0.5307027145))))
    tail = poly * bell
    phi = jnp.where(x >= 0, 1.0 - tail, tail)
    return x * phi, phi + (0.3989422804014327 * x) * bell


def lanes(index, width):
    return pl.ds(pl.multiple_of(index * width, width), width)


FIRST_OUT, SECOND_IN, SECOND_OUT, SECOND_BACK, LAST_OUT, LAST_BACK, STEPS = 7, 12, 19, 24, 31, 36, 43
LAST_TILE = 2


def up_first(index):
    return (index + 3) % TILES_IN


def clip(index, high):
    return jnp.clip(index, 0, high)


def in_tile(t):
    layer = ((t >= FIRST_OUT) & (t < LAST_OUT)).astype(jnp.int32)
    forward = jnp.where(t < FIRST_OUT, t, clip(t - SECOND_IN, 6))
    backward = up_first(jnp.where(t < LAST_OUT, clip(t - SECOND_BACK, 6), clip(t - LAST_BACK, 6)))
    return layer, jnp.where(t < SECOND_OUT, forward, backward)


def out_tile(t):
    layer = ((t >= SECOND_IN) & (t < SECOND_BACK)).astype(jnp.int32)
    tile = jnp.where(t < SECOND_IN, clip(t - FIRST_OUT, 4), jnp.where(t < SECOND_BACK, clip(t - SECOND_OUT, 4), clip(t - LAST_OUT, 4)))
    return layer, tile


def in_terms(t):
    late = t >= LAST_BACK
    tile = up_first(jnp.where(late, t - LAST_BACK, clip(t - SECOND_BACK, 6)))
    return 1 - late.astype(jnp.int32), tile


def out_terms(t):
    late = t >= LAST_OUT
    return 1 - late.astype(jnp.int32), jnp.where(late, clip(t - LAST_OUT, 4), clip(t - SECOND_OUT, 4))


def compute_kernel(h_ref, cot_ref, w_in_ref, w_out_ref, ln_ref, qg_ref, kg_ref, augq_ref, augk_ref, spread_ref,
                   section_out, grad_ref, grad_low, grad_land, gain_ref, terms_in_ref, terms_out_ref,
                   hidden, normed, scale, q, k, v, rq, rk, linv, slope, combined, dy, dproj, acc, dq, dk, do, dhigh, dlow, *swap):
    t = pl.program_id(0)
    layer = in_tile(t)[0]
    project = (t < FIRST_OUT) | ((t >= SECOND_IN) & (t < SECOND_OUT))
    project_back = ((t >= SECOND_BACK) & (t < LAST_OUT)) | (t >= LAST_BACK)
    output = (t >= FIRST_OUT) & (t < SECOND_IN)
    output_both = (t >= SECOND_OUT) & (t < SECOND_BACK)
    back = (t >= LAST_OUT) & (t < LAST_BACK)
    layer = jnp.where(output, 0, layer)
    tile = jnp.where(project | project_back, in_tile(t)[1], out_tile(t)[1])
    section, trade = lax.axis_index("section"), None
    if swap:
        trade = Trade(section, section_out, hidden, dy, grad_land, *swap)
    spread = spread_ref[...]

    def halves(width=256):
        def run(body):
            def step(index):
                body(pl.ds(pl.multiple_of((index % 2) * 256, 256), 256), lanes(index // 2, width))
            loop(2 * D // width, step)
        return run

    def by_rows(body):
        loop(SLOTS // 128, lambda index: body(pl.ds(pl.multiple_of(index * 128, 128), 128)))

    @pl.when(t == 0)
    def _():
        hidden[0] = h_ref[...]
        if trade:
            trade.greet()
        gain_ref[...] = jnp.zeros_like(gain_ref)

    def low_lanes():
        return lax.broadcasted_iota(jnp.int32, (SLOTS, 128), 1) < HD

    @pl.when(project & (tile == 0))
    def _():
        def body(rows):
            h = hidden[layer, rows, :].astype(F32)
            centred = h - jnp.mean(h, -1, keepdims=True)
            root = lax.rsqrt(jnp.mean(centred * centred, -1, keepdims=True) + EPSILON)
            scale[layer, rows, :] = jnp.broadcast_to(root, (128, 128))
            normed[layer, rows, :] = (centred * root * ln_ref[layer]).astype(BF16)
        by_rows(body)

    @pl.when(project)
    def _():
        acc[...] = dot(normed[layer], w_in_ref[...])

        def heads(low_ref, root_ref, gain, factor):
            @halves()
            def _(rows, columns):
                x = acc[rows, columns]
                centred = x - head_means(x, spread)
                root = lax.rsqrt(head_means(centred * centred, spread, False) + EPSILON)
                root_ref[layer, rows, columns] = root.astype(BF16)
                low_ref[layer, rows, columns] = (centred * root * (gain * factor)).astype(BF16)

        pl.when(tile == 0)(lambda: heads(q, rq, qg_ref[layer], SCALE))
        pl.when(tile == 1)(lambda: heads(k, rk, kg_ref[layer], 1.0))

        @pl.when(tile == 2)
        def _():
            v[layer] = acc[...].astype(BF16)
            low = low_lanes()
            augq, augk = augq_ref[...], augk_ref[...]
            ones = jnp.ones((SLOTS, 128), BF16)

            def pair(index):
                part = lanes(index, 128)
                qp, kp, vp = q[layer, :, part], k[layer, :, part], v[layer, :, part]
                results = []
                for head in (0, 1):
                    mine = low if head == 0 else ~low
                    scores = dot(jnp.where(mine, qp, augq), jnp.where(mine, kp, augk), ACROSS)
                    results.append(dot(jnp.exp2(scores).astype(BF16), jnp.where(mine, vp, ones)))
                inverse = 1.0 / pltpu.roll(jnp.where(low, results[1], results[0]), HD, 1)
                linv[layer, :, part] = inverse
                combined[layer, 0, :, part] = (jnp.where(low, results[0], results[1]) * inverse).astype(BF16)
            loop(PAIRS, pair)

        @pl.when(tile > 2)
        def _():
            @halves()
            def _(rows, columns):
                value, rise = gelu_and_slope(acc[rows, columns])
                slope[layer, tile - 3, rows, columns] = rise.astype(BF16)
                combined[layer, tile - 2, rows, columns] = value.astype(BF16)

    @pl.when(output | output_both)
    def _():
        product = dot(combined[layer, tile], w_out_ref[...])
        pl.when(tile == 0)(lambda: dq.__setitem__(..., hidden[layer].astype(F32) + product))
        pl.when(tile > 0)(lambda: dq.__setitem__(..., dq[...] + product))

        @pl.when(tile == TILES_OUT - 1)
        def _():
            result = dq[...].astype(BF16)
            hidden[layer + 1] = result
            if trade:
                trade.give_output(layer)
            else:
                section_out[layer] = result

    @pl.when(output_both & (tile == 0))
    def _():
        dy[...] = cot_ref[...]

    @pl.when(output_both | back)
    def _():
        acc[...] = dot(dy[...], w_out_ref[...], ACROSS)
        terms_out_ref[...] = dot(combined[layer, tile], dy[...], DOWN).astype(BF16)

        @pl.when(tile == 0)
        def _():
            @halves()
            def _(rows, columns):
                grad, inverse = acc[rows, columns], linv[layer, rows, columns]
                do[rows, columns] = (grad * inverse).astype(BF16)
                total = head_means(grad * combined[layer, 0, rows, columns].astype(F32), spread) * (inverse * -HD)
                for half in (0, 128):
                    part = pl.ds(pl.multiple_of(columns.start + half, 128), 128)
                    high, low = split(pltpu.roll(total[:, half : half + 128], HD, 1))
                    dhigh[rows, part] = high
                    dlow[rows, part] = low

        @pl.when(tile > 0)
        def _():
            @halves()
            def _(rows, columns):
                dproj[tile + 2, rows, columns] = (acc[rows, columns] * slope[layer, tile - 1, rows, columns].astype(F32)).astype(BF16)

    @pl.when(project_back & (tile == 0))
    def _():
        low = low_lanes()
        spot = lax.broadcasted_iota(jnp.int32, (SLOTS, 128), 1) % HD
        first = spot == 0
        augv = jnp.where(spot < 2, 1.0, 0.0).astype(BF16)
        augq, augk = augq_ref[...], augk_ref[...]
        none = jnp.zeros((SLOTS, 128), BF16)

        def pair(index):
            part = lanes(index, 128)
            qp, kp, vp, dop = q[layer, :, part], k[layer, :, part], v[layer, :, part], do[:, part]
            augd = jnp.where(first, dhigh[:, part], dlow[:, part])
            sums = [None, None, None]
            for head in (0, 1):
                mine = low if head == 0 else ~low
                e = jnp.exp2(dot(jnp.where(mine, kp, augk), jnp.where(mine, qp, augq), ACROSS))
                dp = dot(jnp.where(mine, vp, augv), jnp.where(mine, dop, augd), ACROSS)
                ds = (e * dp).astype(BF16)
                parts = (dot(ds, jnp.where(mine, kp, none), DOWN), dot(ds, jnp.where(mine, qp, none)),
                         dot(e.astype(BF16), jnp.where(mine, dop, none)))
                sums = [part_sum if total is None else total + part_sum for total, part_sum in zip(sums, parts)]
            dq[:, part] = sums[0] * 0.125
            dk[:, part] = sums[1] * (1.0 / LOG2E)
            dproj[2, :, part] = sums[2].astype(BF16)
        loop(PAIRS, pair)
        for which, grads, low_ref, root_ref, gain, factor in ((0, dq, q, rq, qg_ref, SCALE), (1, dk, k, rk, kg_ref, 1.0)):
            @halves()
            def _(rows, columns):
                grad, gains = grads[rows, columns], gain[layer]
                xhat = low_ref[layer, rows, columns].astype(F32) * (1.0 / (gains * factor))
                scaled = grad * gains
                mean = head_means(scaled, spread, False)
                along = head_means(scaled * xhat, spread, False)
                dproj[which, rows, columns] = (root_ref[layer, rows, columns].astype(F32) * (scaled - mean - xhat * along)).astype(BF16)
                gain_ref[layer, which + 1 : which + 2, columns] += jnp.sum(grad * xhat, 0, keepdims=True)

    @pl.when(project_back)
    def _():
        product = dot(dproj[tile], w_in_ref[...], ACROSS)
        pl.when(tile == up_first(0))(lambda: acc.__setitem__(..., product))
        pl.when(tile != up_first(0))(lambda: acc.__setitem__(..., acc[...] + product))
        terms_in_ref[...] = dot(normed[layer], dproj[tile], DOWN).astype(BF16)

        @pl.when(tile == LAST_TILE)
        def _():
            gains = ln_ref[layer]

            def body(rows):
                grad = acc[rows, :]
                xhat = normed[layer, rows, :].astype(F32) * (1.0 / gains)
                scaled = grad * gains
                mean = jnp.mean(scaled, -1, keepdims=True)
                along = jnp.mean(scaled * xhat, -1, keepdims=True)
                total = dy[rows, :].astype(F32) + scale[layer, rows, :1] * (scaled - mean - xhat * along)
                low = total.astype(BF16)
                if trade:
                    pl.when(layer == section)(lambda: grad_ref.__setitem__((rows, slice(None)), total))
                else:
                    grad_ref[layer, rows, :] = total
                pl.when(layer == 1)(lambda: dy.__setitem__((rows, slice(None)), low))
                pl.when(layer == 0)(lambda: grad_low.__setitem__((rows, slice(None)), low))
                gain_ref[layer, 0:1, :] += jnp.sum(grad * xhat, 0, keepdims=True)
            by_rows(body)
            if trade:
                pl.when(layer == 1)(trade.give_grad)
                pl.when(layer == 0)(trade.finish)


class Trade:
    def __init__(self, section, section_out, hidden, dy, grad_land, own_sem, send_sem, recv_sem):
        self.section, self.section_out, self.hidden, self.dy, self.grad_land = section, section_out, hidden, dy, grad_land
        self.own_sem, self.send_sem, self.recv_sem = own_sem, send_sem, recv_sem
        self.pair = (1 - section, lax.axis_index("wide"))

    def greet(self):
        barrier = pltpu.get_barrier_semaphore()
        pl.semaphore_signal(barrier, inc=1, device_id=self.pair, device_id_type=MESH)
        pl.semaphore_wait(barrier, 1)

    def kept(self):
        return pltpu.make_async_copy(self.hidden.at[self.section + 1], self.section_out.at[self.section], self.own_sem)

    def copy(self, source, target, index):
        return pltpu.make_async_remote_copy(
            src_ref=source, dst_ref=target, send_sem=self.send_sem.at[index], recv_sem=self.recv_sem.at[index],
            device_id=self.pair, device_id_type=MESH)

    def given(self):
        return self.copy(self.hidden.at[2 - self.section], self.section_out.at[self.section], 0)

    def grad(self):
        return self.copy(self.dy, self.grad_land, 1)

    def give_output(self, layer):
        pl.when(layer == self.section)(lambda: self.kept().start())
        pl.when(layer != self.section)(lambda: self.given().start())

    def give_grad(self):
        pl.when(self.section == 0)(lambda: self.grad().start())

    def finish(self):
        self.kept().wait()
        self.given().wait_send()
        self.copy(self.hidden.at[2 - self.section], self.section_out.at[1 - self.section], 0).wait_recv()
        pl.when(self.section == 0)(lambda: self.grad().wait_send())
        pl.when(self.section == 1)(lambda: self.grad().wait_recv())


def both_layers(trading, h, cot, full_in, full_out, ln, qg, kg, augq, augk, spread):
    square = (SLOTS, D)

    def whole(*dims):
        return pl.BlockSpec(dims, lambda t: (0,) * len(dims))

    def of_columns(where):
        return pl.BlockSpec((None, D, D), lambda t: (where(t)[0], 0, where(t)[1]))

    def of_rows(where):
        return pl.BlockSpec((None, D, D), lambda t: (where(t)[0], where(t)[1], 0))

    low, wide = (lambda *dims: pltpu.VMEM(dims, BF16)), (lambda *dims: pltpu.VMEM(dims, F32))
    any_space, dma = pl.BlockSpec(memory_space=pl.ANY), pltpu.SemaphoreType.DMA
    if trading:
        out_specs = [any_space, whole(*square), whole(*square), any_space]
        grad_shape, extra = square, [dma(()), dma((2,)), dma((2,))]
        params = dict(collective_id=2, has_side_effects=True)
    else:
        out_specs = [whole(2, *square), whole(2, *square), whole(*square), whole(*square)]
        grad_shape, extra, params = (2,) + square, [], {}
    return pl.pallas_call(
        compute_kernel,
        grid=(STEPS,),
        in_specs=[
            whole(*square), whole(*square), of_columns(in_tile), of_rows(out_tile), whole(2, 1, D), whole(2, 1, 256), whole(2, 1, 256),
            whole(SLOTS, 128), whole(SLOTS, 128), whole(256, 256),
        ],
        out_specs=out_specs + [whole(2, 8, D), of_columns(in_terms), of_rows(out_terms)],
        scratch_shapes=[
            low(3, *square), low(2, *square), wide(2, SLOTS, 128), low(2, *square), low(2, *square), low(2, *square), low(2, *square),
            low(2, *square), wide(2, *square), low(2, 4, *square), low(2, 5, *square), low(*square), low(7, *square), wide(*square),
            wide(*square), wide(*square), low(*square), low(*square), low(*square),
        ] + extra,
        out_shape=[
            jax.ShapeDtypeStruct((2,) + square, BF16), jax.ShapeDtypeStruct(grad_shape, F32), jax.ShapeDtypeStruct(square, BF16),
            jax.ShapeDtypeStruct(square, BF16), jax.ShapeDtypeStruct((2, 8, D), F32), jax.ShapeDtypeStruct(full_in.shape, BF16),
            jax.ShapeDtypeStruct(full_out.shape, BF16),
        ],
        compiler_params=pltpu.CompilerParams(vmem_limit_bytes=63 * 2**20, **params),
        name="both_layers",
    )(h, cot, full_in, full_out, ln, qg, kg, augq, augk, spread)


def augment(image_id, token_size):
    high, low = split(jnp.log2(token_size.astype(F32)))
    same = (image_id[:, None] == jnp.arange(3)[None, :]).astype(BF16)
    one = jnp.ones_like(high)
    q = jnp.concatenate([one[:, None], one[:, None], same, one[:, None]], 1)
    k = jnp.concatenate([high[:, None], low[:, None], same * APART, one[:, None] * -APART], 1)
    return [jnp.tile(jnp.pad(part, ((0, 0), (0, HD - 6))), (1, 2)) for part in (q, k)]


def spread_matrix():
    head = jnp.arange(256) // HD
    return ((head[:, None] == head[None, :]) / HD).astype(BF16)


def gather_all(piece, axis):
    return lax.all_gather(lax.all_gather(piece, "wide", axis=axis, tiled=True), "section", axis=0, tiled=True)


def scatter_all(terms, axis):
    own = lax.psum_scatter(terms, "section", scatter_dimension=0, tiled=True)
    return lax.psum_scatter(own, "wide", scatter_dimension=axis, tiled=True)


def on_device(inputs, cotangent, token_size, image_id, w_in, w_out, ln_gain, q_gain, k_gain):
    section, wide = lax.axis_index("section"), lax.axis_index("wide")
    width = lax.axis_size("wide")
    blocks_fit = width == 16 and w_in.shape[1:] == BLOCK[0] and w_out.shape[1:] == BLOCK[1]
    ends = [0]
    for gain in (ln_gain, q_gain, k_gain):
        ends.append(ends[-1] + gain.shape[1])
    own_gains = jnp.concatenate([ln_gain, q_gain, k_gain], 1)
    if blocks_fit:
        padded = jnp.pad(own_gains, ((0, BLOCK[2][0] - 1), (0, BLOCK[2][1] - ends[3])))
        full_in, full_out, full_gains = gather_weights(w_in[0], w_out[0], padded)
        full_gains = full_gains.reshape((2, width) + BLOCK[2])[:, :, 0]
    else:
        full_in, full_out = gather_all(w_in, 1), gather_all(w_out, 1)
        full_gains = gather_all(own_gains[:, None], 1)
    ln, qg, kg = [full_gains[:, :, low:high].reshape(2, 1, -1).astype(F32) for low, high in zip(ends, ends[1:])]
    augq, augk = augment(image_id[section, 0], token_size[section, 0])
    outs, grads, grad_low, grad_land, gain_terms, terms_in, terms_out = both_layers(
        blocks_fit, inputs[section, 0], cotangent[section, 0], full_in, full_out, ln, jnp.tile(qg, (1, 1, 4)), jnp.tile(kg, (1, 1, 4)),
        augq, augk, spread_matrix())
    swap = [(0, 1), (1, 0)]

    def both_micro(pair):
        mine = lax.dynamic_index_in_dim(pair, section, 0, False)
        other = lax.dynamic_index_in_dim(pair, 1 - section, 0, False).astype(BF16)
        other = lax.ppermute(other, "section", swap).astype(mine.dtype)
        return jnp.where(section == 0, jnp.stack([mine, other]), jnp.stack([other, mine]))[None, :, None]

    heads = gain_terms[:, 1:3].reshape(2, 2, -1, HD).sum(2).reshape(2, -1)
    totals = jnp.concatenate([gain_terms[:, 0], heads], 1)
    places = (0, D, D + HD, D + 2 * HD)
    if blocks_fit:
        totals = jnp.pad(totals, ((0, 0), (0, 1024 - places[3]))).reshape(BLOCK[2])
        own_in, own_out, totals, last_land = scatter_terms(terms_in, terms_out, totals, grad_low)
        other = jnp.where(section == 0, last_land, grad_land).astype(F32)
        grads = jnp.where(section == 0, jnp.stack([grads, other]), jnp.stack([other, grads]))[None, :, None]
        outs = outs[None, :, None]
        own_in, own_out = own_in[None], own_out[None]
        totals = totals.reshape(2, 1024)
    else:
        own_in = scatter_all(terms_in, 1).astype(F32)
        own_out = scatter_all(terms_out, 1).astype(F32)
        totals = lax.psum(totals, ("section", "wide"))
        outs, grads = both_micro(outs), both_micro(grads)
    mine = lax.dynamic_index_in_dim(totals, section, 0, False)
    gain_grads = [
        lax.dynamic_slice_in_dim(mine[low:high], wide * gain.shape[1], gain.shape[1])[None]
        for low, high, gain in zip(places, places[1:], (ln_gain, q_gain, k_gain))
    ]
    return (outs, grads, own_in, own_out, *gain_grads)


def solution(mesh):
    return jax.shard_map(
        on_device,
        mesh=mesh,
        in_specs=(
            P(None, "wide", None, None),
            P(None, "wide", None, None),
            P(None, "wide", None),
            P(None, "wide", None),
            P("section", "wide", None),
            P("section", "wide", None),
            P("section", "wide"),
            P("section", "wide"),
            P("section", "wide"),
        ),
        out_specs=(
            P("section", None, "wide", None, None),
            P("section", None, "wide", None, None),
            P("section", "wide", None),
            P("section", "wide", None),
            P("section", "wide"),
            P("section", "wide"),
            P("section", "wide"),
        ),
        check_vma=False,
    )
```

```python
import functools

import jax
import jax.numpy as jnp
from jax import lax
from jax.experimental import pallas as pl
from jax.experimental.pallas import tpu as pltpu
from jax.sharding import PartitionSpec as P

MESH = pl.DeviceIdType.MESH
NZ = 4
BLOCK = ((48, 5376), (240, 768), (16, 128))
GATHER_CUTS = (2176, 96)
SCATTER_CUTS = (2176, 96)


class Place:
    def __init__(self):
        self.x, self.wide = lax.axis_index("section"), lax.axis_index("wide")
        self.y, self.z, self.c = (self.wide // 2) % 2, self.wide // 4, self.wide % 2

    def at(self, x, y, z, c=None):
        return (x, z * 4 + y * 2 + (self.c if c is None else c))

    def along(self, colour, block_z, far_first, far_second):
        dx = jnp.where(colour == 0, far_first, far_second)
        dy = jnp.where(colour == 0, far_second, far_first)
        return self.flip(self.x, dx), self.flip(self.y, dy), block_z

    @staticmethod
    def flip(value, far):
        return value + far - 2 * value * far

    def first(self, colour):
        return self.at(*self.along(colour, self.z, 1, 0))

    def second(self, colour):
        return self.at(*self.along(colour, self.z, 0, 1))

    def sibling(self):
        return self.at(self.x, self.y, self.z, 1 - self.c)


def greet(place):
    barrier = pltpu.get_barrier_semaphore()
    x, y, z = place.x, place.y, place.z

    def signal(device):
        pl.semaphore_signal(barrier, inc=1, device_id=device, device_id_type=MESH)

    signal(place.at(1 - x, y, z))
    signal(place.at(x, 1 - y, z))
    signal(place.sibling())
    pl.when(z < NZ - 1)(lambda: signal(place.at(x, y, z + 1)))
    pl.when(z > 0)(lambda: signal(place.at(x, y, z - 1)))
    pl.semaphore_wait(barrier, 3 + (z < NZ - 1).astype(jnp.int32) + (z > 0).astype(jnp.int32))


def number_of(block):
    return block[0] * 8 + block[1] * 4 + block[2]


def part_shape(cuts, array, colour):
    rows, cols = BLOCK[array]
    size = cuts[array]
    if array == 0:
        return rows, cols - 2 * size if colour is None else size
    return rows - 2 * size if colour is None else size, cols


def cut(ref, cuts, array, colour):
    if array == 2:
        return ref
    rows, cols = part_shape(cuts, array, colour)
    size = cuts[array]
    if array == 0:
        return ref.at[:, pl.ds(2 * size if colour is None else pl.multiple_of(colour * size, 128), cols)]
    return ref.at[pl.ds(2 * size if colour is None else pl.multiple_of(colour * size, 16), rows), :]


def loop(count, body):
    def step(index, carry):
        body(index)
        return carry
    lax.fori_loop(0, count, step, 0)


class Gather:
    def __init__(self, place, array, own, full, send_sem, recv_sem, core_sem):
        self.place, self.array, self.own, self.full = place, array, own, full
        self.send_sem, self.recv_sem, self.core_sem = send_sem, recv_sem, core_sem

    def view(self, block, colour, plane=None):
        rows = BLOCK[self.array][0]
        place = self.place
        start = (block[2] * 4 + block[1] * 2 + (place.c if plane is None else plane)) * rows
        return cut(self.full.at[block[0], pl.ds(pl.multiple_of(start, 16), rows), :], GATHER_CUTS, self.array, colour)

    def copy(self, link, device, block, colour, own=False, other_plane=False):
        kind = 2 if colour is None else colour
        number = number_of(block)
        target = self.view(block, colour, 1 - self.place.c if other_plane else None)
        source = cut(self.own, GATHER_CUTS, self.array, colour) if own else target
        sems = self.core_sem if link == 4 else self.recv_sem
        return pltpu.make_async_remote_copy(
            src_ref=source, dst_ref=target, send_sem=self.send_sem.at[link, kind, number], recv_sem=sems.at[kind, number],
            device_id=device, device_id_type=MESH)

    def visit(self, block, colour, onward, first, second, drain, condition=None, own=False):
        place = self.place

        def body():
            if not drain and not own:
                self.copy(0, place.sibling(), block, colour).wait_recv()

            def send(link, device):
                copy = self.copy(link, device, block, colour, own)
                copy.wait_send() if drain else copy.start()

            for link, step in onward:
                target = place.z + step
                pl.when((target >= 0) & (target < NZ))(functools.partial(send, link, place.at(place.x, place.y, target)))
            if first is not None:
                send(2, first)
            if second is not None:
                if isinstance(second, tuple) and len(second) == 3:
                    pl.when(second[2])(functools.partial(send, 3, second[:2]))
                else:
                    send(3, second)
            send(4, place.sibling())
        if condition is None:
            body()
        else:
            pl.when(condition)(body)

    def begin(self, drain=False):
        place = self.place
        me = (place.x, place.y, place.z)
        everywhere = ((0, 1), (1, -1))
        self.visit(me, None, everywhere, place.at(1 - place.x, place.y, place.z), place.at(place.x, 1 - place.y, place.z), drain, own=True)

        def body(colour):
            self.visit(me, colour, everywhere, place.first(colour), place.second(colour), drain, own=True)
        if self.array < 2:
            loop(2, body)

    def square(self, drain=False):
        place = self.place

        def body(index):
            far_x, far_y = (index != 1).astype(jnp.int32), (index != 0).astype(jnp.int32)
            block = (place.flip(place.x, far_x), place.flip(place.y, far_y), place.z)
            self.visit(block, None, ((0, 1), (1, -1)), None, place.at(place.x, 1 - place.y, place.z) + (index == 0,), drain)
        loop(3, body)

    def sided(self, distance, body):
        place = self.place

        def side_body(side):
            step = 1 - 2 * side
            block_z = place.z - step * distance
            body(side, block_z, (block_z >= 0) & (block_z < NZ) & ((distance > 0) | (side == 0)))
        loop(2, side_body)

    def onward(self, side):
        return ((0, 1), (1, -1))[side]

    def z_step(self, distance, drain=False):
        place = self.place
        for side in (0, 1):
            step = 1 - 2 * side
            block_z = place.z - step * distance

            def body(colour):
                self.visit((place.x, place.y, block_z), colour, ((side, step),), place.first(colour), place.second(colour), drain)
            pl.when((block_z >= 0) & (block_z < NZ))(lambda: loop(2, body))

    def line(self, distance, drain=False):
        place = self.place
        for side in (0, 1):
            step = 1 - 2 * side
            block_z = place.z - step * distance

            def body(index):
                block = (place.flip(place.x, index % 2), place.flip(place.y, index // 2), block_z)
                self.visit(block, None, ((side, step),), None, None, drain)
            pl.when((block_z >= 0) & (block_z < NZ))(lambda: loop(4, body))

    def a_step(self, distance, drain=False):
        place = self.place

        def body(side, block_z, there):
            def inner(colour):
                self.visit(place.along(colour, block_z, 1, 0), colour, (), None, place.second(colour), drain)
            pl.when(there)(lambda: loop(2, inner))
        self.sided(distance, body)

    def b_step(self, distance, drain=False):
        place = self.place

        def body(side, block_z, there):
            def inner(index):
                colour = index // 2
                self.visit(place.along(colour, block_z, index % 2, 1), colour, (), None, None, drain)
            pl.when(there)(lambda: loop(4, inner))
        self.sided(distance, body)

    def from_core(self):
        place = self.place

        def body(number):
            block = (number // 8, (number // 4) % 2, number % 4)
            self.copy(4, place.sibling(), block, None, other_plane=True).wait_recv()
            for colour in (0, 1) if self.array < 2 else ():
                self.copy(4, place.sibling(), block, colour, other_plane=True).wait_recv()
        loop(16, body)

    def drain(self):
        self.begin(True)
        self.square(True)

        def body(index):
            self.line(index + 1, True)
            if self.array < 2:
                self.z_step(index + 1, True)
                self.a_step(index, True)
                self.b_step(index, True)
        loop(NZ, body)


class Weights:
    def __init__(self, place, own, full, tiles, tile_sem, sems):
        self.place, self.full, self.tiles, self.tile_sem = place, full, tiles, tile_sem
        self.copies = []
        if place is None:
            return
        self.inner, self.outer, self.gains = [Gather(place, array, own[array], full[array], *sems[3 * array : 3 * array + 3]) for array in range(3)]
        for array in range(3):
            rows = BLOCK[array][0]
            target = full[array].at[place.x, pl.ds(pl.multiple_of(place.wide * rows, 16), rows), :]
            self.copies.append(pltpu.make_async_copy(own[array], target, sems[9].at[array]))

    def begin(self):
        greet(self.place)
        for copy in self.copies:
            copy.start()
        self.gains.begin()
        self.inner.begin()
        self.gains.square()
        self.inner.square()

        def early(index):
            self.inner.z_step(index + 1)
            self.inner.a_step(index)
            self.gains.line(index + 1)
            self.inner.line(index + 1)
        loop(NZ - 1, early)
        self.outer.begin()
        self.inner.a_step(NZ - 1)
        self.outer.square()

        def late(index):
            self.inner.b_step(index)
            pl.when(index == 1)(lambda: self.onward(0))
        loop(NZ, late)
        self.gains.from_core()
        self.inner.from_core()
        for copy in self.copies:
            copy.wait()

    def onward(self, index):
        self.outer.z_step(index + 1)
        self.outer.a_step(index)
        self.outer.line(index + 1)

    def end(self):
        loop(NZ, self.outer.b_step)
        self.outer.from_core()

    def drain(self):
        for array in (self.gains, self.inner, self.outer):
            array.drain()

    def fetch(self, t):
        slot = t % 2
        tile, sem = self.tiles.at[slot], self.tile_sem.at[slot]
        project = uses_in(t)

        def inner():
            layer, index = in_tile(t)
            return pltpu.make_async_copy(self.full[0].at[layer, :, pl.ds(pl.multiple_of(index * D, D), D)], tile, sem)

        def outer():
            layer, index = out_tile(t)
            return pltpu.make_async_copy(self.full[1].at[layer, pl.ds(pl.multiple_of(index * D, D), D), :], tile, sem)
        pl.when(project)(lambda: inner().start())
        pl.when(jnp.logical_not(project))(lambda: outer().start())

    def wait(self, t):
        slot = t % 2
        pltpu.make_async_copy(self.full[0].at[0, :, pl.ds(0, D)], self.tiles.at[slot], self.tile_sem.at[slot]).wait()

    def step(self, t):
        if self.place is not None:
            pl.when(t == 0)(self.begin)
            pl.when((t >= 2) & (t <= NZ))(lambda: self.onward(t - 1))
            pl.when(t == FIRST_OUT)(self.end)
            pl.when(t == STEPS - 1)(self.drain)
            held_back = FIRST_OUT
        else:
            held_back = 0
        pl.when((t == 0) | (t == held_back))(lambda: self.fetch(t))
        pl.when((t + 1 < STEPS) & (t + 1 != held_back))(lambda: self.fetch(t + 1))
        self.wait(t)


def add_into(target, source):
    rows = target.shape[0]

    def body(step):
        part = pl.ds(pl.multiple_of(step * 16, 16), 16)
        target[part, :] = (target[part, :].astype(jnp.float32) + source[part, :].astype(jnp.float32)).astype(jnp.bfloat16)
    loop(rows // 16, body)


class Scatter:
    def __init__(self, place, array, terms, held, core_land, land, rest_land, sems):
        self.place, self.array, self.terms, self.held, self.core_land = place, array, terms, held, core_land
        self.land, self.rest_land = land, rest_land
        self.send_sem, self.recv_sem, self.rest_send, self.rest_recv, self.core_send, self.core_recv, self.local_sem = sems

    def part(self, block, colour):
        return cut(self.held.at[number_of(block)], SCATTER_CUTS, self.array, colour)

    def copy(self, device, block, colour, slot):
        if colour is None:
            target, send_sem, recv_sem = self.rest_land.at[slot], self.rest_send.at[slot], self.rest_recv.at[slot]
        else:
            target, send_sem, recv_sem = self.land.at[colour * 20 + slot], self.send_sem.at[colour, slot], self.recv_sem.at[colour, slot]
        return pltpu.make_async_remote_copy(
            src_ref=self.part(block, colour), dst_ref=target, send_sem=send_sem, recv_sem=recv_sem, device_id=device,
            device_id_type=MESH)

    def send(self, device, block, colour, slot, drain):
        copy = self.copy(device, block, colour, slot)
        copy.wait_send() if drain else copy.start()

    def arrive(self, block, colour, slot, drain):
        if not drain:
            self.copy(self.place.sibling(), block, colour, slot).wait_recv()
            add_into(self.part(block, colour), self.rest_land.at[slot] if colour is None else self.land.at[colour * 20 + slot])

    def core_copy(self, block, mine):
        rows = BLOCK[self.array][0]
        place = self.place
        number = number_of(block)
        start = (block[2] * 4 + block[1] * 2 + (place.c if mine else 1 - place.c)) * rows
        source = self.terms.at[block[0], pl.ds(pl.multiple_of(start, 16), rows), :]
        if mine:
            return pltpu.make_async_copy(source, self.held.at[number], self.local_sem.at[number])
        return pltpu.make_async_remote_copy(
            src_ref=source, dst_ref=self.core_land.at[number], send_sem=self.core_send.at[number],
            recv_sem=self.core_recv.at[number], device_id=place.sibling(), device_id_type=MESH)

    def sided(self, distance, body):
        place = self.place

        def side_body(side):
            block_z = place.z + (2 * side - 1) * distance
            there = (block_z >= 0) & (block_z < NZ) & (distance < NZ) & (distance >= 0) & ((distance > 0) | (side == 0))
            pl.when(there)(lambda: body(block_z))
        loop(2, side_body)

    def start(self, distance):
        place = self.place

        def body(block_z):
            def inner(index):
                block = (place.flip(place.x, 1 - index % 2), place.flip(place.y, 1 - index // 2), block_z)
                self.core_copy(block, False).start()
                self.core_copy(block, True).start()
            loop(4, inner)
        self.sided(distance, body)

    def k_step(self, distance, drain=False):
        place = self.place

        def body(block_z):
            def inner(index):
                far_x, far_y = 1 - index % 2, 1 - index // 2
                block = (place.flip(place.x, far_x), place.flip(place.y, far_y), block_z)
                if not drain:
                    self.core_copy(block, True).wait()
                    copy = self.core_copy(block, False)
                    copy.wait_recv()
                    add_into(self.held.at[number_of(block)], self.core_land.at[number_of(block)])
                    copy.wait_send()

                def out(colour):
                    far_first = jnp.where(colour == 0, far_x, far_y)
                    far_second = jnp.where(colour == 0, far_y, far_x)
                    pl.when(far_second == 1)(lambda: self.send(place.second(colour), block, colour, far_first * 4 + block_z, drain))
                loop(2, out)
            loop(4, inner)
        self.sided(distance, body)

    def a_step(self, distance, drain=False):
        place = self.place

        def body(block_z):
            def inner(index):
                colour, far_first = index % 2, 1 - index // 2
                block = place.along(colour, block_z, far_first, 0)
                self.arrive(block, colour, far_first * 4 + block_z, drain)
                pl.when(far_first == 1)(lambda: self.send(place.first(colour), block, colour, 8 + block_z, drain))
            loop(4, inner)
        self.sided(distance, body)

    def b_step(self, distance):
        place = self.place

        def body(block_z):
            loop(2, lambda colour: self.arrive((place.x, place.y, block_z), colour, 8 + block_z, False))
        self.sided(distance, body)

    def toward(self, distance, body):
        place = self.place
        for side, step in ((0, -1), (1, 1)):
            block_z, behind = place.z + step * distance, place.z - step
            there = (block_z >= 0) & (block_z < NZ) & (distance < NZ) & (distance >= 0)
            pl.when(there)(functools.partial(body, block_z, side, step, (behind >= 0) & (behind < NZ)))

    def z_step(self, distance, drain=False):
        place = self.place

        def body(block_z, side, step, more):
            block = (place.x, place.y, block_z)
            slot = 12 + 4 * side + block_z

            def inner(colour):
                pl.when(more)(lambda: self.arrive(block, colour, slot, drain))
                pl.when(distance > 0)(lambda: self.send(place.at(place.x, place.y, place.z + step), block, colour, slot, drain))
            loop(2, inner)
        self.toward(distance, body)

    def line(self, distance, drain=False):
        place = self.place

        def body(block_z, side, step, more):
            def inner(index):
                block = (place.flip(place.x, 1 - index % 2), place.flip(place.y, 1 - index // 2), block_z)
                slot = 16 * side + number_of(block)
                pl.when(more)(lambda: self.arrive(block, None, slot, drain))
                pl.when(distance > 0)(lambda: self.send(place.at(place.x, place.y, place.z + step), block, None, slot, drain))
            loop(4, inner)
        self.toward(distance, body)

    def square(self, drain=False):
        place = self.place
        over_x, over_y = place.at(1 - place.x, place.y, place.z), place.at(place.x, 1 - place.y, place.z)
        far = (1 - place.x, place.y, place.z)
        self.send(over_y, (1 - place.x, 1 - place.y, place.z), None, 33, drain)
        self.send(over_y, (place.x, 1 - place.y, place.z), None, 32, drain)
        self.arrive(far, None, 33, drain)
        self.send(over_x, far, None, 34, drain)
        self.arrive((place.x, place.y, place.z), None, 32, drain)
        self.arrive((place.x, place.y, place.z), None, 34, drain)

    def drain(self):
        def body(distance):
            self.k_step(distance, True)
            self.a_step(distance, True)
            self.z_step(distance, True)
            self.line(distance, True)
        loop(NZ, body)
        self.square(True)


class Total:
    def __init__(self, place, own, out, run, land, send_sem, recv_sem):
        self.place, self.own, self.out, self.run, self.land = place, own, out, run, land
        self.send_sem, self.recv_sem = send_sem, recv_sem
        x, y, z = place.x, place.y, place.z
        self.routes = (place.sibling(), place.at(x, 1 - y, z), place.at(1 - x, y, z), place.at(x, y, z + 1), place.at(x, y, z - 1))
        self.sends = (None, None, None, z < NZ - 1, z > 0)
        self.gets = (None, None, None, z > 0, z < NZ - 1)

    def copy(self, link):
        source = self.own if link == 0 else self.run.at[link]
        return pltpu.make_async_remote_copy(
            src_ref=source, dst_ref=self.land.at[link], send_sem=self.send_sem.at[link], recv_sem=self.recv_sem.at[link],
            device_id=self.routes[link], device_id_type=MESH)

    def step(self, index):
        def chain(link, base):
            self.run[link] = base[...]

            def get():
                self.copy(link).wait_recv()
                self.run[link] += self.land[link]
            pl.when(self.gets[link])(get)
            pl.when(self.sends[link])(lambda: self.copy(link).start())

        def swap(link):
            if link:
                self.copy(link - 1).wait_recv()
                self.run[link] = (self.own[...] if link == 1 else self.run[link - 1]) + self.land[link - 1]
            if link < 3:
                self.copy(link).start()

        for link in range(3):
            pl.when(index == link)(functools.partial(swap, link))

        @pl.when(index == 3)
        def _():
            self.copy(2).wait_recv()
            self.out[...] = self.run[2] + self.land[2]
            chain(3, self.out)
            chain(4, self.out)
            self.out[...] = self.run[3]

            def add():
                self.out[...] += self.land[4]
            pl.when(self.gets[4])(add)

    def drain(self):
        for link, sent in enumerate(self.sends):
            if sent is None:
                self.copy(link).wait_send()
            else:
                pl.when(sent)(lambda: self.copy(link).wait_send())


def scatter_kernel(terms_in, terms_out, gains, grad, out_in, out_out, out_gains, grad_land, *rest):
    place = Place()
    greet(place)
    grad_copy = pltpu.make_async_remote_copy(
        src_ref=grad, dst_ref=grad_land, send_sem=rest[26].at[0], recv_sem=rest[26].at[1],
        device_id=place.at(1 - place.x, place.y, place.z), device_id_type=MESH)
    pl.when(place.x == 1)(lambda: grad_copy.start())
    total = Total(place, gains, out_gains, *rest[22:26])
    arrays = [Scatter(place, array, (terms_in, terms_out)[array], *rest[4 * array : 4 * array + 4], rest[8 + 7 * array : 15 + 7 * array])
              for array in range(2)]
    order = arrays[::-1]

    def begin(index):
        for array in order:
            array.start(NZ - 1 - index)
    loop(NZ, begin)

    def body(index):
        distance = NZ - 1 - index
        for array in order:
            array.k_step(distance)
        total.step(index)
        for array in order:
            array.line(distance + 1)
        for array in order:
            array.a_step(distance + 1)
        for array in order:
            array.b_step(distance + 2)
            array.z_step(distance + 2)
    loop(NZ + 2, body)
    for array in order:
        array.square()
    for array, out in zip(arrays, (out_in, out_out)):
        number = number_of((place.x, place.y, place.z))

        def last(step):
            part = pl.ds(pl.multiple_of(step * 16, 16), 16)
            out[part, :] = array.held[number, part, :].astype(jnp.float32)
        loop(out.shape[0] // 16, last)
    for array in order:
        array.drain()
    total.drain()
    pl.when(place.x == 1)(lambda: grad_copy.wait_send())
    pl.when(place.x == 0)(lambda: grad_copy.wait_recv())


def scatter_terms(terms_in, terms_out, gains, grad):
    any_space = pl.BlockSpec(memory_space=pl.ANY)
    vmem = pl.BlockSpec(memory_space=pltpu.VMEM)
    dma = pltpu.SemaphoreType.DMA
    buffers, sems = [], []
    for array in range(2):
        buffers += [pltpu.VMEM((16,) + BLOCK[array], jnp.bfloat16)] * 2
        buffers += [
            pltpu.VMEM((count,) + part_shape(SCATTER_CUTS, array, colour), jnp.bfloat16) for count, colour in ((40, 0), (35, None))]
        sems += [dma((2, 20)), dma((2, 20)), dma((35,)), dma((35,)), dma((16,)), dma((16,)), dma((16,))]
    small = [pltpu.VMEM((5,) + BLOCK[2], jnp.float32)] * 2 + [dma((5,))] * 2 + [dma((2,))]
    return pl.pallas_call(
        scatter_kernel,
        out_shape=tuple(jax.ShapeDtypeStruct(block, jnp.float32) for block in BLOCK) + (jax.ShapeDtypeStruct(grad.shape, grad.dtype),),
        in_specs=[any_space] * 2 + [vmem, any_space], out_specs=(vmem,) * 3 + (any_space,),
        scratch_shapes=buffers + sems + small,
        compiler_params=pltpu.CompilerParams(collective_id=1, has_side_effects=True, vmem_limit_bytes=58 * 2**20),
        name="scatter_terms",
    )(terms_in, terms_out, gains, grad)


SLOTS, D, HD, PAIRS = 512, 768, 64, 6
WIDE_PAIRS = 3
TILES_IN, TILES_OUT = 7, 5
EPSILON = 1e-06
LOG2E = 1.4426950408889634
SCALE = 0.125 * LOG2E
APART = 256.0
F32, BF16 = jnp.float32, jnp.bfloat16
ACROSS, DOWN = ((1,), (1,)), ((0,), (0,))


def dot(a, b, dims=((1,), (0,))):
    return lax.dot_general(a, b, (dims, ((), ())), preferred_element_type=F32)


def split(value):
    high = value.astype(BF16)
    return high, (value - high.astype(F32)).astype(BF16)


def head_means(value, spread, exact=True):
    high, low = split(value)
    means = dot(high, spread)
    return means + dot(low, spread) if exact else means


def gelu_and_slope(x):
    t = 1.0 / (1.0 + (0.3275911 * 0.7071067811865476) * jnp.abs(x))
    bell = jnp.exp2((-0.5 * LOG2E) * (x * x))
    poly = t * (0.127414796 + t * (-0.142248368 + t * (0.7107068705 + t * (-0.7265760135 + t * 0.5307027145))))
    tail = poly * bell
    phi = jnp.where(x >= 0, 1.0 - tail, tail)
    return x * phi, phi + (0.3989422804014327 * x) * bell


def lanes(index, width):
    return pl.ds(pl.multiple_of(index * width, width), width)


FIRST_OUT, SECOND_IN, SECOND_OUT, SECOND_BACK, LAST_OUT, LAST_BACK, STEPS = 7, 12, 19, 24, 31, 36, 43
LAST_TILE = 2


def up_first(index):
    return (index + 3) % TILES_IN


def clip(index, high):
    return jnp.clip(index, 0, high)


def in_tile(t):
    layer = ((t >= FIRST_OUT) & (t < LAST_OUT)).astype(jnp.int32)
    forward = jnp.where(t < FIRST_OUT, t, clip(t - SECOND_IN, 6))
    backward = up_first(jnp.where(t < LAST_OUT, clip(t - SECOND_BACK, 6), clip(t - LAST_BACK, 6)))
    return layer, jnp.where(t < SECOND_OUT, forward, backward)


def uses_in(t):
    forward = (t < FIRST_OUT) | ((t >= SECOND_IN) & (t < SECOND_OUT))
    return forward | ((t >= SECOND_BACK) & (t < LAST_OUT)) | (t >= LAST_BACK)


def out_tile(t):
    layer = ((t >= SECOND_IN) & (t < SECOND_BACK)).astype(jnp.int32)
    tile = jnp.where(t < SECOND_IN, clip(t - FIRST_OUT, 4), jnp.where(t < SECOND_BACK, clip(t - SECOND_OUT, 4), clip(t - LAST_OUT, 4)))
    return layer, tile


def in_terms(t):
    late = t >= LAST_BACK
    tile = up_first(jnp.where(late, t - LAST_BACK, clip(t - SECOND_BACK, 6)))
    return 1 - late.astype(jnp.int32), tile


def out_terms(t):
    late = t >= LAST_OUT
    return 1 - late.astype(jnp.int32), jnp.where(late, clip(t - LAST_OUT, 4), clip(t - SECOND_OUT, 4))


def gains_of(rows, width, start, count, columns):
    lane, column = lax.broadcasted_iota(jnp.int32, (128, columns), 0), lax.broadcasted_iota(jnp.int32, (128, columns), 1)
    place = column % (count * width)
    picked = dot(rows, jnp.where(lane == start + place % count, 1.0, 0.0).astype(BF16))
    row = lax.broadcasted_iota(jnp.int32, picked.shape, 0)
    owner = (lax.broadcasted_iota(jnp.int32, picked.shape, 1) % (count * width)) // count
    return jnp.sum(jnp.where(row == owner * BLOCK[2][0], picked, 0.0), 0, keepdims=True)


def compute_kernel(trading, counts, *refs):
    if trading:
        own, refs = refs[:3], refs[3:]
        (h_ref, cot_ref, augq_ref, augk_ref, spread_ref, section_out, grad_ref, grad_low, grad_land, gain_ref, terms_in_ref, terms_out_ref,
         full_in, full_out) = refs[:14]
        sems, swap, refs = refs[14:24], refs[24:27], refs[27:]
    else:
        (full_in, full_out, full_gains, h_ref, cot_ref, augq_ref, augk_ref, spread_ref, section_out, grad_ref, grad_low, grad_land,
         gain_ref, terms_in_ref, terms_out_ref) = refs[:15]
        own, sems, swap, refs = None, None, (), refs[15:]
    if trading:
        full_gains, refs = refs[0], refs[1:]
    (tiles, tile_sem, ln_ref, qg_ref, kg_ref, hidden, normed, scale, q, k, v, rq, rk, linv, slope, combined, dy, dproj, acc, dq, dk, do,
     dhigh, dlow) = refs
    t = pl.program_id(0)
    layer = in_tile(t)[0]
    project = (t < FIRST_OUT) | ((t >= SECOND_IN) & (t < SECOND_OUT))
    project_back = ((t >= SECOND_BACK) & (t < LAST_OUT)) | (t >= LAST_BACK)
    output = (t >= FIRST_OUT) & (t < SECOND_IN)
    output_both = (t >= SECOND_OUT) & (t < SECOND_BACK)
    back = (t >= LAST_OUT) & (t < LAST_BACK)
    layer = jnp.where(output, 0, layer)
    tile = jnp.where(project | project_back, in_tile(t)[1], out_tile(t)[1])
    section, trade = lax.axis_index("section"), None
    if swap:
        trade = Trade(section, section_out, hidden, dy, grad_land, *swap)
    spread = spread_ref[...]
    weights = Weights(Place() if trading else None, own, (full_in, full_out, full_gains), tiles, tile_sem, sems)
    weights.step(t)
    w_ref = tiles.at[t % 2]

    def halves(width=256):
        def run(body):
            def step(index):
                body(pl.ds(pl.multiple_of((index % 2) * 256, 256), 256), lanes(index // 2, width))
            loop(2 * D // width, step)
        return run

    def by_rows(body):
        loop(SLOTS // 128, lambda index: body(pl.ds(pl.multiple_of(index * 128, 128), 128)))

    @pl.when(t == 0)
    def _():
        hidden[0] = h_ref[...]
        gain_ref[...] = jnp.zeros_like(gain_ref)
        starts = (0, counts[0], counts[0] + counts[1])
        for which in range(2):
            rows = full_gains[which]
            for target, start, count, columns in zip((ln_ref, qg_ref, kg_ref), starts, counts, (D, 256, 256)):
                target[which] = gains_of(rows, D // counts[0], start, count, columns)

    def low_lanes():
        return lax.broadcasted_iota(jnp.int32, (SLOTS, 128), 1) < HD

    @pl.when(project & (tile == 0))
    def _():
        def body(rows):
            h = hidden[layer, rows, :].astype(F32)
            centred = h - jnp.mean(h, -1, keepdims=True)
            root = lax.rsqrt(jnp.mean(centred * centred, -1, keepdims=True) + EPSILON)
            scale[layer, rows, :] = jnp.broadcast_to(root, (128, 128))
            normed[layer, rows, :] = (centred * root * ln_ref[layer]).astype(BF16)
        by_rows(body)

    @pl.when(project)
    def _():
        acc[...] = dot(normed[layer], w_ref[...])

        def heads(low_ref, root_ref, gain, factor):
            @halves()
            def _(rows, columns):
                x = acc[rows, columns]
                centred = x - head_means(x, spread)
                root = lax.rsqrt(head_means(centred * centred, spread, False) + EPSILON)
                root_ref[layer, rows, columns] = root.astype(BF16)
                low_ref[layer, rows, columns] = (centred * root * (gain * factor)).astype(BF16)

        pl.when(tile == 0)(lambda: heads(q, rq, qg_ref[layer], SCALE))
        pl.when(tile == 1)(lambda: heads(k, rk, kg_ref[layer], 1.0))

        @pl.when(tile == 2)
        def _():
            v[layer] = acc[...].astype(BF16)
            low = low_lanes()
            augq, augk = augq_ref[...], augk_ref[...]
            ones = jnp.ones((SLOTS, 128), BF16)

            def pair(index):
                part = lanes(index, 128)
                qp, kp, vp = q[layer, :, part], k[layer, :, part], v[layer, :, part]
                results = []
                for head in (0, 1):
                    mine = low if head == 0 else ~low
                    scores = dot(jnp.where(mine, qp, augq), jnp.where(mine, kp, augk), ACROSS)
                    results.append(dot(jnp.exp2(scores).astype(BF16), jnp.where(mine, vp, ones)))
                inverse = 1.0 / pltpu.roll(jnp.where(low, results[1], results[0]), HD, 1)
                linv[layer, :, part] = inverse
                combined[layer, 0, :, part] = (jnp.where(low, results[0], results[1]) * inverse).astype(BF16)
            loop(PAIRS, pair)

        @pl.when(tile > 2)
        def _():
            @halves()
            def _(rows, columns):
                value, rise = gelu_and_slope(acc[rows, columns])
                slope[layer, tile - 3, rows, columns] = rise.astype(BF16)
                combined[layer, tile - 2, rows, columns] = value.astype(BF16)

    @pl.when(output | output_both)
    def _():
        product = dot(combined[layer, tile], w_ref[...])
        pl.when(tile == 0)(lambda: dq.__setitem__(..., hidden[layer].astype(F32) + product))
        pl.when(tile > 0)(lambda: dq.__setitem__(..., dq[...] + product))

        @pl.when(tile == TILES_OUT - 1)
        def _():
            result = dq[...].astype(BF16)
            hidden[layer + 1] = result
            if trade:
                trade.give_output(layer)
            else:
                section_out[layer] = result

    @pl.when(output_both & (tile == 0))
    def _():
        dy[...] = cot_ref[...]

    @pl.when(output_both | back)
    def _():
        acc[...] = dot(dy[...], w_ref[...], ACROSS)
        terms_out_ref[...] = dot(combined[layer, tile], dy[...], DOWN).astype(BF16)

        @pl.when(tile == 0)
        def _():
            @halves()
            def _(rows, columns):
                grad, inverse = acc[rows, columns], linv[layer, rows, columns]
                do[rows, columns] = (grad * inverse).astype(BF16)
                total = head_means(grad * combined[layer, 0, rows, columns].astype(F32), spread) * (inverse * -HD)
                for half in (0, 128):
                    part = pl.ds(pl.multiple_of(columns.start + half, 128), 128)
                    high, low = split(pltpu.roll(total[:, half : half + 128], HD, 1))
                    dhigh[rows, part] = high
                    dlow[rows, part] = low

        @pl.when(tile > 0)
        def _():
            @halves()
            def _(rows, columns):
                dproj[tile + 2, rows, columns] = (acc[rows, columns] * slope[layer, tile - 1, rows, columns].astype(F32)).astype(BF16)

    @pl.when(project_back & (tile == 0))
    def _():
        low = low_lanes()
        spot = lax.broadcasted_iota(jnp.int32, (SLOTS, 128), 1) % HD
        first = spot == 0
        augv = jnp.where(spot < 2, 1.0, 0.0).astype(BF16)
        augq, augk = augq_ref[...], augk_ref[...]
        none = jnp.zeros((SLOTS, 128), BF16)

        def pair(index):
            part = lanes(index, 128)
            qp, kp, vp, dop = q[layer, :, part], k[layer, :, part], v[layer, :, part], do[:, part]
            augd = jnp.where(first, dhigh[:, part], dlow[:, part])
            sums = [None, None, None]
            for head in (0, 1):
                mine = low if head == 0 else ~low
                e = jnp.exp2(dot(jnp.where(mine, kp, augk), jnp.where(mine, qp, augq), ACROSS))
                dp = dot(jnp.where(mine, vp, augv), jnp.where(mine, dop, augd), ACROSS)
                ds = (e * dp).astype(BF16)
                parts = (dot(ds, jnp.where(mine, kp, none), DOWN), dot(ds, jnp.where(mine, qp, none)),
                         dot(e.astype(BF16), jnp.where(mine, dop, none)))
                sums = [part_sum if total is None else total + part_sum for total, part_sum in zip(sums, parts)]
            dq[:, part] = sums[0] * 0.125
            dk[:, part] = sums[1] * (1.0 / LOG2E)
            dproj[2, :, part] = sums[2].astype(BF16)
        loop(PAIRS, pair)
        for which, grads, low_ref, root_ref, gain, factor in ((0, dq, q, rq, qg_ref, SCALE), (1, dk, k, rk, kg_ref, 1.0)):
            @halves()
            def _(rows, columns):
                grad, gains = grads[rows, columns], gain[layer]
                xhat = low_ref[layer, rows, columns].astype(F32) * (1.0 / (gains * factor))
                scaled = grad * gains
                mean = head_means(scaled, spread, False)
                along = head_means(scaled * xhat, spread, False)
                dproj[which, rows, columns] = (root_ref[layer, rows, columns].astype(F32) * (scaled - mean - xhat * along)).astype(BF16)
                gain_ref[layer, which + 1 : which + 2, columns] += jnp.sum(grad * xhat, 0, keepdims=True)

    @pl.when(project_back)
    def _():
        product = dot(dproj[tile], w_ref[...], ACROSS)
        pl.when(tile == up_first(0))(lambda: acc.__setitem__(..., product))
        pl.when(tile != up_first(0))(lambda: acc.__setitem__(..., acc[...] + product))
        terms_in_ref[...] = dot(normed[layer], dproj[tile], DOWN).astype(BF16)

        @pl.when(tile == LAST_TILE)
        def _():
            gains = ln_ref[layer]

            def body(rows):
                grad = acc[rows, :]
                xhat = normed[layer, rows, :].astype(F32) * (1.0 / gains)
                scaled = grad * gains
                mean = jnp.mean(scaled, -1, keepdims=True)
                along = jnp.mean(scaled * xhat, -1, keepdims=True)
                total = dy[rows, :].astype(F32) + scale[layer, rows, :1] * (scaled - mean - xhat * along)
                low = total.astype(BF16)
                if trade:
                    pl.when(layer == section)(lambda: grad_ref.__setitem__((rows, slice(None)), total))
                else:
                    grad_ref[layer, rows, :] = total
                pl.when(layer == 1)(lambda: dy.__setitem__((rows, slice(None)), low))
                pl.when(layer == 0)(lambda: grad_low.__setitem__((rows, slice(None)), low))
                gain_ref[layer, 0:1, :] += jnp.sum(grad * xhat, 0, keepdims=True)
            by_rows(body)
            if trade:
                pl.when(layer == 1)(trade.give_grad)
                pl.when(layer == 0)(trade.finish)


class Trade:
    def __init__(self, section, section_out, hidden, dy, grad_land, own_sem, send_sem, recv_sem):
        self.section, self.section_out, self.hidden, self.dy, self.grad_land = section, section_out, hidden, dy, grad_land
        self.own_sem, self.send_sem, self.recv_sem = own_sem, send_sem, recv_sem
        self.pair = (1 - section, lax.axis_index("wide"))

    def kept(self):
        return pltpu.make_async_copy(self.hidden.at[self.section + 1], self.section_out.at[self.section], self.own_sem)

    def copy(self, source, target, index):
        return pltpu.make_async_remote_copy(
            src_ref=source, dst_ref=target, send_sem=self.send_sem.at[index], recv_sem=self.recv_sem.at[index],
            device_id=self.pair, device_id_type=MESH)

    def given(self):
        return self.copy(self.hidden.at[2 - self.section], self.section_out.at[self.section], 0)

    def grad(self):
        return self.copy(self.dy, self.grad_land, 1)

    def give_output(self, layer):
        pl.when(layer == self.section)(lambda: self.kept().start())
        pl.when(layer != self.section)(lambda: self.given().start())

    def give_grad(self):
        pl.when(self.section == 0)(lambda: self.grad().start())

    def finish(self):
        self.kept().wait()
        self.given().wait_send()
        self.copy(self.hidden.at[2 - self.section], self.section_out.at[1 - self.section], 0).wait_recv()
        pl.when(self.section == 0)(lambda: self.grad().wait_send())
        pl.when(self.section == 1)(lambda: self.grad().wait_recv())


def both_layers(trading, counts, weights, gains, h, cot, augq, augk, spread):
    square = (SLOTS, D)

    def whole(*dims):
        return pl.BlockSpec(dims, lambda t: (0,) * len(dims))

    low, wide = (lambda *dims: pltpu.VMEM(dims, BF16)), (lambda *dims: pltpu.VMEM(dims, F32))
    any_space, dma = pl.BlockSpec(memory_space=pl.ANY), pltpu.SemaphoreType.DMA
    full = [jax.ShapeDtypeStruct(dims, BF16) for dims in ((2, D, TILES_IN * D), (2, TILES_OUT * D, D))]
    if trading:
        in_specs, operands = [any_space] * 3, (*weights, gains)
        out_specs, more_specs = [any_space, whole(*square), whole(*square), any_space], [any_space] * 2
        sems = [dma((5, 3, 16)), dma((3, 16)), dma((3, 16))] * 3 + [dma((3,))]
        grad_shape, extra, more = square, sems + [dma(()), dma((2,)), dma((2,)), low(2, 16 * BLOCK[2][0], 128)], full
        params = dict(collective_id=2, has_side_effects=True)
    else:
        in_specs, operands = [any_space] * 2 + [whole(*gains.shape)], (*weights, gains)
        out_specs, more_specs = [whole(2, *square), whole(2, *square), whole(*square), whole(*square)], []
        grad_shape, extra, more, params = (2,) + square, [], [], {}
    return pl.pallas_call(
        functools.partial(compute_kernel, trading, counts),
        grid=(STEPS,),
        in_specs=in_specs + [whole(*square), whole(*square), whole(SLOTS, 128), whole(SLOTS, 128), whole(256, 256)],
        out_specs=out_specs + [
            whole(2, 8, D), pl.BlockSpec((None, D, D), lambda t: (in_terms(t)[0], 0, in_terms(t)[1])),
            pl.BlockSpec((None, D, D), lambda t: (out_terms(t)[0], out_terms(t)[1], 0)),
        ] + more_specs,
        scratch_shapes=extra + [
            low(2, D, D), dma((2,)), wide(2, 1, D), wide(2, 1, 256), wide(2, 1, 256),
            low(3, *square), low(2, *square), wide(2, SLOTS, 128), low(2, *square), low(2, *square), low(2, *square), low(2, *square),
            low(2, *square), wide(2, *square), low(2, 4, *square), low(2, 5, *square), low(*square), low(7, *square), wide(*square),
            wide(*square), wide(*square), low(*square), low(*square), low(*square),
        ],
        out_shape=[
            jax.ShapeDtypeStruct((2,) + square, BF16), jax.ShapeDtypeStruct(grad_shape, F32), jax.ShapeDtypeStruct(square, BF16),
            jax.ShapeDtypeStruct(square, BF16), jax.ShapeDtypeStruct((2, 8, D), F32), *full,
        ] + more,
        compiler_params=pltpu.CompilerParams(vmem_limit_bytes=63 * 2**20, **params),
        name="both_layers",
    )(*operands, h, cot, augq, augk, spread)[:7]


def augment(image_id, token_size):
    high, low = split(jnp.log2(token_size.astype(F32)))
    same = (image_id[:, None] == jnp.arange(3)[None, :]).astype(BF16)
    one = jnp.ones_like(high)
    q = jnp.concatenate([one[:, None], one[:, None], same, one[:, None]], 1)
    k = jnp.concatenate([high[:, None], low[:, None], same * APART, one[:, None] * -APART], 1)
    return [jnp.tile(jnp.pad(part, ((0, 0), (0, HD - 6))), (1, 2)) for part in (q, k)]


def spread_matrix():
    head = jnp.arange(256) // HD
    return ((head[:, None] == head[None, :]) / HD).astype(BF16)


def gather_all(piece, axis):
    return lax.all_gather(lax.all_gather(piece, "wide", axis=axis, tiled=True), "section", axis=0, tiled=True)


def scatter_all(terms, axis):
    own = lax.psum_scatter(terms, "section", scatter_dimension=0, tiled=True)
    return lax.psum_scatter(own, "wide", scatter_dimension=axis, tiled=True)


def on_device(inputs, cotangent, token_size, image_id, w_in, w_out, ln_gain, q_gain, k_gain):
    section, wide = lax.axis_index("section"), lax.axis_index("wide")
    width = lax.axis_size("wide")
    blocks_fit = width == 16 and w_in.shape[1:] == BLOCK[0] and w_out.shape[1:] == BLOCK[1]
    ends = [0]
    for gain in (ln_gain, q_gain, k_gain):
        ends.append(ends[-1] + gain.shape[1])
    own_gains = jnp.concatenate([ln_gain, q_gain, k_gain], 1)
    gains = jnp.pad(own_gains, ((0, BLOCK[2][0] - 1), (0, BLOCK[2][1] - ends[3])))
    weights = (w_in[0], w_out[0])
    if not blocks_fit:
        weights = (gather_all(w_in, 1), gather_all(w_out, 1))
        gains = gather_all(gains[None], 1)
    augq, augk = augment(image_id[section, 0], token_size[section, 0])
    outs, grads, grad_low, grad_land, gain_terms, terms_in, terms_out = both_layers(
        blocks_fit, tuple(gain.shape[1] for gain in (ln_gain, q_gain, k_gain)), weights, gains, inputs[section, 0],
        cotangent[section, 0], augq, augk, spread_matrix())
    swap = [(0, 1), (1, 0)]

    def both_micro(pair):
        mine = lax.dynamic_index_in_dim(pair, section, 0, False)
        other = lax.dynamic_index_in_dim(pair, 1 - section, 0, False).astype(BF16)
        other = lax.ppermute(other, "section", swap).astype(mine.dtype)
        return jnp.where(section == 0, jnp.stack([mine, other]), jnp.stack([other, mine]))[None, :, None]

    heads = gain_terms[:, 1:3].reshape(2, 2, -1, HD).sum(2).reshape(2, -1)
    totals = jnp.concatenate([gain_terms[:, 0], heads], 1)
    places = (0, D, D + HD, D + 2 * HD)
    if blocks_fit:
        totals = jnp.pad(totals, ((0, 0), (0, 1024 - places[3]))).reshape(BLOCK[2])
        own_in, own_out, totals, last_land = scatter_terms(terms_in, terms_out, totals, grad_low)
        other = jnp.where(section == 0, last_land, grad_land).astype(F32)
        grads = jnp.where(section == 0, jnp.stack([grads, other]), jnp.stack([other, grads]))[None, :, None]
        outs = outs[None, :, None]
        own_in, own_out = own_in[None], own_out[None]
        totals = totals.reshape(2, 1024)
    else:
        own_in = scatter_all(terms_in, 1).astype(F32)
        own_out = scatter_all(terms_out, 1).astype(F32)
        totals = lax.psum(totals, ("section", "wide"))
        outs, grads = both_micro(outs), both_micro(grads)
    mine = lax.dynamic_index_in_dim(totals, section, 0, False)
    gain_grads = [
        lax.dynamic_slice_in_dim(mine[low:high], wide * gain.shape[1], gain.shape[1])[None]
        for low, high, gain in zip(places, places[1:], (ln_gain, q_gain, k_gain))
    ]
    return (outs, grads, own_in, own_out, *gain_grads)


def solution(mesh):
    return jax.shard_map(
        on_device,
        mesh=mesh,
        in_specs=(
            P(None, "wide", None, None),
            P(None, "wide", None, None),
            P(None, "wide", None),
            P(None, "wide", None),
            P("section", "wide", None),
            P("section", "wide", None),
            P("section", "wide"),
            P("section", "wide"),
            P("section", "wide"),
        ),
        out_specs=(
            P("section", None, "wide", None, None),
            P("section", None, "wide", None, None),
            P("section", "wide", None),
            P("section", "wide", None),
            P("section", "wide"),
            P("section", "wide"),
            P("section", "wide"),
        ),
        check_vma=False,
    )
```

```python
import functools

import jax
import jax.numpy as jnp
from jax import lax
from jax.experimental import pallas as pl
from jax.experimental.pallas import tpu as pltpu
from jax.sharding import PartitionSpec as P

MESH = pl.DeviceIdType.MESH
NZ = 4
BLOCK = ((48, 5376), (240, 768), (16, 128))
GATHER_CUTS = (2176, 96)
SCATTER_CUTS = (2176, 96)


class Place:
    def __init__(self):
        self.x, self.wide = lax.axis_index("section"), lax.axis_index("wide")
        self.y, self.z, self.c = (self.wide // 2) % 2, self.wide // 4, self.wide % 2

    def at(self, x, y, z, c=None):
        return (x, z * 4 + y * 2 + (self.c if c is None else c))

    def along(self, colour, block_z, far_first, far_second):
        dx = jnp.where(colour == 0, far_first, far_second)
        dy = jnp.where(colour == 0, far_second, far_first)
        return self.flip(self.x, dx), self.flip(self.y, dy), block_z

    @staticmethod
    def flip(value, far):
        return value + far - 2 * value * far

    def first(self, colour):
        return self.at(*self.along(colour, self.z, 1, 0))

    def second(self, colour):
        return self.at(*self.along(colour, self.z, 0, 1))

    def sibling(self):
        return self.at(self.x, self.y, self.z, 1 - self.c)


def greet(place, barrier=None):
    barrier = pltpu.get_barrier_semaphore() if barrier is None else barrier
    x, y, z = place.x, place.y, place.z

    def signal(device):
        pl.semaphore_signal(barrier, inc=1, device_id=device, device_id_type=MESH)

    signal(place.at(1 - x, y, z))
    signal(place.at(x, 1 - y, z))
    signal(place.sibling())
    pl.when(z < NZ - 1)(lambda: signal(place.at(x, y, z + 1)))
    pl.when(z > 0)(lambda: signal(place.at(x, y, z - 1)))
    pl.semaphore_wait(barrier, 3 + (z < NZ - 1).astype(jnp.int32) + (z > 0).astype(jnp.int32))


def number_of(block):
    return block[0] * 8 + block[1] * 4 + block[2]


def part_shape(cuts, array, colour):
    rows, cols = BLOCK[array]
    size = cuts[array]
    if array == 0:
        return rows, cols - 2 * size if colour is None else size
    return rows - 2 * size if colour is None else size, cols


def cut(ref, cuts, array, colour):
    if array == 2:
        return ref
    rows, cols = part_shape(cuts, array, colour)
    size = cuts[array]
    if array == 0:
        return ref.at[:, pl.ds(2 * size if colour is None else pl.multiple_of(colour * size, 128), cols)]
    return ref.at[pl.ds(2 * size if colour is None else pl.multiple_of(colour * size, 16), rows), :]


def loop(count, body):
    def step(index, carry):
        body(index)
        return carry
    lax.fori_loop(0, count, step, 0)


class Gather:
    def __init__(self, place, array, own, full, send_sem, recv_sem, core_sem):
        self.place, self.array, self.own, self.full = place, array, own, full
        self.send_sem, self.recv_sem, self.core_sem = send_sem, recv_sem, core_sem

    def view(self, block, colour, plane=None):
        rows = BLOCK[self.array][0]
        place = self.place
        start = (block[2] * 4 + block[1] * 2 + (place.c if plane is None else plane)) * rows
        return cut(self.full.at[block[0], pl.ds(pl.multiple_of(start, 16), rows), :], GATHER_CUTS, self.array, colour)

    def copy(self, link, device, block, colour, own=False, other_plane=False):
        kind = 2 if colour is None else colour
        number = number_of(block)
        target = self.view(block, colour, 1 - self.place.c if other_plane else None)
        source = cut(self.own, GATHER_CUTS, self.array, colour) if own else target
        sems = self.core_sem if link == 4 else self.recv_sem
        return pltpu.make_async_remote_copy(
            src_ref=source, dst_ref=target, send_sem=self.send_sem.at[link, kind, number], recv_sem=sems.at[kind, number],
            device_id=device, device_id_type=MESH)

    def visit(self, block, colour, onward, first, second, drain, condition=None, own=False):
        place = self.place

        def body():
            if not drain and not own:
                self.copy(0, place.sibling(), block, colour).wait_recv()

            def send(link, device):
                copy = self.copy(link, device, block, colour, own)
                copy.wait_send() if drain else copy.start()

            for link, step in onward:
                target = place.z + step
                pl.when((target >= 0) & (target < NZ))(functools.partial(send, link, place.at(place.x, place.y, target)))
            if first is not None:
                send(2, first)
            if second is not None:
                if isinstance(second, tuple) and len(second) == 3:
                    pl.when(second[2])(functools.partial(send, 3, second[:2]))
                else:
                    send(3, second)
            send(4, place.sibling())
        if condition is None:
            body()
        else:
            pl.when(condition)(body)

    def begin(self, drain=False):
        place = self.place
        me = (place.x, place.y, place.z)
        everywhere = ((0, 1), (1, -1))
        self.visit(me, None, everywhere, place.at(1 - place.x, place.y, place.z), place.at(place.x, 1 - place.y, place.z), drain, own=True)

        def body(colour):
            self.visit(me, colour, everywhere, place.first(colour), place.second(colour), drain, own=True)
        if self.array < 2:
            loop(2, body)

    def square(self, drain=False):
        place = self.place

        def body(index):
            far_x, far_y = (index != 1).astype(jnp.int32), (index != 0).astype(jnp.int32)
            block = (place.flip(place.x, far_x), place.flip(place.y, far_y), place.z)
            self.visit(block, None, ((0, 1), (1, -1)), None, place.at(place.x, 1 - place.y, place.z) + (index == 0,), drain)
        loop(3, body)

    def sided(self, distance, body):
        place = self.place

        def side_body(side):
            step = 1 - 2 * side
            block_z = place.z - step * distance
            body(side, block_z, (block_z >= 0) & (block_z < NZ) & ((distance > 0) | (side == 0)))
        loop(2, side_body)

    def onward(self, side):
        return ((0, 1), (1, -1))[side]

    def z_step(self, distance, drain=False):
        place = self.place
        for side in (0, 1):
            step = 1 - 2 * side
            block_z = place.z - step * distance

            def body(colour):
                self.visit((place.x, place.y, block_z), colour, ((side, step),), place.first(colour), place.second(colour), drain)
            pl.when((block_z >= 0) & (block_z < NZ))(lambda: loop(2, body))

    def line(self, distance, drain=False):
        place = self.place
        for side in (0, 1):
            step = 1 - 2 * side
            block_z = place.z - step * distance

            def body(index):
                block = (place.flip(place.x, index % 2), place.flip(place.y, index // 2), block_z)
                self.visit(block, None, ((side, step),), None, None, drain)
            pl.when((block_z >= 0) & (block_z < NZ))(lambda: loop(4, body))

    def a_step(self, distance, drain=False):
        place = self.place

        def body(side, block_z, there):
            def inner(colour):
                self.visit(place.along(colour, block_z, 1, 0), colour, (), None, place.second(colour), drain)
            pl.when(there)(lambda: loop(2, inner))
        self.sided(distance, body)

    def b_step(self, distance, drain=False):
        place = self.place

        def body(side, block_z, there):
            def inner(index):
                colour = index // 2
                self.visit(place.along(colour, block_z, index % 2, 1), colour, (), None, None, drain)
            pl.when(there)(lambda: loop(4, inner))
        self.sided(distance, body)

    def from_core(self):
        place = self.place

        def body(number):
            block = (number // 8, (number // 4) % 2, number % 4)
            self.copy(4, place.sibling(), block, None, other_plane=True).wait_recv()
            for colour in (0, 1) if self.array < 2 else ():
                self.copy(4, place.sibling(), block, colour, other_plane=True).wait_recv()
        loop(16, body)

    def drain(self):
        self.begin(True)
        self.square(True)

        def body(index):
            self.line(index + 1, True)
            if self.array < 2:
                self.z_step(index + 1, True)
                self.a_step(index, True)
                self.b_step(index, True)
        loop(NZ, body)


class Weights:
    def __init__(self, place, own, full, tiles, tile_sem, sems):
        self.place, self.full, self.tiles, self.tile_sem = place, full, tiles, tile_sem
        self.copies = []
        if place is None:
            return
        self.inner, self.outer, self.gains = [Gather(place, array, own[array], full[array], *sems[3 * array : 3 * array + 3]) for array in range(3)]
        for array in range(3):
            rows = BLOCK[array][0]
            target = full[array].at[place.x, pl.ds(pl.multiple_of(place.wide * rows, 16), rows), :]
            self.copies.append(pltpu.make_async_copy(own[array], target, sems[9].at[array]))

    def begin(self):
        greet(self.place)
        for copy in self.copies:
            copy.start()
        self.gains.begin()
        self.inner.begin()
        self.gains.square()
        self.inner.square()

        def early(index):
            self.inner.z_step(index + 1)
            self.inner.a_step(index)
            self.gains.line(index + 1)
            self.inner.line(index + 1)
        loop(NZ - 1, early)
        self.outer.begin()
        self.inner.a_step(NZ - 1)
        self.outer.square()

        def late(index):
            self.inner.b_step(index)
            pl.when(index == 1)(lambda: self.onward(0))
        loop(NZ, late)
        self.gains.from_core()
        self.inner.from_core()
        for copy in self.copies:
            copy.wait()

    def onward(self, index):
        self.outer.z_step(index + 1)
        self.outer.a_step(index)
        self.outer.line(index + 1)

    def end(self):
        loop(NZ, self.outer.b_step)
        self.outer.from_core()

    def drain(self):
        for array in (self.gains, self.inner, self.outer):
            array.drain()

    def fetch(self, t):
        slot = tile_slot(t)
        tile, sem = self.tiles.at[slot], self.tile_sem.at[slot]
        project = uses_in(t)

        def inner():
            layer, index = in_tile(t)
            return pltpu.make_async_copy(self.full[0].at[layer, :, pl.ds(pl.multiple_of(index * D, D), D)], tile, sem)

        def outer():
            layer, index = out_tile(t)
            return pltpu.make_async_copy(self.full[1].at[layer, pl.ds(pl.multiple_of(index * D, D), D), :], tile, sem)
        pl.when(project)(lambda: inner().start())
        pl.when(jnp.logical_not(project))(lambda: outer().start())

    def wait(self, t):
        slot = tile_slot(t)
        pltpu.make_async_copy(self.full[0].at[0, :, pl.ds(0, D)], self.tiles.at[slot], self.tile_sem.at[slot]).wait()

    def step(self, t):
        if self.place is not None:
            pl.when(t == 0)(self.begin)
            pl.when((t >= 2) & (t <= NZ))(lambda: self.onward(t - 1))
            pl.when(t == FIRST_OUT)(self.end)
            pl.when(t == LAST_OUT)(self.drain)
            held_back = FIRST_OUT
        else:
            held_back = 0
        following = jnp.where(t == LAST_HEADS - 1, LAST_PROJECT, t + 1)
        pl.when((t == 0) | (t == held_back))(lambda: self.fetch(t))
        pl.when(has_tile(t) & (following < STEPS) & (following != held_back))(lambda: self.fetch(following))
        pl.when(has_tile(t))(lambda: self.wait(t))


def add_into(target, source):
    rows = target.shape[0]

    def body(step):
        part = pl.ds(pl.multiple_of(step * 16, 16), 16)
        target[part, :] = (target[part, :].astype(jnp.float32) + source[part, :].astype(jnp.float32)).astype(jnp.bfloat16)
    loop(rows // 16, body)


class Scatter:
    def __init__(self, place, array, terms, held, core_land, land, rest_land, sems):
        self.place, self.array, self.terms, self.held, self.core_land = place, array, terms, held, core_land
        self.land, self.rest_land = land, rest_land
        self.send_sem, self.recv_sem, self.rest_send, self.rest_recv, self.core_send, self.core_recv, self.local_sem = sems

    def part(self, block, colour):
        return cut(self.held(number_of(block)), SCATTER_CUTS, self.array, colour)

    def copy(self, device, block, colour, slot):
        if colour is None:
            target, send_sem, recv_sem = self.rest_land(slot), self.rest_send.at[slot], self.rest_recv.at[slot]
        else:
            target, send_sem, recv_sem = self.land(colour, slot), self.send_sem.at[colour, slot], self.recv_sem.at[colour, slot]
        return pltpu.make_async_remote_copy(
            src_ref=self.part(block, colour), dst_ref=target, send_sem=send_sem, recv_sem=recv_sem, device_id=device,
            device_id_type=MESH)

    def send(self, device, block, colour, slot, drain):
        copy = self.copy(device, block, colour, slot)
        copy.wait_send() if drain else copy.start()

    def arrive(self, block, colour, slot, drain):
        if not drain:
            self.copy(self.place.sibling(), block, colour, slot).wait_recv()
            add_into(self.part(block, colour), self.rest_land(slot) if colour is None else self.land(colour, slot))

    def core_copy(self, block, mine):
        rows = BLOCK[self.array][0]
        place = self.place
        number = number_of(block)
        start = (block[2] * 4 + block[1] * 2 + (place.c if mine else 1 - place.c)) * rows
        source = self.terms.at[block[0], pl.ds(pl.multiple_of(start, 16), rows), :]
        if mine:
            return pltpu.make_async_copy(source, self.held(number), self.local_sem.at[number])
        return pltpu.make_async_remote_copy(
            src_ref=source, dst_ref=self.core_land(number), send_sem=self.core_send.at[number],
            recv_sem=self.core_recv.at[number], device_id=place.sibling(), device_id_type=MESH)

    def sided(self, distance, body):
        place = self.place

        def side_body(side):
            block_z = place.z + (2 * side - 1) * distance
            there = (block_z >= 0) & (block_z < NZ) & (distance < NZ) & (distance >= 0) & ((distance > 0) | (side == 0))
            pl.when(there)(lambda: body(block_z))
        loop(2, side_body)

    def start(self, distance):
        place = self.place

        def body(block_z):
            def inner(index):
                block = (place.flip(place.x, 1 - index % 2), place.flip(place.y, 1 - index // 2), block_z)
                self.core_copy(block, False).start()
                self.core_copy(block, True).start()
            loop(4, inner)
        self.sided(distance, body)

    def k_step(self, distance, drain=False):
        place = self.place

        def body(block_z):
            def inner(index):
                far_x, far_y = 1 - index % 2, 1 - index // 2
                block = (place.flip(place.x, far_x), place.flip(place.y, far_y), block_z)
                if not drain:
                    self.core_copy(block, True).wait()
                    copy = self.core_copy(block, False)
                    copy.wait_recv()
                    add_into(self.held(number_of(block)), self.core_land(number_of(block)))
                    copy.wait_send()

                def out(colour):
                    far_first = jnp.where(colour == 0, far_x, far_y)
                    far_second = jnp.where(colour == 0, far_y, far_x)
                    pl.when(far_second == 1)(lambda: self.send(place.second(colour), block, colour, far_first * 4 + block_z, drain))
                loop(2, out)
            loop(4, inner)
        self.sided(distance, body)

    def a_step(self, distance, drain=False):
        place = self.place

        def body(block_z):
            def inner(index):
                colour, far_first = index % 2, 1 - index // 2
                block = place.along(colour, block_z, far_first, 0)
                self.arrive(block, colour, far_first * 4 + block_z, drain)
                pl.when(far_first == 1)(lambda: self.send(place.first(colour), block, colour, 8 + block_z, drain))
            loop(4, inner)
        self.sided(distance, body)

    def b_step(self, distance):
        place = self.place

        def body(block_z):
            loop(2, lambda colour: self.arrive((place.x, place.y, block_z), colour, 8 + block_z, False))
        self.sided(distance, body)

    def toward(self, distance, body):
        place = self.place
        for side, step in ((0, -1), (1, 1)):
            block_z, behind = place.z + step * distance, place.z - step
            there = (block_z >= 0) & (block_z < NZ) & (distance < NZ) & (distance >= 0)
            pl.when(there)(functools.partial(body, block_z, side, step, (behind >= 0) & (behind < NZ)))

    def z_step(self, distance, drain=False):
        place = self.place

        def body(block_z, side, step, more):
            block = (place.x, place.y, block_z)
            slot = 12 + 4 * side + block_z

            def inner(colour):
                pl.when(more)(lambda: self.arrive(block, colour, slot, drain))
                pl.when(distance > 0)(lambda: self.send(place.at(place.x, place.y, place.z + step), block, colour, slot, drain))
            loop(2, inner)
        self.toward(distance, body)

    def line(self, distance, drain=False):
        place = self.place

        def body(block_z, side, step, more):
            def inner(index):
                block = (place.flip(place.x, 1 - index % 2), place.flip(place.y, 1 - index // 2), block_z)
                slot = 16 * side + number_of(block)
                pl.when(more)(lambda: self.arrive(block, None, slot, drain))
                pl.when(distance > 0)(lambda: self.send(place.at(place.x, place.y, place.z + step), block, None, slot, drain))
            loop(4, inner)
        self.toward(distance, body)

    def square(self, drain=False):
        place = self.place
        over_x, over_y = place.at(1 - place.x, place.y, place.z), place.at(place.x, 1 - place.y, place.z)
        far = (1 - place.x, place.y, place.z)
        self.send(over_y, (1 - place.x, 1 - place.y, place.z), None, 33, drain)
        self.send(over_y, (place.x, 1 - place.y, place.z), None, 32, drain)
        self.arrive(far, None, 33, drain)
        self.send(over_x, far, None, 34, drain)
        self.arrive((place.x, place.y, place.z), None, 32, drain)
        self.arrive((place.x, place.y, place.z), None, 34, drain)

    def drain(self):
        def body(distance):
            self.k_step(distance, True)
            self.a_step(distance, True)
            self.z_step(distance, True)
            self.line(distance, True)
        loop(NZ, body)
        self.square(True)


    MICRO = 19

    def begin(self):
        loop(NZ, lambda index: self.start(NZ - 1 - index))

    def micro(self, index):
        distance = NZ - 1 - index // 4
        turn = jnp.where(index < 16, index % 4, index - 12)
        pl.when(turn == 0)(lambda: self.k_step(distance))
        pl.when(turn == 1)(lambda: self.line(distance))

        @pl.when((turn == 2) | (turn == 5))
        def _():
            self.b_step(jnp.where(turn == 2, distance + 1, 0))

        @pl.when((turn == 2) | (turn == 6))
        def _():
            self.z_step(jnp.where(turn == 2, distance + 1, 0))
        pl.when(turn == 3)(lambda: self.a_step(distance))
        pl.when(turn == 4)(self.square)

    def finish(self, result, sem):
        copy = pltpu.make_async_copy(self.held(number_of((self.place.x, self.place.y, self.place.z))), result, sem)
        copy.start()
        self.drain()
        copy.wait()


def scatter_sems():
    dma = pltpu.SemaphoreType.DMA
    return [dma((2, 20)), dma((2, 20)), dma((35,)), dma((35,)), dma((16,)), dma((16,)), dma((16,)), dma(())]


class Total:
    def __init__(self, place, own, out, run, land, send_sem, recv_sem):
        self.place, self.own, self.out, self.run, self.land = place, own, out, run, land
        self.send_sem, self.recv_sem = send_sem, recv_sem
        x, y, z = place.x, place.y, place.z
        self.routes = (place.sibling(), place.at(x, 1 - y, z), place.at(1 - x, y, z), place.at(x, y, z + 1), place.at(x, y, z - 1))
        self.sends = (None, None, None, z < NZ - 1, z > 0)
        self.gets = (None, None, None, z > 0, z < NZ - 1)

    def copy(self, link):
        source = self.own if link == 0 else self.run.at[link]
        return pltpu.make_async_remote_copy(
            src_ref=source, dst_ref=self.land.at[link], send_sem=self.send_sem.at[link], recv_sem=self.recv_sem.at[link],
            device_id=self.routes[link], device_id_type=MESH)

    def step(self, index):
        def chain(link, base):
            self.run[link] = base[...]

            def get():
                self.copy(link).wait_recv()
                self.run[link] += self.land[link]
            pl.when(self.gets[link])(get)
            pl.when(self.sends[link])(lambda: self.copy(link).start())

        def swap(link):
            if link:
                self.copy(link - 1).wait_recv()
                self.run[link] = (self.own[...] if link == 1 else self.run[link - 1]) + self.land[link - 1]
            if link < 3:
                self.copy(link).start()

        for link in range(3):
            pl.when(index == link)(functools.partial(swap, link))

        @pl.when(index == 3)
        def _():
            self.copy(2).wait_recv()
            self.out[...] = self.run[2] + self.land[2]
            chain(3, self.out)
            chain(4, self.out)
            self.out[...] = self.run[3]

            def add():
                self.out[...] += self.land[4]
            pl.when(self.gets[4])(add)

    def drain(self):
        for link, sent in enumerate(self.sends):
            if sent is None:
                self.copy(link).wait_send()
            else:
                pl.when(sent)(lambda: self.copy(link).wait_send())


def scatter_kernel(terms, gains, grad, result, out_gains, grad_land, held, core_land, land, rest_land, run, small_land, send_sem, recv_sem,
                   grad_sem, *sems):
    place = Place()
    greet(place)
    grad_copy = pltpu.make_async_remote_copy(
        src_ref=grad, dst_ref=grad_land, send_sem=grad_sem.at[0], recv_sem=grad_sem.at[1],
        device_id=place.at(1 - place.x, place.y, place.z), device_id_type=MESH)
    total = Total(place, gains, out_gains, run, small_land, send_sem, recv_sem)
    scatter = Scatter(place, 0, terms, lambda number: held.at[number], lambda number: core_land.at[number],
                      lambda colour, slot: land.at[colour * 20 + slot], lambda slot: rest_land.at[slot], sems[:7])
    scatter.begin()

    def body(index):
        scatter.micro(index)
        pl.when(index % 4 == 0)(lambda: total.step(index // 4))
        pl.when((index == 15) & (place.x == 1))(lambda: grad_copy.start())
    loop(Scatter.MICRO, body)
    scatter.finish(result, sems[7])
    total.drain()
    pl.when(place.x == 1)(lambda: grad_copy.wait_send())
    pl.when(place.x == 0)(lambda: grad_copy.wait_recv())


def scatter_terms(terms, gains, grad):
    any_space, vmem, dma = pl.BlockSpec(memory_space=pl.ANY), pl.BlockSpec(memory_space=pltpu.VMEM), pltpu.SemaphoreType.DMA
    low = lambda *dims: pltpu.VMEM(dims, jnp.bfloat16)
    return pl.pallas_call(
        scatter_kernel,
        out_shape=(jax.ShapeDtypeStruct(BLOCK[0], jnp.bfloat16), jax.ShapeDtypeStruct(BLOCK[2], jnp.float32),
                   jax.ShapeDtypeStruct(grad.shape, grad.dtype)),
        in_specs=[any_space, vmem, any_space], out_specs=(any_space, vmem, any_space),
        scratch_shapes=[
            low(16, *BLOCK[0]), low(16, *BLOCK[0]), low(40, *part_shape(SCATTER_CUTS, 0, 0)), low(35, *part_shape(SCATTER_CUTS, 0, None)),
            *[pltpu.VMEM((5,) + BLOCK[2], jnp.float32)] * 2, dma((5,)), dma((5,)), dma((2,)), *scatter_sems()],
        compiler_params=pltpu.CompilerParams(collective_id=1, has_side_effects=True, vmem_limit_bytes=48 * 2**20),
        name="scatter_terms",
    )(terms, gains, grad)


SLOTS, D, HD, PAIRS = 512, 768, 64, 6
WIDE_PAIRS = 3
TILES_IN, TILES_OUT = 7, 5
EPSILON = 1e-06
LOG2E = 1.4426950408889634
SCALE = 0.125 * LOG2E
APART = 256.0
F32, BF16 = jnp.float32, jnp.bfloat16
ACROSS, DOWN = ((1,), (1,)), ((0,), (0,))


def dot(a, b, dims=((1,), (0,))):
    return lax.dot_general(a, b, (dims, ((), ())), preferred_element_type=F32)


def split(value):
    high = value.astype(BF16)
    return high, (value - high.astype(F32)).astype(BF16)


def head_means(value, spread, exact=True):
    high, low = split(value)
    means = dot(high, spread)
    return means + dot(low, spread) if exact else means


def gelu_and_slope(x):
    t = 1.0 / (1.0 + (0.3275911 * 0.7071067811865476) * jnp.abs(x))
    bell = jnp.exp2((-0.5 * LOG2E) * (x * x))
    poly = t * (0.127414796 + t * (-0.142248368 + t * (0.7107068705 + t * (-0.7265760135 + t * 0.5307027145))))
    tail = poly * bell
    phi = jnp.where(x >= 0, 1.0 - tail, tail)
    return x * phi, phi + (0.3989422804014327 * x) * bell


def lanes(index, width):
    return pl.ds(pl.multiple_of(index * width, width), width)


FIRST_OUT, SECOND_IN, SECOND_OUT, SECOND_BACK, LAST_OUT, LAST_BACK, LAST_HEADS, LAST_PROJECT, STEPS = 7, 12, 19, 24, 31, 36, 40, 46, 49
LAST_TILE = 2


def up_first(index):
    return (index + 3) % TILES_IN


def clip(index, high):
    return jnp.clip(index, 0, high)


def last_back(t):
    return up_first(jnp.where(t < LAST_HEADS, clip(t - LAST_BACK, 3), 4 + clip(t - LAST_PROJECT, 2)))


def in_tile(t):
    layer = ((t >= FIRST_OUT) & (t < LAST_OUT)).astype(jnp.int32)
    forward = jnp.where(t < FIRST_OUT, t, clip(t - SECOND_IN, 6))
    backward = jnp.where(t < LAST_OUT, up_first(clip(t - SECOND_BACK, 6)), last_back(t))
    return layer, jnp.where(t < SECOND_OUT, forward, backward)


def has_tile(t):
    return (t < LAST_HEADS) | (t >= LAST_PROJECT)


def tile_slot(t):
    return (t - (LAST_PROJECT - LAST_HEADS) * (t >= LAST_PROJECT)) % 2


def uses_in(t):
    forward = (t < FIRST_OUT) | ((t >= SECOND_IN) & (t < SECOND_OUT))
    return forward | ((t >= SECOND_BACK) & (t < LAST_OUT)) | ((t >= LAST_BACK) & has_tile(t))


def out_tile(t):
    layer = ((t >= SECOND_IN) & (t < SECOND_BACK)).astype(jnp.int32)
    tile = jnp.where(t < SECOND_IN, clip(t - FIRST_OUT, 4), jnp.where(t < SECOND_BACK, clip(t - SECOND_OUT, 4), clip(t - LAST_OUT, 4)))
    return layer, tile


def in_terms(t):
    late = t >= LAST_BACK
    return 1 - late.astype(jnp.int32), jnp.where(late, last_back(t), up_first(clip(t - SECOND_BACK, 6)))


def gains_of(rows, width, start, count, columns):
    lane, column = lax.broadcasted_iota(jnp.int32, (128, columns), 0), lax.broadcasted_iota(jnp.int32, (128, columns), 1)
    place = column % (count * width)
    picked = dot(rows, jnp.where(lane == start + place % count, 1.0, 0.0).astype(BF16))
    row = lax.broadcasted_iota(jnp.int32, picked.shape, 0)
    owner = (lax.broadcasted_iota(jnp.int32, picked.shape, 1) % (count * width)) // count
    return jnp.sum(jnp.where(row == owner * BLOCK[2][0], picked, 0.0), 0, keepdims=True)


def compute_kernel(trading, counts, *refs):
    if trading:
        own, refs = refs[:3], refs[3:]
    else:
        (full_in, full_out, full_gains), refs, own = refs[:3], refs[3:], None
    (inputs, cotangent, augq_ref, augk_ref, spread_ref, section_out, grad_ref, grad_low, grad_land, gain_ref, terms_in_ref, terms_out), refs = (
        refs[:12], refs[12:])
    (tiles, tile_sem, ln_ref, qg_ref, kg_ref, hidden, saved, scale, slope, combined, dy, dproj, acc, dq, dk, do, dhigh, dlow, terms_tile,
     terms_sem, entry_sem), refs = (refs[:21], refs[21:]) if not trading else (refs[3:24], refs[:3] + refs[24:])
    sems, swap, scatter_refs = None, (), None
    if trading:
        (full_in, full_out, own_out, full_gains), sems, swap, scatter_refs = refs[:4], refs[4:14], refs[14:17], refs[17:]
    normed, q, k, v, rq, rk, linv = [Saved(saved, which) for which in range(7)]
    t = pl.program_id(0)
    layer = in_tile(t)[0]
    project = (t < FIRST_OUT) | ((t >= SECOND_IN) & (t < SECOND_OUT))
    project_back = ((t >= SECOND_BACK) & (t < LAST_OUT)) | ((t >= LAST_BACK) & has_tile(t))
    output = (t >= FIRST_OUT) & (t < SECOND_IN)
    output_both = (t >= SECOND_OUT) & (t < SECOND_BACK)
    back = (t >= LAST_OUT) & (t < LAST_BACK)
    heads_now = (t == SECOND_BACK + 4) | ((t >= LAST_HEADS) & (t < LAST_PROJECT))
    layer = jnp.where(output, 0, layer)
    tile = jnp.where(project | project_back, in_tile(t)[1], out_tile(t)[1])
    section, trade = lax.axis_index("section"), None
    if swap:
        trade = Trade(section, section_out, hidden, dy, grad_land, *swap)
    spread = spread_ref[...]
    weights = Weights(Place() if trading else None, own, (full_in, full_out, full_gains), tiles, tile_sem, sems)
    weights.step(t)
    w_ref = tiles.at[tile_slot(t)]
    if trading:
        pl.when(t >= LAST_BACK)(lambda: outer_scatter(t, terms_out, terms_tile, terms_sem, own_out, combined, slope, saved, *scatter_refs))

    def halves(width=256):
        def run(body):
            def step(index):
                body(pl.ds(pl.multiple_of((index % 2) * 256, 256), 256), lanes(index // 2, width))
            loop(2 * D // width, step)
        return run

    def by_rows(body):
        loop(SLOTS // 128, lambda index: body(pl.ds(pl.multiple_of(index * 128, 128), 128)))

    @pl.when(t == 0)
    def _():
        entries = [pltpu.make_async_copy(inputs.at[section, 0], hidden.at[0], entry_sem.at[0]),
                   pltpu.make_async_copy(cotangent.at[section, 0], dy, entry_sem.at[1])]
        for entry in entries:
            entry.start()
        for entry in entries:
            entry.wait()
        gain_ref[...] = jnp.zeros_like(gain_ref)
        starts = (0, counts[0], counts[0] + counts[1])
        for which in range(2):
            rows = full_gains[which]
            for target, start, count, columns in zip((ln_ref, qg_ref, kg_ref), starts, counts, (D, 256, 256)):
                target[which] = gains_of(rows, D // counts[0], start, count, columns)

    def low_lanes():
        return lax.broadcasted_iota(jnp.int32, (SLOTS, 128), 1) < HD

    @pl.when(project & (tile == 0))
    def _():
        def body(rows):
            h = hidden[layer, rows, :].astype(F32)
            centred = h - jnp.mean(h, -1, keepdims=True)
            root = lax.rsqrt(jnp.mean(centred * centred, -1, keepdims=True) + EPSILON)
            scale[layer, rows, :] = jnp.broadcast_to(root, (128, 128))
            normed[layer, rows, :] = (centred * root * ln_ref[layer]).astype(BF16)
        by_rows(body)

    @pl.when(project)
    def _():
        acc[...] = dot(normed[layer, :, :], w_ref[...])

        def heads(low_ref, root_ref, gain, factor):
            @halves()
            def _(rows, columns):
                x = acc[rows, columns]
                centred = x - head_means(x, spread)
                root = lax.rsqrt(head_means(centred * centred, spread, False) + EPSILON)
                root_ref[layer, rows, columns] = root.astype(BF16)
                low_ref[layer, rows, columns] = (centred * root * (gain * factor)).astype(BF16)

        pl.when(tile == 0)(lambda: heads(q, rq, qg_ref[layer], SCALE))
        pl.when(tile == 1)(lambda: heads(k, rk, kg_ref[layer], 1.0))

        @pl.when(tile == 2)
        def _():
            v[layer, :, :] = acc[...].astype(BF16)
            low = low_lanes()
            augq, augk = augq_ref[...], augk_ref[...]
            ones = jnp.ones((SLOTS, 128), BF16)

            def pair(index):
                part = lanes(index, 128)
                qp, kp, vp = q[layer, :, part], k[layer, :, part], v[layer, :, part]
                results = []
                for head in (0, 1):
                    mine = low if head == 0 else ~low
                    scores = dot(jnp.where(mine, qp, augq), jnp.where(mine, kp, augk), ACROSS)
                    results.append(dot(jnp.exp2(scores).astype(BF16), jnp.where(mine, vp, ones)))
                inverse = 1.0 / pltpu.roll(jnp.where(low, results[1], results[0]), HD, 1)
                linv[layer, :, part] = inverse.astype(BF16)
                combined[layer, 0, :, part] = (jnp.where(low, results[0], results[1]) * inverse).astype(BF16)
            loop(PAIRS, pair)

        @pl.when(tile > 2)
        def _():
            @halves()
            def _(rows, columns):
                value, rise = gelu_and_slope(acc[rows, columns])
                slope[layer, tile - 3, rows, columns] = rise.astype(BF16)
                combined[layer, tile - 2, rows, columns] = value.astype(BF16)

    @pl.when(output | output_both)
    def _():
        product = dot(combined[layer, tile], w_ref[...])
        pl.when(tile == 0)(lambda: dq.__setitem__(..., hidden[layer].astype(F32) + product))
        pl.when(tile > 0)(lambda: dq.__setitem__(..., dq[...] + product))

        @pl.when(tile == TILES_OUT - 1)
        def _():
            result = dq[...].astype(BF16)
            hidden[layer + 1] = result
            if trade:
                trade.give_output(layer)
            else:
                section_out[layer] = result

    @pl.when(output_both | back)
    def _():
        acc[...] = dot(dy[...], w_ref[...], ACROSS)
        made = jnp.where(t < LAST_OUT, t - SECOND_OUT, TILES_OUT + t - LAST_OUT)
        pl.when(made >= 2)(lambda: terms_copy(terms_out, terms_tile, terms_sem, made % 2, 0, 0).wait())
        terms_tile[made % 2] = dot(combined[layer, tile], dy[...], DOWN).astype(BF16)
        terms_copy(terms_out, terms_tile, terms_sem, made % 2, layer, tile).start()
        if not trading:
            pl.when(t == LAST_BACK - 1)(lambda: terms_settled(terms_out, terms_tile, terms_sem))

        @pl.when(tile == 0)
        def _():
            @halves()
            def _(rows, columns):
                grad, inverse = acc[rows, columns], linv[layer, rows, columns].astype(F32)
                do[rows, columns] = (grad * inverse).astype(BF16)
                total = head_means(grad * combined[layer, 0, rows, columns].astype(F32), spread) * (inverse * -HD)
                for half in (0, 128):
                    part = pl.ds(pl.multiple_of(columns.start + half, 128), 128)
                    high, low = split(pltpu.roll(total[:, half : half + 128], HD, 1))
                    dhigh[rows, part] = high
                    dlow[rows, part] = low

        @pl.when(tile > 0)
        def _():
            @halves()
            def _(rows, columns):
                dproj[tile + 2, rows, columns] = (acc[rows, columns] * slope[layer, tile - 1, rows, columns].astype(F32)).astype(BF16)

    @pl.when(heads_now)
    def _():
        low = low_lanes()
        spot = lax.broadcasted_iota(jnp.int32, (SLOTS, 128), 1) % HD
        first = spot == 0
        augv = jnp.where(spot < 2, 1.0, 0.0).astype(BF16)
        augq, augk = augq_ref[...], augk_ref[...]
        none = jnp.zeros((SLOTS, 128), BF16)

        def pair(index):
            part = lanes(index, 128)
            qp, kp, vp, dop = q[layer, :, part], k[layer, :, part], v[layer, :, part], do[:, part]
            augd = jnp.where(first, dhigh[:, part], dlow[:, part])
            sums = [None, None, None]
            for head in (0, 1):
                mine = low if head == 0 else ~low
                e = jnp.exp2(dot(jnp.where(mine, kp, augk), jnp.where(mine, qp, augq), ACROSS))
                dp = dot(jnp.where(mine, vp, augv), jnp.where(mine, dop, augd), ACROSS)
                ds = (e * dp).astype(BF16)
                parts = (dot(ds, jnp.where(mine, kp, none), DOWN), dot(ds, jnp.where(mine, qp, none)),
                         dot(e.astype(BF16), jnp.where(mine, dop, none)))
                sums = [part_sum if total is None else total + part_sum for total, part_sum in zip(sums, parts)]
            dq[:, part] = sums[0] * 0.125
            dk[:, part] = sums[1] * (1.0 / LOG2E)
            dproj[2, :, part] = sums[2].astype(BF16)
        late = t >= LAST_HEADS
        first_pair = jnp.where(late, t - LAST_HEADS, 0)
        loop(jnp.where(late, 1, PAIRS), lambda index: pair(first_pair + index))

    @pl.when(project_back & (tile == 0))
    def _():
        for which, grads, low_ref, root_ref, gain, factor in ((0, dq, q, rq, qg_ref, SCALE), (1, dk, k, rk, kg_ref, 1.0)):
            @halves()
            def _(rows, columns):
                grad, gains = grads[rows, columns], gain[layer]
                xhat = low_ref[layer, rows, columns].astype(F32) * (1.0 / (gains * factor))
                scaled = grad * gains
                mean = head_means(scaled, spread, False)
                along = head_means(scaled * xhat, spread, False)
                dproj[which, rows, columns] = (root_ref[layer, rows, columns].astype(F32) * (scaled - mean - xhat * along)).astype(BF16)
                gain_ref[layer, which + 1 : which + 2, columns] += jnp.sum(grad * xhat, 0, keepdims=True)

    @pl.when(project_back)
    def _():
        product = dot(dproj[tile], w_ref[...], ACROSS)
        pl.when(tile == up_first(0))(lambda: acc.__setitem__(..., product))
        pl.when(tile != up_first(0))(lambda: acc.__setitem__(..., acc[...] + product))
        terms_in_ref[...] = dot(normed[layer, :, :], dproj[tile], DOWN).astype(BF16)

        @pl.when(tile == LAST_TILE)
        def _():
            gains = ln_ref[layer]

            def body(rows):
                grad = acc[rows, :]
                xhat = normed[layer, rows, :].astype(F32) * (1.0 / gains)
                scaled = grad * gains
                mean = jnp.mean(scaled, -1, keepdims=True)
                along = jnp.mean(scaled * xhat, -1, keepdims=True)
                total = dy[rows, :].astype(F32) + scale[layer, rows, :1] * (scaled - mean - xhat * along)
                low = total.astype(BF16)
                if trade:
                    pl.when(layer == section)(lambda: grad_ref.__setitem__((rows, slice(None)), total))
                else:
                    grad_ref[layer, rows, :] = total
                pl.when(layer == 1)(lambda: dy.__setitem__((rows, slice(None)), low))
                pl.when(layer == 0)(lambda: grad_low.__setitem__((rows, slice(None)), low))
                gain_ref[layer, 0:1, :] += jnp.sum(grad * xhat, 0, keepdims=True)
            by_rows(body)
            if trade:
                pl.when(layer == 1)(trade.give_grad)
                pl.when(layer == 0)(trade.finish)


class Saved:
    def __init__(self, ref, which):
        self.ref, self.which = ref, which

    def __getitem__(self, index):
        return self.ref[(index[0], self.which) + index[1:]]

    def __setitem__(self, index, value):
        self.ref[(index[0], self.which) + index[1:]] = value


def terms_copy(terms_out, terms_tile, terms_sem, slot, layer, tile):
    target = terms_out.at[layer, pl.ds(pl.multiple_of(tile * D, D), D), :]
    return pltpu.make_async_copy(terms_tile.at[slot], target, terms_sem.at[slot])


def terms_settled(terms_out, terms_tile, terms_sem):
    for slot in range(2):
        terms_copy(terms_out, terms_tile, terms_sem, slot, 0, 0).wait()


def outer_scatter(t, terms_out, terms_tile, terms_sem, own_out, combined, slope, saved, rest_land, ready_sem, *sems):
    place = Place()
    rows = BLOCK[1][0]

    def half(number):
        return pl.ds(pl.multiple_of((number % 2) * rows, 16), rows)

    def held(number):
        return combined.at[number // 10, (number // 2) % 5, half(number)]

    def core_land(number):
        return slope.at[number // 8, (number // 2) % 4, half(number)]

    def land(colour, slot):
        piece = colour * 20 + slot
        return saved.at[1, piece // 5, pl.ds(pl.multiple_of((piece % 5) * 96, 16), 96)]

    scatter = Scatter(place, 1, terms_out, held, core_land, land, lambda slot: rest_land.at[slot], sems[:7])

    @pl.when(t == LAST_BACK)
    def _():
        terms_settled(terms_out, terms_tile, terms_sem)
        greet(place, ready_sem)
        scatter.begin()

    turn = t - LAST_BACK
    count = jnp.where(turn == 0, 2, jnp.where(t == STEPS - 1, Scatter.MICRO - 13, 1))
    loop(count, lambda index: scatter.micro(jnp.where(turn == 0, 0, turn + 1) + index))
    pl.when(t == STEPS - 1)(lambda: scatter.finish(own_out, sems[7]))


class Trade:
    def __init__(self, section, section_out, hidden, dy, grad_land, own_sem, send_sem, recv_sem):
        self.section, self.section_out, self.hidden, self.dy, self.grad_land = section, section_out, hidden, dy, grad_land
        self.own_sem, self.send_sem, self.recv_sem = own_sem, send_sem, recv_sem
        self.pair = (1 - section, lax.axis_index("wide"))

    def kept(self):
        return pltpu.make_async_copy(self.hidden.at[self.section + 1], self.section_out.at[self.section], self.own_sem)

    def copy(self, source, target, index):
        return pltpu.make_async_remote_copy(
            src_ref=source, dst_ref=target, send_sem=self.send_sem.at[index], recv_sem=self.recv_sem.at[index],
            device_id=self.pair, device_id_type=MESH)

    def given(self):
        return self.copy(self.hidden.at[2 - self.section], self.section_out.at[self.section], 0)

    def grad(self):
        return self.copy(self.dy, self.grad_land, 1)

    def give_output(self, layer):
        pl.when(layer == self.section)(lambda: self.kept().start())
        pl.when(layer != self.section)(lambda: self.given().start())

    def give_grad(self):
        pl.when(self.section == 0)(lambda: self.grad().start())

    def finish(self):
        self.kept().wait()
        self.given().wait_send()
        self.copy(self.hidden.at[2 - self.section], self.section_out.at[1 - self.section], 0).wait_recv()
        pl.when(self.section == 0)(lambda: self.grad().wait_send())
        pl.when(self.section == 1)(lambda: self.grad().wait_recv())


def both_layers(trading, counts, weights, gains, inputs, cotangent, augq, augk, spread):
    square = (SLOTS, D)

    def whole(*dims):
        return pl.BlockSpec(dims, lambda t: (0,) * len(dims))

    low, wide = (lambda *dims: pltpu.VMEM(dims, BF16)), (lambda *dims: pltpu.VMEM(dims, F32))
    any_space, dma = pl.BlockSpec(memory_space=pl.ANY), pltpu.SemaphoreType.DMA
    full = [jax.ShapeDtypeStruct(dims, BF16) for dims in ((2, D, TILES_IN * D), (2, TILES_OUT * D, D))]
    if trading:
        in_specs, operands = [any_space] * 3, (*weights, gains)
        out_specs, more_specs = [any_space, whole(*square), whole(*square), any_space], [any_space] * 3
        sems = [dma((5, 3, 16)), dma((3, 16)), dma((3, 16))] * 3 + [dma((3,))]
        extra = [low(2, 16 * BLOCK[2][0], 128)] + sems + [dma(()), dma((2,)), dma((2,))]
        extra += [low(35, *part_shape(SCATTER_CUTS, 1, None)), pltpu.SemaphoreType.REGULAR] + scatter_sems()
        grad_shape, more = square, full + [jax.ShapeDtypeStruct(BLOCK[1], BF16)]
        params = dict(collective_id=2, has_side_effects=True)
    else:
        in_specs, operands = [any_space] * 2 + [whole(*gains.shape)], (*weights, gains)
        out_specs, more_specs = [whole(2, *square), whole(2, *square), whole(*square), whole(*square)], []
        grad_shape, extra, more, params = (2,) + square, [], [], {}
    return pl.pallas_call(
        functools.partial(compute_kernel, trading, counts),
        grid=(STEPS,),
        in_specs=in_specs + [any_space, any_space, whole(SLOTS, 128), whole(SLOTS, 128), whole(256, 256)],
        out_specs=out_specs + [
            whole(2, 8, D), pl.BlockSpec((None, D, D), lambda t: (in_terms(t)[0], 0, in_terms(t)[1])), any_space,
        ] + more_specs,
        scratch_shapes=[
            low(2, D, D), dma((2,)), wide(2, 1, D), wide(2, 1, 256), wide(2, 1, 256),
            low(3, *square), low(2, 8, *square), wide(2, SLOTS, 128), low(2, 4, *square), low(2, 5, *square), low(*square), low(7, *square),
            wide(*square), wide(*square), wide(*square), low(*square), low(*square), low(*square), low(2, D, D), dma((2,)), dma((2,)),
        ] + extra,
        out_shape=[
            jax.ShapeDtypeStruct((2,) + square, BF16), jax.ShapeDtypeStruct(grad_shape, F32), jax.ShapeDtypeStruct(square, BF16),
            jax.ShapeDtypeStruct(square, BF16), jax.ShapeDtypeStruct((2, 8, D), F32), *full,
        ] + more,
        compiler_params=pltpu.CompilerParams(vmem_limit_bytes=63 * 2**20, **params),
        name="both_layers",
    )(*operands, inputs, cotangent, augq, augk, spread)


def augment(image_id, token_size):
    high, low = split(jnp.log2(token_size.astype(F32)))
    same = (image_id[:, None] == jnp.arange(3)[None, :]).astype(BF16)
    one = jnp.ones_like(high)
    q = jnp.concatenate([one[:, None], one[:, None], same, one[:, None]], 1)
    k = jnp.concatenate([high[:, None], low[:, None], same * APART, one[:, None] * -APART], 1)
    return [jnp.tile(jnp.pad(part, ((0, 0), (0, HD - 6))), (1, 2)) for part in (q, k)]


def spread_matrix():
    head = jnp.arange(256) // HD
    return ((head[:, None] == head[None, :]) / HD).astype(BF16)


def gather_all(piece, axis):
    return lax.all_gather(lax.all_gather(piece, "wide", axis=axis, tiled=True), "section", axis=0, tiled=True)


def scatter_all(terms, axis):
    own = lax.psum_scatter(terms, "section", scatter_dimension=0, tiled=True)
    return lax.psum_scatter(own, "wide", scatter_dimension=axis, tiled=True)


def on_device(inputs, cotangent, token_size, image_id, w_in, w_out, ln_gain, q_gain, k_gain):
    section, wide = lax.axis_index("section"), lax.axis_index("wide")
    width = lax.axis_size("wide")
    blocks_fit = width == 16 and w_in.shape[1:] == BLOCK[0] and w_out.shape[1:] == BLOCK[1]
    ends = [0]
    for gain in (ln_gain, q_gain, k_gain):
        ends.append(ends[-1] + gain.shape[1])
    own_gains = jnp.concatenate([ln_gain, q_gain, k_gain], 1)
    gains = jnp.pad(own_gains, ((0, BLOCK[2][0] - 1), (0, BLOCK[2][1] - ends[3])))
    weights = (w_in[0], w_out[0])
    if not blocks_fit:
        weights = (gather_all(w_in, 1), gather_all(w_out, 1))
        gains = gather_all(gains[None], 1)
    augq, augk = augment(image_id[section, 0], token_size[section, 0])
    outs, grads, grad_low, grad_land, gain_terms, terms_in, terms_out, *more = both_layers(
        blocks_fit, tuple(gain.shape[1] for gain in (ln_gain, q_gain, k_gain)), weights, gains, inputs,
        cotangent, augq, augk, spread_matrix())
    swap = [(0, 1), (1, 0)]

    def both_micro(pair):
        mine = lax.dynamic_index_in_dim(pair, section, 0, False)
        other = lax.dynamic_index_in_dim(pair, 1 - section, 0, False).astype(BF16)
        other = lax.ppermute(other, "section", swap).astype(mine.dtype)
        return jnp.where(section == 0, jnp.stack([mine, other]), jnp.stack([other, mine]))[None, :, None]

    heads = gain_terms[:, 1:3].reshape(2, 2, -1, HD).sum(2).reshape(2, -1)
    totals = jnp.concatenate([gain_terms[:, 0], heads], 1)
    places = (0, D, D + HD, D + 2 * HD)
    if blocks_fit:
        totals = jnp.pad(totals, ((0, 0), (0, 1024 - places[3]))).reshape(BLOCK[2])
        own_in, totals, last_land = scatter_terms(terms_in, totals, grad_low)
        other = jnp.where(section == 0, last_land, grad_land).astype(F32)
        grads = jnp.where(section == 0, jnp.stack([grads, other]), jnp.stack([other, grads]))[None, :, None]
        outs = outs[None, :, None]
        own_in, own_out = own_in[None].astype(F32), more[2][None].astype(F32)
        totals = totals.reshape(2, 1024)
    else:
        own_in = scatter_all(terms_in, 1).astype(F32)
        own_out = scatter_all(terms_out, 1).astype(F32)
        totals = lax.psum(totals, ("section", "wide"))
        outs, grads = both_micro(outs), both_micro(grads)
    mine = lax.dynamic_index_in_dim(totals, section, 0, False)
    gain_grads = [
        lax.dynamic_slice_in_dim(mine[low:high], wide * gain.shape[1], gain.shape[1])[None]
        for low, high, gain in zip(places, places[1:], (ln_gain, q_gain, k_gain))
    ]
    return (outs, grads, own_in, own_out, *gain_grads)


def solution(mesh):
    return jax.shard_map(
        on_device,
        mesh=mesh,
        in_specs=(
            P(None, "wide", None, None),
            P(None, "wide", None, None),
            P(None, "wide", None),
            P(None, "wide", None),
            P("section", "wide", None),
            P("section", "wide", None),
            P("section", "wide"),
            P("section", "wide"),
            P("section", "wide"),
        ),
        out_specs=(
            P("section", None, "wide", None, None),
            P("section", None, "wide", None, None),
            P("section", "wide", None),
            P("section", "wide", None),
            P("section", "wide"),
            P("section", "wide"),
            P("section", "wide"),
        ),
        check_vma=False,
    )
```

```python
import functools

import jax
import jax.numpy as jnp
from jax import lax
from jax.experimental import pallas as pl
from jax.experimental.pallas import tpu as pltpu
from jax.sharding import PartitionSpec as P

MESH = pl.DeviceIdType.MESH
NZ = 4
BLOCK = ((48, 5376), (240, 768), (16, 128))
GATHER_CUTS = (2176, 96)
SCATTER_CUTS = (2048, 96)


class Place:
    def __init__(self):
        self.x, self.wide = lax.axis_index("section"), lax.axis_index("wide")
        self.y, self.z, self.c = (self.wide // 2) % 2, self.wide // 4, self.wide % 2

    def at(self, x, y, z, c=None):
        return (x, z * 4 + y * 2 + (self.c if c is None else c))

    def along(self, colour, block_z, far_first, far_second):
        dx = jnp.where(colour == 0, far_first, far_second)
        dy = jnp.where(colour == 0, far_second, far_first)
        return self.flip(self.x, dx), self.flip(self.y, dy), block_z

    @staticmethod
    def flip(value, far):
        return value + far - 2 * value * far

    def first(self, colour):
        return self.at(*self.along(colour, self.z, 1, 0))

    def second(self, colour):
        return self.at(*self.along(colour, self.z, 0, 1))

    def sibling(self):
        return self.at(self.x, self.y, self.z, 1 - self.c)


def greet(place, barrier=None):
    barrier = pltpu.get_barrier_semaphore() if barrier is None else barrier
    x, y, z = place.x, place.y, place.z

    def signal(device):
        pl.semaphore_signal(barrier, inc=1, device_id=device, device_id_type=MESH)

    signal(place.at(1 - x, y, z))
    signal(place.at(x, 1 - y, z))
    signal(place.sibling())
    pl.when(z < NZ - 1)(lambda: signal(place.at(x, y, z + 1)))
    pl.when(z > 0)(lambda: signal(place.at(x, y, z - 1)))
    pl.semaphore_wait(barrier, 3 + (z < NZ - 1).astype(jnp.int32) + (z > 0).astype(jnp.int32))


def number_of(block):
    return block[0] * 8 + block[1] * 4 + block[2]


def part_shape(cuts, array, colour):
    rows, cols = BLOCK[array]
    size = cuts[array]
    if array == 0:
        return rows, cols - 2 * size if colour is None else size
    return rows - 2 * size if colour is None else size, cols


def cut(ref, cuts, array, colour):
    if array == 2:
        return ref
    rows, cols = part_shape(cuts, array, colour)
    size = cuts[array]
    if array == 0:
        return ref.at[:, pl.ds(2 * size if colour is None else pl.multiple_of(colour * size, 128), cols)]
    return ref.at[pl.ds(2 * size if colour is None else pl.multiple_of(colour * size, 16), rows), :]


def loop(count, body):
    def step(index, carry):
        body(index)
        return carry
    lax.fori_loop(0, count, step, 0)


class Gather:
    def __init__(self, place, array, own, full, send_sem, recv_sem, core_sem):
        self.place, self.array, self.own, self.full = place, array, own, full
        self.send_sem, self.recv_sem, self.core_sem = send_sem, recv_sem, core_sem

    def view(self, block, colour, plane=None):
        rows = BLOCK[self.array][0]
        place = self.place
        start = (block[2] * 4 + block[1] * 2 + (place.c if plane is None else plane)) * rows
        return cut(self.full.at[block[0], pl.ds(pl.multiple_of(start, 16), rows), :], GATHER_CUTS, self.array, colour)

    def copy(self, link, device, block, colour, own=False, other_plane=False):
        kind = 2 if colour is None else colour
        number = number_of(block)
        target = self.view(block, colour, 1 - self.place.c if other_plane else None)
        source = cut(self.own, GATHER_CUTS, self.array, colour) if own else target
        sems = self.core_sem if link == 4 else self.recv_sem
        return pltpu.make_async_remote_copy(
            src_ref=source, dst_ref=target, send_sem=self.send_sem.at[link, kind, number], recv_sem=sems.at[kind, number],
            device_id=device, device_id_type=MESH)

    def visit(self, block, colour, onward, first, second, drain, condition=None, own=False):
        place = self.place

        def body():
            if not drain and not own:
                self.copy(0, place.sibling(), block, colour).wait_recv()

            def send(link, device):
                copy = self.copy(link, device, block, colour, own)
                copy.wait_send() if drain else copy.start()

            for link, step in onward:
                target = place.z + step
                pl.when((target >= 0) & (target < NZ))(functools.partial(send, link, place.at(place.x, place.y, target)))
            if first is not None:
                send(2, first)
            if second is not None:
                if isinstance(second, tuple) and len(second) == 3:
                    pl.when(second[2])(functools.partial(send, 3, second[:2]))
                else:
                    send(3, second)
            send(4, place.sibling())
        if condition is None:
            body()
        else:
            pl.when(condition)(body)

    def begin(self, drain=False):
        place = self.place
        me = (place.x, place.y, place.z)
        everywhere = ((0, 1), (1, -1))
        self.visit(me, None, everywhere, place.at(1 - place.x, place.y, place.z), place.at(place.x, 1 - place.y, place.z), drain, own=True)

        def body(colour):
            self.visit(me, colour, everywhere, place.first(colour), place.second(colour), drain, own=True)
        if self.array < 2:
            loop(2, body)

    def square(self, drain=False):
        place = self.place

        def body(index):
            far_x, far_y = (index != 1).astype(jnp.int32), (index != 0).astype(jnp.int32)
            block = (place.flip(place.x, far_x), place.flip(place.y, far_y), place.z)
            self.visit(block, None, ((0, 1), (1, -1)), None, place.at(place.x, 1 - place.y, place.z) + (index == 0,), drain)
        loop(3, body)

    def sided(self, distance, body):
        place = self.place

        def side_body(side):
            step = 1 - 2 * side
            block_z = place.z - step * distance
            body(side, block_z, (block_z >= 0) & (block_z < NZ) & ((distance > 0) | (side == 0)))
        loop(2, side_body)

    def onward(self, side):
        return ((0, 1), (1, -1))[side]

    def z_step(self, distance, drain=False):
        place = self.place
        for side in (0, 1):
            step = 1 - 2 * side
            block_z = place.z - step * distance

            def body(colour):
                self.visit((place.x, place.y, block_z), colour, ((side, step),), place.first(colour), place.second(colour), drain)
            pl.when((block_z >= 0) & (block_z < NZ))(lambda: loop(2, body))

    def line(self, distance, drain=False):
        place = self.place
        for side in (0, 1):
            step = 1 - 2 * side
            block_z = place.z - step * distance

            def body(index):
                block = (place.flip(place.x, index % 2), place.flip(place.y, index // 2), block_z)
                self.visit(block, None, ((side, step),), None, None, drain)
            pl.when((block_z >= 0) & (block_z < NZ))(lambda: loop(4, body))

    def a_step(self, distance, drain=False):
        place = self.place

        def body(side, block_z, there):
            def inner(colour):
                self.visit(place.along(colour, block_z, 1, 0), colour, (), None, place.second(colour), drain)
            pl.when(there)(lambda: loop(2, inner))
        self.sided(distance, body)

    def b_step(self, distance, drain=False):
        place = self.place

        def body(side, block_z, there):
            def inner(index):
                colour = index // 2
                self.visit(place.along(colour, block_z, index % 2, 1), colour, (), None, None, drain)
            pl.when(there)(lambda: loop(4, inner))
        self.sided(distance, body)

    def from_core(self):
        place = self.place

        def body(number):
            block = (number // 8, (number // 4) % 2, number % 4)
            self.copy(4, place.sibling(), block, None, other_plane=True).wait_recv()
            for colour in (0, 1) if self.array < 2 else ():
                self.copy(4, place.sibling(), block, colour, other_plane=True).wait_recv()
        loop(16, body)

    def drain(self):
        self.begin(True)
        self.square(True)

        def body(index):
            self.line(index + 1, True)
            if self.array < 2:
                self.z_step(index + 1, True)
                self.a_step(index, True)
                self.b_step(index, True)
        loop(NZ, body)


class Weights:
    def __init__(self, place, own, full, tiles, tile_sem, sems):
        self.place, self.full, self.tiles, self.tile_sem = place, full, tiles, tile_sem
        self.copies = []
        if place is None:
            return
        self.inner, self.outer, self.gains = [Gather(place, array, own[array], full[array], *sems[3 * array : 3 * array + 3]) for array in range(3)]
        for array in range(3):
            rows = BLOCK[array][0]
            target = full[array].at[place.x, pl.ds(pl.multiple_of(place.wide * rows, 16), rows), :]
            self.copies.append(pltpu.make_async_copy(own[array], target, sems[9].at[array]))

    def begin(self):
        greet(self.place)
        for copy in self.copies:
            copy.start()
        self.gains.begin()
        self.inner.begin()
        self.gains.square()
        self.inner.square()

        def early(index):
            self.inner.z_step(index + 1)
            self.inner.a_step(index)
            self.gains.line(index + 1)
            self.inner.line(index + 1)
        loop(NZ - 1, early)
        self.outer.begin()
        self.inner.a_step(NZ - 1)
        self.outer.square()

        def late(index):
            self.inner.b_step(index)
            pl.when(index == 1)(lambda: self.onward(0))
        loop(NZ, late)
        self.gains.from_core()
        self.inner.from_core()
        for copy in self.copies:
            copy.wait()

    def onward(self, index):
        self.outer.z_step(index + 1)
        self.outer.a_step(index)
        self.outer.line(index + 1)

    def end(self):
        loop(NZ, self.outer.b_step)
        self.outer.from_core()

    def drain(self):
        for array in (self.gains, self.inner, self.outer):
            array.drain()

    def fetch(self, t):
        slot = tile_slot(t)
        tile, sem = self.tiles.at[slot], self.tile_sem.at[slot]
        project = uses_in(t)

        def inner():
            layer, index = in_tile(t)
            return pltpu.make_async_copy(self.full[0].at[layer, :, pl.ds(pl.multiple_of(index * D, D), D)], tile, sem)

        def outer():
            layer, index = out_tile(t)
            return pltpu.make_async_copy(self.full[1].at[layer, pl.ds(pl.multiple_of(index * D, D), D), :], tile, sem)
        pl.when(project)(lambda: inner().start())
        pl.when(jnp.logical_not(project))(lambda: outer().start())

    def wait(self, t):
        slot = tile_slot(t)
        pltpu.make_async_copy(self.full[0].at[0, :, pl.ds(0, D)], self.tiles.at[slot], self.tile_sem.at[slot]).wait()

    def step(self, t):
        if self.place is not None:
            pl.when(t == 0)(self.begin)
            pl.when((t >= 2) & (t <= NZ))(lambda: self.onward(t - 1))
            pl.when(t == FIRST_OUT)(self.end)
            pl.when(t == LAST_OUT)(self.drain)
            held_back = FIRST_OUT
        else:
            held_back = 0
        following = jnp.where(t == LAST_HEADS - 1, LAST_PROJECT, t + 1)
        pl.when((t == 0) | (t == held_back))(lambda: self.fetch(t))
        pl.when(has_tile(t) & (following < STEPS) & (following != held_back))(lambda: self.fetch(following))
        pl.when(has_tile(t))(lambda: self.wait(t))


def add_into(target, source):
    def body(step):
        part = pl.ds(pl.multiple_of(step * 48, 16), 48)
        target[part, :] = target[part, :] + source[part, :]
    loop(target.shape[0] // 48, body)


OUTER_ORDER = (
    ("k3", "l3"), (), ("a3", "k2"), (), ("l2",), ("b3", "k1"), ("a2", "z3"), (), ("l1",), (), ("k0", "b2"), ("z2", "a1", "l0"), (),
    ("a0", "b1", "z1", "s", "b0", "z0"))
INNER_ORDER = (
    "k3", "k2", "l3", "k1", "l2", "a3", "k0", "l1", "b3", "a2", "z3", "a1", "l0", "b2", "z2", "b1", "a0", "z1", "s", "b0", "z0")
INNER_GRAD = 14


class Scatter:
    def __init__(self, place, array, terms, held, core_land, land, rest_land, sems):
        self.place, self.array, self.terms, self.held, self.core_land = place, array, terms, held, core_land
        self.land, self.rest_land = land, rest_land
        self.send_sem, self.recv_sem, self.rest_send, self.rest_recv, self.core_send, self.core_recv, self.local_sem = sems

    def part(self, block, colour):
        return cut(self.held(number_of(block)), SCATTER_CUTS, self.array, colour)

    def copy(self, device, block, colour, slot):
        if colour is None:
            target, send_sem, recv_sem = self.rest_land(slot), self.rest_send.at[slot], self.rest_recv.at[slot]
        else:
            target, send_sem, recv_sem = self.land(colour, slot), self.send_sem.at[colour, slot], self.recv_sem.at[colour, slot]
        return pltpu.make_async_remote_copy(
            src_ref=self.part(block, colour), dst_ref=target, send_sem=send_sem, recv_sem=recv_sem, device_id=device,
            device_id_type=MESH)

    def send(self, device, block, colour, slot, drain):
        copy = self.copy(device, block, colour, slot)
        copy.wait_send() if drain else copy.start()

    def arrive(self, block, colour, slot, drain):
        if not drain:
            self.copy(self.place.sibling(), block, colour, slot).wait_recv()
            add_into(self.part(block, colour), self.rest_land(slot) if colour is None else self.land(colour, slot))

    def core_copy(self, block, mine):
        rows = BLOCK[self.array][0]
        place = self.place
        number = number_of(block)
        start = (block[2] * 4 + block[1] * 2 + (place.c if mine else 1 - place.c)) * rows
        source = self.terms.at[block[0], pl.ds(pl.multiple_of(start, 16), rows), :]
        if mine:
            return pltpu.make_async_copy(source, self.held(number), self.local_sem.at[number])
        return pltpu.make_async_remote_copy(
            src_ref=source, dst_ref=self.core_land(number), send_sem=self.core_send.at[number],
            recv_sem=self.core_recv.at[number], device_id=place.sibling(), device_id_type=MESH)

    def sided(self, distance, body):
        place = self.place

        def side_body(side):
            block_z = place.z + (2 * side - 1) * distance
            there = (block_z >= 0) & (block_z < NZ) & (distance < NZ) & (distance >= 0) & ((distance > 0) | (side == 0))
            pl.when(there)(lambda: body(block_z))
        loop(2, side_body)

    def start(self, distance):
        place = self.place

        def body(block_z):
            def inner(index):
                block = (place.flip(place.x, 1 - index % 2), place.flip(place.y, 1 - index // 2), block_z)
                self.core_copy(block, False).start()
                self.core_copy(block, True).start()
            loop(4, inner)
        self.sided(distance, body)

    def k_step(self, distance, drain=False):
        place = self.place

        def body(block_z):
            def inner(index):
                far_x, far_y = 1 - index % 2, 1 - index // 2
                block = (place.flip(place.x, far_x), place.flip(place.y, far_y), block_z)
                if not drain:
                    self.core_copy(block, True).wait()
                    copy = self.core_copy(block, False)
                    copy.wait_recv()
                    add_into(self.held(number_of(block)), self.core_land(number_of(block)))
                    copy.wait_send()

                def out(colour):
                    far_first = jnp.where(colour == 0, far_x, far_y)
                    far_second = jnp.where(colour == 0, far_y, far_x)
                    pl.when(far_second == 1)(lambda: self.send(place.second(colour), block, colour, far_first * 4 + block_z, drain))
                loop(2, out)
            loop(4, inner)
        self.sided(distance, body)

    def a_step(self, distance, drain=False):
        place = self.place

        def body(block_z):
            def inner(index):
                colour, far_first = index % 2, 1 - index // 2
                block = place.along(colour, block_z, far_first, 0)
                self.arrive(block, colour, far_first * 4 + block_z, drain)
                pl.when(far_first == 1)(lambda: self.send(place.first(colour), block, colour, 8 + block_z, drain))
            loop(4, inner)
        self.sided(distance, body)

    def b_step(self, distance):
        place = self.place

        def body(block_z):
            loop(2, lambda colour: self.arrive((place.x, place.y, block_z), colour, 8 + block_z, False))
        self.sided(distance, body)

    def toward(self, distance, body):
        place = self.place
        for side, step in ((0, -1), (1, 1)):
            block_z, behind = place.z + step * distance, place.z - step
            there = (block_z >= 0) & (block_z < NZ) & (distance < NZ) & (distance >= 0)
            pl.when(there)(functools.partial(body, block_z, side, step, (behind >= 0) & (behind < NZ)))

    def z_step(self, distance, drain=False):
        place = self.place

        def body(block_z, side, step, more):
            block = (place.x, place.y, block_z)
            slot = 12 + 4 * side + block_z

            def inner(colour):
                pl.when(more)(lambda: self.arrive(block, colour, slot, drain))
                pl.when(distance > 0)(lambda: self.send(place.at(place.x, place.y, place.z + step), block, colour, slot, drain))
            loop(2, inner)
        self.toward(distance, body)

    def line(self, distance, drain=False):
        place = self.place

        def body(block_z, side, step, more):
            def inner(index):
                block = (place.flip(place.x, 1 - index % 2), place.flip(place.y, 1 - index // 2), block_z)
                slot = 16 * side + number_of(block)
                pl.when(more)(lambda: self.arrive(block, None, slot, drain))
                pl.when(distance > 0)(lambda: self.send(place.at(place.x, place.y, place.z + step), block, None, slot, drain))
            loop(4, inner)
        self.toward(distance, body)

    def square(self, drain=False):
        place = self.place
        over_x, over_y = place.at(1 - place.x, place.y, place.z), place.at(place.x, 1 - place.y, place.z)
        far = (1 - place.x, place.y, place.z)
        self.send(over_y, (1 - place.x, 1 - place.y, place.z), None, 33, drain)
        self.send(over_y, (place.x, 1 - place.y, place.z), None, 32, drain)
        self.arrive(far, None, 33, drain)
        self.send(over_x, far, None, 34, drain)
        self.arrive((place.x, place.y, place.z), None, 32, drain)
        self.arrive((place.x, place.y, place.z), None, 34, drain)

    def drain(self):
        def body(distance):
            self.k_step(distance, True)
            self.a_step(distance, True)
            self.z_step(distance, True)
            self.line(distance, True)
        loop(NZ, body)
        self.square(True)


    STEPS = "klabzs"

    def begin(self):
        loop(NZ, lambda index: self.start(NZ - 1 - index))

    def run(self, order, first, count, also=None):
        codes = [(self.STEPS.index(step[0]), int(step[1:] or 0)) for step in order]

        def body(index):
            index = first + index
            which, distance = [sum((index == place).astype(jnp.int32) * code[part] for place, code in enumerate(codes)) for part in (0, 1)]
            calls = (self.k_step, self.line, self.a_step, self.b_step, self.z_step)
            for code, call in enumerate(calls):
                pl.when(which == code)(lambda: call(distance))
            pl.when(which == len(calls))(self.square)
            if also:
                also(index)
        loop(count, body)

    def finish(self, result, sem):
        copy = pltpu.make_async_copy(self.held(number_of((self.place.x, self.place.y, self.place.z))), result, sem)
        copy.start()
        self.drain()
        copy.wait()


def scatter_sems():
    dma = pltpu.SemaphoreType.DMA
    return [dma((2, 20)), dma((2, 20)), dma((35,)), dma((35,)), dma((16,)), dma((16,)), dma((16,)), dma(())]


class Total:
    def __init__(self, place, own, out, run, land, send_sem, recv_sem):
        self.place, self.own, self.out, self.run, self.land = place, own, out, run, land
        self.send_sem, self.recv_sem = send_sem, recv_sem
        x, y, z = place.x, place.y, place.z
        self.routes = (place.sibling(), place.at(x, 1 - y, z), place.at(1 - x, y, z), place.at(x, y, z + 1), place.at(x, y, z - 1))
        self.sends = (None, None, None, z < NZ - 1, z > 0)
        self.gets = (None, None, None, z > 0, z < NZ - 1)

    def copy(self, link):
        source = self.own if link == 0 else self.run.at[link]
        return pltpu.make_async_remote_copy(
            src_ref=source, dst_ref=self.land.at[link], send_sem=self.send_sem.at[link], recv_sem=self.recv_sem.at[link],
            device_id=self.routes[link], device_id_type=MESH)

    def step(self, index):
        def chain(link, base):
            self.run[link] = base[...]

            def get():
                self.copy(link).wait_recv()
                self.run[link] += self.land[link]
            pl.when(self.gets[link])(get)
            pl.when(self.sends[link])(lambda: self.copy(link).start())

        def swap(link):
            if link:
                self.copy(link - 1).wait_recv()
                self.run[link] = (self.own[...] if link == 1 else self.run[link - 1]) + self.land[link - 1]
            if link < 3:
                self.copy(link).start()

        for link in range(3):
            pl.when(index == link)(functools.partial(swap, link))

        @pl.when(index == 3)
        def _():
            self.copy(2).wait_recv()
            self.out[...] = self.run[2] + self.land[2]
            chain(3, self.out)
            chain(4, self.out)
            self.out[...] = self.run[3]

            def add():
                self.out[...] += self.land[4]
            pl.when(self.gets[4])(add)

    def drain(self):
        for link, sent in enumerate(self.sends):
            if sent is None:
                self.copy(link).wait_send()
            else:
                pl.when(sent)(lambda: self.copy(link).wait_send())


def scatter_kernel(terms, gains, grad, result, out_gains, grad_land, held, core_land, land, rest_land, run, small_land, send_sem, recv_sem,
                   grad_sem, *sems):
    place = Place()
    greet(place)
    grad_copy = pltpu.make_async_remote_copy(
        src_ref=grad, dst_ref=grad_land, send_sem=grad_sem.at[0], recv_sem=grad_sem.at[1],
        device_id=place.at(1 - place.x, place.y, place.z), device_id_type=MESH)
    total = Total(place, gains, out_gains, run, small_land, send_sem, recv_sem)
    scatter = Scatter(place, 0, terms, lambda number: held.at[number], lambda number: core_land.at[number],
                      lambda colour, slot: land.at[colour * 20 + slot], lambda slot: rest_land.at[slot], sems[:7])
    scatter.begin()

    def also(index):
        pl.when(index % 4 == 0)(lambda: total.step(index // 4))
        pl.when((index == INNER_GRAD) & (place.x == 1))(lambda: grad_copy.start())
    scatter.run(INNER_ORDER, 0, len(INNER_ORDER), also)
    scatter.finish(result, sems[7])
    total.drain()
    pl.when(place.x == 1)(lambda: grad_copy.wait_send())
    pl.when(place.x == 0)(lambda: grad_copy.wait_recv())


def scatter_terms(terms, gains, grad):
    any_space, vmem, dma = pl.BlockSpec(memory_space=pl.ANY), pl.BlockSpec(memory_space=pltpu.VMEM), pltpu.SemaphoreType.DMA
    low = lambda *dims: pltpu.VMEM(dims, jnp.bfloat16)
    return pl.pallas_call(
        scatter_kernel,
        out_shape=(jax.ShapeDtypeStruct(BLOCK[0], jnp.bfloat16), jax.ShapeDtypeStruct(BLOCK[2], jnp.float32),
                   jax.ShapeDtypeStruct(grad.shape, grad.dtype)),
        in_specs=[any_space, vmem, any_space], out_specs=(any_space, vmem, any_space),
        scratch_shapes=[
            low(16, *BLOCK[0]), low(16, *BLOCK[0]), low(40, *part_shape(SCATTER_CUTS, 0, 0)), low(35, *part_shape(SCATTER_CUTS, 0, None)),
            *[pltpu.VMEM((5,) + BLOCK[2], jnp.float32)] * 2, dma((5,)), dma((5,)), dma((2,)), *scatter_sems()],
        compiler_params=pltpu.CompilerParams(collective_id=1, has_side_effects=True, vmem_limit_bytes=48 * 2**20),
        name="scatter_terms",
    )(terms, gains, grad)


SLOTS, D, HD, PAIRS = 512, 768, 64, 6
WIDE_PAIRS = 3
TILES_IN, TILES_OUT = 7, 5
EPSILON = 1e-06
LOG2E = 1.4426950408889634
SCALE = 0.125 * LOG2E
APART = 256.0
F32, BF16 = jnp.float32, jnp.bfloat16
ACROSS, DOWN = ((1,), (1,)), ((0,), (0,))


def dot(a, b, dims=((1,), (0,))):
    return lax.dot_general(a, b, (dims, ((), ())), preferred_element_type=F32)


def split(value):
    high = value.astype(BF16)
    return high, (value - high.astype(F32)).astype(BF16)


def head_means(value, spread, exact=True):
    high, low = split(value)
    means = dot(high, spread)
    return means + dot(low, spread) if exact else means


def gelu_and_slope(x):
    t = 1.0 / (1.0 + (0.3275911 * 0.7071067811865476) * jnp.abs(x))
    bell = jnp.exp2((-0.5 * LOG2E) * (x * x))
    poly = t * (0.127414796 + t * (-0.142248368 + t * (0.7107068705 + t * (-0.7265760135 + t * 0.5307027145))))
    tail = poly * bell
    phi = jnp.where(x >= 0, 1.0 - tail, tail)
    return x * phi, phi + (0.3989422804014327 * x) * bell


def lanes(index, width):
    return pl.ds(pl.multiple_of(index * width, width), width)


FIRST_OUT, SECOND_IN, SECOND_OUT, SECOND_BACK, LAST_OUT, LAST_BACK, LAST_HEADS, LAST_PROJECT, STEPS = 7, 12, 19, 24, 31, 36, 40, 46, 49
LAST_TILE = 2


def up_first(index):
    return (index + 3) % TILES_IN


def clip(index, high):
    return jnp.clip(index, 0, high)


def last_back(t):
    return up_first(jnp.where(t < LAST_HEADS, clip(t - LAST_BACK, 3), 4 + clip(t - LAST_PROJECT, 2)))


def in_tile(t):
    layer = ((t >= FIRST_OUT) & (t < LAST_OUT)).astype(jnp.int32)
    forward = jnp.where(t < FIRST_OUT, t, clip(t - SECOND_IN, 6))
    backward = jnp.where(t < LAST_OUT, up_first(clip(t - SECOND_BACK, 6)), last_back(t))
    return layer, jnp.where(t < SECOND_OUT, forward, backward)


def has_tile(t):
    return (t < LAST_HEADS) | (t >= LAST_PROJECT)


def tile_slot(t):
    return (t - (LAST_PROJECT - LAST_HEADS) * (t >= LAST_PROJECT)) % 2


def uses_in(t):
    forward = (t < FIRST_OUT) | ((t >= SECOND_IN) & (t < SECOND_OUT))
    return forward | ((t >= SECOND_BACK) & (t < LAST_OUT)) | ((t >= LAST_BACK) & has_tile(t))


def out_tile(t):
    layer = ((t >= SECOND_IN) & (t < SECOND_BACK)).astype(jnp.int32)
    tile = jnp.where(t < SECOND_IN, clip(t - FIRST_OUT, 4), jnp.where(t < SECOND_BACK, clip(t - SECOND_OUT, 4), clip(t - LAST_OUT, 4)))
    return layer, tile


def in_terms(t):
    late = t >= LAST_BACK
    return 1 - late.astype(jnp.int32), jnp.where(late, last_back(t), up_first(clip(t - SECOND_BACK, 6)))


def gains_of(rows, width, start, count, columns):
    lane, column = lax.broadcasted_iota(jnp.int32, (128, columns), 0), lax.broadcasted_iota(jnp.int32, (128, columns), 1)
    place = column % (count * width)
    picked = dot(rows, jnp.where(lane == start + place % count, 1.0, 0.0).astype(BF16))
    row = lax.broadcasted_iota(jnp.int32, picked.shape, 0)
    owner = (lax.broadcasted_iota(jnp.int32, picked.shape, 1) % (count * width)) // count
    return jnp.sum(jnp.where(row == owner * BLOCK[2][0], picked, 0.0), 0, keepdims=True)


def compute_kernel(trading, counts, *refs):
    if trading:
        own, refs = refs[:3], refs[3:]
    else:
        (full_in, full_out, full_gains), refs, own = refs[:3], refs[3:], None
    (inputs, cotangent, augq_ref, augk_ref, spread_ref, section_out, grad_ref, grad_low, grad_land, totals_ref, terms_in_ref, terms_out), refs = (
        refs[:12], refs[12:])
    (tiles, tile_sem, ln_ref, qg_ref, kg_ref, hidden, saved, scale, slope, combined, dy, dproj, acc, dq, dk, do, dhigh, dlow, terms_tile,
     terms_sem, entry_sem, gain_ref), refs = (refs[:22], refs[22:]) if not trading else (refs[3:25], refs[:3] + refs[25:])
    sems, swap, scatter_refs = None, (), None
    if trading:
        (full_in, full_out, own_out, full_gains), sems, swap, scatter_refs = refs[:4], refs[4:14], refs[14:17], refs[17:]
    normed, q, k, v, rq, rk, linv = [Saved(saved, which) for which in range(7)]
    t = pl.program_id(0)
    layer = in_tile(t)[0]
    project = (t < FIRST_OUT) | ((t >= SECOND_IN) & (t < SECOND_OUT))
    project_back = ((t >= SECOND_BACK) & (t < LAST_OUT)) | ((t >= LAST_BACK) & has_tile(t))
    output = (t >= FIRST_OUT) & (t < SECOND_IN)
    output_both = (t >= SECOND_OUT) & (t < SECOND_BACK)
    back = (t >= LAST_OUT) & (t < LAST_BACK)
    heads_now = (t == SECOND_BACK + 4) | ((t >= LAST_HEADS) & (t < LAST_PROJECT))
    layer = jnp.where(output, 0, layer)
    tile = jnp.where(project | project_back, in_tile(t)[1], out_tile(t)[1])
    section, trade = lax.axis_index("section"), None
    if swap:
        trade = Trade(section, section_out, hidden, dy, grad_land, *swap)
    spread = spread_ref[...]
    weights = Weights(Place() if trading else None, own, (full_in, full_out, full_gains), tiles, tile_sem, sems)
    weights.step(t)
    w_ref = tiles.at[tile_slot(t)]

    def halves(width=256):
        def run(body):
            def step(index):
                body(pl.ds(pl.multiple_of((index % 2) * 256, 256), 256), lanes(index // 2, width))
            loop(2 * D // width, step)
        return run

    def by_rows(body):
        loop(SLOTS // 128, lambda index: body(pl.ds(pl.multiple_of(index * 128, 128), 128)))

    @pl.when(t == 0)
    def _():
        entries = [pltpu.make_async_copy(inputs.at[section, 0], hidden.at[0], entry_sem.at[0]),
                   pltpu.make_async_copy(cotangent.at[section, 0], dy, entry_sem.at[1])]
        for entry in entries:
            entry.start()
        for entry in entries:
            entry.wait()
        gain_ref[...] = jnp.zeros_like(gain_ref)
        starts = (0, counts[0], counts[0] + counts[1])
        for which in range(2):
            rows = full_gains[which]
            for target, start, count, columns in zip((ln_ref, qg_ref, kg_ref), starts, counts, (D, 256, 256)):
                target[which] = gains_of(rows, D // counts[0], start, count, columns)

    def low_lanes():
        return lax.broadcasted_iota(jnp.int32, (SLOTS, 128), 1) < HD

    def fold_gains():
        for which in range(2):
            parts = [[gain_ref[which, row : row + 1, 128 * part : 128 * (part + 1)] for part in range(PAIRS)] for row in range(3)]
            sums = [functools.reduce(jnp.add, row) for row in parts[1:]]
            sums = [total + pltpu.roll(total, HD, 1) for total in sums]
            for part in range(PAIRS):
                totals_ref[8 * which + part : 8 * which + part + 1, :] = parts[0][part]
            first = lax.broadcasted_iota(jnp.int32, (1, 128), 1) < HD
            totals_ref[8 * which + 6 : 8 * which + 7, :] = jnp.where(first, *sums)
            totals_ref[8 * which + 7 : 8 * which + 8, :] = jnp.zeros((1, 128), F32)

    @pl.when(project & (tile == 0))
    def _():
        def body(rows):
            h = hidden[layer, rows, :].astype(F32)
            centred = h - jnp.mean(h, -1, keepdims=True)
            root = lax.rsqrt(jnp.mean(centred * centred, -1, keepdims=True) + EPSILON)
            scale[layer, rows, :] = jnp.broadcast_to(root, (128, 128))
            normed[layer, rows, :] = (centred * root * ln_ref[layer]).astype(BF16)
        by_rows(body)

    @pl.when(project)
    def _():
        acc[...] = dot(normed[layer, :, :], w_ref[...])

        def heads(low_ref, root_ref, gain, factor):
            @halves()
            def _(rows, columns):
                x = acc[rows, columns]
                centred = x - head_means(x, spread)
                root = lax.rsqrt(head_means(centred * centred, spread, False) + EPSILON)
                root_ref[layer, rows, columns] = root.astype(BF16)
                low_ref[layer, rows, columns] = (centred * root * (gain * factor)).astype(BF16)

        pl.when(tile == 0)(lambda: heads(q, rq, qg_ref[layer], SCALE))
        pl.when(tile == 1)(lambda: heads(k, rk, kg_ref[layer], 1.0))

        @pl.when(tile == 2)
        def _():
            v[layer, :, :] = acc[...].astype(BF16)
            low = low_lanes()
            augq, augk = augq_ref[...], augk_ref[...]
            ones = jnp.ones((SLOTS, 128), BF16)

            def pair(index):
                part = lanes(index, 128)
                qp, kp, vp = q[layer, :, part], k[layer, :, part], v[layer, :, part]
                results = []
                for head in (0, 1):
                    mine = low if head == 0 else ~low
                    scores = dot(jnp.where(mine, qp, augq), jnp.where(mine, kp, augk), ACROSS)
                    results.append(dot(jnp.exp2(scores).astype(BF16), jnp.where(mine, vp, ones)))
                inverse = 1.0 / pltpu.roll(jnp.where(low, results[1], results[0]), HD, 1)
                linv[layer, :, part] = inverse.astype(BF16)
                combined[layer, 0, :, part] = (jnp.where(low, results[0], results[1]) * inverse).astype(BF16)
            loop(PAIRS, pair)

        @pl.when(tile > 2)
        def _():
            @halves()
            def _(rows, columns):
                value, rise = gelu_and_slope(acc[rows, columns])
                slope[layer, tile - 3, rows, columns] = rise.astype(BF16)
                combined[layer, tile - 2, rows, columns] = value.astype(BF16)

    @pl.when(output | output_both)
    def _():
        product = dot(combined[layer, tile], w_ref[...])
        pl.when(tile == 0)(lambda: dq.__setitem__(..., hidden[layer].astype(F32) + product))
        pl.when(tile > 0)(lambda: dq.__setitem__(..., dq[...] + product))

        @pl.when(tile == TILES_OUT - 1)
        def _():
            result = dq[...].astype(BF16)
            hidden[layer + 1] = result
            if trade:
                trade.give_output(layer)
            else:
                section_out[layer] = result

    @pl.when(output_both | back)
    def _():
        acc[...] = dot(dy[...], w_ref[...], ACROSS)
        made = jnp.where(t < LAST_OUT, t - SECOND_OUT, TILES_OUT + t - LAST_OUT)
        pl.when(made >= 2)(lambda: terms_copy(terms_out, terms_tile, terms_sem, made % 2, 0, 0).wait())
        terms_tile[made % 2] = dot(combined[layer, tile], dy[...], DOWN).astype(BF16)
        terms_copy(terms_out, terms_tile, terms_sem, made % 2, layer, tile).start()
        if not trading:
            pl.when(t == LAST_BACK - 1)(lambda: terms_settled(terms_out, terms_tile, terms_sem))

        @pl.when(tile == 0)
        def _():
            @halves()
            def _(rows, columns):
                grad, inverse = acc[rows, columns], linv[layer, rows, columns].astype(F32)
                do[rows, columns] = (grad * inverse).astype(BF16)
                total = head_means(grad * combined[layer, 0, rows, columns].astype(F32), spread) * (inverse * -HD)
                for half in (0, 128):
                    part = pl.ds(pl.multiple_of(columns.start + half, 128), 128)
                    high, low = split(pltpu.roll(total[:, half : half + 128], HD, 1))
                    dhigh[rows, part] = high
                    dlow[rows, part] = low

        @pl.when(tile > 0)
        def _():
            @halves()
            def _(rows, columns):
                dproj[tile + 2, rows, columns] = (acc[rows, columns] * slope[layer, tile - 1, rows, columns].astype(F32)).astype(BF16)

    @pl.when(heads_now)
    def _():
        low = low_lanes()
        spot = lax.broadcasted_iota(jnp.int32, (SLOTS, 128), 1) % HD
        first = spot == 0
        augv = jnp.where(spot < 2, 1.0, 0.0).astype(BF16)
        augq, augk = augq_ref[...], augk_ref[...]
        none = jnp.zeros((SLOTS, 128), BF16)

        def pair(index):
            part = lanes(index, 128)
            qp, kp, vp, dop = q[layer, :, part], k[layer, :, part], v[layer, :, part], do[:, part]
            augd = jnp.where(first, dhigh[:, part], dlow[:, part])
            sums = [None, None, None]
            for head in (0, 1):
                mine = low if head == 0 else ~low
                e = jnp.exp2(dot(jnp.where(mine, kp, augk), jnp.where(mine, qp, augq), ACROSS))
                dp = dot(jnp.where(mine, vp, augv), jnp.where(mine, dop, augd), ACROSS)
                ds = (e * dp).astype(BF16)
                parts = (dot(ds, jnp.where(mine, kp, none), DOWN), dot(ds, jnp.where(mine, qp, none)),
                         dot(e.astype(BF16), jnp.where(mine, dop, none)))
                sums = [part_sum if total is None else total + part_sum for total, part_sum in zip(sums, parts)]
            dq[:, part] = sums[0] * 0.125
            dk[:, part] = sums[1] * (1.0 / LOG2E)
            dproj[2, :, part] = sums[2].astype(BF16)
        late = t >= LAST_HEADS
        first_pair = jnp.where(late, t - LAST_HEADS, 0)
        loop(jnp.where(late, 1, PAIRS), lambda index: pair(first_pair + index))

    @pl.when(project_back & (tile == 0))
    def _():
        for which, grads, low_ref, root_ref, gain, factor in ((0, dq, q, rq, qg_ref, SCALE), (1, dk, k, rk, kg_ref, 1.0)):
            @halves()
            def _(rows, columns):
                grad, gains = grads[rows, columns], gain[layer]
                xhat = low_ref[layer, rows, columns].astype(F32) * (1.0 / (gains * factor))
                scaled = grad * gains
                mean = head_means(scaled, spread, False)
                along = head_means(scaled * xhat, spread, False)
                dproj[which, rows, columns] = (root_ref[layer, rows, columns].astype(F32) * (scaled - mean - xhat * along)).astype(BF16)
                gain_ref[layer, which + 1 : which + 2, columns] += jnp.sum(grad * xhat, 0, keepdims=True)

    @pl.when(project_back)
    def _():
        product = dot(dproj[tile], w_ref[...], ACROSS)
        pl.when(tile == up_first(0))(lambda: acc.__setitem__(..., product))
        pl.when(tile != up_first(0))(lambda: acc.__setitem__(..., acc[...] + product))
        terms_in_ref[...] = dot(normed[layer, :, :], dproj[tile], DOWN).astype(BF16)

        @pl.when(tile == LAST_TILE)
        def _():
            gains = ln_ref[layer]

            def body(rows):
                grad = acc[rows, :]
                xhat = normed[layer, rows, :].astype(F32) * (1.0 / gains)
                scaled = grad * gains
                mean = jnp.mean(scaled, -1, keepdims=True)
                along = jnp.mean(scaled * xhat, -1, keepdims=True)
                total = dy[rows, :].astype(F32) + scale[layer, rows, :1] * (scaled - mean - xhat * along)
                low = total.astype(BF16)
                if trade:
                    pl.when(layer == section)(lambda: grad_ref.__setitem__((rows, slice(None)), total))
                else:
                    grad_ref[layer, rows, :] = total
                pl.when(layer == 1)(lambda: dy.__setitem__((rows, slice(None)), low))
                pl.when(layer == 0)(lambda: grad_low.__setitem__((rows, slice(None)), low))
                gain_ref[layer, 0:1, :] += jnp.sum(grad * xhat, 0, keepdims=True)
            by_rows(body)
            if trade:
                pl.when(layer == 1)(trade.give_grad)
                pl.when(layer == 0)(trade.finish)
            pl.when(layer == 0)(fold_gains)

    if trading:
        pl.when(t >= LAST_BACK - 1)(
            lambda: outer_scatter(t, terms_out, terms_tile, terms_sem, own_out, combined, slope, saved, *scatter_refs))


class Saved:
    def __init__(self, ref, which):
        self.ref, self.which = ref, which

    def __getitem__(self, index):
        return self.ref[(index[0], self.which) + index[1:]]

    def __setitem__(self, index, value):
        self.ref[(index[0], self.which) + index[1:]] = value


def terms_copy(terms_out, terms_tile, terms_sem, slot, layer, tile):
    target = terms_out.at[layer, pl.ds(pl.multiple_of(tile * D, D), D), :]
    return pltpu.make_async_copy(terms_tile.at[slot], target, terms_sem.at[slot])


def terms_settled(terms_out, terms_tile, terms_sem):
    for slot in range(2):
        terms_copy(terms_out, terms_tile, terms_sem, slot, 0, 0).wait()


def outer_scatter(t, terms_out, terms_tile, terms_sem, own_out, combined, slope, saved, rest_land, ready_sem, *sems):
    place = Place()
    rows = BLOCK[1][0]

    def half(number):
        return pl.ds(pl.multiple_of((number % 2) * rows, 16), rows)

    def held(number):
        return combined.at[number // 10, (number // 2) % 5, half(number)]

    def core_land(number):
        return slope.at[number // 8, (number // 2) % 4, half(number)]

    def land(colour, slot):
        piece = colour * 20 + slot
        return saved.at[1, piece // 5, pl.ds(pl.multiple_of((piece % 5) * 96, 16), 96)]

    scatter = Scatter(place, 1, terms_out, held, core_land, land, lambda slot: rest_land.at[slot], sems[:7])

    @pl.when(t == LAST_BACK - 1)
    def _():
        terms_settled(terms_out, terms_tile, terms_sem)
        greet(place, ready_sem)
        scatter.begin()

    first, count = 0, 0
    for slot, steps in enumerate(OUTER_ORDER):
        here = (t == LAST_BACK - 1 + slot).astype(jnp.int32)
        first += here * sum(map(len, OUTER_ORDER[:slot]))
        count += here * len(steps)
    scatter.run([step for steps in OUTER_ORDER for step in steps], first, count)
    pl.when(t == STEPS - 1)(lambda: scatter.finish(own_out, sems[7]))


class Trade:
    def __init__(self, section, section_out, hidden, dy, grad_land, own_sem, send_sem, recv_sem):
        self.section, self.section_out, self.hidden, self.dy, self.grad_land = section, section_out, hidden, dy, grad_land
        self.own_sem, self.send_sem, self.recv_sem = own_sem, send_sem, recv_sem
        self.pair = (1 - section, lax.axis_index("wide"))

    def kept(self):
        return pltpu.make_async_copy(self.hidden.at[self.section + 1], self.section_out.at[self.section], self.own_sem)

    def copy(self, source, target, index):
        return pltpu.make_async_remote_copy(
            src_ref=source, dst_ref=target, send_sem=self.send_sem.at[index], recv_sem=self.recv_sem.at[index],
            device_id=self.pair, device_id_type=MESH)

    def given(self):
        return self.copy(self.hidden.at[2 - self.section], self.section_out.at[self.section], 0)

    def grad(self):
        return self.copy(self.dy, self.grad_land, 1)

    def give_output(self, layer):
        pl.when(layer == self.section)(lambda: self.kept().start())
        pl.when(layer != self.section)(lambda: self.given().start())

    def give_grad(self):
        pl.when(self.section == 0)(lambda: self.grad().start())

    def finish(self):
        self.kept().wait()
        self.given().wait_send()
        self.copy(self.hidden.at[2 - self.section], self.section_out.at[1 - self.section], 0).wait_recv()
        pl.when(self.section == 0)(lambda: self.grad().wait_send())
        pl.when(self.section == 1)(lambda: self.grad().wait_recv())


def both_layers(trading, counts, weights, gains, inputs, cotangent, augq, augk, spread):
    square = (SLOTS, D)

    def whole(*dims):
        return pl.BlockSpec(dims, lambda t: (0,) * len(dims))

    low, wide = (lambda *dims: pltpu.VMEM(dims, BF16)), (lambda *dims: pltpu.VMEM(dims, F32))
    any_space, dma = pl.BlockSpec(memory_space=pl.ANY), pltpu.SemaphoreType.DMA
    full = [jax.ShapeDtypeStruct(dims, BF16) for dims in ((2, D, TILES_IN * D), (2, TILES_OUT * D, D))]
    if trading:
        in_specs, operands = [any_space] * 3, (*weights, gains)
        out_specs, more_specs = [any_space, whole(*square), whole(*square), any_space], [any_space] * 3
        sems = [dma((5, 3, 16)), dma((3, 16)), dma((3, 16))] * 3 + [dma((3,))]
        extra = [low(2, 16 * BLOCK[2][0], 128)] + sems + [dma(()), dma((2,)), dma((2,))]
        extra += [low(35, *part_shape(SCATTER_CUTS, 1, None)), pltpu.SemaphoreType.REGULAR] + scatter_sems()
        grad_shape, more = square, full + [jax.ShapeDtypeStruct(BLOCK[1], BF16)]
        params = dict(collective_id=2, has_side_effects=True)
    else:
        in_specs, operands = [any_space] * 2 + [whole(*gains.shape)], (*weights, gains)
        out_specs, more_specs = [whole(2, *square), whole(2, *square), whole(*square), whole(*square)], []
        grad_shape, extra, more, params = (2,) + square, [], [], {}
    return pl.pallas_call(
        functools.partial(compute_kernel, trading, counts),
        grid=(STEPS,),
        in_specs=in_specs + [any_space, any_space, whole(SLOTS, 128), whole(SLOTS, 128), whole(256, 256)],
        out_specs=out_specs + [
            whole(16, 128), pl.BlockSpec((None, D, D), lambda t: (in_terms(t)[0], 0, in_terms(t)[1])), any_space,
        ] + more_specs,
        scratch_shapes=[
            low(2, D, D), dma((2,)), wide(2, 1, D), wide(2, 1, 256), wide(2, 1, 256),
            low(3, *square), low(2, 8, *square), wide(2, SLOTS, 128), low(2, 4, *square), low(2, 5, *square), low(*square), low(7, *square),
            wide(*square), wide(*square), wide(*square), low(*square), low(*square), low(*square), low(2, D, D), dma((2,)), dma((2,)),
            wide(2, 8, D),
        ] + extra,
        out_shape=[
            jax.ShapeDtypeStruct((2,) + square, BF16), jax.ShapeDtypeStruct(grad_shape, F32), jax.ShapeDtypeStruct(square, BF16),
            jax.ShapeDtypeStruct(square, BF16), jax.ShapeDtypeStruct((16, 128), F32), *full,
        ] + more,
        compiler_params=pltpu.CompilerParams(vmem_limit_bytes=63 * 2**20, **params),
        name="both_layers",
    )(*operands, inputs, cotangent, augq, augk, spread)


def augment(image_id, token_size):
    high, low = split(jnp.log2(token_size.astype(F32)))
    same = (image_id[:, None] == jnp.arange(3)[None, :]).astype(BF16)
    one = jnp.ones_like(high)
    q = jnp.concatenate([one[:, None], one[:, None], same, one[:, None]], 1)
    k = jnp.concatenate([high[:, None], low[:, None], same * APART, one[:, None] * -APART], 1)
    return [jnp.tile(jnp.pad(part, ((0, 0), (0, HD - 6))), (1, 2)) for part in (q, k)]


def spread_matrix():
    head = jnp.arange(256) // HD
    return ((head[:, None] == head[None, :]) / HD).astype(BF16)


def gather_all(piece, axis):
    return lax.all_gather(lax.all_gather(piece, "wide", axis=axis, tiled=True), "section", axis=0, tiled=True)


def scatter_all(terms, axis):
    own = lax.psum_scatter(terms, "section", scatter_dimension=0, tiled=True)
    return lax.psum_scatter(own, "wide", scatter_dimension=axis, tiled=True)


def on_device(inputs, cotangent, token_size, image_id, w_in, w_out, ln_gain, q_gain, k_gain):
    section, wide = lax.axis_index("section"), lax.axis_index("wide")
    width = lax.axis_size("wide")
    blocks_fit = width == 16 and w_in.shape[1:] == BLOCK[0] and w_out.shape[1:] == BLOCK[1]
    ends = [0]
    for gain in (ln_gain, q_gain, k_gain):
        ends.append(ends[-1] + gain.shape[1])
    own_gains = jnp.concatenate([ln_gain, q_gain, k_gain], 1)
    gains = jnp.pad(own_gains, ((0, BLOCK[2][0] - 1), (0, BLOCK[2][1] - ends[3])))
    weights = (w_in[0], w_out[0])
    if not blocks_fit:
        weights = (gather_all(w_in, 1), gather_all(w_out, 1))
        gains = gather_all(gains[None], 1)
    augq, augk = augment(image_id[section, 0], token_size[section, 0])
    outs, grads, grad_low, grad_land, totals, terms_in, terms_out, *more = both_layers(
        blocks_fit, tuple(gain.shape[1] for gain in (ln_gain, q_gain, k_gain)), weights, gains, inputs,
        cotangent, augq, augk, spread_matrix())
    swap = [(0, 1), (1, 0)]

    def both_micro(pair):
        mine = lax.dynamic_index_in_dim(pair, section, 0, False)
        other = lax.dynamic_index_in_dim(pair, 1 - section, 0, False).astype(BF16)
        other = lax.ppermute(other, "section", swap).astype(mine.dtype)
        return jnp.where(section == 0, jnp.stack([mine, other]), jnp.stack([other, mine]))[None, :, None]

    places = (0, D, D + HD, D + 2 * HD)
    if blocks_fit:
        own_in, totals, last_land = scatter_terms(terms_in, totals, grad_low)
        other = jnp.where(section == 0, last_land, grad_land).astype(F32)
        is_own = (jnp.arange(2) == section)[:, None, None]
        grads = jnp.where(is_own, grads[None], other[None])[None, :, None]
        outs = outs[None, :, None]
        own_in, own_out = own_in[None].astype(F32), more[2][None].astype(F32)
    else:
        own_in = scatter_all(terms_in, 1).astype(F32)
        own_out = scatter_all(terms_out, 1).astype(F32)
        totals = lax.psum(totals, ("section", "wide"))
        outs, grads = both_micro(outs), both_micro(grads)
    mine = lax.dynamic_index_in_dim(totals.reshape(2, 1024), section, 0, False)
    gain_grads = [
        lax.dynamic_slice_in_dim(mine[low:high], wide * gain.shape[1], gain.shape[1])[None]
        for low, high, gain in zip(places, places[1:], (ln_gain, q_gain, k_gain))
    ]
    return (outs, grads, own_in, own_out, *gain_grads)


def solution(mesh):
    return jax.shard_map(
        on_device,
        mesh=mesh,
        in_specs=(
            P(None, "wide", None, None),
            P(None, "wide", None, None),
            P(None, "wide", None),
            P(None, "wide", None),
            P("section", "wide", None),
            P("section", "wide", None),
            P("section", "wide"),
            P("section", "wide"),
            P("section", "wide"),
        ),
        out_specs=(
            P("section", None, "wide", None, None),
            P("section", None, "wide", None, None),
            P("section", "wide", None),
            P("section", "wide", None),
            P("section", "wide"),
            P("section", "wide"),
            P("section", "wide"),
        ),
        check_vma=False,
    )
```

```python
import functools

import jax
import jax.numpy as jnp
from jax import lax
from jax.experimental import pallas as pl
from jax.experimental.pallas import tpu as pltpu
from jax.sharding import PartitionSpec as P

MESH = pl.DeviceIdType.MESH
NZ = 4
BLOCK = ((48, 5376), (240, 768), (16, 128))
GATHER_CUTS = (2176, 96)
SCATTER_CUTS = (2048, 96)


class Place:
    def __init__(self):
        self.x, self.wide = lax.axis_index("section"), lax.axis_index("wide")
        self.y, self.z, self.c = (self.wide // 2) % 2, self.wide // 4, self.wide % 2

    def at(self, x, y, z, c=None):
        return (x, z * 4 + y * 2 + (self.c if c is None else c))

    def along(self, colour, block_z, far_first, far_second):
        dx = jnp.where(colour == 0, far_first, far_second)
        dy = jnp.where(colour == 0, far_second, far_first)
        return self.flip(self.x, dx), self.flip(self.y, dy), block_z

    @staticmethod
    def flip(value, far):
        return value + far - 2 * value * far

    def first(self, colour):
        return self.at(*self.along(colour, self.z, 1, 0))

    def second(self, colour):
        return self.at(*self.along(colour, self.z, 0, 1))

    def sibling(self):
        return self.at(self.x, self.y, self.z, 1 - self.c)


def greet(place, barrier=None):
    barrier = pltpu.get_barrier_semaphore() if barrier is None else barrier
    x, y, z = place.x, place.y, place.z

    def signal(device):
        pl.semaphore_signal(barrier, inc=1, device_id=device, device_id_type=MESH)

    signal(place.at(1 - x, y, z))
    signal(place.at(x, 1 - y, z))
    signal(place.sibling())
    pl.when(z < NZ - 1)(lambda: signal(place.at(x, y, z + 1)))
    pl.when(z > 0)(lambda: signal(place.at(x, y, z - 1)))
    pl.semaphore_wait(barrier, 3 + (z < NZ - 1).astype(jnp.int32) + (z > 0).astype(jnp.int32))


def number_of(block):
    return block[0] * 8 + block[1] * 4 + block[2]


def part_shape(cuts, array, colour):
    rows, cols = BLOCK[array]
    size = cuts[array]
    if array == 0:
        return rows, cols - 2 * size if colour is None else size
    return rows - 2 * size if colour is None else size, cols


def cut(ref, cuts, array, colour):
    if array == 2:
        return ref
    rows, cols = part_shape(cuts, array, colour)
    size = cuts[array]
    if array == 0:
        return ref.at[:, pl.ds(2 * size if colour is None else pl.multiple_of(colour * size, 128), cols)]
    return ref.at[pl.ds(2 * size if colour is None else pl.multiple_of(colour * size, 16), rows), :]


def loop(count, body):
    def step(index, carry):
        body(index)
        return carry
    lax.fori_loop(0, count, step, 0)


class Gather:
    def __init__(self, place, array, own, full, send_sem, recv_sem, core_sem):
        self.place, self.array, self.own, self.full = place, array, own, full
        self.send_sem, self.recv_sem, self.core_sem = send_sem, recv_sem, core_sem

    def view(self, block, colour, plane=None):
        rows = BLOCK[self.array][0]
        place = self.place
        start = (block[2] * 4 + block[1] * 2 + (place.c if plane is None else plane)) * rows
        return cut(self.full.at[block[0], pl.ds(pl.multiple_of(start, 16), rows), :], GATHER_CUTS, self.array, colour)

    def copy(self, link, device, block, colour, own=False, other_plane=False):
        kind = 2 if colour is None else colour
        number = number_of(block)
        target = self.view(block, colour, 1 - self.place.c if other_plane else None)
        source = cut(self.own, GATHER_CUTS, self.array, colour) if own else target
        sems = self.core_sem if link == 4 else self.recv_sem
        return pltpu.make_async_remote_copy(
            src_ref=source, dst_ref=target, send_sem=self.send_sem.at[link, kind, number], recv_sem=sems.at[kind, number],
            device_id=device, device_id_type=MESH)

    def visit(self, block, colour, onward, first, second, drain, condition=None, own=False):
        place = self.place

        def body():
            if not drain and not own:
                self.copy(0, place.sibling(), block, colour).wait_recv()

            def send(link, device):
                copy = self.copy(link, device, block, colour, own)
                copy.wait_send() if drain else copy.start()

            for link, step in onward:
                target = place.z + step
                pl.when((target >= 0) & (target < NZ))(functools.partial(send, link, place.at(place.x, place.y, target)))
            if first is not None:
                send(2, first)
            if second is not None:
                if isinstance(second, tuple) and len(second) == 3:
                    pl.when(second[2])(functools.partial(send, 3, second[:2]))
                else:
                    send(3, second)
            send(4, place.sibling())
        if condition is None:
            body()
        else:
            pl.when(condition)(body)

    def begin(self, drain=False):
        place = self.place
        me = (place.x, place.y, place.z)
        everywhere = ((0, 1), (1, -1))
        self.visit(me, None, everywhere, place.at(1 - place.x, place.y, place.z), place.at(place.x, 1 - place.y, place.z), drain, own=True)

        def body(colour):
            self.visit(me, colour, everywhere, place.first(colour), place.second(colour), drain, own=True)
        if self.array < 2:
            loop(2, body)

    def square(self, drain=False):
        place = self.place

        def body(index):
            far_x, far_y = (index != 1).astype(jnp.int32), (index != 0).astype(jnp.int32)
            block = (place.flip(place.x, far_x), place.flip(place.y, far_y), place.z)
            self.visit(block, None, ((0, 1), (1, -1)), None, place.at(place.x, 1 - place.y, place.z) + (index == 0,), drain)
        loop(3, body)

    def sided(self, distance, body):
        place = self.place

        def side_body(side):
            step = 1 - 2 * side
            block_z = place.z - step * distance
            body(side, block_z, (block_z >= 0) & (block_z < NZ) & ((distance > 0) | (side == 0)))
        loop(2, side_body)

    def onward(self, side):
        return ((0, 1), (1, -1))[side]

    def z_step(self, distance, drain=False):
        place = self.place
        for side in (0, 1):
            step = 1 - 2 * side
            block_z = place.z - step * distance

            def body(colour):
                self.visit((place.x, place.y, block_z), colour, ((side, step),), place.first(colour), place.second(colour), drain)
            pl.when((block_z >= 0) & (block_z < NZ))(lambda: loop(2, body))

    def line(self, distance, drain=False):
        place = self.place
        for side in (0, 1):
            step = 1 - 2 * side
            block_z = place.z - step * distance

            def body(index):
                block = (place.flip(place.x, index % 2), place.flip(place.y, index // 2), block_z)
                self.visit(block, None, ((side, step),), None, None, drain)
            pl.when((block_z >= 0) & (block_z < NZ))(lambda: loop(4, body))

    def a_step(self, distance, drain=False):
        place = self.place

        def body(side, block_z, there):
            def inner(colour):
                self.visit(place.along(colour, block_z, 1, 0), colour, (), None, place.second(colour), drain)
            pl.when(there)(lambda: loop(2, inner))
        self.sided(distance, body)

    def b_step(self, distance, drain=False):
        place = self.place

        def body(side, block_z, there):
            def inner(index):
                colour = index // 2
                self.visit(place.along(colour, block_z, index % 2, 1), colour, (), None, None, drain)
            pl.when(there)(lambda: loop(4, inner))
        self.sided(distance, body)

    def from_core(self):
        place = self.place

        def body(number):
            block = (number // 8, (number // 4) % 2, number % 4)
            self.copy(4, place.sibling(), block, None, other_plane=True).wait_recv()
            for colour in (0, 1) if self.array < 2 else ():
                self.copy(4, place.sibling(), block, colour, other_plane=True).wait_recv()
        loop(16, body)

    def drain(self):
        self.begin(True)
        self.square(True)

        def body(index):
            self.line(index + 1, True)
            if self.array < 2:
                self.z_step(index + 1, True)
                self.a_step(index, True)
                self.b_step(index, True)
        loop(NZ, body)


class Weights:
    def __init__(self, place, own, full, tiles, tile_sem, sems):
        self.place, self.full, self.tiles, self.tile_sem = place, full, tiles, tile_sem
        self.copies = []
        if place is None:
            return
        self.inner, self.outer, self.gains = [Gather(place, array, own[array], full[array], *sems[3 * array : 3 * array + 3]) for array in range(3)]
        for array in range(3):
            rows = BLOCK[array][0]
            target = full[array].at[place.x, pl.ds(pl.multiple_of(place.wide * rows, 16), rows), :]
            self.copies.append(pltpu.make_async_copy(own[array], target, sems[9].at[array]))

    def begin(self):
        greet(self.place)
        for copy in self.copies:
            copy.start()
        self.gains.begin()
        self.inner.begin()
        self.gains.square()
        self.inner.square()

        def early(index):
            self.inner.z_step(index + 1)
            self.inner.a_step(index)
            self.gains.line(index + 1)
            self.inner.line(index + 1)
        loop(NZ - 1, early)
        self.outer.begin()
        self.inner.a_step(NZ - 1)
        self.outer.square()

        def late(index):
            self.inner.b_step(index)
            pl.when(index == 1)(lambda: self.onward(0))
        loop(NZ, late)
        self.gains.from_core()
        self.inner.from_core()
        for copy in self.copies:
            copy.wait()

    def onward(self, index):
        self.outer.z_step(index + 1)
        self.outer.a_step(index)
        self.outer.line(index + 1)

    def end(self):
        loop(NZ, self.outer.b_step)
        self.outer.from_core()

    def drain(self):
        for array in (self.gains, self.inner, self.outer):
            array.drain()

    def fetch(self, t):
        slot = tile_slot(t)
        tile, sem = self.tiles.at[slot], self.tile_sem.at[slot]
        project = uses_in(t)

        def inner():
            layer, index = in_tile(t)
            return pltpu.make_async_copy(self.full[0].at[layer, :, pl.ds(pl.multiple_of(index * D, D), D)], tile, sem)

        def outer():
            layer, index = out_tile(t)
            return pltpu.make_async_copy(self.full[1].at[layer, pl.ds(pl.multiple_of(index * D, D), D), :], tile, sem)
        pl.when(project)(lambda: inner().start())
        pl.when(jnp.logical_not(project))(lambda: outer().start())

    def wait(self, t):
        slot = tile_slot(t)
        pltpu.make_async_copy(self.full[0].at[0, :, pl.ds(0, D)], self.tiles.at[slot], self.tile_sem.at[slot]).wait()

    def step(self, t):
        if self.place is not None:
            pl.when(t == 0)(self.begin)
            pl.when((t >= 2) & (t <= NZ))(lambda: self.onward(t - 1))
            pl.when(t == FIRST_OUT)(self.end)
            pl.when(t == LAST_OUT)(self.drain)
            held_back = FIRST_OUT
        else:
            held_back = 0
        following = jnp.where(t == LAST_HEADS - 1, LAST_PROJECT, t + 1)
        pl.when((t == 0) | (t == held_back))(lambda: self.fetch(t))
        pl.when(has_tile(t) & (following < STEPS) & (following != held_back))(lambda: self.fetch(following))
        pl.when(has_tile(t))(lambda: self.wait(t))


def add_into(target, source):
    def body(step):
        part = pl.ds(pl.multiple_of(step * 48, 16), 48)
        target[part, :] = target[part, :] + source[part, :]
    loop(target.shape[0] // 48, body)


OUTER_ORDER = (
    ("k3", "l3"), (), ("a3", "k2"), (), ("l2",), ("b3", "k1", "a2", "z3"), ("l1",), ("k0", "b2"), ("z2", "a1", "l0"), (),
    ("a0", "b1", "z1", "s", "b0", "z0"))
INNER_ORDER = (
    "k3", "k2", "l3", "k1", "l2", "a3", "k0", "l1", "b3", "a2", "z3", "a1", "l0", "b2", "z2", "b1", "a0", "z1", "s", "b0", "z0")
INNER_GRAD = 14


class Scatter:
    def __init__(self, place, array, terms, held, core_land, land, rest_land, sems):
        self.place, self.array, self.terms, self.held, self.core_land = place, array, terms, held, core_land
        self.land, self.rest_land = land, rest_land
        self.send_sem, self.recv_sem, self.rest_send, self.rest_recv, self.core_send, self.core_recv, self.local_sem = sems

    def part(self, block, colour):
        return cut(self.held(number_of(block)), SCATTER_CUTS, self.array, colour)

    def copy(self, device, block, colour, slot):
        if colour is None:
            target, send_sem, recv_sem = self.rest_land(slot), self.rest_send.at[slot], self.rest_recv.at[slot]
        else:
            target, send_sem, recv_sem = self.land(colour, slot), self.send_sem.at[colour, slot], self.recv_sem.at[colour, slot]
        return pltpu.make_async_remote_copy(
            src_ref=self.part(block, colour), dst_ref=target, send_sem=send_sem, recv_sem=recv_sem, device_id=device,
            device_id_type=MESH)

    def send(self, device, block, colour, slot, drain):
        copy = self.copy(device, block, colour, slot)
        copy.wait_send() if drain else copy.start()

    def arrive(self, block, colour, slot, drain):
        if not drain:
            self.copy(self.place.sibling(), block, colour, slot).wait_recv()
            add_into(self.part(block, colour), self.rest_land(slot) if colour is None else self.land(colour, slot))

    def core_copy(self, block, mine):
        rows = BLOCK[self.array][0]
        place = self.place
        number = number_of(block)
        start = (block[2] * 4 + block[1] * 2 + (place.c if mine else 1 - place.c)) * rows
        source = self.terms.at[block[0], pl.ds(pl.multiple_of(start, 16), rows), :]
        if mine:
            return pltpu.make_async_copy(source, self.held(number), self.local_sem.at[number])
        return pltpu.make_async_remote_copy(
            src_ref=source, dst_ref=self.core_land(number), send_sem=self.core_send.at[number],
            recv_sem=self.core_recv.at[number], device_id=place.sibling(), device_id_type=MESH)

    def sided(self, distance, body):
        place = self.place

        def side_body(side):
            block_z = place.z + (2 * side - 1) * distance
            there = (block_z >= 0) & (block_z < NZ) & (distance < NZ) & (distance >= 0) & ((distance > 0) | (side == 0))
            pl.when(there)(lambda: body(block_z))
        loop(2, side_body)

    def start(self, distance):
        place = self.place

        def body(block_z):
            def inner(index):
                block = (place.flip(place.x, 1 - index % 2), place.flip(place.y, 1 - index // 2), block_z)
                self.core_copy(block, False).start()
                self.core_copy(block, True).start()
            loop(4, inner)
        self.sided(distance, body)

    def k_step(self, distance, drain=False):
        place = self.place

        def body(block_z):
            def inner(index):
                far_x, far_y = 1 - index % 2, 1 - index // 2
                block = (place.flip(place.x, far_x), place.flip(place.y, far_y), block_z)
                if not drain:
                    self.core_copy(block, True).wait()
                    copy = self.core_copy(block, False)
                    copy.wait_recv()
                    add_into(self.held(number_of(block)), self.core_land(number_of(block)))
                    copy.wait_send()

                def out(colour):
                    far_first = jnp.where(colour == 0, far_x, far_y)
                    far_second = jnp.where(colour == 0, far_y, far_x)
                    pl.when(far_second == 1)(lambda: self.send(place.second(colour), block, colour, far_first * 4 + block_z, drain))
                loop(2, out)
            loop(4, inner)
        self.sided(distance, body)

    def a_step(self, distance, drain=False):
        place = self.place

        def body(block_z):
            def inner(index):
                colour, far_first = index % 2, 1 - index // 2
                block = place.along(colour, block_z, far_first, 0)
                self.arrive(block, colour, far_first * 4 + block_z, drain)
                pl.when(far_first == 1)(lambda: self.send(place.first(colour), block, colour, 8 + block_z, drain))
            loop(4, inner)
        self.sided(distance, body)

    def b_step(self, distance):
        place = self.place

        def body(block_z):
            loop(2, lambda colour: self.arrive((place.x, place.y, block_z), colour, 8 + block_z, False))
        self.sided(distance, body)

    def toward(self, distance, body):
        place = self.place
        for side, step in ((0, -1), (1, 1)):
            block_z, behind = place.z + step * distance, place.z - step
            there = (block_z >= 0) & (block_z < NZ) & (distance < NZ) & (distance >= 0)
            pl.when(there)(functools.partial(body, block_z, side, step, (behind >= 0) & (behind < NZ)))

    def z_step(self, distance, drain=False):
        place = self.place

        def body(block_z, side, step, more):
            block = (place.x, place.y, block_z)
            slot = 12 + 4 * side + block_z

            def inner(colour):
                pl.when(more)(lambda: self.arrive(block, colour, slot, drain))
                pl.when(distance > 0)(lambda: self.send(place.at(place.x, place.y, place.z + step), block, colour, slot, drain))
            loop(2, inner)
        self.toward(distance, body)

    def line(self, distance, drain=False):
        place = self.place

        def body(block_z, side, step, more):
            def inner(index):
                block = (place.flip(place.x, 1 - index % 2), place.flip(place.y, 1 - index // 2), block_z)
                slot = 16 * side + number_of(block)
                pl.when(more)(lambda: self.arrive(block, None, slot, drain))
                pl.when(distance > 0)(lambda: self.send(place.at(place.x, place.y, place.z + step), block, None, slot, drain))
            loop(4, inner)
        self.toward(distance, body)

    def square(self, drain=False):
        place = self.place
        over_x, over_y = place.at(1 - place.x, place.y, place.z), place.at(place.x, 1 - place.y, place.z)
        far = (1 - place.x, place.y, place.z)
        self.send(over_y, (1 - place.x, 1 - place.y, place.z), None, 33, drain)
        self.send(over_y, (place.x, 1 - place.y, place.z), None, 32, drain)
        self.arrive(far, None, 33, drain)
        self.send(over_x, far, None, 34, drain)
        self.arrive((place.x, place.y, place.z), None, 32, drain)
        self.arrive((place.x, place.y, place.z), None, 34, drain)

    def drain(self):
        def body(distance):
            self.k_step(distance, True)
            self.a_step(distance, True)
            self.z_step(distance, True)
            self.line(distance, True)
        loop(NZ, body)
        self.square(True)


    STEPS = "klabzs"

    def begin(self):
        loop(NZ, lambda index: self.start(NZ - 1 - index))

    def run(self, order, first, count, also=None):
        codes = [(self.STEPS.index(step[0]), int(step[1:] or 0)) for step in order]

        def body(index):
            index = first + index
            which, distance = [sum((index == place).astype(jnp.int32) * code[part] for place, code in enumerate(codes)) for part in (0, 1)]
            calls = (self.k_step, self.line, self.a_step, self.b_step, self.z_step)
            for code, call in enumerate(calls):
                pl.when(which == code)(lambda: call(distance))
            pl.when(which == len(calls))(self.square)
            if also:
                also(index)
        loop(count, body)

    def finish(self, result, sem):
        copy = pltpu.make_async_copy(self.held(number_of((self.place.x, self.place.y, self.place.z))), result, sem)
        copy.start()
        self.drain()
        copy.wait()


def scatter_sems():
    dma = pltpu.SemaphoreType.DMA
    return [dma((2, 20)), dma((2, 20)), dma((35,)), dma((35,)), dma((16,)), dma((16,)), dma((16,)), dma(())]


class Total:
    def __init__(self, place, own, out, run, land, send_sem, recv_sem):
        self.place, self.own, self.out, self.run, self.land = place, own, out, run, land
        self.send_sem, self.recv_sem = send_sem, recv_sem
        x, y, z = place.x, place.y, place.z
        self.routes = (place.sibling(), place.at(x, 1 - y, z), place.at(1 - x, y, z), place.at(x, y, z + 1), place.at(x, y, z - 1))
        self.sends = (None, None, None, z < NZ - 1, z > 0)
        self.gets = (None, None, None, z > 0, z < NZ - 1)

    def copy(self, link):
        source = self.own if link == 0 else self.run.at[link]
        return pltpu.make_async_remote_copy(
            src_ref=source, dst_ref=self.land.at[link], send_sem=self.send_sem.at[link], recv_sem=self.recv_sem.at[link],
            device_id=self.routes[link], device_id_type=MESH)

    def step(self, index):
        def chain(link, base):
            self.run[link] = base[...]

            def get():
                self.copy(link).wait_recv()
                self.run[link] += self.land[link]
            pl.when(self.gets[link])(get)
            pl.when(self.sends[link])(lambda: self.copy(link).start())

        def swap(link):
            if link:
                self.copy(link - 1).wait_recv()
                self.run[link] = (self.own[...] if link == 1 else self.run[link - 1]) + self.land[link - 1]
            if link < 3:
                self.copy(link).start()

        for link in range(3):
            pl.when(index == link)(functools.partial(swap, link))

        @pl.when(index == 3)
        def _():
            self.copy(2).wait_recv()
            self.out[...] = self.run[2] + self.land[2]
            chain(3, self.out)
            chain(4, self.out)
            self.out[...] = self.run[3]

            def add():
                self.out[...] += self.land[4]
            pl.when(self.gets[4])(add)

    def drain(self):
        for link, sent in enumerate(self.sends):
            if sent is None:
                self.copy(link).wait_send()
            else:
                pl.when(sent)(lambda: self.copy(link).wait_send())


def scatter_kernel(terms, gains, grad, result, out_gains, grad_land, held, core_land, land, rest_land, run, small_land, send_sem, recv_sem,
                   grad_sem, *sems):
    place = Place()
    greet(place)
    grad_copy = pltpu.make_async_remote_copy(
        src_ref=grad, dst_ref=grad_land, send_sem=grad_sem.at[0], recv_sem=grad_sem.at[1],
        device_id=place.at(1 - place.x, place.y, place.z), device_id_type=MESH)
    total = Total(place, gains, out_gains, run, small_land, send_sem, recv_sem)
    scatter = Scatter(place, 0, terms, lambda number: held.at[number], lambda number: core_land.at[number],
                      lambda colour, slot: land.at[colour * 20 + slot], lambda slot: rest_land.at[slot], sems[:7])
    scatter.begin()

    def also(index):
        pl.when(index % 4 == 0)(lambda: total.step(index // 4))
        pl.when((index == INNER_GRAD) & (place.x == 1))(lambda: grad_copy.start())
    scatter.run(INNER_ORDER, 0, len(INNER_ORDER), also)
    scatter.finish(result, sems[7])
    total.drain()
    pl.when(place.x == 1)(lambda: grad_copy.wait_send())
    pl.when(place.x == 0)(lambda: grad_copy.wait_recv())


def scatter_terms(terms, gains, grad):
    any_space, vmem, dma = pl.BlockSpec(memory_space=pl.ANY), pl.BlockSpec(memory_space=pltpu.VMEM), pltpu.SemaphoreType.DMA
    low = lambda *dims: pltpu.VMEM(dims, jnp.bfloat16)
    return pl.pallas_call(
        scatter_kernel,
        out_shape=(jax.ShapeDtypeStruct(BLOCK[0], jnp.bfloat16), jax.ShapeDtypeStruct(BLOCK[2], jnp.float32),
                   jax.ShapeDtypeStruct(grad.shape, grad.dtype)),
        in_specs=[any_space, vmem, any_space], out_specs=(any_space, vmem, any_space),
        scratch_shapes=[
            low(16, *BLOCK[0]), low(16, *BLOCK[0]), low(40, *part_shape(SCATTER_CUTS, 0, 0)), low(35, *part_shape(SCATTER_CUTS, 0, None)),
            *[pltpu.VMEM((5,) + BLOCK[2], jnp.float32)] * 2, dma((5,)), dma((5,)), dma((2,)), *scatter_sems()],
        compiler_params=pltpu.CompilerParams(collective_id=1, has_side_effects=True, vmem_limit_bytes=48 * 2**20),
        name="scatter_terms",
    )(terms, gains, grad)


SLOTS, D, HD, PAIRS = 512, 768, 64, 6
WIDE_PAIRS = 3
TILES_IN, TILES_OUT = 7, 5
EPSILON = 1e-06
LOG2E = 1.4426950408889634
SCALE = 0.125 * LOG2E
APART = 256.0
F32, BF16 = jnp.float32, jnp.bfloat16
ACROSS, DOWN = ((1,), (1,)), ((0,), (0,))


def dot(a, b, dims=((1,), (0,))):
    return lax.dot_general(a, b, (dims, ((), ())), preferred_element_type=F32)


def split(value):
    high = value.astype(BF16)
    return high, (value - high.astype(F32)).astype(BF16)


def head_means(value, spread, exact=True):
    high, low = split(value)
    means = dot(high, spread)
    return means + dot(low, spread) if exact else means


def gelu_and_slope(x):
    t = 1.0 / (1.0 + (0.3275911 * 0.7071067811865476) * jnp.abs(x))
    bell = jnp.exp2((-0.5 * LOG2E) * (x * x))
    poly = t * (0.127414796 + t * (-0.142248368 + t * (0.7107068705 + t * (-0.7265760135 + t * 0.5307027145))))
    tail = poly * bell
    phi = jnp.where(x >= 0, 1.0 - tail, tail)
    return x * phi, phi + (0.3989422804014327 * x) * bell


def lanes(index, width):
    return pl.ds(index * width if isinstance(index, int) else pl.multiple_of(index * width, width), width)


FIRST_OUT, SECOND_IN, SECOND_OUT, SECOND_BACK, LAST_OUT, LAST_BACK, LAST_HEADS, LAST_PROJECT, STEPS = 7, 12, 19, 24, 31, 36, 40, 43, 46
LAST_TILE = 2


def up_first(index):
    return (index + 3) % TILES_IN


def clip(index, high):
    return jnp.clip(index, 0, high)


def last_back(t):
    return up_first(jnp.where(t < LAST_HEADS, clip(t - LAST_BACK, 3), 4 + clip(t - LAST_PROJECT, 2)))


def in_tile(t):
    layer = ((t >= FIRST_OUT) & (t < LAST_OUT)).astype(jnp.int32)
    forward = jnp.where(t < FIRST_OUT, t, clip(t - SECOND_IN, 6))
    backward = jnp.where(t < LAST_OUT, up_first(clip(t - SECOND_BACK, 6)), last_back(t))
    return layer, jnp.where(t < SECOND_OUT, forward, backward)


def has_tile(t):
    return (t < LAST_HEADS) | (t >= LAST_PROJECT)


def tile_slot(t):
    return (t - (LAST_PROJECT - LAST_HEADS) * (t >= LAST_PROJECT)) % 2


def uses_in(t):
    forward = (t < FIRST_OUT) | ((t >= SECOND_IN) & (t < SECOND_OUT))
    return forward | ((t >= SECOND_BACK) & (t < LAST_OUT)) | ((t >= LAST_BACK) & has_tile(t))


def out_tile(t):
    layer = ((t >= SECOND_IN) & (t < SECOND_BACK)).astype(jnp.int32)
    tile = jnp.where(t < SECOND_IN, clip(t - FIRST_OUT, 4), jnp.where(t < SECOND_BACK, clip(t - SECOND_OUT, 4), clip(t - LAST_OUT, 4)))
    return layer, tile


def in_terms(t):
    late = t >= LAST_BACK
    return 1 - late.astype(jnp.int32), jnp.where(late, last_back(t), up_first(clip(t - SECOND_BACK, 6)))


def gains_of(rows, width, start, count, columns):
    lane, column = lax.broadcasted_iota(jnp.int32, (128, columns), 0), lax.broadcasted_iota(jnp.int32, (128, columns), 1)
    place = column % (count * width)
    picked = dot(rows, jnp.where(lane == start + place % count, 1.0, 0.0).astype(BF16))
    row = lax.broadcasted_iota(jnp.int32, picked.shape, 0)
    owner = (lax.broadcasted_iota(jnp.int32, picked.shape, 1) % (count * width)) // count
    return jnp.sum(jnp.where(row == owner * BLOCK[2][0], picked, 0.0), 0, keepdims=True)


def compute_kernel(trading, counts, *refs):
    if trading:
        own, refs = refs[:3], refs[3:]
    else:
        (full_in, full_out, full_gains), refs, own = refs[:3], refs[3:], None
    (inputs, cotangent, augq_ref, augk_ref, spread_ref, section_out, grad_ref, grad_low, grad_land, totals_ref, terms_in_ref, terms_out), refs = (
        refs[:12], refs[12:])
    (tiles, tile_sem, ln_ref, qg_ref, kg_ref, hidden, saved, scale, slope, combined, dy, dproj, acc, dq, dk, do, dhigh, dlow, terms_tile,
     terms_sem, entry_sem, gain_ref), refs = (refs[:22], refs[22:]) if not trading else (refs[3:25], refs[:3] + refs[25:])
    sems, swap, scatter_refs = None, (), None
    if trading:
        (full_in, full_out, own_out, full_gains), sems, swap, scatter_refs = refs[:4], refs[4:14], refs[14:17], refs[17:]
    normed, q, k, v, rq, rk, linv = [Saved(saved, which) for which in range(7)]
    t = pl.program_id(0)
    layer = in_tile(t)[0]
    project = (t < FIRST_OUT) | ((t >= SECOND_IN) & (t < SECOND_OUT))
    project_back = ((t >= SECOND_BACK) & (t < LAST_OUT)) | ((t >= LAST_BACK) & has_tile(t))
    output = (t >= FIRST_OUT) & (t < SECOND_IN)
    output_both = (t >= SECOND_OUT) & (t < SECOND_BACK)
    back = (t >= LAST_OUT) & (t < LAST_BACK)
    heads_now = (t == SECOND_BACK + 4) | ((t >= LAST_HEADS) & (t < LAST_PROJECT))
    layer = jnp.where(output, 0, layer)
    tile = jnp.where(project | project_back, in_tile(t)[1], out_tile(t)[1])
    section, trade = lax.axis_index("section"), None
    if swap:
        trade = Trade(section, section_out, hidden, dy, grad_land, *swap)
    spread = spread_ref[...]
    weights = Weights(Place() if trading else None, own, (full_in, full_out, full_gains), tiles, tile_sem, sems)
    weights.step(t)
    w_ref = tiles.at[tile_slot(t)]

    def thirds(body):
        for part in range(WIDE_PAIRS):
            body(pl.ds(256 * part, 256))

    def by_rows(body):
        loop(SLOTS // 128, lambda index: body(pl.ds(pl.multiple_of(index * 128, 128), 128)))

    @pl.when(t == 0)
    def _():
        entries = [pltpu.make_async_copy(inputs.at[section, 0], hidden.at[0], entry_sem.at[0]),
                   pltpu.make_async_copy(cotangent.at[section, 0], dy, entry_sem.at[1])]
        for entry in entries:
            entry.start()
        for entry in entries:
            entry.wait()
        gain_ref[...] = jnp.zeros_like(gain_ref)
        starts = (0, counts[0], counts[0] + counts[1])
        for which in range(2):
            rows = full_gains[which]
            for target, start, count, columns in zip((ln_ref, qg_ref, kg_ref), starts, counts, (D, 256, 256)):
                target[which] = gains_of(rows, D // counts[0], start, count, columns)

    def low_lanes():
        return lax.broadcasted_iota(jnp.int32, (SLOTS, 128), 1) < HD

    def fold_gains():
        for which in range(2):
            parts = [[gain_ref[which, row : row + 1, 128 * part : 128 * (part + 1)] for part in range(PAIRS)] for row in range(3)]
            sums = [functools.reduce(jnp.add, row) for row in parts[1:]]
            sums = [total + pltpu.roll(total, HD, 1) for total in sums]
            for part in range(PAIRS):
                totals_ref[8 * which + part : 8 * which + part + 1, :] = parts[0][part]
            first = lax.broadcasted_iota(jnp.int32, (1, 128), 1) < HD
            totals_ref[8 * which + 6 : 8 * which + 7, :] = jnp.where(first, *sums)
            totals_ref[8 * which + 7 : 8 * which + 8, :] = jnp.zeros((1, 128), F32)

    @pl.when(project & (tile == 0))
    def _():
        def body(rows):
            h = hidden[layer, rows, :].astype(F32)
            centred = h - jnp.mean(h, -1, keepdims=True)
            root = lax.rsqrt(jnp.mean(centred * centred, -1, keepdims=True) + EPSILON)
            scale[layer, rows, :] = jnp.broadcast_to(root, (128, 128))
            normed[layer, rows, :] = (centred * root * ln_ref[layer]).astype(BF16)
        by_rows(body)

    @pl.when(project)
    def _():
        def projected(columns):
            return dot(normed[layer, :, :], w_ref[:, columns])

        def heads(low_ref, root_ref, gain, factor):
            @thirds
            def _(columns):
                x = projected(columns)
                centred = x - head_means(x, spread)
                root = lax.rsqrt(head_means(centred * centred, spread, False) + EPSILON)
                root_ref[layer, :, columns] = root.astype(BF16)
                low_ref[layer, :, columns] = (centred * root * (gain * factor)).astype(BF16)

        pl.when(tile == 0)(lambda: heads(q, rq, qg_ref[layer], SCALE))
        pl.when(tile == 1)(lambda: heads(k, rk, kg_ref[layer], 1.0))

        @pl.when(tile == 2)
        def _():
            v[layer, :, :] = projected(slice(None)).astype(BF16)
            low = low_lanes()
            augq, augk = augq_ref[...], augk_ref[...]
            ones = jnp.ones((SLOTS, 128), BF16)

            def pair(index):
                part = lanes(index, 128)
                qp, kp, vp = q[layer, :, part], k[layer, :, part], v[layer, :, part]
                results = []
                for head in (0, 1):
                    mine = low if head == 0 else ~low
                    scores = dot(jnp.where(mine, qp, augq), jnp.where(mine, kp, augk), ACROSS)
                    results.append(dot(jnp.exp2(scores).astype(BF16), jnp.where(mine, vp, ones)))
                inverse = 1.0 / pltpu.roll(jnp.where(low, results[1], results[0]), HD, 1)
                linv[layer, :, part] = inverse.astype(BF16)
                combined[layer, 0, :, part] = (jnp.where(low, results[0], results[1]) * inverse).astype(BF16)
            for index in range(PAIRS):
                pair(index)

        @pl.when(tile > 2)
        def _():
            @thirds
            def _(columns):
                value, rise = gelu_and_slope(projected(columns))
                slope[layer, tile - 3, :, columns] = rise.astype(BF16)
                combined[layer, tile - 2, :, columns] = value.astype(BF16)

    @pl.when(output | output_both)
    def _():
        dq[...] = jnp.where(tile == 0, hidden[layer].astype(F32), dq[...]) + dot(combined[layer, tile], w_ref[...])

        @pl.when(tile == TILES_OUT - 1)
        def _():
            result = dq[...].astype(BF16)
            hidden[layer + 1] = result
            if trade:
                trade.give_output(layer)
            else:
                section_out[layer] = result

    @pl.when(output_both | back)
    def _():
        made = jnp.where(t < LAST_OUT, t - SECOND_OUT, TILES_OUT + t - LAST_OUT)
        pl.when(made >= 2)(lambda: terms_copy(terms_out, terms_tile, terms_sem, made % 2, 0, 0).wait())

        def grads(columns):
            return dot(dy[...], w_ref[columns, :], ACROSS)

        terms_tile[made % 2] = dot(combined[layer, tile], dy[...], DOWN).astype(BF16)
        terms_copy(terms_out, terms_tile, terms_sem, made % 2, layer, tile).start()
        if not trading:
            pl.when(t == LAST_BACK - 1)(lambda: terms_settled(terms_out, terms_tile, terms_sem))

        @pl.when(tile == 0)
        def _():
            @thirds
            def _(columns):
                grad, inverse = grads(columns), linv[layer, :, columns].astype(F32)
                do[:, columns] = (grad * inverse).astype(BF16)
                total = head_means(grad * combined[layer, 0, :, columns].astype(F32), spread) * (inverse * -HD)
                for half in (0, 128):
                    part = pl.ds(columns.start + half, 128)
                    high, low = split(pltpu.roll(total[:, half : half + 128], HD, 1))
                    dhigh[:, part] = high
                    dlow[:, part] = low

        @pl.when(tile > 0)
        def _():
            @thirds
            def _(columns):
                dproj[tile + 2, :, columns] = (grads(columns) * slope[layer, tile - 1, :, columns].astype(F32)).astype(BF16)

    @pl.when(heads_now)
    def _():
        low = low_lanes()
        spot = lax.broadcasted_iota(jnp.int32, (SLOTS, 128), 1) % HD
        first = spot == 0
        augv = jnp.where(spot < 2, 1.0, 0.0).astype(BF16)
        augq, augk = augq_ref[...], augk_ref[...]
        none = jnp.zeros((SLOTS, 128), BF16)

        def pair(index):
            part = lanes(index, 128)
            qp, kp, vp, dop = q[layer, :, part], k[layer, :, part], v[layer, :, part], do[:, part]
            augd = jnp.where(first, dhigh[:, part], dlow[:, part])
            sums = [None, None, None]
            for head in (0, 1):
                mine = low if head == 0 else ~low
                e = jnp.exp2(dot(jnp.where(mine, kp, augk), jnp.where(mine, qp, augq), ACROSS))
                dp = dot(jnp.where(mine, vp, augv), jnp.where(mine, dop, augd), ACROSS)
                ds = (e * dp).astype(BF16)
                parts = (dot(ds, jnp.where(mine, kp, none), DOWN), dot(ds, jnp.where(mine, qp, none)),
                         dot(e.astype(BF16), jnp.where(mine, dop, none)))
                sums = [part_sum if total is None else total + part_sum for total, part_sum in zip(sums, parts)]
            dq[:, part] = sums[0] * 0.125
            dk[:, part] = sums[1] * (1.0 / LOG2E)
            dproj[2, :, part] = sums[2].astype(BF16)
        late = t >= LAST_HEADS
        first_pair = jnp.where(late, 2 * (t - LAST_HEADS), 0)

        def two_pairs(index):
            pair(first_pair + 2 * index)
            pair(first_pair + 2 * index + 1)
        loop(jnp.where(late, 1, PAIRS // 2), two_pairs)

    @pl.when(project_back & (tile == 0))
    def _():
        for which, grads, low_ref, root_ref, gain, factor in ((0, dq, q, rq, qg_ref, SCALE), (1, dk, k, rk, kg_ref, 1.0)):
            @thirds
            def _(columns):
                grad, gains = grads[:, columns], gain[layer]
                xhat = low_ref[layer, :, columns].astype(F32) * (1.0 / (gains * factor))
                scaled = grad * gains
                mean = head_means(scaled, spread, False)
                along = head_means(scaled * xhat, spread, False)
                dproj[which, :, columns] = (root_ref[layer, :, columns].astype(F32) * (scaled - mean - xhat * along)).astype(BF16)
                gain_ref[layer, which + 1 : which + 2, columns] += jnp.sum(grad * xhat, 0, keepdims=True)

    @pl.when(project_back)
    def _():
        acc[...] = jnp.where(tile == up_first(0), 0.0, acc[...]) + dot(dproj[tile], w_ref[...], ACROSS)
        terms_in_ref[...] = dot(normed[layer, :, :], dproj[tile], DOWN).astype(BF16)

        @pl.when(tile == LAST_TILE)
        def _():
            gains = ln_ref[layer]

            def body(rows):
                grad = acc[rows, :]
                xhat = normed[layer, rows, :].astype(F32) * (1.0 / gains)
                scaled = grad * gains
                mean = jnp.mean(scaled, -1, keepdims=True)
                along = jnp.mean(scaled * xhat, -1, keepdims=True)
                total = dy[rows, :].astype(F32) + scale[layer, rows, :1] * (scaled - mean - xhat * along)
                low = total.astype(BF16)
                if trade:
                    pl.when(layer == section)(lambda: grad_ref.__setitem__((rows, slice(None)), total))
                else:
                    grad_ref[layer, rows, :] = total
                pl.when(layer == 1)(lambda: dy.__setitem__((rows, slice(None)), low))
                pl.when(layer == 0)(lambda: grad_low.__setitem__((rows, slice(None)), low))
                gain_ref[layer, 0:1, :] += jnp.sum(grad * xhat, 0, keepdims=True)
            by_rows(body)
            if trade:
                pl.when(layer == 1)(trade.give_grad)
                pl.when(layer == 0)(trade.finish)
            pl.when(layer == 0)(fold_gains)

    if trading:
        pl.when(t >= LAST_BACK - 1)(
            lambda: outer_scatter(t, terms_out, terms_tile, terms_sem, own_out, combined, slope, saved, *scatter_refs))


class Saved:
    def __init__(self, ref, which):
        self.ref, self.which = ref, which

    def __getitem__(self, index):
        return self.ref[(index[0], self.which) + index[1:]]

    def __setitem__(self, index, value):
        self.ref[(index[0], self.which) + index[1:]] = value


def terms_copy(terms_out, terms_tile, terms_sem, slot, layer, tile):
    target = terms_out.at[layer, pl.ds(pl.multiple_of(tile * D, D), D), :]
    return pltpu.make_async_copy(terms_tile.at[slot], target, terms_sem.at[slot])


def terms_settled(terms_out, terms_tile, terms_sem):
    for slot in range(2):
        terms_copy(terms_out, terms_tile, terms_sem, slot, 0, 0).wait()


def outer_scatter(t, terms_out, terms_tile, terms_sem, own_out, combined, slope, saved, rest_land, ready_sem, *sems):
    place = Place()
    rows = BLOCK[1][0]

    def half(number):
        return pl.ds(pl.multiple_of((number % 2) * rows, 16), rows)

    def held(number):
        return combined.at[number // 10, (number // 2) % 5, half(number)]

    def core_land(number):
        return slope.at[number // 8, (number // 2) % 4, half(number)]

    def land(colour, slot):
        piece = colour * 20 + slot
        return saved.at[1, piece // 5, pl.ds(pl.multiple_of((piece % 5) * 96, 16), 96)]

    scatter = Scatter(place, 1, terms_out, held, core_land, land, lambda slot: rest_land.at[slot], sems[:7])

    @pl.when(t == LAST_BACK - 1)
    def _():
        terms_settled(terms_out, terms_tile, terms_sem)
        greet(place, ready_sem)
        scatter.begin()

    first, count = 0, 0
    for slot, steps in enumerate(OUTER_ORDER):
        here = (t == LAST_BACK - 1 + slot).astype(jnp.int32)
        first += here * sum(map(len, OUTER_ORDER[:slot]))
        count += here * len(steps)
    scatter.run([step for steps in OUTER_ORDER for step in steps], first, count)
    pl.when(t == STEPS - 1)(lambda: scatter.finish(own_out, sems[7]))


class Trade:
    def __init__(self, section, section_out, hidden, dy, grad_land, own_sem, send_sem, recv_sem):
        self.section, self.section_out, self.hidden, self.dy, self.grad_land = section, section_out, hidden, dy, grad_land
        self.own_sem, self.send_sem, self.recv_sem = own_sem, send_sem, recv_sem
        self.pair = (1 - section, lax.axis_index("wide"))

    def kept(self):
        return pltpu.make_async_copy(self.hidden.at[self.section + 1], self.section_out.at[self.section], self.own_sem)

    def copy(self, source, target, index):
        return pltpu.make_async_remote_copy(
            src_ref=source, dst_ref=target, send_sem=self.send_sem.at[index], recv_sem=self.recv_sem.at[index],
            device_id=self.pair, device_id_type=MESH)

    def given(self):
        return self.copy(self.hidden.at[2 - self.section], self.section_out.at[self.section], 0)

    def grad(self):
        return self.copy(self.dy, self.grad_land, 1)

    def give_output(self, layer):
        pl.when(layer == self.section)(lambda: self.kept().start())
        pl.when(layer != self.section)(lambda: self.given().start())

    def give_grad(self):
        pl.when(self.section == 0)(lambda: self.grad().start())

    def finish(self):
        self.kept().wait()
        self.given().wait_send()
        self.copy(self.hidden.at[2 - self.section], self.section_out.at[1 - self.section], 0).wait_recv()
        pl.when(self.section == 0)(lambda: self.grad().wait_send())
        pl.when(self.section == 1)(lambda: self.grad().wait_recv())


def both_layers(trading, counts, weights, gains, inputs, cotangent, augq, augk, spread):
    square = (SLOTS, D)

    def whole(*dims):
        return pl.BlockSpec(dims, lambda t: (0,) * len(dims))

    low, wide = (lambda *dims: pltpu.VMEM(dims, BF16)), (lambda *dims: pltpu.VMEM(dims, F32))
    any_space, dma = pl.BlockSpec(memory_space=pl.ANY), pltpu.SemaphoreType.DMA
    full = [jax.ShapeDtypeStruct(dims, BF16) for dims in ((2, D, TILES_IN * D), (2, TILES_OUT * D, D))]
    if trading:
        in_specs, operands = [any_space] * 3, (*weights, gains)
        out_specs, more_specs = [any_space, whole(*square), whole(*square), any_space], [any_space] * 3
        sems = [dma((5, 3, 16)), dma((3, 16)), dma((3, 16))] * 3 + [dma((3,))]
        extra = [low(2, 16 * BLOCK[2][0], 128)] + sems + [dma(()), dma((2,)), dma((2,))]
        extra += [low(35, *part_shape(SCATTER_CUTS, 1, None)), pltpu.SemaphoreType.REGULAR] + scatter_sems()
        grad_shape, more = square, full + [jax.ShapeDtypeStruct(BLOCK[1], BF16)]
        params = dict(collective_id=2, has_side_effects=True)
    else:
        in_specs, operands = [any_space] * 2 + [whole(*gains.shape)], (*weights, gains)
        out_specs, more_specs = [whole(2, *square), whole(2, *square), whole(*square), whole(*square)], []
        grad_shape, extra, more, params = (2,) + square, [], [], {}
    return pl.pallas_call(
        functools.partial(compute_kernel, trading, counts),
        grid=(STEPS,),
        in_specs=in_specs + [any_space, any_space, whole(SLOTS, 128), whole(SLOTS, 128), whole(256, 256)],
        out_specs=out_specs + [
            whole(16, 128), pl.BlockSpec((None, D, D), lambda t: (in_terms(t)[0], 0, in_terms(t)[1])), any_space,
        ] + more_specs,
        scratch_shapes=[
            low(2, D, D), dma((2,)), wide(2, 1, D), wide(2, 1, 256), wide(2, 1, 256),
            low(3, *square), low(2, 8, *square), wide(2, SLOTS, 128), low(2, 4, *square), low(2, 5, *square), low(*square), low(7, *square),
            wide(*square), wide(*square), wide(*square), low(*square), low(*square), low(*square), low(2, D, D), dma((2,)), dma((2,)),
            wide(2, 8, D),
        ] + extra,
        out_shape=[
            jax.ShapeDtypeStruct((2,) + square, BF16), jax.ShapeDtypeStruct(grad_shape, F32), jax.ShapeDtypeStruct(square, BF16),
            jax.ShapeDtypeStruct(square, BF16), jax.ShapeDtypeStruct((16, 128), F32), *full,
        ] + more,
        compiler_params=pltpu.CompilerParams(vmem_limit_bytes=63 * 2**20, **params),
        name="both_layers",
    )(*operands, inputs, cotangent, augq, augk, spread)


def augment(image_id, token_size):
    lane = jnp.arange(128)[None, :] % HD
    size = jnp.log2(token_size.astype(F32))[:, None]
    high = size.astype(BF16).astype(F32)
    same = image_id[:, None] == lane - 2
    q = jnp.where((lane < 2) | (lane == 5) | same, 1.0, 0.0)
    k = jnp.where(lane == 0, high, jnp.where(lane == 1, size - high, jnp.where(lane == 5, -APART, jnp.where(same, APART, 0.0))))
    return q.astype(BF16), k.astype(BF16)


def spread_matrix():
    head = jnp.arange(256) // HD
    return ((head[:, None] == head[None, :]) / HD).astype(BF16)


def gather_all(piece, axis):
    return lax.all_gather(lax.all_gather(piece, "wide", axis=axis, tiled=True), "section", axis=0, tiled=True)


def scatter_all(terms, axis):
    own = lax.psum_scatter(terms, "section", scatter_dimension=0, tiled=True)
    return lax.psum_scatter(own, "wide", scatter_dimension=axis, tiled=True)


def on_device(inputs, cotangent, token_size, image_id, w_in, w_out, ln_gain, q_gain, k_gain):
    section, wide = lax.axis_index("section"), lax.axis_index("wide")
    width = lax.axis_size("wide")
    blocks_fit = width == 16 and w_in.shape[1:] == BLOCK[0] and w_out.shape[1:] == BLOCK[1]
    ends = [0]
    for gain in (ln_gain, q_gain, k_gain):
        ends.append(ends[-1] + gain.shape[1])
    own_gains = jnp.concatenate([ln_gain, q_gain, k_gain], 1)
    gains = jnp.pad(own_gains, ((0, BLOCK[2][0] - 1), (0, BLOCK[2][1] - ends[3])))
    weights = (w_in[0], w_out[0])
    if not blocks_fit:
        weights = (gather_all(w_in, 1), gather_all(w_out, 1))
        gains = gather_all(gains[None], 1)
    augq, augk = augment(image_id[section, 0], token_size[section, 0])
    outs, grads, grad_low, grad_land, totals, terms_in, terms_out, *more = both_layers(
        blocks_fit, tuple(gain.shape[1] for gain in (ln_gain, q_gain, k_gain)), weights, gains, inputs,
        cotangent, augq, augk, spread_matrix())
    swap = [(0, 1), (1, 0)]

    def both_micro(pair):
        mine = lax.dynamic_index_in_dim(pair, section, 0, False)
        other = lax.dynamic_index_in_dim(pair, 1 - section, 0, False).astype(BF16)
        other = lax.ppermute(other, "section", swap).astype(mine.dtype)
        return jnp.where(section == 0, jnp.stack([mine, other]), jnp.stack([other, mine]))[None, :, None]

    places = (0, D, D + HD, D + 2 * HD)
    if blocks_fit:
        own_in, totals, last_land = scatter_terms(terms_in, totals, grad_low)
        other = jnp.where(section == 0, last_land, grad_land).astype(F32)
        is_own = (jnp.arange(2) == section)[:, None, None]
        grads = jnp.where(is_own, grads[None], other[None])[None, :, None]
        outs = outs[None, :, None]
        own_in, own_out = own_in[None].astype(F32), more[2][None].astype(F32)
    else:
        own_in = scatter_all(terms_in, 1).astype(F32)
        own_out = scatter_all(terms_out, 1).astype(F32)
        totals = lax.psum(totals, ("section", "wide"))
        outs, grads = both_micro(outs), both_micro(grads)
    mine = lax.dynamic_index_in_dim(totals.reshape(2, 1024), section, 0, False)
    gain_grads = [
        lax.dynamic_slice_in_dim(mine[low:high], wide * gain.shape[1], gain.shape[1])[None]
        for low, high, gain in zip(places, places[1:], (ln_gain, q_gain, k_gain))
    ]
    return (outs, grads, own_in, own_out, *gain_grads)


def solution(mesh):
    return jax.shard_map(
        on_device,
        mesh=mesh,
        in_specs=(
            P(None, "wide", None, None),
            P(None, "wide", None, None),
            P(None, "wide", None),
            P(None, "wide", None),
            P("section", "wide", None),
            P("section", "wide", None),
            P("section", "wide"),
            P("section", "wide"),
            P("section", "wide"),
        ),
        out_specs=(
            P("section", None, "wide", None, None),
            P("section", None, "wide", None, None),
            P("section", "wide", None),
            P("section", "wide", None),
            P("section", "wide"),
            P("section", "wide"),
            P("section", "wide"),
        ),
        check_vma=False,
    )
```

```python
import functools

import jax
import jax.numpy as jnp
from jax import lax
from jax.experimental import pallas as pl
from jax.experimental.pallas import tpu as pltpu
from jax.sharding import PartitionSpec as P

MESH = pl.DeviceIdType.MESH
NZ = 4
BLOCK = ((48, 5376), (240, 768), (16, 128))
GATHER_CUTS = (2176, 96)
SCATTER_CUTS = (2048, 96)


class Place:
    def __init__(self):
        self.x, self.wide = lax.axis_index("section"), lax.axis_index("wide")
        self.y, self.z, self.c = (self.wide // 2) % 2, self.wide // 4, self.wide % 2

    def at(self, x, y, z, c=None):
        return (x, z * 4 + y * 2 + (self.c if c is None else c))

    def along(self, colour, block_z, far_first, far_second):
        dx = jnp.where(colour == 0, far_first, far_second)
        dy = jnp.where(colour == 0, far_second, far_first)
        return self.flip(self.x, dx), self.flip(self.y, dy), block_z

    @staticmethod
    def flip(value, far):
        return value + far - 2 * value * far

    def first(self, colour):
        return self.at(*self.along(colour, self.z, 1, 0))

    def second(self, colour):
        return self.at(*self.along(colour, self.z, 0, 1))

    def sibling(self):
        return self.at(self.x, self.y, self.z, 1 - self.c)


def greet(place, barrier=None):
    barrier = pltpu.get_barrier_semaphore() if barrier is None else barrier
    x, y, z = place.x, place.y, place.z

    def signal(device):
        pl.semaphore_signal(barrier, inc=1, device_id=device, device_id_type=MESH)

    signal(place.at(1 - x, y, z))
    signal(place.at(x, 1 - y, z))
    signal(place.sibling())
    pl.when(z < NZ - 1)(lambda: signal(place.at(x, y, z + 1)))
    pl.when(z > 0)(lambda: signal(place.at(x, y, z - 1)))
    pl.semaphore_wait(barrier, 3 + (z < NZ - 1).astype(jnp.int32) + (z > 0).astype(jnp.int32))


def number_of(block):
    return block[0] * 8 + block[1] * 4 + block[2]


def part_shape(cuts, array, colour):
    rows, cols = BLOCK[array]
    size = cuts[array]
    if array == 0:
        return rows, cols - 2 * size if colour is None else size
    return rows - 2 * size if colour is None else size, cols


def cut(ref, cuts, array, colour):
    if array == 2:
        return ref
    rows, cols = part_shape(cuts, array, colour)
    size = cuts[array]
    if array == 0:
        return ref.at[:, pl.ds(2 * size if colour is None else pl.multiple_of(colour * size, 128), cols)]
    return ref.at[pl.ds(2 * size if colour is None else pl.multiple_of(colour * size, 16), rows), :]


def loop(count, body):
    def step(index, carry):
        body(index)
        return carry
    lax.fori_loop(0, count, step, 0)


class Gather:
    def __init__(self, place, array, own, full, send_sem, recv_sem, core_sem):
        self.place, self.array, self.own, self.full = place, array, own, full
        self.send_sem, self.recv_sem, self.core_sem = send_sem, recv_sem, core_sem

    def view(self, block, colour, plane=None):
        rows = BLOCK[self.array][0]
        place = self.place
        start = (block[2] * 4 + block[1] * 2 + (place.c if plane is None else plane)) * rows
        return cut(self.full.at[block[0], pl.ds(pl.multiple_of(start, 16), rows), :], GATHER_CUTS, self.array, colour)

    def copy(self, link, device, block, colour, own=False, other_plane=False):
        kind = 2 if colour is None else colour
        number = number_of(block)
        target = self.view(block, colour, 1 - self.place.c if other_plane else None)
        source = cut(self.own, GATHER_CUTS, self.array, colour) if own else target
        sems = self.core_sem if link == 4 else self.recv_sem
        return pltpu.make_async_remote_copy(
            src_ref=source, dst_ref=target, send_sem=self.send_sem.at[link, kind, number], recv_sem=sems.at[kind, number],
            device_id=device, device_id_type=MESH)

    def visit(self, block, colour, onward, first, second, drain, condition=None, own=False):
        place = self.place

        def body():
            if not drain and not own:
                self.copy(0, place.sibling(), block, colour).wait_recv()

            def send(link, device):
                copy = self.copy(link, device, block, colour, own)
                copy.wait_send() if drain else copy.start()

            for link, step in onward:
                target = place.z + step
                pl.when((target >= 0) & (target < NZ))(functools.partial(send, link, place.at(place.x, place.y, target)))
            if first is not None:
                send(2, first)
            if second is not None:
                if isinstance(second, tuple) and len(second) == 3:
                    pl.when(second[2])(functools.partial(send, 3, second[:2]))
                else:
                    send(3, second)
            send(4, place.sibling())
        if condition is None:
            body()
        else:
            pl.when(condition)(body)

    def begin(self, drain=False):
        place = self.place
        me = (place.x, place.y, place.z)
        everywhere = ((0, 1), (1, -1))
        self.visit(me, None, everywhere, place.at(1 - place.x, place.y, place.z), place.at(place.x, 1 - place.y, place.z), drain, own=True)

        def body(colour):
            self.visit(me, colour, everywhere, place.first(colour), place.second(colour), drain, own=True)
        if self.array < 2:
            loop(2, body)

    def square(self, drain=False):
        place = self.place

        def body(index):
            far_x, far_y = (index != 1).astype(jnp.int32), (index != 0).astype(jnp.int32)
            block = (place.flip(place.x, far_x), place.flip(place.y, far_y), place.z)
            self.visit(block, None, ((0, 1), (1, -1)), None, place.at(place.x, 1 - place.y, place.z) + (index == 0,), drain)
        loop(3, body)

    def sided(self, distance, body):
        place = self.place

        def side_body(side):
            step = 1 - 2 * side
            block_z = place.z - step * distance
            body(side, block_z, (block_z >= 0) & (block_z < NZ) & ((distance > 0) | (side == 0)))
        loop(2, side_body)

    def onward(self, side):
        return ((0, 1), (1, -1))[side]

    def z_step(self, distance, drain=False):
        place = self.place
        for side in (0, 1):
            step = 1 - 2 * side
            block_z = place.z - step * distance

            def body(colour):
                self.visit((place.x, place.y, block_z), colour, ((side, step),), place.first(colour), place.second(colour), drain)
            pl.when((block_z >= 0) & (block_z < NZ))(lambda: loop(2, body))

    def line(self, distance, drain=False):
        place = self.place
        for side in (0, 1):
            step = 1 - 2 * side
            block_z = place.z - step * distance

            def body(index):
                block = (place.flip(place.x, index % 2), place.flip(place.y, index // 2), block_z)
                self.visit(block, None, ((side, step),), None, None, drain)
            pl.when((block_z >= 0) & (block_z < NZ))(lambda: loop(4, body))

    def a_step(self, distance, drain=False):
        place = self.place

        def body(side, block_z, there):
            def inner(colour):
                self.visit(place.along(colour, block_z, 1, 0), colour, (), None, place.second(colour), drain)
            pl.when(there)(lambda: loop(2, inner))
        self.sided(distance, body)

    def b_step(self, distance, drain=False):
        place = self.place

        def body(side, block_z, there):
            def inner(index):
                colour = index // 2
                self.visit(place.along(colour, block_z, index % 2, 1), colour, (), None, None, drain)
            pl.when(there)(lambda: loop(4, inner))
        self.sided(distance, body)

    def from_core(self):
        place = self.place

        def body(number):
            block = (number // 8, (number // 4) % 2, number % 4)
            self.copy(4, place.sibling(), block, None, other_plane=True).wait_recv()
            for colour in (0, 1) if self.array < 2 else ():
                self.copy(4, place.sibling(), block, colour, other_plane=True).wait_recv()
        loop(16, body)

    def drain(self):
        self.begin(True)
        self.square(True)

        def body(index):
            self.line(index + 1, True)
            if self.array < 2:
                self.z_step(index + 1, True)
                self.a_step(index, True)
                self.b_step(index, True)
        loop(NZ, body)


class Weights:
    def __init__(self, place, own, full, tiles, tile_sem, sems):
        self.place, self.full, self.tiles, self.tile_sem = place, full, tiles, tile_sem
        self.copies = []
        if place is None:
            return
        self.inner, self.outer, self.gains = [Gather(place, array, own[array], full[array], *sems[3 * array : 3 * array + 3]) for array in range(3)]
        for array in range(3):
            rows = BLOCK[array][0]
            target = full[array].at[place.x, pl.ds(pl.multiple_of(place.wide * rows, 16), rows), :]
            self.copies.append(pltpu.make_async_copy(own[array], target, sems[9].at[array]))

    def begin(self):
        greet(self.place)
        for copy in self.copies:
            copy.start()
        self.gains.begin()
        self.inner.begin()
        self.gains.square()
        self.inner.square()

        def early(index):
            self.inner.z_step(index + 1)
            self.inner.a_step(index)
            self.gains.line(index + 1)
            self.inner.line(index + 1)
        loop(NZ - 1, early)
        self.outer.begin()
        self.inner.a_step(NZ - 1)
        self.outer.square()

        def late(index):
            self.inner.b_step(index)
            pl.when(index == 1)(lambda: self.onward(0))
        loop(NZ, late)
        self.gains.from_core()
        self.inner.from_core()
        for copy in self.copies:
            copy.wait()

    def onward(self, index):
        self.outer.z_step(index + 1)
        self.outer.a_step(index)
        self.outer.line(index + 1)

    def end(self):
        loop(NZ, self.outer.b_step)
        self.outer.from_core()

    def drain(self):
        for array in (self.gains, self.inner, self.outer):
            array.drain()

    def fetch(self, t):
        slot = tile_slot(t)
        tile, sem = self.tiles.at[slot], self.tile_sem.at[slot]
        project = uses_in(t)

        def inner():
            layer, index = in_tile(t)
            return pltpu.make_async_copy(self.full[0].at[layer, :, pl.ds(pl.multiple_of(index * D, D), D)], tile, sem)

        def outer():
            layer, index = out_tile(t)
            return pltpu.make_async_copy(self.full[1].at[layer, pl.ds(pl.multiple_of(index * D, D), D), :], tile, sem)
        pl.when(project)(lambda: inner().start())
        pl.when(jnp.logical_not(project))(lambda: outer().start())

    def wait(self, t):
        slot = tile_slot(t)
        pltpu.make_async_copy(self.full[0].at[0, :, pl.ds(0, D)], self.tiles.at[slot], self.tile_sem.at[slot]).wait()

    def step(self, t):
        if self.place is not None:
            pl.when(t == 0)(self.begin)
            pl.when((t >= 2) & (t <= NZ))(lambda: self.onward(t - 1))
            pl.when(t == FIRST_OUT)(self.end)
            pl.when(t == LAST_OUT)(self.drain)
            held_back = FIRST_OUT
        else:
            held_back = 0
        following = jnp.where(t == LAST_HEADS - 1, LAST_PROJECT, t + 1)
        pl.when((t == 0) | (t == held_back))(lambda: self.fetch(t))
        pl.when(has_tile(t) & (following < STEPS) & (following != held_back))(lambda: self.fetch(following))
        pl.when(has_tile(t))(lambda: self.wait(t))


def add_into(target, source):
    def body(step):
        part = pl.ds(pl.multiple_of(step * 48, 16), 48)
        target[part, :] = target[part, :] + source[part, :]
    loop(target.shape[0] // 48, body)


OUTER_ORDER = (
    ("k3", "l3"), (), ("a3", "k2"), (), ("l2",), ("b3", "k1", "a2", "z3"), ("l1",), ("k0", "b2"), ("z2", "a1", "l0"), (),
    ("a0", "b1", "z1", "s", "b0", "z0"))
INNER_ORDER = (
    "k3", "k2", "l3", "k1", "l2", "a3", "k0", "l1", "b3", "a2", "z3", "a1", "l0", "b2", "z2", "b1", "a0", "z1", "s", "b0", "z0")
INNER_GRAD = 14


class Scatter:
    def __init__(self, place, array, terms, held, core_land, land, rest_land, sems):
        self.place, self.array, self.terms, self.held, self.core_land = place, array, terms, held, core_land
        self.land, self.rest_land = land, rest_land
        self.send_sem, self.recv_sem, self.rest_send, self.rest_recv, self.core_send, self.core_recv, self.local_sem = sems

    def part(self, block, colour):
        return cut(self.held(number_of(block)), SCATTER_CUTS, self.array, colour)

    def copy(self, device, block, colour, slot):
        if colour is None:
            target, send_sem, recv_sem = self.rest_land(slot), self.rest_send.at[slot], self.rest_recv.at[slot]
        else:
            target, send_sem, recv_sem = self.land(colour, slot), self.send_sem.at[colour, slot], self.recv_sem.at[colour, slot]
        return pltpu.make_async_remote_copy(
            src_ref=self.part(block, colour), dst_ref=target, send_sem=send_sem, recv_sem=recv_sem, device_id=device,
            device_id_type=MESH)

    def send(self, device, block, colour, slot, drain):
        copy = self.copy(device, block, colour, slot)
        copy.wait_send() if drain else copy.start()

    def arrive(self, block, colour, slot, drain):
        if not drain:
            self.copy(self.place.sibling(), block, colour, slot).wait_recv()
            add_into(self.part(block, colour), self.rest_land(slot) if colour is None else self.land(colour, slot))

    def core_copy(self, block, mine):
        rows = BLOCK[self.array][0]
        place = self.place
        number = number_of(block)
        start = (block[2] * 4 + block[1] * 2 + (place.c if mine else 1 - place.c)) * rows
        source = self.terms.at[block[0], pl.ds(pl.multiple_of(start, 16), rows), :]
        if mine:
            return pltpu.make_async_copy(source, self.held(number), self.local_sem.at[number])
        return pltpu.make_async_remote_copy(
            src_ref=source, dst_ref=self.core_land(number), send_sem=self.core_send.at[number],
            recv_sem=self.core_recv.at[number], device_id=place.sibling(), device_id_type=MESH)

    def sided(self, distance, body):
        place = self.place

        def side_body(side):
            block_z = place.z + (2 * side - 1) * distance
            there = (block_z >= 0) & (block_z < NZ) & (distance < NZ) & (distance >= 0) & ((distance > 0) | (side == 0))
            pl.when(there)(lambda: body(block_z))
        loop(2, side_body)

    def start(self, distance):
        place = self.place

        def body(block_z):
            def inner(index):
                block = (place.flip(place.x, 1 - index % 2), place.flip(place.y, 1 - index // 2), block_z)
                self.core_copy(block, False).start()
                self.core_copy(block, True).start()
            loop(4, inner)
        self.sided(distance, body)

    def k_step(self, distance, drain=False):
        place = self.place

        def body(block_z):
            def inner(index):
                far_x, far_y = 1 - index % 2, 1 - index // 2
                block = (place.flip(place.x, far_x), place.flip(place.y, far_y), block_z)
                if not drain:
                    self.core_copy(block, True).wait()
                    copy = self.core_copy(block, False)
                    copy.wait_recv()
                    add_into(self.held(number_of(block)), self.core_land(number_of(block)))
                    copy.wait_send()

                def out(colour):
                    far_first = jnp.where(colour == 0, far_x, far_y)
                    far_second = jnp.where(colour == 0, far_y, far_x)
                    pl.when(far_second == 1)(lambda: self.send(place.second(colour), block, colour, far_first * 4 + block_z, drain))
                loop(2, out)
            loop(4, inner)
        self.sided(distance, body)

    def a_step(self, distance, drain=False):
        place = self.place

        def body(block_z):
            def inner(index):
                colour, far_first = index % 2, 1 - index // 2
                block = place.along(colour, block_z, far_first, 0)
                self.arrive(block, colour, far_first * 4 + block_z, drain)
                pl.when(far_first == 1)(lambda: self.send(place.first(colour), block, colour, 8 + block_z, drain))
            loop(4, inner)
        self.sided(distance, body)

    def b_step(self, distance):
        place = self.place

        def body(block_z):
            loop(2, lambda colour: self.arrive((place.x, place.y, block_z), colour, 8 + block_z, False))
        self.sided(distance, body)

    def toward(self, distance, body):
        place = self.place
        for side, step in ((0, -1), (1, 1)):
            block_z, behind = place.z + step * distance, place.z - step
            there = (block_z >= 0) & (block_z < NZ) & (distance < NZ) & (distance >= 0)
            pl.when(there)(functools.partial(body, block_z, side, step, (behind >= 0) & (behind < NZ)))

    def z_step(self, distance, drain=False):
        place = self.place

        def body(block_z, side, step, more):
            block = (place.x, place.y, block_z)
            slot = 12 + 4 * side + block_z

            def inner(colour):
                pl.when(more)(lambda: self.arrive(block, colour, slot, drain))
                pl.when(distance > 0)(lambda: self.send(place.at(place.x, place.y, place.z + step), block, colour, slot, drain))
            loop(2, inner)
        self.toward(distance, body)

    def line(self, distance, drain=False):
        place = self.place

        def body(block_z, side, step, more):
            def inner(index):
                block = (place.flip(place.x, 1 - index % 2), place.flip(place.y, 1 - index // 2), block_z)
                slot = 16 * side + number_of(block)
                pl.when(more)(lambda: self.arrive(block, None, slot, drain))
                pl.when(distance > 0)(lambda: self.send(place.at(place.x, place.y, place.z + step), block, None, slot, drain))
            loop(4, inner)
        self.toward(distance, body)

    def square(self, drain=False):
        place = self.place
        over_x, over_y = place.at(1 - place.x, place.y, place.z), place.at(place.x, 1 - place.y, place.z)
        far = (1 - place.x, place.y, place.z)
        self.send(over_y, (1 - place.x, 1 - place.y, place.z), None, 33, drain)
        self.send(over_y, (place.x, 1 - place.y, place.z), None, 32, drain)
        self.arrive(far, None, 33, drain)
        self.send(over_x, far, None, 34, drain)
        self.arrive((place.x, place.y, place.z), None, 32, drain)
        self.arrive((place.x, place.y, place.z), None, 34, drain)

    def drain(self):
        def body(distance):
            self.k_step(distance, True)
            self.a_step(distance, True)
            self.z_step(distance, True)
            self.line(distance, True)
        loop(NZ, body)
        self.square(True)


    STEPS = "klabzs"

    def begin(self):
        loop(NZ, lambda index: self.start(NZ - 1 - index))

    def run(self, order, first, count, also=None):
        codes = [(self.STEPS.index(step[0]), int(step[1:] or 0)) for step in order]

        def body(index):
            index = first + index
            which, distance = [sum((index == place).astype(jnp.int32) * code[part] for place, code in enumerate(codes)) for part in (0, 1)]
            calls = (self.k_step, self.line, self.a_step, self.b_step, self.z_step)
            for code, call in enumerate(calls):
                pl.when(which == code)(lambda: call(distance))
            pl.when(which == len(calls))(self.square)
            if also:
                also(index)
        loop(count, body)

    def finish(self, result, sem):
        copy = pltpu.make_async_copy(self.held(number_of((self.place.x, self.place.y, self.place.z))), result, sem)
        copy.start()
        self.drain()
        copy.wait()


def scatter_sems():
    dma = pltpu.SemaphoreType.DMA
    return [dma((2, 20)), dma((2, 20)), dma((35,)), dma((35,)), dma((16,)), dma((16,)), dma((16,)), dma(())]


class Total:
    def __init__(self, place, own, out, run, land, send_sem, recv_sem):
        self.place, self.own, self.out, self.run, self.land = place, own, out, run, land
        self.send_sem, self.recv_sem = send_sem, recv_sem
        x, y, z = place.x, place.y, place.z
        self.routes = (place.sibling(), place.at(x, 1 - y, z), place.at(1 - x, y, z), place.at(x, y, z + 1), place.at(x, y, z - 1))
        self.sends = (None, None, None, z < NZ - 1, z > 0)
        self.gets = (None, None, None, z > 0, z < NZ - 1)

    def copy(self, link):
        source = self.own if link == 0 else self.run.at[link]
        return pltpu.make_async_remote_copy(
            src_ref=source, dst_ref=self.land.at[link], send_sem=self.send_sem.at[link], recv_sem=self.recv_sem.at[link],
            device_id=self.routes[link], device_id_type=MESH)

    def step(self, index):
        def chain(link, base):
            self.run[link] = base[...]

            def get():
                self.copy(link).wait_recv()
                self.run[link] += self.land[link]
            pl.when(self.gets[link])(get)
            pl.when(self.sends[link])(lambda: self.copy(link).start())

        def swap(link):
            if link:
                self.copy(link - 1).wait_recv()
                self.run[link] = (self.own[...] if link == 1 else self.run[link - 1]) + self.land[link - 1]
            if link < 3:
                self.copy(link).start()

        for link in range(3):
            pl.when(index == link)(functools.partial(swap, link))

        @pl.when(index == 3)
        def _():
            self.copy(2).wait_recv()
            self.out[...] = self.run[2] + self.land[2]
            chain(3, self.out)
            chain(4, self.out)
            self.out[...] = self.run[3]

            def add():
                self.out[...] += self.land[4]
            pl.when(self.gets[4])(add)

    def drain(self):
        for link, sent in enumerate(self.sends):
            if sent is None:
                self.copy(link).wait_send()
            else:
                pl.when(sent)(lambda: self.copy(link).wait_send())


def scatter_kernel(terms, gains, grad, result, out_gains, grad_land, held, core_land, land, rest_land, run, small_land, send_sem, recv_sem,
                   grad_sem, *sems):
    place = Place()
    greet(place)
    grad_copy = pltpu.make_async_remote_copy(
        src_ref=grad, dst_ref=grad_land, send_sem=grad_sem.at[0], recv_sem=grad_sem.at[1],
        device_id=place.at(1 - place.x, place.y, place.z), device_id_type=MESH)
    total = Total(place, gains, out_gains, run, small_land, send_sem, recv_sem)
    scatter = Scatter(place, 0, terms, lambda number: held.at[number], lambda number: core_land.at[number],
                      lambda colour, slot: land.at[colour * 20 + slot], lambda slot: rest_land.at[slot], sems[:7])
    scatter.begin()

    def also(index):
        pl.when(index % 4 == 0)(lambda: total.step(index // 4))
        pl.when((index == INNER_GRAD) & (place.x == 1))(lambda: grad_copy.start())
    scatter.run(INNER_ORDER, 0, len(INNER_ORDER), also)
    scatter.finish(result, sems[7])
    total.drain()
    pl.when(place.x == 1)(lambda: grad_copy.wait_send())
    pl.when(place.x == 0)(lambda: grad_copy.wait_recv())


def scatter_terms(terms, gains, grad):
    any_space, vmem, dma = pl.BlockSpec(memory_space=pl.ANY), pl.BlockSpec(memory_space=pltpu.VMEM), pltpu.SemaphoreType.DMA
    low = lambda *dims: pltpu.VMEM(dims, jnp.bfloat16)
    return pl.pallas_call(
        scatter_kernel,
        out_shape=(jax.ShapeDtypeStruct(BLOCK[0], jnp.bfloat16), jax.ShapeDtypeStruct(BLOCK[2], jnp.float32),
                   jax.ShapeDtypeStruct(grad.shape, grad.dtype)),
        in_specs=[any_space, vmem, any_space], out_specs=(any_space, vmem, any_space),
        scratch_shapes=[
            low(16, *BLOCK[0]), low(16, *BLOCK[0]), low(40, *part_shape(SCATTER_CUTS, 0, 0)), low(35, *part_shape(SCATTER_CUTS, 0, None)),
            *[pltpu.VMEM((5,) + BLOCK[2], jnp.float32)] * 2, dma((5,)), dma((5,)), dma((2,)), *scatter_sems()],
        compiler_params=pltpu.CompilerParams(collective_id=1, has_side_effects=True, vmem_limit_bytes=48 * 2**20),
        name="scatter_terms",
    )(terms, gains, grad)


SLOTS, D, HD, PAIRS = 512, 768, 64, 6
WIDE_PAIRS = 3
TILES_IN, TILES_OUT = 7, 5
EPSILON = 1e-06
LOG2E = 1.4426950408889634
SCALE = 0.125 * LOG2E
APART = 256.0
F32, BF16 = jnp.float32, jnp.bfloat16
ACROSS, DOWN = ((1,), (1,)), ((0,), (0,))


def dot(a, b, dims=((1,), (0,))):
    return lax.dot_general(a, b, (dims, ((), ())), preferred_element_type=F32)


def split(value):
    high = value.astype(BF16)
    return high, (value - high.astype(F32)).astype(BF16)


def head_means(value, spread, exact=True):
    high, low = split(value)
    means = dot(high, spread)
    return means + dot(low, spread) if exact else means


def gelu_and_slope(x):
    t = 1.0 / (1.0 + (0.3275911 * 0.7071067811865476) * jnp.abs(x))
    bell = jnp.exp2((-0.5 * LOG2E) * (x * x))
    poly = t * (0.127414796 + t * (-0.142248368 + t * (0.7107068705 + t * (-0.7265760135 + t * 0.5307027145))))
    tail = poly * bell
    phi = jnp.where(x >= 0, 1.0 - tail, tail)
    return x * phi, phi + (0.3989422804014327 * x) * bell


def lanes(index, width):
    return pl.ds(index * width if isinstance(index, int) else pl.multiple_of(index * width, width), width)


FIRST_OUT, SECOND_IN, SECOND_OUT, SECOND_BACK, LAST_OUT, LAST_BACK, LAST_HEADS, LAST_PROJECT, STEPS = 7, 12, 19, 24, 31, 36, 40, 43, 46
LAST_TILE = 2


def up_first(index):
    return (index + 3) % TILES_IN


def clip(index, high):
    return jnp.clip(index, 0, high)


def last_back(t):
    return up_first(jnp.where(t < LAST_HEADS, clip(t - LAST_BACK, 3), 4 + clip(t - LAST_PROJECT, 2)))


def in_tile(t):
    layer = ((t >= FIRST_OUT) & (t < LAST_OUT)).astype(jnp.int32)
    forward = jnp.where(t < FIRST_OUT, t, clip(t - SECOND_IN, 6))
    backward = jnp.where(t < LAST_OUT, up_first(clip(t - SECOND_BACK, 6)), last_back(t))
    return layer, jnp.where(t < SECOND_OUT, forward, backward)


def has_tile(t):
    return (t < LAST_HEADS) | (t >= LAST_PROJECT)


def tile_slot(t):
    return (t - (LAST_PROJECT - LAST_HEADS) * (t >= LAST_PROJECT)) % 2


def uses_in(t):
    forward = (t < FIRST_OUT) | ((t >= SECOND_IN) & (t < SECOND_OUT))
    return forward | ((t >= SECOND_BACK) & (t < LAST_OUT)) | ((t >= LAST_BACK) & has_tile(t))


def out_tile(t):
    layer = ((t >= SECOND_IN) & (t < SECOND_BACK)).astype(jnp.int32)
    tile = jnp.where(t < SECOND_IN, clip(t - FIRST_OUT, 4), jnp.where(t < SECOND_BACK, clip(t - SECOND_OUT, 4), clip(t - LAST_OUT, 4)))
    return layer, tile


def in_terms(t):
    late = t >= LAST_BACK
    return 1 - late.astype(jnp.int32), jnp.where(late, last_back(t), up_first(clip(t - SECOND_BACK, 6)))


def gains_of(rows, width, start, count, columns):
    lane, column = lax.broadcasted_iota(jnp.int32, (128, columns), 0), lax.broadcasted_iota(jnp.int32, (128, columns), 1)
    place = column % (count * width)
    picked = dot(rows, jnp.where(lane == start + place % count, 1.0, 0.0).astype(BF16))
    row = lax.broadcasted_iota(jnp.int32, picked.shape, 0)
    owner = (lax.broadcasted_iota(jnp.int32, picked.shape, 1) % (count * width)) // count
    return jnp.sum(jnp.where(row == owner * BLOCK[2][0], picked, 0.0), 0, keepdims=True)


def compute_kernel(trading, counts, *refs):
    if trading:
        own, refs = refs[:3], refs[3:]
    else:
        (full_in, full_out, full_gains), refs, own = refs[:3], refs[3:], None
    (inputs, cotangent, augq_ref, augk_ref, spread_ref, section_out, grad_ref, grad_low, grad_land, totals_ref, terms_in_ref, terms_out), refs = (
        refs[:12], refs[12:])
    (tiles, tile_sem, ln_ref, qg_ref, kg_ref, hidden, saved, scale, slope, combined, dy, dproj, acc, dq, dk, do, dhigh, dlow, terms_tile,
     terms_sem, entry_sem, gain_ref), refs = (refs[:22], refs[22:]) if not trading else (refs[3:25], refs[:3] + refs[25:])
    sems, swap, scatter_refs = None, (), None
    if trading:
        (full_in, full_out, own_out, full_gains), sems, swap, scatter_refs = refs[:4], refs[4:14], refs[14:17], refs[17:]
    normed, q, k, v, rq, rk, linv = [Saved(saved, which) for which in range(7)]
    t = pl.program_id(0)
    layer = in_tile(t)[0]
    project = (t < FIRST_OUT) | ((t >= SECOND_IN) & (t < SECOND_OUT))
    project_back = ((t >= SECOND_BACK) & (t < LAST_OUT)) | ((t >= LAST_BACK) & has_tile(t))
    output = (t >= FIRST_OUT) & (t < SECOND_IN)
    output_both = (t >= SECOND_OUT) & (t < SECOND_BACK)
    back = (t >= LAST_OUT) & (t < LAST_BACK)
    heads_now = (t == SECOND_BACK + 4) | ((t >= LAST_HEADS) & (t < LAST_PROJECT))
    layer = jnp.where(output, 0, layer)
    tile = jnp.where(project | project_back, in_tile(t)[1], out_tile(t)[1])
    section, trade = lax.axis_index("section"), None
    if swap:
        trade = Trade(section, section_out, hidden, dy, grad_land, *swap)
    spread = spread_ref[...]
    weights = Weights(Place() if trading else None, own, (full_in, full_out, full_gains), tiles, tile_sem, sems)
    weights.step(t)
    w_ref = tiles.at[tile_slot(t)]

    def thirds(body):
        for part in range(WIDE_PAIRS):
            body(pl.ds(256 * part, 256))

    def by_rows(body):
        for index in range(SLOTS // 128):
            body(pl.ds(index * 128, 128))

    @pl.when(t == 0)
    def _():
        entries = [pltpu.make_async_copy(inputs.at[section, 0], hidden.at[0], entry_sem.at[0]),
                   pltpu.make_async_copy(cotangent.at[section, 0], dy, entry_sem.at[1])]
        for entry in entries:
            entry.start()
        for entry in entries:
            entry.wait()
        gain_ref[...] = jnp.zeros_like(gain_ref)
        starts = (0, counts[0], counts[0] + counts[1])
        for which in range(2):
            rows = full_gains[which]
            for target, start, count, columns in zip((ln_ref, qg_ref, kg_ref), starts, counts, (D, 256, 256)):
                target[which] = gains_of(rows, D // counts[0], start, count, columns)

    def low_lanes():
        return lax.broadcasted_iota(jnp.int32, (SLOTS, 128), 1) < HD

    def fold_gains():
        for which in range(2):
            parts = [[gain_ref[which, row : row + 1, 128 * part : 128 * (part + 1)] for part in range(PAIRS)] for row in range(3)]
            sums = [functools.reduce(jnp.add, row) for row in parts[1:]]
            sums = [total + pltpu.roll(total, HD, 1) for total in sums]
            for part in range(PAIRS):
                totals_ref[8 * which + part : 8 * which + part + 1, :] = parts[0][part]
            first = lax.broadcasted_iota(jnp.int32, (1, 128), 1) < HD
            totals_ref[8 * which + 6 : 8 * which + 7, :] = jnp.where(first, *sums)
            totals_ref[8 * which + 7 : 8 * which + 8, :] = jnp.zeros((1, 128), F32)

    @pl.when(project & (tile == 0))
    def _():
        def body(rows):
            h = hidden[layer, rows, :].astype(F32)
            centred = h - jnp.mean(h, -1, keepdims=True)
            root = lax.rsqrt(jnp.mean(centred * centred, -1, keepdims=True) + EPSILON)
            scale[layer, rows, :] = jnp.broadcast_to(root, (128, 128))
            normed[layer, rows, :] = (centred * root * ln_ref[layer]).astype(BF16)
        by_rows(body)

    @pl.when(project)
    def _():
        def projected(columns):
            return dot(normed[layer, :, :], w_ref[:, columns])

        def heads(low_ref, root_ref, gain, factor):
            @thirds
            def _(columns):
                x = projected(columns)
                centred = x - head_means(x, spread)
                root = lax.rsqrt(head_means(centred * centred, spread, False) + EPSILON)
                root_ref[layer, :, columns] = root.astype(BF16)
                low_ref[layer, :, columns] = (centred * root * (gain * factor)).astype(BF16)

        pl.when(tile == 0)(lambda: heads(q, rq, qg_ref[layer], SCALE))
        pl.when(tile == 1)(lambda: heads(k, rk, kg_ref[layer], 1.0))

        @pl.when(tile == 2)
        def _():
            v[layer, :, :] = projected(slice(None)).astype(BF16)
            low = low_lanes()
            augq, augk = augq_ref[...], augk_ref[...]
            ones = jnp.ones((SLOTS, 128), BF16)

            def pair(index):
                part = lanes(index, 128)
                qp, kp, vp = q[layer, :, part], k[layer, :, part], v[layer, :, part]
                results = []
                for head in (0, 1):
                    mine = low if head == 0 else ~low
                    scores = dot(jnp.where(mine, qp, augq), jnp.where(mine, kp, augk), ACROSS)
                    results.append(dot(jnp.exp2(scores).astype(BF16), jnp.where(mine, vp, ones)))
                inverse = 1.0 / pltpu.roll(jnp.where(low, results[1], results[0]), HD, 1)
                linv[layer, :, part] = inverse.astype(BF16)
                combined[layer, 0, :, part] = (jnp.where(low, results[0], results[1]) * inverse).astype(BF16)
            for index in range(PAIRS):
                pair(index)

        @pl.when(tile > 2)
        def _():
            @thirds
            def _(columns):
                value, rise = gelu_and_slope(projected(columns))
                slope[layer, tile - 3, :, columns] = rise.astype(BF16)
                combined[layer, tile - 2, :, columns] = value.astype(BF16)

    @pl.when(output | output_both)
    def _():
        dq[...] = jnp.where(tile == 0, hidden[layer].astype(F32), dq[...]) + dot(combined[layer, tile], w_ref[...])

        @pl.when(tile == TILES_OUT - 1)
        def _():
            result = dq[...].astype(BF16)
            hidden[layer + 1] = result
            if trade:
                trade.give_output(layer)
            else:
                section_out[layer] = result

    @pl.when(output_both | back)
    def _():
        made = jnp.where(t < LAST_OUT, t - SECOND_OUT, TILES_OUT + t - LAST_OUT)
        pl.when(made >= 2)(lambda: terms_copy(terms_out, terms_tile, terms_sem, made % 2, 0, 0).wait())

        def grads(columns):
            return dot(dy[...], w_ref[columns, :], ACROSS)

        def terms():
            terms_tile[made % 2] = dot(combined[layer, tile], dy[...], DOWN).astype(BF16)

        @pl.when(tile == 0)
        def _():
            terms()

            @thirds
            def _(columns):
                grad, inverse = grads(columns), linv[layer, :, columns].astype(F32)
                do[:, columns] = (grad * inverse).astype(BF16)
                total = head_means(grad * combined[layer, 0, :, columns].astype(F32), spread) * (inverse * -HD)
                for half in (0, 128):
                    part = pl.ds(columns.start + half, 128)
                    high, low = split(pltpu.roll(total[:, half : half + 128], HD, 1))
                    dhigh[:, part] = high
                    dlow[:, part] = low

        @pl.when(tile > 0)
        def _():
            terms()

            @thirds
            def _(columns):
                dproj[tile + 2, :, columns] = (grads(columns) * slope[layer, tile - 1, :, columns].astype(F32)).astype(BF16)

        terms_copy(terms_out, terms_tile, terms_sem, made % 2, layer, tile).start()
        if not trading:
            pl.when(t == LAST_BACK - 1)(lambda: terms_settled(terms_out, terms_tile, terms_sem))

    @pl.when(heads_now)
    def _():
        low = low_lanes()
        spot = lax.broadcasted_iota(jnp.int32, (SLOTS, 128), 1) % HD
        first = spot == 0
        augv = jnp.where(spot < 2, 1.0, 0.0).astype(BF16)
        augq, augk = augq_ref[...], augk_ref[...]
        none = jnp.zeros((SLOTS, 128), BF16)

        def pair(index):
            part = lanes(index, 128)
            qp, kp, vp, dop = q[layer, :, part], k[layer, :, part], v[layer, :, part], do[:, part]
            augd = jnp.where(first, dhigh[:, part], dlow[:, part])
            sums = [None, None, None]
            for head in (0, 1):
                mine = low if head == 0 else ~low
                e = jnp.exp2(dot(jnp.where(mine, kp, augk), jnp.where(mine, qp, augq), ACROSS))
                dp = dot(jnp.where(mine, vp, augv), jnp.where(mine, dop, augd), ACROSS)
                ds = (e * dp).astype(BF16)
                parts = (dot(ds, jnp.where(mine, kp, none), DOWN), dot(ds, jnp.where(mine, qp, none)),
                         dot(e.astype(BF16), jnp.where(mine, dop, none)))
                sums = [part_sum if total is None else total + part_sum for total, part_sum in zip(sums, parts)]
            dq[:, part] = sums[0] * 0.125
            dk[:, part] = sums[1] * (1.0 / LOG2E)
            dproj[2, :, part] = sums[2].astype(BF16)
        late = t >= LAST_HEADS
        first_pair = jnp.where(late, 2 * (t - LAST_HEADS), 0)

        def two_pairs(index):
            pair(first_pair + 2 * index)
            pair(first_pair + 2 * index + 1)
        loop(jnp.where(late, 1, PAIRS // 2), two_pairs)

    @pl.when(project_back & (tile == 0))
    def _():
        for which, grads, low_ref, root_ref, gain, factor in ((0, dq, q, rq, qg_ref, SCALE), (1, dk, k, rk, kg_ref, 1.0)):
            @thirds
            def _(columns):
                grad, gains = grads[:, columns], gain[layer]
                xhat = low_ref[layer, :, columns].astype(F32) * (1.0 / (gains * factor))
                scaled = grad * gains
                mean = head_means(scaled, spread, False)
                along = head_means(scaled * xhat, spread, False)
                dproj[which, :, columns] = (root_ref[layer, :, columns].astype(F32) * (scaled - mean - xhat * along)).astype(BF16)
                gain_ref[layer, which + 1 : which + 2, columns] += jnp.sum(grad * xhat, 0, keepdims=True)

    @pl.when(project_back)
    def _():
        acc[...] = jnp.where(tile == up_first(0), 0.0, acc[...]) + dot(dproj[tile], w_ref[...], ACROSS)
        terms_in_ref[...] = dot(normed[layer, :, :], dproj[tile], DOWN).astype(BF16)

        @pl.when(tile == LAST_TILE)
        def _():
            gains = ln_ref[layer]

            def body(rows):
                grad = acc[rows, :]
                xhat = normed[layer, rows, :].astype(F32) * (1.0 / gains)
                scaled = grad * gains
                mean = jnp.mean(scaled, -1, keepdims=True)
                along = jnp.mean(scaled * xhat, -1, keepdims=True)
                total = dy[rows, :].astype(F32) + scale[layer, rows, :1] * (scaled - mean - xhat * along)
                low = total.astype(BF16)
                if trade:
                    pl.when(layer == section)(lambda: grad_ref.__setitem__((rows, slice(None)), total))
                else:
                    grad_ref[layer, rows, :] = total
                pl.when(layer == 1)(lambda: dy.__setitem__((rows, slice(None)), low))
                pl.when(layer == 0)(lambda: grad_low.__setitem__((rows, slice(None)), low))
                gain_ref[layer, 0:1, :] += jnp.sum(grad * xhat, 0, keepdims=True)
            by_rows(body)
            if trade:
                pl.when(layer == 1)(trade.give_grad)
                pl.when(layer == 0)(trade.finish)
            pl.when(layer == 0)(fold_gains)

    if trading:
        pl.when(t >= LAST_BACK - 1)(
            lambda: outer_scatter(t, terms_out, terms_tile, terms_sem, own_out, combined, slope, saved, *scatter_refs))


class Saved:
    def __init__(self, ref, which):
        self.ref, self.which = ref, which

    def __getitem__(self, index):
        return self.ref[(index[0], self.which) + index[1:]]

    def __setitem__(self, index, value):
        self.ref[(index[0], self.which) + index[1:]] = value


def terms_copy(terms_out, terms_tile, terms_sem, slot, layer, tile):
    target = terms_out.at[layer, pl.ds(pl.multiple_of(tile * D, D), D), :]
    return pltpu.make_async_copy(terms_tile.at[slot], target, terms_sem.at[slot])


def terms_settled(terms_out, terms_tile, terms_sem):
    for slot in range(2):
        terms_copy(terms_out, terms_tile, terms_sem, slot, 0, 0).wait()


def outer_scatter(t, terms_out, terms_tile, terms_sem, own_out, combined, slope, saved, rest_land, ready_sem, *sems):
    place = Place()
    rows = BLOCK[1][0]

    def half(number):
        return pl.ds(pl.multiple_of((number % 2) * rows, 16), rows)

    def held(number):
        return combined.at[number // 10, (number // 2) % 5, half(number)]

    def core_land(number):
        return slope.at[number // 8, (number // 2) % 4, half(number)]

    def land(colour, slot):
        piece = colour * 20 + slot
        return saved.at[1, piece // 5, pl.ds(pl.multiple_of((piece % 5) * 96, 16), 96)]

    scatter = Scatter(place, 1, terms_out, held, core_land, land, lambda slot: rest_land.at[slot], sems[:7])

    @pl.when(t == LAST_BACK - 1)
    def _():
        terms_settled(terms_out, terms_tile, terms_sem)
        greet(place, ready_sem)
        scatter.begin()

    first, count = 0, 0
    for slot, steps in enumerate(OUTER_ORDER):
        here = (t == LAST_BACK - 1 + slot).astype(jnp.int32)
        first += here * sum(map(len, OUTER_ORDER[:slot]))
        count += here * len(steps)
    scatter.run([step for steps in OUTER_ORDER for step in steps], first, count)
    pl.when(t == STEPS - 1)(lambda: scatter.finish(own_out, sems[7]))


class Trade:
    def __init__(self, section, section_out, hidden, dy, grad_land, own_sem, send_sem, recv_sem):
        self.section, self.section_out, self.hidden, self.dy, self.grad_land = section, section_out, hidden, dy, grad_land
        self.own_sem, self.send_sem, self.recv_sem = own_sem, send_sem, recv_sem
        self.pair = (1 - section, lax.axis_index("wide"))

    def kept(self):
        return pltpu.make_async_copy(self.hidden.at[self.section + 1], self.section_out.at[self.section], self.own_sem)

    def copy(self, source, target, index):
        return pltpu.make_async_remote_copy(
            src_ref=source, dst_ref=target, send_sem=self.send_sem.at[index], recv_sem=self.recv_sem.at[index],
            device_id=self.pair, device_id_type=MESH)

    def given(self):
        return self.copy(self.hidden.at[2 - self.section], self.section_out.at[self.section], 0)

    def grad(self):
        return self.copy(self.dy, self.grad_land, 1)

    def give_output(self, layer):
        pl.when(layer == self.section)(lambda: self.kept().start())
        pl.when(layer != self.section)(lambda: self.given().start())

    def give_grad(self):
        pl.when(self.section == 0)(lambda: self.grad().start())

    def finish(self):
        self.kept().wait()
        self.given().wait_send()
        self.copy(self.hidden.at[2 - self.section], self.section_out.at[1 - self.section], 0).wait_recv()
        pl.when(self.section == 0)(lambda: self.grad().wait_send())
        pl.when(self.section == 1)(lambda: self.grad().wait_recv())


def both_layers(trading, counts, weights, gains, inputs, cotangent, augq, augk, spread):
    square = (SLOTS, D)

    def whole(*dims):
        return pl.BlockSpec(dims, lambda t: (0,) * len(dims))

    low, wide = (lambda *dims: pltpu.VMEM(dims, BF16)), (lambda *dims: pltpu.VMEM(dims, F32))
    any_space, dma = pl.BlockSpec(memory_space=pl.ANY), pltpu.SemaphoreType.DMA
    full = [jax.ShapeDtypeStruct(dims, BF16) for dims in ((2, D, TILES_IN * D), (2, TILES_OUT * D, D))]
    if trading:
        in_specs, operands = [any_space] * 3, (*weights, gains)
        out_specs, more_specs = [any_space, whole(*square), whole(*square), any_space], [any_space] * 3
        sems = [dma((5, 3, 16)), dma((3, 16)), dma((3, 16))] * 3 + [dma((3,))]
        extra = [low(2, 16 * BLOCK[2][0], 128)] + sems + [dma(()), dma((2,)), dma((2,))]
        extra += [low(35, *part_shape(SCATTER_CUTS, 1, None)), pltpu.SemaphoreType.REGULAR] + scatter_sems()
        grad_shape, more = square, full + [jax.ShapeDtypeStruct(BLOCK[1], BF16)]
        params = dict(collective_id=2, has_side_effects=True)
    else:
        in_specs, operands = [any_space] * 2 + [whole(*gains.shape)], (*weights, gains)
        out_specs, more_specs = [whole(2, *square), whole(2, *square), whole(*square), whole(*square)], []
        grad_shape, extra, more, params = (2,) + square, [], [], {}
    return pl.pallas_call(
        functools.partial(compute_kernel, trading, counts),
        grid=(STEPS,),
        in_specs=in_specs + [any_space, any_space, whole(SLOTS, 128), whole(SLOTS, 128), whole(256, 256)],
        out_specs=out_specs + [
            whole(16, 128), pl.BlockSpec((None, D, D), lambda t: (in_terms(t)[0], 0, in_terms(t)[1])), any_space,
        ] + more_specs,
        scratch_shapes=[
            low(2, D, D), dma((2,)), wide(2, 1, D), wide(2, 1, 256), wide(2, 1, 256),
            low(3, *square), low(2, 8, *square), wide(2, SLOTS, 128), low(2, 4, *square), low(2, 5, *square), low(*square), low(7, *square),
            wide(*square), wide(*square), wide(*square), low(*square), low(*square), low(*square), low(2, D, D), dma((2,)), dma((2,)),
            wide(2, 8, D),
        ] + extra,
        out_shape=[
            jax.ShapeDtypeStruct((2,) + square, BF16), jax.ShapeDtypeStruct(grad_shape, F32), jax.ShapeDtypeStruct(square, BF16),
            jax.ShapeDtypeStruct(square, BF16), jax.ShapeDtypeStruct((16, 128), F32), *full,
        ] + more,
        compiler_params=pltpu.CompilerParams(vmem_limit_bytes=63 * 2**20, **params),
        name="both_layers",
    )(*operands, inputs, cotangent, augq, augk, spread)


def augment(image_id, token_size):
    lane = jnp.arange(128)[None, :] % HD
    size = jnp.log2(token_size.astype(F32))[:, None]
    high = size.astype(BF16).astype(F32)
    same = image_id[:, None] == lane - 2
    q = jnp.where((lane < 2) | (lane == 5) | same, 1.0, 0.0)
    k = jnp.where(lane == 0, high, jnp.where(lane == 1, size - high, jnp.where(lane == 5, -APART, jnp.where(same, APART, 0.0))))
    return q.astype(BF16), k.astype(BF16)


def spread_matrix():
    head = jnp.arange(256) // HD
    return ((head[:, None] == head[None, :]) / HD).astype(BF16)


def gather_all(piece, axis):
    return lax.all_gather(lax.all_gather(piece, "wide", axis=axis, tiled=True), "section", axis=0, tiled=True)


def scatter_all(terms, axis):
    own = lax.psum_scatter(terms, "section", scatter_dimension=0, tiled=True)
    return lax.psum_scatter(own, "wide", scatter_dimension=axis, tiled=True)


def on_device(inputs, cotangent, token_size, image_id, w_in, w_out, ln_gain, q_gain, k_gain):
    section, wide = lax.axis_index("section"), lax.axis_index("wide")
    width = lax.axis_size("wide")
    blocks_fit = width == 16 and w_in.shape[1:] == BLOCK[0] and w_out.shape[1:] == BLOCK[1]
    ends = [0]
    for gain in (ln_gain, q_gain, k_gain):
        ends.append(ends[-1] + gain.shape[1])
    own_gains = jnp.concatenate([ln_gain, q_gain, k_gain], 1)
    gains = jnp.pad(own_gains, ((0, BLOCK[2][0] - 1), (0, BLOCK[2][1] - ends[3])))
    weights = (w_in[0], w_out[0])
    if not blocks_fit:
        weights = (gather_all(w_in, 1), gather_all(w_out, 1))
        gains = gather_all(gains[None], 1)
    augq, augk = augment(image_id[section, 0], token_size[section, 0])
    outs, grads, grad_low, grad_land, totals, terms_in, terms_out, *more = both_layers(
        blocks_fit, tuple(gain.shape[1] for gain in (ln_gain, q_gain, k_gain)), weights, gains, inputs,
        cotangent, augq, augk, spread_matrix())
    swap = [(0, 1), (1, 0)]

    def both_micro(pair):
        mine = lax.dynamic_index_in_dim(pair, section, 0, False)
        other = lax.dynamic_index_in_dim(pair, 1 - section, 0, False).astype(BF16)
        other = lax.ppermute(other, "section", swap).astype(mine.dtype)
        return jnp.where(section == 0, jnp.stack([mine, other]), jnp.stack([other, mine]))[None, :, None]

    places = (0, D, D + HD, D + 2 * HD)
    if blocks_fit:
        own_in, totals, last_land = scatter_terms(terms_in, totals, grad_low)
        other = jnp.where(section == 0, last_land, grad_land).astype(F32)
        is_own = (jnp.arange(2) == section)[:, None, None]
        grads = jnp.where(is_own, grads[None], other[None])[None, :, None]
        outs = outs[None, :, None]
        own_in, own_out = own_in[None].astype(F32), more[2][None].astype(F32)
    else:
        own_in = scatter_all(terms_in, 1).astype(F32)
        own_out = scatter_all(terms_out, 1).astype(F32)
        totals = lax.psum(totals, ("section", "wide"))
        outs, grads = both_micro(outs), both_micro(grads)
    mine = lax.dynamic_index_in_dim(totals.reshape(2, 1024), section, 0, False)
    gain_grads = [
        lax.dynamic_slice_in_dim(mine[low:high], wide * gain.shape[1], gain.shape[1])[None]
        for low, high, gain in zip(places, places[1:], (ln_gain, q_gain, k_gain))
    ]
    return (outs, grads, own_in, own_out, *gain_grads)


def solution(mesh):
    return jax.shard_map(
        on_device,
        mesh=mesh,
        in_specs=(
            P(None, "wide", None, None),
            P(None, "wide", None, None),
            P(None, "wide", None),
            P(None, "wide", None),
            P("section", "wide", None),
            P("section", "wide", None),
            P("section", "wide"),
            P("section", "wide"),
            P("section", "wide"),
        ),
        out_specs=(
            P("section", None, "wide", None, None),
            P("section", None, "wide", None, None),
            P("section", "wide", None),
            P("section", "wide", None),
            P("section", "wide"),
            P("section", "wide"),
            P("section", "wide"),
        ),
        check_vma=False,
    )
```

```python
import functools

import jax
import jax.numpy as jnp
from jax import lax
from jax.experimental import pallas as pl
from jax.experimental.pallas import tpu as pltpu
from jax.sharding import PartitionSpec as P

MESH = pl.DeviceIdType.MESH
NZ = 4
BLOCK = ((48, 5376), (240, 768), (16, 128))
GATHER_CUTS = (2176, 96)
SCATTER_CUTS = (2048, 96)


class Place:
    def __init__(self):
        self.x, self.wide = lax.axis_index("section"), lax.axis_index("wide")
        self.y, self.z, self.c = (self.wide // 2) % 2, self.wide // 4, self.wide % 2

    def at(self, x, y, z, c=None):
        return (x, z * 4 + y * 2 + (self.c if c is None else c))

    def along(self, colour, block_z, far_first, far_second):
        dx = jnp.where(colour == 0, far_first, far_second)
        dy = jnp.where(colour == 0, far_second, far_first)
        return self.flip(self.x, dx), self.flip(self.y, dy), block_z

    @staticmethod
    def flip(value, far):
        return value + far - 2 * value * far

    def first(self, colour):
        return self.at(*self.along(colour, self.z, 1, 0))

    def second(self, colour):
        return self.at(*self.along(colour, self.z, 0, 1))

    def sibling(self):
        return self.at(self.x, self.y, self.z, 1 - self.c)


def greet(place, barrier=None):
    barrier = pltpu.get_barrier_semaphore() if barrier is None else barrier
    x, y, z = place.x, place.y, place.z

    def signal(device):
        pl.semaphore_signal(barrier, inc=1, device_id=device, device_id_type=MESH)

    signal(place.at(1 - x, y, z))
    signal(place.at(x, 1 - y, z))
    signal(place.sibling())
    pl.when(z < NZ - 1)(lambda: signal(place.at(x, y, z + 1)))
    pl.when(z > 0)(lambda: signal(place.at(x, y, z - 1)))
    pl.semaphore_wait(barrier, 3 + (z < NZ - 1).astype(jnp.int32) + (z > 0).astype(jnp.int32))


def number_of(block):
    return block[0] * 8 + block[1] * 4 + block[2]


def part_shape(cuts, array, colour):
    rows, cols = BLOCK[array]
    size = cuts[array]
    if array == 0:
        return rows, cols - 2 * size if colour is None else size
    return rows - 2 * size if colour is None else size, cols


def cut(ref, cuts, array, colour):
    if array == 2:
        return ref
    rows, cols = part_shape(cuts, array, colour)
    size = cuts[array]
    if array == 0:
        return ref.at[:, pl.ds(2 * size if colour is None else pl.multiple_of(colour * size, 128), cols)]
    return ref.at[pl.ds(2 * size if colour is None else pl.multiple_of(colour * size, 16), rows), :]


def loop(count, body):
    def step(index, carry):
        body(index)
        return carry
    lax.fori_loop(0, count, step, 0)


class Gather:
    def __init__(self, place, array, own, full, send_sem, recv_sem, core_sem):
        self.place, self.array, self.own, self.full = place, array, own, full
        self.send_sem, self.recv_sem, self.core_sem = send_sem, recv_sem, core_sem

    def view(self, block, colour, plane=None):
        rows = BLOCK[self.array][0]
        place = self.place
        start = (block[2] * 4 + block[1] * 2 + (place.c if plane is None else plane)) * rows
        return cut(self.full.at[block[0], pl.ds(pl.multiple_of(start, 16), rows), :], GATHER_CUTS, self.array, colour)

    def copy(self, link, device, block, colour, own=False, other_plane=False):
        kind = 2 if colour is None else colour
        number = number_of(block)
        target = self.view(block, colour, 1 - self.place.c if other_plane else None)
        source = cut(self.own, GATHER_CUTS, self.array, colour) if own else target
        sems = self.core_sem if link == 4 else self.recv_sem
        return pltpu.make_async_remote_copy(
            src_ref=source, dst_ref=target, send_sem=self.send_sem.at[link, kind, number], recv_sem=sems.at[kind, number],
            device_id=device, device_id_type=MESH)

    def visit(self, block, colour, onward, first, second, drain, condition=None, own=False):
        place = self.place

        def body():
            if not drain and not own:
                self.copy(0, place.sibling(), block, colour).wait_recv()

            def send(link, device):
                copy = self.copy(link, device, block, colour, own)
                copy.wait_send() if drain else copy.start()

            for link, step in onward:
                target = place.z + step
                pl.when((target >= 0) & (target < NZ))(functools.partial(send, link, place.at(place.x, place.y, target)))
            if first is not None:
                send(2, first)
            if second is not None:
                if isinstance(second, tuple) and len(second) == 3:
                    pl.when(second[2])(functools.partial(send, 3, second[:2]))
                else:
                    send(3, second)
            send(4, place.sibling())
        if condition is None:
            body()
        else:
            pl.when(condition)(body)

    def begin(self, drain=False):
        place = self.place
        me = (place.x, place.y, place.z)
        everywhere = ((0, 1), (1, -1))
        self.visit(me, None, everywhere, place.at(1 - place.x, place.y, place.z), place.at(place.x, 1 - place.y, place.z), drain, own=True)

        def body(colour):
            self.visit(me, colour, everywhere, place.first(colour), place.second(colour), drain, own=True)
        if self.array < 2:
            loop(2, body)

    def square(self, drain=False):
        place = self.place

        def body(index):
            far_x, far_y = (index != 1).astype(jnp.int32), (index != 0).astype(jnp.int32)
            block = (place.flip(place.x, far_x), place.flip(place.y, far_y), place.z)
            self.visit(block, None, ((0, 1), (1, -1)), None, place.at(place.x, 1 - place.y, place.z) + (index == 0,), drain)
        loop(3, body)

    def sided(self, distance, body):
        place = self.place

        def side_body(side):
            step = 1 - 2 * side
            block_z = place.z - step * distance
            body(side, block_z, (block_z >= 0) & (block_z < NZ) & ((distance > 0) | (side == 0)))
        loop(2, side_body)

    def onward(self, side):
        return ((0, 1), (1, -1))[side]

    def z_step(self, distance, drain=False):
        place = self.place
        for side in (0, 1):
            step = 1 - 2 * side
            block_z = place.z - step * distance

            def body(colour):
                self.visit((place.x, place.y, block_z), colour, ((side, step),), place.first(colour), place.second(colour), drain)
            pl.when((block_z >= 0) & (block_z < NZ))(lambda: loop(2, body))

    def line(self, distance, drain=False):
        place = self.place
        for side in (0, 1):
            step = 1 - 2 * side
            block_z = place.z - step * distance

            def body(index):
                block = (place.flip(place.x, index % 2), place.flip(place.y, index // 2), block_z)
                self.visit(block, None, ((side, step),), None, None, drain)
            pl.when((block_z >= 0) & (block_z < NZ))(lambda: loop(4, body))

    def a_step(self, distance, drain=False):
        place = self.place

        def body(side, block_z, there):
            def inner(colour):
                self.visit(place.along(colour, block_z, 1, 0), colour, (), None, place.second(colour), drain)
            pl.when(there)(lambda: loop(2, inner))
        self.sided(distance, body)

    def b_step(self, distance, drain=False):
        place = self.place

        def body(side, block_z, there):
            def inner(index):
                colour = index // 2
                self.visit(place.along(colour, block_z, index % 2, 1), colour, (), None, None, drain)
            pl.when(there)(lambda: loop(4, inner))
        self.sided(distance, body)

    def from_core(self):
        place = self.place

        def body(number):
            block = (number // 8, (number // 4) % 2, number % 4)
            self.copy(4, place.sibling(), block, None, other_plane=True).wait_recv()
            for colour in (0, 1) if self.array < 2 else ():
                self.copy(4, place.sibling(), block, colour, other_plane=True).wait_recv()
        loop(16, body)

    def drain(self):
        self.begin(True)
        self.square(True)

        def body(index):
            self.line(index + 1, True)
            if self.array < 2:
                self.z_step(index + 1, True)
                self.a_step(index, True)
                self.b_step(index, True)
        loop(NZ, body)


class Weights:
    def __init__(self, place, own, full, tiles, tile_sem, sems):
        self.place, self.full, self.tiles, self.tile_sem = place, full, tiles, tile_sem
        self.copies = []
        if place is None:
            return
        self.inner, self.outer, self.gains = [Gather(place, array, own[array], full[array], *sems[3 * array : 3 * array + 3]) for array in range(3)]
        for array in range(3):
            rows = BLOCK[array][0]
            target = full[array].at[place.x, pl.ds(pl.multiple_of(place.wide * rows, 16), rows), :]
            self.copies.append(pltpu.make_async_copy(own[array], target, sems[9].at[array]))

    def begin(self):
        greet(self.place)
        for copy in self.copies:
            copy.start()
        self.gains.begin()
        self.inner.begin()
        self.gains.square()
        self.inner.square()

        def early(index):
            self.inner.z_step(index + 1)
            self.inner.a_step(index)
            self.gains.line(index + 1)
            self.inner.line(index + 1)
        loop(NZ - 1, early)
        self.outer.begin()
        self.inner.a_step(NZ - 1)
        self.outer.square()

        def late(index):
            self.inner.b_step(index)
            pl.when(index == 1)(lambda: self.onward(0))
        loop(NZ, late)
        self.gains.from_core()
        self.inner.from_core()
        for copy in self.copies:
            copy.wait()

    def onward(self, index):
        self.outer.z_step(index + 1)
        self.outer.a_step(index)
        self.outer.line(index + 1)

    def end(self):
        loop(NZ, self.outer.b_step)
        self.outer.from_core()

    def drain(self):
        for array in (self.gains, self.inner, self.outer):
            array.drain()

    def fetch(self, t):
        slot = tile_slot(t)
        tile, sem = self.tiles.at[slot], self.tile_sem.at[slot]
        project = uses_in(t)

        def inner():
            layer, index = in_tile(t)
            return pltpu.make_async_copy(self.full[0].at[layer, :, pl.ds(pl.multiple_of(index * D, D), D)], tile, sem)

        def outer():
            layer, index = out_tile(t)
            return pltpu.make_async_copy(self.full[1].at[layer, pl.ds(pl.multiple_of(index * D, D), D), :], tile, sem)
        pl.when(project)(lambda: inner().start())
        pl.when(jnp.logical_not(project))(lambda: outer().start())

    def wait(self, t):
        slot = tile_slot(t)
        pltpu.make_async_copy(self.full[0].at[0, :, pl.ds(0, D)], self.tiles.at[slot], self.tile_sem.at[slot]).wait()

    def step(self, t):
        if self.place is not None:
            pl.when(t == 0)(self.begin)
            pl.when((t >= 2) & (t <= NZ))(lambda: self.onward(t - 1))
            pl.when(t == FIRST_OUT)(self.end)
            pl.when(t == LAST_OUT)(self.drain)
            held_back = FIRST_OUT
        else:
            held_back = 0
        following = jnp.where(t == LAST_HEADS - 1, LAST_PROJECT, t + 1)
        pl.when((t == 0) | (t == held_back))(lambda: self.fetch(t))
        pl.when(has_tile(t) & (following < STEPS) & (following != held_back))(lambda: self.fetch(following))
        pl.when(has_tile(t))(lambda: self.wait(t))


def add_into(target, source):
    def body(step):
        part = pl.ds(pl.multiple_of(step * 48, 16), 48)
        target[part, :] = target[part, :] + source[part, :]
    loop(target.shape[0] // 48, body)


OUTER_ORDER = (
    ("k3", "l3"), (), ("a3", "k2"), (), ("l2", "b3", "k1"), ("a2", "z3", "l1"), ("k0", "b2"), ("z2", "a1", "l0"), (),
    ("a0", "b1", "z1", "s", "b0", "z0"))
INNER_ORDER = (
    "k3", "k2", "l3", "k1", "l2", "a3", "k0", "l1", "b3", "a2", "z3", "a1", "l0", "b2", "z2", "b1", "a0", "z1", "s", "b0", "z0")
INNER_GRAD = 14


class Scatter:
    def __init__(self, place, array, terms, held, core_land, land, rest_land, sems):
        self.place, self.array, self.terms, self.held, self.core_land = place, array, terms, held, core_land
        self.land, self.rest_land = land, rest_land
        self.send_sem, self.recv_sem, self.rest_send, self.rest_recv, self.core_send, self.core_recv, self.local_sem = sems

    def part(self, block, colour):
        return cut(self.held(number_of(block)), SCATTER_CUTS, self.array, colour)

    def copy(self, device, block, colour, slot):
        if colour is None:
            target, send_sem, recv_sem = self.rest_land(slot), self.rest_send.at[slot], self.rest_recv.at[slot]
        else:
            target, send_sem, recv_sem = self.land(colour, slot), self.send_sem.at[colour, slot], self.recv_sem.at[colour, slot]
        return pltpu.make_async_remote_copy(
            src_ref=self.part(block, colour), dst_ref=target, send_sem=send_sem, recv_sem=recv_sem, device_id=device,
            device_id_type=MESH)

    def send(self, device, block, colour, slot, drain):
        copy = self.copy(device, block, colour, slot)
        copy.wait_send() if drain else copy.start()

    def arrive(self, block, colour, slot, drain):
        if not drain:
            self.copy(self.place.sibling(), block, colour, slot).wait_recv()
            add_into(self.part(block, colour), self.rest_land(slot) if colour is None else self.land(colour, slot))

    def core_copy(self, block, mine):
        rows = BLOCK[self.array][0]
        place = self.place
        number = number_of(block)
        start = (block[2] * 4 + block[1] * 2 + (place.c if mine else 1 - place.c)) * rows
        source = self.terms.at[block[0], pl.ds(pl.multiple_of(start, 16), rows), :]
        if mine:
            return pltpu.make_async_copy(source, self.held(number), self.local_sem.at[number])
        return pltpu.make_async_remote_copy(
            src_ref=source, dst_ref=self.core_land(number), send_sem=self.core_send.at[number],
            recv_sem=self.core_recv.at[number], device_id=place.sibling(), device_id_type=MESH)

    def sided(self, distance, body):
        place = self.place

        def side_body(side):
            block_z = place.z + (2 * side - 1) * distance
            there = (block_z >= 0) & (block_z < NZ) & (distance < NZ) & (distance >= 0) & ((distance > 0) | (side == 0))
            pl.when(there)(lambda: body(block_z))
        loop(2, side_body)

    def start(self, distance):
        place = self.place

        def body(block_z):
            def inner(index):
                block = (place.flip(place.x, 1 - index % 2), place.flip(place.y, 1 - index // 2), block_z)
                self.core_copy(block, False).start()
                self.core_copy(block, True).start()
            loop(4, inner)
        self.sided(distance, body)

    def k_step(self, distance, drain=False):
        place = self.place

        def body(block_z):
            def inner(index):
                far_x, far_y = 1 - index % 2, 1 - index // 2
                block = (place.flip(place.x, far_x), place.flip(place.y, far_y), block_z)
                if not drain:
                    self.core_copy(block, True).wait()
                    copy = self.core_copy(block, False)
                    copy.wait_recv()
                    add_into(self.held(number_of(block)), self.core_land(number_of(block)))
                    copy.wait_send()

                def out(colour):
                    far_first = jnp.where(colour == 0, far_x, far_y)
                    far_second = jnp.where(colour == 0, far_y, far_x)
                    pl.when(far_second == 1)(lambda: self.send(place.second(colour), block, colour, far_first * 4 + block_z, drain))
                loop(2, out)
            loop(4, inner)
        self.sided(distance, body)

    def a_step(self, distance, drain=False):
        place = self.place

        def body(block_z):
            def inner(index):
                colour, far_first = index % 2, 1 - index // 2
                block = place.along(colour, block_z, far_first, 0)
                self.arrive(block, colour, far_first * 4 + block_z, drain)
                pl.when(far_first == 1)(lambda: self.send(place.first(colour), block, colour, 8 + block_z, drain))
            loop(4, inner)
        self.sided(distance, body)

    def b_step(self, distance):
        place = self.place

        def body(block_z):
            loop(2, lambda colour: self.arrive((place.x, place.y, block_z), colour, 8 + block_z, False))
        self.sided(distance, body)

    def toward(self, distance, body):
        place = self.place
        for side, step in ((0, -1), (1, 1)):
            block_z, behind = place.z + step * distance, place.z - step
            there = (block_z >= 0) & (block_z < NZ) & (distance < NZ) & (distance >= 0)
            pl.when(there)(functools.partial(body, block_z, side, step, (behind >= 0) & (behind < NZ)))

    def z_step(self, distance, drain=False):
        place = self.place

        def body(block_z, side, step, more):
            block = (place.x, place.y, block_z)
            slot = 12 + 4 * side + block_z

            def inner(colour):
                pl.when(more)(lambda: self.arrive(block, colour, slot, drain))
                pl.when(distance > 0)(lambda: self.send(place.at(place.x, place.y, place.z + step), block, colour, slot, drain))
            loop(2, inner)
        self.toward(distance, body)

    def line(self, distance, drain=False):
        place = self.place

        def body(block_z, side, step, more):
            def inner(index):
                block = (place.flip(place.x, 1 - index % 2), place.flip(place.y, 1 - index // 2), block_z)
                slot = 16 * side + number_of(block)
                pl.when(more)(lambda: self.arrive(block, None, slot, drain))
                pl.when(distance > 0)(lambda: self.send(place.at(place.x, place.y, place.z + step), block, None, slot, drain))
            loop(4, inner)
        self.toward(distance, body)

    def square(self, drain=False):
        place = self.place
        over_x, over_y = place.at(1 - place.x, place.y, place.z), place.at(place.x, 1 - place.y, place.z)
        far = (1 - place.x, place.y, place.z)
        self.send(over_y, (1 - place.x, 1 - place.y, place.z), None, 33, drain)
        self.send(over_y, (place.x, 1 - place.y, place.z), None, 32, drain)
        self.arrive(far, None, 33, drain)
        self.send(over_x, far, None, 34, drain)
        self.arrive((place.x, place.y, place.z), None, 32, drain)
        self.arrive((place.x, place.y, place.z), None, 34, drain)

    def drain(self):
        def body(distance):
            self.k_step(distance, True)
            self.a_step(distance, True)
            self.z_step(distance, True)
            self.line(distance, True)
        loop(NZ, body)
        self.square(True)


    STEPS = "klabzs"

    def begin(self):
        loop(NZ, lambda index: self.start(NZ - 1 - index))

    def run(self, order, first, count, also=None):
        codes = [(self.STEPS.index(step[0]), int(step[1:] or 0)) for step in order]

        def body(index):
            index = first + index
            which, distance = [sum((index == place).astype(jnp.int32) * code[part] for place, code in enumerate(codes)) for part in (0, 1)]
            calls = (self.k_step, self.line, self.a_step, self.b_step, self.z_step)
            for code, call in enumerate(calls):
                pl.when(which == code)(lambda: call(distance))
            pl.when(which == len(calls))(self.square)
            if also:
                also(index)
        loop(count, body)

    def finish(self, result, sem):
        copy = pltpu.make_async_copy(self.held(number_of((self.place.x, self.place.y, self.place.z))), result, sem)
        copy.start()
        self.drain()
        copy.wait()


def scatter_sems():
    dma = pltpu.SemaphoreType.DMA
    return [dma((2, 20)), dma((2, 20)), dma((35,)), dma((35,)), dma((16,)), dma((16,)), dma((16,)), dma(())]


class Total:
    def __init__(self, place, own, out, run, land, send_sem, recv_sem):
        self.place, self.own, self.out, self.run, self.land = place, own, out, run, land
        self.send_sem, self.recv_sem = send_sem, recv_sem
        x, y, z = place.x, place.y, place.z
        self.routes = (place.sibling(), place.at(x, 1 - y, z), place.at(1 - x, y, z), place.at(x, y, z + 1), place.at(x, y, z - 1))
        self.sends = (None, None, None, z < NZ - 1, z > 0)
        self.gets = (None, None, None, z > 0, z < NZ - 1)

    def copy(self, link):
        source = self.own if link == 0 else self.run.at[link]
        return pltpu.make_async_remote_copy(
            src_ref=source, dst_ref=self.land.at[link], send_sem=self.send_sem.at[link], recv_sem=self.recv_sem.at[link],
            device_id=self.routes[link], device_id_type=MESH)

    def step(self, index):
        def chain(link, base):
            self.run[link] = base[...]

            def get():
                self.copy(link).wait_recv()
                self.run[link] += self.land[link]
            pl.when(self.gets[link])(get)
            pl.when(self.sends[link])(lambda: self.copy(link).start())

        def swap(link):
            if link:
                self.copy(link - 1).wait_recv()
                self.run[link] = (self.own[...] if link == 1 else self.run[link - 1]) + self.land[link - 1]
            if link < 3:
                self.copy(link).start()

        for link in range(3):
            pl.when(index == link)(functools.partial(swap, link))

        @pl.when(index == 3)
        def _():
            self.copy(2).wait_recv()
            self.out[...] = self.run[2] + self.land[2]
            chain(3, self.out)
            chain(4, self.out)
            self.out[...] = self.run[3]

            def add():
                self.out[...] += self.land[4]
            pl.when(self.gets[4])(add)

    def drain(self):
        for link, sent in enumerate(self.sends):
            if sent is None:
                self.copy(link).wait_send()
            else:
                pl.when(sent)(lambda: self.copy(link).wait_send())


def scatter_kernel(terms, gains, grad, result, out_gains, grad_land, held, core_land, land, rest_land, run, small_land, send_sem, recv_sem,
                   grad_sem, *sems):
    place = Place()
    greet(place)
    grad_copy = pltpu.make_async_remote_copy(
        src_ref=grad, dst_ref=grad_land, send_sem=grad_sem.at[0], recv_sem=grad_sem.at[1],
        device_id=place.at(1 - place.x, place.y, place.z), device_id_type=MESH)
    total = Total(place, gains, out_gains, run, small_land, send_sem, recv_sem)
    scatter = Scatter(place, 0, terms, lambda number: held.at[number], lambda number: core_land.at[number],
                      lambda colour, slot: land.at[colour * 20 + slot], lambda slot: rest_land.at[slot], sems[:7])
    scatter.begin()

    def also(index):
        pl.when(index % 4 == 0)(lambda: total.step(index // 4))
        pl.when((index == INNER_GRAD) & (place.x == 1))(lambda: grad_copy.start())
    scatter.run(INNER_ORDER, 0, len(INNER_ORDER), also)
    scatter.finish(result, sems[7])
    total.drain()
    pl.when(place.x == 1)(lambda: grad_copy.wait_send())
    pl.when(place.x == 0)(lambda: grad_copy.wait_recv())


def scatter_terms(terms, gains, grad):
    any_space, vmem, dma = pl.BlockSpec(memory_space=pl.ANY), pl.BlockSpec(memory_space=pltpu.VMEM), pltpu.SemaphoreType.DMA
    low = lambda *dims: pltpu.VMEM(dims, jnp.bfloat16)
    return pl.pallas_call(
        scatter_kernel,
        out_shape=(jax.ShapeDtypeStruct(BLOCK[0], jnp.bfloat16), jax.ShapeDtypeStruct(BLOCK[2], jnp.float32),
                   jax.ShapeDtypeStruct(grad.shape, grad.dtype)),
        in_specs=[any_space, vmem, any_space], out_specs=(any_space, vmem, any_space),
        scratch_shapes=[
            low(16, *BLOCK[0]), low(16, *BLOCK[0]), low(40, *part_shape(SCATTER_CUTS, 0, 0)), low(35, *part_shape(SCATTER_CUTS, 0, None)),
            *[pltpu.VMEM((5,) + BLOCK[2], jnp.float32)] * 2, dma((5,)), dma((5,)), dma((2,)), *scatter_sems()],
        compiler_params=pltpu.CompilerParams(collective_id=1, has_side_effects=True, vmem_limit_bytes=48 * 2**20),
        name="scatter_terms",
    )(terms, gains, grad)


SLOTS, D, HD, PAIRS = 512, 768, 64, 6
WIDE_PAIRS = 3
TILES_IN, TILES_OUT = 7, 5
EPSILON = 1e-06
LOG2E = 1.4426950408889634
SCALE = 0.125 * LOG2E
APART = 256.0
F32, BF16 = jnp.float32, jnp.bfloat16
ACROSS, DOWN = ((1,), (1,)), ((0,), (0,))


def dot(a, b, dims=((1,), (0,))):
    return lax.dot_general(a, b, (dims, ((), ())), preferred_element_type=F32)


def split(value):
    high = value.astype(BF16)
    return high, (value - high.astype(F32)).astype(BF16)


def head_means(value, spread, exact=True):
    high, low = split(value)
    means = dot(high, spread)
    return means + dot(low, spread) if exact else means


def gelu_and_slope(x):
    t = 1.0 / (1.0 + (0.3275911 * 0.7071067811865476) * jnp.abs(x))
    bell = jnp.exp2((-0.5 * LOG2E) * (x * x))
    poly = t * (0.127414796 + t * (-0.142248368 + t * (0.7107068705 + t * (-0.7265760135 + t * 0.5307027145))))
    tail = poly * bell
    phi = jnp.where(x >= 0, 1.0 - tail, tail)
    return x * phi, phi + (0.3989422804014327 * x) * bell


def lanes(index, width):
    return pl.ds(index * width if isinstance(index, int) else pl.multiple_of(index * width, width), width)


FIRST_OUT, SECOND_IN, SECOND_OUT, SECOND_BACK, LAST_OUT, LAST_BACK, LAST_HEADS, LAST_PROJECT, STEPS = 7, 12, 19, 24, 31, 36, 40, 42, 45
LAST_TILE = 2


def up_first(index):
    return (index + 3) % TILES_IN


def clip(index, high):
    return jnp.clip(index, 0, high)


def last_back(t):
    return up_first(jnp.where(t < LAST_HEADS, clip(t - LAST_BACK, 3), 4 + clip(t - LAST_PROJECT, 2)))


def in_tile(t):
    layer = ((t >= FIRST_OUT) & (t < LAST_OUT)).astype(jnp.int32)
    forward = jnp.where(t < FIRST_OUT, t, clip(t - SECOND_IN, 6))
    backward = jnp.where(t < LAST_OUT, up_first(clip(t - SECOND_BACK, 6)), last_back(t))
    return layer, jnp.where(t < SECOND_OUT, forward, backward)


def has_tile(t):
    return (t < LAST_HEADS) | (t >= LAST_PROJECT)


def tile_slot(t):
    return (t - (LAST_PROJECT - LAST_HEADS) * (t >= LAST_PROJECT)) % 2


def uses_in(t):
    forward = (t < FIRST_OUT) | ((t >= SECOND_IN) & (t < SECOND_OUT))
    return forward | ((t >= SECOND_BACK) & (t < LAST_OUT)) | ((t >= LAST_BACK) & has_tile(t))


def out_tile(t):
    layer = ((t >= SECOND_IN) & (t < SECOND_BACK)).astype(jnp.int32)
    tile = jnp.where(t < SECOND_IN, clip(t - FIRST_OUT, 4), jnp.where(t < SECOND_BACK, clip(t - SECOND_OUT, 4), clip(t - LAST_OUT, 4)))
    return layer, tile


def in_terms(t):
    late = t >= LAST_BACK
    return 1 - late.astype(jnp.int32), jnp.where(late, last_back(t), up_first(clip(t - SECOND_BACK, 6)))


def gains_of(rows, width, start, count, columns):
    lane, column = lax.broadcasted_iota(jnp.int32, (128, columns), 0), lax.broadcasted_iota(jnp.int32, (128, columns), 1)
    place = column % (count * width)
    picked = dot(rows, jnp.where(lane == start + place % count, 1.0, 0.0).astype(BF16))
    row = lax.broadcasted_iota(jnp.int32, picked.shape, 0)
    owner = (lax.broadcasted_iota(jnp.int32, picked.shape, 1) % (count * width)) // count
    return jnp.sum(jnp.where(row == owner * BLOCK[2][0], picked, 0.0), 0, keepdims=True)


def compute_kernel(trading, counts, *refs):
    if trading:
        own, refs = refs[:3], refs[3:]
    else:
        (full_in, full_out, full_gains), refs, own = refs[:3], refs[3:], None
    (inputs, cotangent, augq_ref, augk_ref, spread_ref, section_out, grad_ref, grad_low, grad_land, totals_ref, terms_in_ref, terms_out), refs = (
        refs[:12], refs[12:])
    (tiles, tile_sem, ln_ref, qg_ref, kg_ref, hidden, saved, scale, slope, combined, dy, dproj, acc, dq, dk, do, dhigh, dlow, terms_tile,
     terms_sem, entry_sem, gain_ref), refs = (refs[:22], refs[22:]) if not trading else (refs[3:25], refs[:3] + refs[25:])
    sems, swap, scatter_refs = None, (), None
    if trading:
        (full_in, full_out, own_out, full_gains), sems, swap, scatter_refs = refs[:4], refs[4:14], refs[14:17], refs[17:]
    normed, q, k, v, rq, rk, linv = [Saved(saved, which) for which in range(7)]
    t = pl.program_id(0)
    layer = in_tile(t)[0]
    project = (t < FIRST_OUT) | ((t >= SECOND_IN) & (t < SECOND_OUT))
    project_back = ((t >= SECOND_BACK) & (t < LAST_OUT)) | ((t >= LAST_BACK) & has_tile(t))
    output = (t >= FIRST_OUT) & (t < SECOND_IN)
    output_both = (t >= SECOND_OUT) & (t < SECOND_BACK)
    back = (t >= LAST_OUT) & (t < LAST_BACK)
    heads_now = (t == SECOND_BACK + 4) | ((t >= LAST_HEADS) & (t < LAST_PROJECT))
    layer = jnp.where(output, 0, layer)
    tile = jnp.where(project | project_back, in_tile(t)[1], out_tile(t)[1])
    section, trade = lax.axis_index("section"), None
    if swap:
        trade = Trade(section, section_out, hidden, dy, grad_land, *swap)
    spread = spread_ref[...]
    weights = Weights(Place() if trading else None, own, (full_in, full_out, full_gains), tiles, tile_sem, sems)
    weights.step(t)
    w_ref = tiles.at[tile_slot(t)]

    def thirds(body):
        for part in range(WIDE_PAIRS):
            body(pl.ds(256 * part, 256))

    def by_rows(body):
        for index in range(SLOTS // 128):
            body(pl.ds(index * 128, 128))

    @pl.when(t == 0)
    def _():
        entries = [pltpu.make_async_copy(inputs.at[section, 0], hidden.at[0], entry_sem.at[0]),
                   pltpu.make_async_copy(cotangent.at[section, 0], dy, entry_sem.at[1])]
        for entry in entries:
            entry.start()
        for entry in entries:
            entry.wait()
        gain_ref[...] = jnp.zeros_like(gain_ref)
        starts = (0, counts[0], counts[0] + counts[1])
        for which in range(2):
            rows = full_gains[which]
            for target, start, count, columns in zip((ln_ref, qg_ref, kg_ref), starts, counts, (D, 256, 256)):
                target[which] = gains_of(rows, D // counts[0], start, count, columns)

    def low_lanes():
        return lax.broadcasted_iota(jnp.int32, (SLOTS, 128), 1) < HD

    def fold_gains():
        for which in range(2):
            parts = [[gain_ref[which, row : row + 1, 128 * part : 128 * (part + 1)] for part in range(PAIRS)] for row in range(3)]
            sums = [functools.reduce(jnp.add, row) for row in parts[1:]]
            sums = [total + pltpu.roll(total, HD, 1) for total in sums]
            for part in range(PAIRS):
                totals_ref[8 * which + part : 8 * which + part + 1, :] = parts[0][part]
            first = lax.broadcasted_iota(jnp.int32, (1, 128), 1) < HD
            totals_ref[8 * which + 6 : 8 * which + 7, :] = jnp.where(first, *sums)
            totals_ref[8 * which + 7 : 8 * which + 8, :] = jnp.zeros((1, 128), F32)

    @pl.when(project & (tile == 0))
    def _():
        def body(rows):
            h = hidden[layer, rows, :].astype(F32)
            centred = h - jnp.mean(h, -1, keepdims=True)
            root = lax.rsqrt(jnp.mean(centred * centred, -1, keepdims=True) + EPSILON)
            scale[layer, rows, :] = jnp.broadcast_to(root, (128, 128))
            normed[layer, rows, :] = (centred * root * ln_ref[layer]).astype(BF16)
        by_rows(body)

    @pl.when(project)
    def _():
        def projected(columns):
            return dot(normed[layer, :, :], w_ref[:, columns])

        def heads(low_ref, root_ref, gain, factor):
            @thirds
            def _(columns):
                x = projected(columns)
                centred = x - head_means(x, spread)
                root = lax.rsqrt(head_means(centred * centred, spread, False) + EPSILON)
                root_ref[layer, :, columns] = root.astype(BF16)
                low_ref[layer, :, columns] = (centred * root * (gain * factor)).astype(BF16)

        pl.when(tile == 0)(lambda: heads(q, rq, qg_ref[layer], SCALE))
        pl.when(tile == 1)(lambda: heads(k, rk, kg_ref[layer], 1.0))

        @pl.when(tile == 2)
        def _():
            v[layer, :, :] = projected(slice(None)).astype(BF16)
            low = low_lanes()
            augq, augk = augq_ref[...], augk_ref[...]
            ones = jnp.ones((SLOTS, 128), BF16)

            def pair(index):
                part = lanes(index, 128)
                qp, kp, vp = q[layer, :, part], k[layer, :, part], v[layer, :, part]
                results = []
                for head in (0, 1):
                    mine = low if head == 0 else ~low
                    scores = dot(jnp.where(mine, qp, augq), jnp.where(mine, kp, augk), ACROSS)
                    results.append(dot(jnp.exp2(scores).astype(BF16), jnp.where(mine, vp, ones)))
                inverse = 1.0 / pltpu.roll(jnp.where(low, results[1], results[0]), HD, 1)
                linv[layer, :, part] = inverse.astype(BF16)
                combined[layer, 0, :, part] = (jnp.where(low, results[0], results[1]) * inverse).astype(BF16)
            for index in range(PAIRS):
                pair(index)

        @pl.when(tile > 2)
        def _():
            @thirds
            def _(columns):
                value, rise = gelu_and_slope(projected(columns))
                slope[layer, tile - 3, :, columns] = rise.astype(BF16)
                combined[layer, tile - 2, :, columns] = value.astype(BF16)

    @pl.when(output | output_both)
    def _():
        dq[...] = jnp.where(tile == 0, hidden[layer].astype(F32), dq[...]) + dot(combined[layer, tile], w_ref[...])

        @pl.when(tile == TILES_OUT - 1)
        def _():
            result = dq[...].astype(BF16)
            hidden[layer + 1] = result
            if trade:
                trade.give_output(layer)
            else:
                section_out[layer] = result

    @pl.when(output_both | back)
    def _():
        made = jnp.where(t < LAST_OUT, t - SECOND_OUT, TILES_OUT + t - LAST_OUT)
        pl.when(made >= 2)(lambda: terms_copy(terms_out, terms_tile, terms_sem, made % 2, 0, 0).wait())

        def grads(columns):
            return dot(dy[...], w_ref[columns, :], ACROSS)

        def terms():
            terms_tile[made % 2] = dot(combined[layer, tile], dy[...], DOWN).astype(BF16)

        @pl.when(tile == 0)
        def _():
            terms()

            @thirds
            def _(columns):
                grad, inverse = grads(columns), linv[layer, :, columns].astype(F32)
                do[:, columns] = (grad * inverse).astype(BF16)
                total = head_means(grad * combined[layer, 0, :, columns].astype(F32), spread) * (inverse * -HD)
                for half in (0, 128):
                    part = pl.ds(columns.start + half, 128)
                    high, low = split(pltpu.roll(total[:, half : half + 128], HD, 1))
                    dhigh[:, part] = high
                    dlow[:, part] = low

        @pl.when(tile > 0)
        def _():
            terms()

            @thirds
            def _(columns):
                dproj[tile + 2, :, columns] = (grads(columns) * slope[layer, tile - 1, :, columns].astype(F32)).astype(BF16)

        terms_copy(terms_out, terms_tile, terms_sem, made % 2, layer, tile).start()
        if not trading:
            pl.when(t == LAST_BACK - 1)(lambda: terms_settled(terms_out, terms_tile, terms_sem))

    @pl.when(heads_now)
    def _():
        low = low_lanes()
        spot = lax.broadcasted_iota(jnp.int32, (SLOTS, 128), 1) % HD
        first = spot == 0
        augv = jnp.where(spot < 2, 1.0, 0.0).astype(BF16)
        augq, augk = augq_ref[...], augk_ref[...]
        none = jnp.zeros((SLOTS, 128), BF16)

        def pair(index):
            part = lanes(index, 128)
            qp, kp, vp, dop = q[layer, :, part], k[layer, :, part], v[layer, :, part], do[:, part]
            augd = jnp.where(first, dhigh[:, part], dlow[:, part])
            sums = [None, None, None]
            for head in (0, 1):
                mine = low if head == 0 else ~low
                e = jnp.exp2(dot(jnp.where(mine, kp, augk), jnp.where(mine, qp, augq), ACROSS))
                dp = dot(jnp.where(mine, vp, augv), jnp.where(mine, dop, augd), ACROSS)
                ds = (e * dp).astype(BF16)
                parts = (dot(ds, jnp.where(mine, kp, none), DOWN), dot(ds, jnp.where(mine, qp, none)),
                         dot(e.astype(BF16), jnp.where(mine, dop, none)))
                sums = [part_sum if total is None else total + part_sum for total, part_sum in zip(sums, parts)]
            dq[:, part] = sums[0] * 0.125
            dk[:, part] = sums[1] * (1.0 / LOG2E)
            dproj[2, :, part] = sums[2].astype(BF16)
        late = t >= LAST_HEADS
        first_pair = jnp.where(late, 3 * (t - LAST_HEADS), 0)

        def three_pairs(index):
            for part in range(3):
                pair(first_pair + 3 * index + part)
        loop(jnp.where(late, 1, PAIRS // 3), three_pairs)

    @pl.when(project_back & (tile == 0))
    def _():
        for which, grads, low_ref, root_ref, gain, factor in ((0, dq, q, rq, qg_ref, SCALE), (1, dk, k, rk, kg_ref, 1.0)):
            @thirds
            def _(columns):
                grad, gains = grads[:, columns], gain[layer]
                xhat = low_ref[layer, :, columns].astype(F32) * (1.0 / (gains * factor))
                scaled = grad * gains
                mean = head_means(scaled, spread, False)
                along = head_means(scaled * xhat, spread, False)
                dproj[which, :, columns] = (root_ref[layer, :, columns].astype(F32) * (scaled - mean - xhat * along)).astype(BF16)
                gain_ref[layer, which + 1 : which + 2, columns] += jnp.sum(grad * xhat, 0, keepdims=True)

    @pl.when(project_back)
    def _():
        acc[...] = jnp.where(tile == up_first(0), 0.0, acc[...]) + dot(dproj[tile], w_ref[...], ACROSS)
        terms_in_ref[...] = dot(normed[layer, :, :], dproj[tile], DOWN).astype(BF16)

        @pl.when(tile == LAST_TILE)
        def _():
            gains = ln_ref[layer]

            def body(rows):
                grad = acc[rows, :]
                xhat = normed[layer, rows, :].astype(F32) * (1.0 / gains)
                scaled = grad * gains
                mean = jnp.mean(scaled, -1, keepdims=True)
                along = jnp.mean(scaled * xhat, -1, keepdims=True)
                total = dy[rows, :].astype(F32) + scale[layer, rows, :1] * (scaled - mean - xhat * along)
                low = total.astype(BF16)
                if trade:
                    pl.when(layer == section)(lambda: grad_ref.__setitem__((rows, slice(None)), total))
                else:
                    grad_ref[layer, rows, :] = total
                pl.when(layer == 1)(lambda: dy.__setitem__((rows, slice(None)), low))
                pl.when(layer == 0)(lambda: grad_low.__setitem__((rows, slice(None)), low))
                gain_ref[layer, 0:1, :] += jnp.sum(grad * xhat, 0, keepdims=True)
            by_rows(body)
            if trade:
                pl.when(layer == 1)(trade.give_grad)
                pl.when(layer == 0)(trade.finish)
            pl.when(layer == 0)(fold_gains)

    if trading:
        pl.when(t >= LAST_BACK - 1)(
            lambda: outer_scatter(t, terms_out, terms_tile, terms_sem, own_out, combined, slope, saved, *scatter_refs))


class Saved:
    def __init__(self, ref, which):
        self.ref, self.which = ref, which

    def __getitem__(self, index):
        return self.ref[(index[0], self.which) + index[1:]]

    def __setitem__(self, index, value):
        self.ref[(index[0], self.which) + index[1:]] = value


def terms_copy(terms_out, terms_tile, terms_sem, slot, layer, tile):
    target = terms_out.at[layer, pl.ds(pl.multiple_of(tile * D, D), D), :]
    return pltpu.make_async_copy(terms_tile.at[slot], target, terms_sem.at[slot])


def terms_settled(terms_out, terms_tile, terms_sem):
    for slot in range(2):
        terms_copy(terms_out, terms_tile, terms_sem, slot, 0, 0).wait()


def outer_scatter(t, terms_out, terms_tile, terms_sem, own_out, combined, slope, saved, rest_land, ready_sem, *sems):
    place = Place()
    rows = BLOCK[1][0]

    def half(number):
        return pl.ds(pl.multiple_of((number % 2) * rows, 16), rows)

    def held(number):
        return combined.at[number // 10, (number // 2) % 5, half(number)]

    def core_land(number):
        return slope.at[number // 8, (number // 2) % 4, half(number)]

    def land(colour, slot):
        piece = colour * 20 + slot
        return saved.at[1, piece // 5, pl.ds(pl.multiple_of((piece % 5) * 96, 16), 96)]

    scatter = Scatter(place, 1, terms_out, held, core_land, land, lambda slot: rest_land.at[slot], sems[:7])

    @pl.when(t == LAST_BACK - 1)
    def _():
        terms_settled(terms_out, terms_tile, terms_sem)
        greet(place, ready_sem)
        scatter.begin()

    first, count = 0, 0
    for slot, steps in enumerate(OUTER_ORDER):
        here = (t == LAST_BACK - 1 + slot).astype(jnp.int32)
        first += here * sum(map(len, OUTER_ORDER[:slot]))
        count += here * len(steps)
    scatter.run([step for steps in OUTER_ORDER for step in steps], first, count)
    pl.when(t == STEPS - 1)(lambda: scatter.finish(own_out, sems[7]))


class Trade:
    def __init__(self, section, section_out, hidden, dy, grad_land, own_sem, send_sem, recv_sem):
        self.section, self.section_out, self.hidden, self.dy, self.grad_land = section, section_out, hidden, dy, grad_land
        self.own_sem, self.send_sem, self.recv_sem = own_sem, send_sem, recv_sem
        self.pair = (1 - section, lax.axis_index("wide"))

    def kept(self):
        return pltpu.make_async_copy(self.hidden.at[self.section + 1], self.section_out.at[self.section], self.own_sem)

    def copy(self, source, target, index):
        return pltpu.make_async_remote_copy(
            src_ref=source, dst_ref=target, send_sem=self.send_sem.at[index], recv_sem=self.recv_sem.at[index],
            device_id=self.pair, device_id_type=MESH)

    def given(self):
        return self.copy(self.hidden.at[2 - self.section], self.section_out.at[self.section], 0)

    def grad(self):
        return self.copy(self.dy, self.grad_land, 1)

    def give_output(self, layer):
        pl.when(layer == self.section)(lambda: self.kept().start())
        pl.when(layer != self.section)(lambda: self.given().start())

    def give_grad(self):
        pl.when(self.section == 0)(lambda: self.grad().start())

    def finish(self):
        self.kept().wait()
        self.given().wait_send()
        self.copy(self.hidden.at[2 - self.section], self.section_out.at[1 - self.section], 0).wait_recv()
        pl.when(self.section == 0)(lambda: self.grad().wait_send())
        pl.when(self.section == 1)(lambda: self.grad().wait_recv())


def both_layers(trading, counts, weights, gains, inputs, cotangent, augq, augk, spread):
    square = (SLOTS, D)

    def whole(*dims):
        return pl.BlockSpec(dims, lambda t: (0,) * len(dims))

    low, wide = (lambda *dims: pltpu.VMEM(dims, BF16)), (lambda *dims: pltpu.VMEM(dims, F32))
    any_space, dma = pl.BlockSpec(memory_space=pl.ANY), pltpu.SemaphoreType.DMA
    full = [jax.ShapeDtypeStruct(dims, BF16) for dims in ((2, D, TILES_IN * D), (2, TILES_OUT * D, D))]
    if trading:
        in_specs, operands = [any_space] * 3, (*weights, gains)
        out_specs, more_specs = [any_space, whole(*square), whole(*square), any_space], [any_space] * 3
        sems = [dma((5, 3, 16)), dma((3, 16)), dma((3, 16))] * 3 + [dma((3,))]
        extra = [low(2, 16 * BLOCK[2][0], 128)] + sems + [dma(()), dma((2,)), dma((2,))]
        extra += [low(35, *part_shape(SCATTER_CUTS, 1, None)), pltpu.SemaphoreType.REGULAR] + scatter_sems()
        grad_shape, more = square, full + [jax.ShapeDtypeStruct(BLOCK[1], BF16)]
        params = dict(collective_id=2, has_side_effects=True)
    else:
        in_specs, operands = [any_space] * 2 + [whole(*gains.shape)], (*weights, gains)
        out_specs, more_specs = [whole(2, *square), whole(2, *square), whole(*square), whole(*square)], []
        grad_shape, extra, more, params = (2,) + square, [], [], {}
    return pl.pallas_call(
        functools.partial(compute_kernel, trading, counts),
        grid=(STEPS,),
        in_specs=in_specs + [any_space, any_space, whole(SLOTS, 128), whole(SLOTS, 128), whole(256, 256)],
        out_specs=out_specs + [
            whole(16, 128), pl.BlockSpec((None, D, D), lambda t: (in_terms(t)[0], 0, in_terms(t)[1])), any_space,
        ] + more_specs,
        scratch_shapes=[
            low(2, D, D), dma((2,)), wide(2, 1, D), wide(2, 1, 256), wide(2, 1, 256),
            low(3, *square), low(2, 8, *square), wide(2, SLOTS, 128), low(2, 4, *square), low(2, 5, *square), low(*square), low(7, *square),
            wide(*square), wide(*square), wide(*square), low(*square), low(*square), low(*square), low(2, D, D), dma((2,)), dma((2,)),
            wide(2, 8, D),
        ] + extra,
        out_shape=[
            jax.ShapeDtypeStruct((2,) + square, BF16), jax.ShapeDtypeStruct(grad_shape, F32), jax.ShapeDtypeStruct(square, BF16),
            jax.ShapeDtypeStruct(square, BF16), jax.ShapeDtypeStruct((16, 128), F32), *full,
        ] + more,
        compiler_params=pltpu.CompilerParams(vmem_limit_bytes=63 * 2**20, **params),
        name="both_layers",
    )(*operands, inputs, cotangent, augq, augk, spread)


def augment(image_id, token_size):
    lane = jnp.arange(128)[None, :] % HD
    size = jnp.log2(token_size.astype(F32))[:, None]
    high = size.astype(BF16).astype(F32)
    same = image_id[:, None] == lane - 2
    q = jnp.where((lane < 2) | (lane == 5) | same, 1.0, 0.0)
    k = jnp.where(lane == 0, high, jnp.where(lane == 1, size - high, jnp.where(lane == 5, -APART, jnp.where(same, APART, 0.0))))
    return q.astype(BF16), k.astype(BF16)


def spread_matrix():
    head = jnp.arange(256) // HD
    return ((head[:, None] == head[None, :]) / HD).astype(BF16)


def gather_all(piece, axis):
    return lax.all_gather(lax.all_gather(piece, "wide", axis=axis, tiled=True), "section", axis=0, tiled=True)


def scatter_all(terms, axis):
    own = lax.psum_scatter(terms, "section", scatter_dimension=0, tiled=True)
    return lax.psum_scatter(own, "wide", scatter_dimension=axis, tiled=True)


def on_device(inputs, cotangent, token_size, image_id, w_in, w_out, ln_gain, q_gain, k_gain):
    section, wide = lax.axis_index("section"), lax.axis_index("wide")
    width = lax.axis_size("wide")
    blocks_fit = width == 16 and w_in.shape[1:] == BLOCK[0] and w_out.shape[1:] == BLOCK[1]
    ends = [0]
    for gain in (ln_gain, q_gain, k_gain):
        ends.append(ends[-1] + gain.shape[1])
    own_gains = jnp.concatenate([ln_gain, q_gain, k_gain], 1)
    gains = jnp.pad(own_gains, ((0, BLOCK[2][0] - 1), (0, BLOCK[2][1] - ends[3])))
    weights = (w_in[0], w_out[0])
    if not blocks_fit:
        weights = (gather_all(w_in, 1), gather_all(w_out, 1))
        gains = gather_all(gains[None], 1)
    augq, augk = augment(image_id[section, 0], token_size[section, 0])
    outs, grads, grad_low, grad_land, totals, terms_in, terms_out, *more = both_layers(
        blocks_fit, tuple(gain.shape[1] for gain in (ln_gain, q_gain, k_gain)), weights, gains, inputs,
        cotangent, augq, augk, spread_matrix())
    swap = [(0, 1), (1, 0)]

    def both_micro(pair):
        mine = lax.dynamic_index_in_dim(pair, section, 0, False)
        other = lax.dynamic_index_in_dim(pair, 1 - section, 0, False).astype(BF16)
        other = lax.ppermute(other, "section", swap).astype(mine.dtype)
        return jnp.where(section == 0, jnp.stack([mine, other]), jnp.stack([other, mine]))[None, :, None]

    places = (0, D, D + HD, D + 2 * HD)
    if blocks_fit:
        own_in, totals, last_land = scatter_terms(terms_in, totals, grad_low)
        other = jnp.where(section == 0, last_land, grad_land).astype(F32)
        is_own = (jnp.arange(2) == section)[:, None, None]
        grads = jnp.where(is_own, grads[None], other[None])[None, :, None]
        outs = outs[None, :, None]
        own_in, own_out = own_in[None].astype(F32), more[2][None].astype(F32)
    else:
        own_in = scatter_all(terms_in, 1).astype(F32)
        own_out = scatter_all(terms_out, 1).astype(F32)
        totals = lax.psum(totals, ("section", "wide"))
        outs, grads = both_micro(outs), both_micro(grads)
    mine = lax.dynamic_index_in_dim(totals.reshape(2, 1024), section, 0, False)
    gain_grads = [
        lax.dynamic_slice_in_dim(mine[low:high], wide * gain.shape[1], gain.shape[1])[None]
        for low, high, gain in zip(places, places[1:], (ln_gain, q_gain, k_gain))
    ]
    return (outs, grads, own_in, own_out, *gain_grads)


def solution(mesh):
    return jax.shard_map(
        on_device,
        mesh=mesh,
        in_specs=(
            P(None, "wide", None, None),
            P(None, "wide", None, None),
            P(None, "wide", None),
            P(None, "wide", None),
            P("section", "wide", None),
            P("section", "wide", None),
            P("section", "wide"),
            P("section", "wide"),
            P("section", "wide"),
        ),
        out_specs=(
            P("section", None, "wide", None, None),
            P("section", None, "wide", None, None),
            P("section", "wide", None),
            P("section", "wide", None),
            P("section", "wide"),
            P("section", "wide"),
            P("section", "wide"),
        ),
        check_vma=False,
    )
```

```python
import functools

import jax
import jax.numpy as jnp
from jax import lax
from jax.experimental import pallas as pl
from jax.experimental.pallas import tpu as pltpu
from jax.sharding import PartitionSpec as P

MESH = pl.DeviceIdType.MESH
NZ = 4
BLOCK = ((48, 5376), (240, 768), (16, 128))
GATHER_CUTS = (2176, 96)
SCATTER_CUTS = (2048, 96)


class Place:
    def __init__(self):
        self.x, self.wide = lax.axis_index("section"), lax.axis_index("wide")
        self.y, self.z, self.c = (self.wide // 2) % 2, self.wide // 4, self.wide % 2

    def at(self, x, y, z, c=None):
        return (x, z * 4 + y * 2 + (self.c if c is None else c))

    def along(self, colour, block_z, far_first, far_second):
        dx = jnp.where(colour == 0, far_first, far_second)
        dy = jnp.where(colour == 0, far_second, far_first)
        return self.flip(self.x, dx), self.flip(self.y, dy), block_z

    @staticmethod
    def flip(value, far):
        return value + far - 2 * value * far

    def first(self, colour):
        return self.at(*self.along(colour, self.z, 1, 0))

    def second(self, colour):
        return self.at(*self.along(colour, self.z, 0, 1))

    def sibling(self):
        return self.at(self.x, self.y, self.z, 1 - self.c)


def greet(place, barrier=None):
    barrier = pltpu.get_barrier_semaphore() if barrier is None else barrier
    x, y, z = place.x, place.y, place.z

    def signal(device):
        pl.semaphore_signal(barrier, inc=1, device_id=device, device_id_type=MESH)

    signal(place.at(1 - x, y, z))
    signal(place.at(x, 1 - y, z))
    signal(place.sibling())
    pl.when(z < NZ - 1)(lambda: signal(place.at(x, y, z + 1)))
    pl.when(z > 0)(lambda: signal(place.at(x, y, z - 1)))
    pl.semaphore_wait(barrier, 3 + (z < NZ - 1).astype(jnp.int32) + (z > 0).astype(jnp.int32))


def number_of(block):
    return block[0] * 8 + block[1] * 4 + block[2]


def part_shape(cuts, array, colour):
    rows, cols = BLOCK[array]
    size = cuts[array]
    if array == 0:
        return rows, cols - 2 * size if colour is None else size
    return rows - 2 * size if colour is None else size, cols


def cut(ref, cuts, array, colour):
    if array == 2:
        return ref
    rows, cols = part_shape(cuts, array, colour)
    size = cuts[array]
    if array == 0:
        return ref.at[:, pl.ds(2 * size if colour is None else pl.multiple_of(colour * size, 128), cols)]
    return ref.at[pl.ds(2 * size if colour is None else pl.multiple_of(colour * size, 16), rows), :]


def loop(count, body):
    def step(index, carry):
        body(index)
        return carry
    lax.fori_loop(0, count, step, 0)


class Gather:
    def __init__(self, place, array, own, full, send_sem, recv_sem, core_sem):
        self.place, self.array, self.own, self.full = place, array, own, full
        self.send_sem, self.recv_sem, self.core_sem = send_sem, recv_sem, core_sem

    def view(self, block, colour, plane=None):
        rows = BLOCK[self.array][0]
        place = self.place
        start = (block[2] * 4 + block[1] * 2 + (place.c if plane is None else plane)) * rows
        return cut(self.full.at[block[0], pl.ds(pl.multiple_of(start, 16), rows), :], GATHER_CUTS, self.array, colour)

    def copy(self, link, device, block, colour, own=False, other_plane=False):
        kind = 2 if colour is None else colour
        number = number_of(block)
        target = self.view(block, colour, 1 - self.place.c if other_plane else None)
        source = cut(self.own, GATHER_CUTS, self.array, colour) if own else target
        sems = self.core_sem if link == 4 else self.recv_sem
        return pltpu.make_async_remote_copy(
            src_ref=source, dst_ref=target, send_sem=self.send_sem.at[link, kind, number], recv_sem=sems.at[kind, number],
            device_id=device, device_id_type=MESH)

    def visit(self, block, colour, onward, first, second, drain, condition=None, own=False):
        place = self.place

        def body():
            if not drain and not own:
                self.copy(0, place.sibling(), block, colour).wait_recv()

            def send(link, device):
                copy = self.copy(link, device, block, colour, own)
                copy.wait_send() if drain else copy.start()

            for link, step in onward:
                target = place.z + step
                pl.when((target >= 0) & (target < NZ))(functools.partial(send, link, place.at(place.x, place.y, target)))
            if first is not None:
                send(2, first)
            if second is not None:
                if isinstance(second, tuple) and len(second) == 3:
                    pl.when(second[2])(functools.partial(send, 3, second[:2]))
                else:
                    send(3, second)
            send(4, place.sibling())
        if condition is None:
            body()
        else:
            pl.when(condition)(body)

    def begin(self, drain=False):
        place = self.place
        me = (place.x, place.y, place.z)
        everywhere = ((0, 1), (1, -1))
        self.visit(me, None, everywhere, place.at(1 - place.x, place.y, place.z), place.at(place.x, 1 - place.y, place.z), drain, own=True)

        def body(colour):
            self.visit(me, colour, everywhere, place.first(colour), place.second(colour), drain, own=True)
        if self.array < 2:
            loop(2, body)

    def square(self, drain=False):
        place = self.place

        def body(index):
            far_x, far_y = (index != 1).astype(jnp.int32), (index != 0).astype(jnp.int32)
            block = (place.flip(place.x, far_x), place.flip(place.y, far_y), place.z)
            self.visit(block, None, ((0, 1), (1, -1)), None, place.at(place.x, 1 - place.y, place.z) + (index == 0,), drain)
        loop(3, body)

    def sided(self, distance, body):
        place = self.place

        def side_body(side):
            step = 1 - 2 * side
            block_z = place.z - step * distance
            body(side, block_z, (block_z >= 0) & (block_z < NZ) & ((distance > 0) | (side == 0)))
        loop(2, side_body)

    def onward(self, side):
        return ((0, 1), (1, -1))[side]

    def z_step(self, distance, drain=False):
        place = self.place
        for side in (0, 1):
            step = 1 - 2 * side
            block_z = place.z - step * distance

            def body(colour):
                self.visit((place.x, place.y, block_z), colour, ((side, step),), place.first(colour), place.second(colour), drain)
            pl.when((block_z >= 0) & (block_z < NZ))(lambda: loop(2, body))

    def line(self, distance, drain=False):
        place = self.place
        for side in (0, 1):
            step = 1 - 2 * side
            block_z = place.z - step * distance

            def body(index):
                block = (place.flip(place.x, index % 2), place.flip(place.y, index // 2), block_z)
                self.visit(block, None, ((side, step),), None, None, drain)
            pl.when((block_z >= 0) & (block_z < NZ))(lambda: loop(4, body))

    def a_step(self, distance, drain=False):
        place = self.place

        def body(side, block_z, there):
            def inner(colour):
                self.visit(place.along(colour, block_z, 1, 0), colour, (), None, place.second(colour), drain)
            pl.when(there)(lambda: loop(2, inner))
        self.sided(distance, body)

    def b_step(self, distance, drain=False):
        place = self.place

        def body(side, block_z, there):
            def inner(index):
                colour = index // 2
                self.visit(place.along(colour, block_z, index % 2, 1), colour, (), None, None, drain)
            pl.when(there)(lambda: loop(4, inner))
        self.sided(distance, body)

    def from_core(self):
        place = self.place

        def body(number):
            block = (number // 8, (number // 4) % 2, number % 4)
            self.copy(4, place.sibling(), block, None, other_plane=True).wait_recv()
            for colour in (0, 1) if self.array < 2 else ():
                self.copy(4, place.sibling(), block, colour, other_plane=True).wait_recv()
        loop(16, body)

    def drain(self):
        self.begin(True)
        self.square(True)

        def body(index):
            self.line(index + 1, True)
            if self.array < 2:
                self.z_step(index + 1, True)
                self.a_step(index, True)
                self.b_step(index, True)
        loop(NZ, body)


class Weights:
    def __init__(self, place, own, full, tiles, tile_sem, sems):
        self.place, self.full, self.tiles, self.tile_sem = place, full, tiles, tile_sem
        self.copies = []
        if place is None:
            return
        self.inner, self.outer, self.gains = [Gather(place, array, own[array], full[array], *sems[3 * array : 3 * array + 3]) for array in range(3)]
        for array in range(3):
            rows = BLOCK[array][0]
            target = full[array].at[place.x, pl.ds(pl.multiple_of(place.wide * rows, 16), rows), :]
            self.copies.append(pltpu.make_async_copy(own[array], target, sems[9].at[array]))

    def begin(self):
        greet(self.place)
        for copy in self.copies:
            copy.start()
        self.gains.begin()
        self.inner.begin()
        self.gains.square()
        self.inner.square()

        def early(index):
            self.inner.z_step(index + 1)
            self.inner.a_step(index)
            self.gains.line(index + 1)
            self.inner.line(index + 1)
        loop(NZ - 1, early)
        self.outer.begin()
        self.inner.a_step(NZ - 1)
        self.outer.square()

        def late(index):
            self.inner.b_step(index)
            pl.when(index == 1)(lambda: self.onward(0))
        loop(NZ, late)
        self.gains.from_core()
        self.inner.from_core()
        for copy in self.copies:
            copy.wait()

    def onward(self, index):
        self.outer.z_step(index + 1)
        self.outer.a_step(index)
        self.outer.line(index + 1)

    def end(self):
        loop(NZ, self.outer.b_step)
        self.outer.from_core()

    def drain(self):
        for array in (self.gains, self.inner, self.outer):
            array.drain()

    def fetch(self, t):
        slot = tile_slot(t)
        tile, sem = self.tiles.at[slot], self.tile_sem.at[slot]
        project = uses_in(t)

        def inner():
            layer, index = in_tile(t)
            return pltpu.make_async_copy(self.full[0].at[layer, :, pl.ds(pl.multiple_of(index * D, D), D)], tile, sem)

        def outer():
            layer, index = out_tile(t)
            return pltpu.make_async_copy(self.full[1].at[layer, pl.ds(pl.multiple_of(index * D, D), D), :], tile, sem)
        pl.when(project)(lambda: inner().start())
        pl.when(jnp.logical_not(project))(lambda: outer().start())

    def wait(self, t):
        slot = tile_slot(t)
        pltpu.make_async_copy(self.full[0].at[0, :, pl.ds(0, D)], self.tiles.at[slot], self.tile_sem.at[slot]).wait()

    def step(self, t):
        if self.place is not None:
            pl.when(t == 0)(self.begin)
            pl.when((t >= 2) & (t <= NZ))(lambda: self.onward(t - 1))
            pl.when(t == FIRST_OUT)(self.end)
            pl.when(t == LAST_OUT)(self.drain)
            held_back = FIRST_OUT
        else:
            held_back = 0
        following = jnp.where(t == LAST_HEADS - 1, LAST_PROJECT, t + 1)
        pl.when((t == 0) | (t == held_back))(lambda: self.fetch(t))
        pl.when(has_tile(t) & (following < STEPS) & (following != held_back))(lambda: self.fetch(following))
        pl.when(has_tile(t))(lambda: self.wait(t))


def add_into(target, source):
    def body(step):
        part = pl.ds(pl.multiple_of(step * 48, 16), 48)
        target[part, :] = target[part, :] + source[part, :]
    loop(target.shape[0] // 48, body)


OUTER_ORDER = (
    ("k3", "l3"), (), ("a3", "k2"), (), ("l2", "b3", "k1", "k0"), ("a2", "z3", "l1", "b2"), ("z2", "a1", "l0"), (),
    ("a0", "b1", "z1", "s", "b0", "z0"))
INNER_ORDER = (
    "k3", "k2", "l3", "k1", "l2", "a3", "k0", "l1", "b3", "a2", "z3", "a1", "l0", "b2", "z2", "b1", "a0", "z1", "s", "b0", "z0")
INNER_GRAD = 14


class Scatter:
    def __init__(self, place, array, terms, held, core_land, land, rest_land, sems):
        self.place, self.array, self.terms, self.held, self.core_land = place, array, terms, held, core_land
        self.land, self.rest_land = land, rest_land
        self.send_sem, self.recv_sem, self.rest_send, self.rest_recv, self.core_send, self.core_recv, self.local_sem = sems

    def part(self, block, colour):
        return cut(self.held(number_of(block)), SCATTER_CUTS, self.array, colour)

    def copy(self, device, block, colour, slot):
        if colour is None:
            target, send_sem, recv_sem = self.rest_land(slot), self.rest_send.at[slot], self.rest_recv.at[slot]
        else:
            target, send_sem, recv_sem = self.land(colour, slot), self.send_sem.at[colour, slot], self.recv_sem.at[colour, slot]
        return pltpu.make_async_remote_copy(
            src_ref=self.part(block, colour), dst_ref=target, send_sem=send_sem, recv_sem=recv_sem, device_id=device,
            device_id_type=MESH)

    def send(self, device, block, colour, slot, drain):
        copy = self.copy(device, block, colour, slot)
        copy.wait_send() if drain else copy.start()

    def arrive(self, block, colour, slot, drain):
        if not drain:
            self.copy(self.place.sibling(), block, colour, slot).wait_recv()
            add_into(self.part(block, colour), self.rest_land(slot) if colour is None else self.land(colour, slot))

    def core_copy(self, block, mine):
        rows = BLOCK[self.array][0]
        place = self.place
        number = number_of(block)
        start = (block[2] * 4 + block[1] * 2 + (place.c if mine else 1 - place.c)) * rows
        source = self.terms.at[block[0], pl.ds(pl.multiple_of(start, 16), rows), :]
        if mine:
            return pltpu.make_async_copy(source, self.held(number), self.local_sem.at[number])
        return pltpu.make_async_remote_copy(
            src_ref=source, dst_ref=self.core_land(number), send_sem=self.core_send.at[number],
            recv_sem=self.core_recv.at[number], device_id=place.sibling(), device_id_type=MESH)

    def sided(self, distance, body):
        place = self.place

        def side_body(side):
            block_z = place.z + (2 * side - 1) * distance
            there = (block_z >= 0) & (block_z < NZ) & (distance < NZ) & (distance >= 0) & ((distance > 0) | (side == 0))
            pl.when(there)(lambda: body(block_z))
        loop(2, side_body)

    def start(self, distance):
        place = self.place

        def body(block_z):
            def inner(index):
                block = (place.flip(place.x, 1 - index % 2), place.flip(place.y, 1 - index // 2), block_z)
                self.core_copy(block, False).start()
                self.core_copy(block, True).start()
            loop(4, inner)
        self.sided(distance, body)

    def k_step(self, distance, drain=False):
        place = self.place

        def body(block_z):
            def inner(index):
                far_x, far_y = 1 - index % 2, 1 - index // 2
                block = (place.flip(place.x, far_x), place.flip(place.y, far_y), block_z)
                if not drain:
                    self.core_copy(block, True).wait()
                    copy = self.core_copy(block, False)
                    copy.wait_recv()
                    add_into(self.held(number_of(block)), self.core_land(number_of(block)))
                    copy.wait_send()

                def out(colour):
                    far_first = jnp.where(colour == 0, far_x, far_y)
                    far_second = jnp.where(colour == 0, far_y, far_x)
                    pl.when(far_second == 1)(lambda: self.send(place.second(colour), block, colour, far_first * 4 + block_z, drain))
                loop(2, out)
            loop(4, inner)
        self.sided(distance, body)

    def a_step(self, distance, drain=False):
        place = self.place

        def body(block_z):
            def inner(index):
                colour, far_first = index % 2, 1 - index // 2
                block = place.along(colour, block_z, far_first, 0)
                self.arrive(block, colour, far_first * 4 + block_z, drain)
                pl.when(far_first == 1)(lambda: self.send(place.first(colour), block, colour, 8 + block_z, drain))
            loop(4, inner)
        self.sided(distance, body)

    def b_step(self, distance):
        place = self.place

        def body(block_z):
            loop(2, lambda colour: self.arrive((place.x, place.y, block_z), colour, 8 + block_z, False))
        self.sided(distance, body)

    def toward(self, distance, body):
        place = self.place
        for side, step in ((0, -1), (1, 1)):
            block_z, behind = place.z + step * distance, place.z - step
            there = (block_z >= 0) & (block_z < NZ) & (distance < NZ) & (distance >= 0)
            pl.when(there)(functools.partial(body, block_z, side, step, (behind >= 0) & (behind < NZ)))

    def z_step(self, distance, drain=False):
        place = self.place

        def body(block_z, side, step, more):
            block = (place.x, place.y, block_z)
            slot = 12 + 4 * side + block_z

            def inner(colour):
                pl.when(more)(lambda: self.arrive(block, colour, slot, drain))
                pl.when(distance > 0)(lambda: self.send(place.at(place.x, place.y, place.z + step), block, colour, slot, drain))
            loop(2, inner)
        self.toward(distance, body)

    def line(self, distance, drain=False):
        place = self.place

        def body(block_z, side, step, more):
            def inner(index):
                block = (place.flip(place.x, 1 - index % 2), place.flip(place.y, 1 - index // 2), block_z)
                slot = 16 * side + number_of(block)
                pl.when(more)(lambda: self.arrive(block, None, slot, drain))
                pl.when(distance > 0)(lambda: self.send(place.at(place.x, place.y, place.z + step), block, None, slot, drain))
            loop(4, inner)
        self.toward(distance, body)

    def square(self, drain=False):
        place = self.place
        over_x, over_y = place.at(1 - place.x, place.y, place.z), place.at(place.x, 1 - place.y, place.z)
        far = (1 - place.x, place.y, place.z)
        self.send(over_y, (1 - place.x, 1 - place.y, place.z), None, 33, drain)
        self.send(over_y, (place.x, 1 - place.y, place.z), None, 32, drain)
        self.arrive(far, None, 33, drain)
        self.send(over_x, far, None, 34, drain)
        self.arrive((place.x, place.y, place.z), None, 32, drain)
        self.arrive((place.x, place.y, place.z), None, 34, drain)

    def drain(self):
        def body(distance):
            self.k_step(distance, True)
            self.a_step(distance, True)
            self.z_step(distance, True)
            self.line(distance, True)
        loop(NZ, body)
        self.square(True)


    STEPS = "klabzs"

    def begin(self):
        loop(NZ, lambda index: self.start(NZ - 1 - index))

    def run(self, order, first, count, also=None):
        codes = [(self.STEPS.index(step[0]), int(step[1:] or 0)) for step in order]

        def body(index):
            index = first + index
            which, distance = [sum((index == place).astype(jnp.int32) * code[part] for place, code in enumerate(codes)) for part in (0, 1)]
            calls = (self.k_step, self.line, self.a_step, self.b_step, self.z_step)
            for code, call in enumerate(calls):
                pl.when(which == code)(lambda: call(distance))
            pl.when(which == len(calls))(self.square)
            if also:
                also(index)
        loop(count, body)

    def finish(self, result, sem):
        copy = pltpu.make_async_copy(self.held(number_of((self.place.x, self.place.y, self.place.z))), result, sem)
        copy.start()
        self.drain()
        copy.wait()


def scatter_sems():
    dma = pltpu.SemaphoreType.DMA
    return [dma((2, 20)), dma((2, 20)), dma((35,)), dma((35,)), dma((16,)), dma((16,)), dma((16,)), dma(())]


class Total:
    def __init__(self, place, own, out, run, land, send_sem, recv_sem):
        self.place, self.own, self.out, self.run, self.land = place, own, out, run, land
        self.send_sem, self.recv_sem = send_sem, recv_sem
        x, y, z = place.x, place.y, place.z
        self.routes = (place.sibling(), place.at(x, 1 - y, z), place.at(1 - x, y, z), place.at(x, y, z + 1), place.at(x, y, z - 1))
        self.sends = (None, None, None, z < NZ - 1, z > 0)
        self.gets = (None, None, None, z > 0, z < NZ - 1)

    def copy(self, link):
        source = self.own if link == 0 else self.run.at[link]
        return pltpu.make_async_remote_copy(
            src_ref=source, dst_ref=self.land.at[link], send_sem=self.send_sem.at[link], recv_sem=self.recv_sem.at[link],
            device_id=self.routes[link], device_id_type=MESH)

    def step(self, index):
        def chain(link, base):
            self.run[link] = base[...]

            def get():
                self.copy(link).wait_recv()
                self.run[link] += self.land[link]
            pl.when(self.gets[link])(get)
            pl.when(self.sends[link])(lambda: self.copy(link).start())

        def swap(link):
            if link:
                self.copy(link - 1).wait_recv()
                self.run[link] = (self.own[...] if link == 1 else self.run[link - 1]) + self.land[link - 1]
            if link < 3:
                self.copy(link).start()

        for link in range(3):
            pl.when(index == link)(functools.partial(swap, link))

        @pl.when(index == 3)
        def _():
            self.copy(2).wait_recv()
            self.out[...] = self.run[2] + self.land[2]
            chain(3, self.out)
            chain(4, self.out)
            self.out[...] = self.run[3]

            def add():
                self.out[...] += self.land[4]
            pl.when(self.gets[4])(add)

    def drain(self):
        for link, sent in enumerate(self.sends):
            if sent is None:
                self.copy(link).wait_send()
            else:
                pl.when(sent)(lambda: self.copy(link).wait_send())


def scatter_kernel(terms, gains, grad, result, out_gains, grad_land, held, core_land, land, rest_land, run, small_land, send_sem, recv_sem,
                   grad_sem, *sems):
    place = Place()
    greet(place)
    grad_copy = pltpu.make_async_remote_copy(
        src_ref=grad, dst_ref=grad_land, send_sem=grad_sem.at[0], recv_sem=grad_sem.at[1],
        device_id=place.at(1 - place.x, place.y, place.z), device_id_type=MESH)
    total = Total(place, gains, out_gains, run, small_land, send_sem, recv_sem)
    scatter = Scatter(place, 0, terms, lambda number: held.at[number], lambda number: core_land.at[number],
                      lambda colour, slot: land.at[colour * 20 + slot], lambda slot: rest_land.at[slot], sems[:7])
    scatter.begin()

    def also(index):
        pl.when(index % 4 == 0)(lambda: total.step(index // 4))
        pl.when((index == INNER_GRAD) & (place.x == 1))(lambda: grad_copy.start())
    scatter.run(INNER_ORDER, 0, len(INNER_ORDER), also)
    scatter.finish(result, sems[7])
    total.drain()
    pl.when(place.x == 1)(lambda: grad_copy.wait_send())
    pl.when(place.x == 0)(lambda: grad_copy.wait_recv())


def scatter_terms(terms, gains, grad):
    any_space, vmem, dma = pl.BlockSpec(memory_space=pl.ANY), pl.BlockSpec(memory_space=pltpu.VMEM), pltpu.SemaphoreType.DMA
    low = lambda *dims: pltpu.VMEM(dims, jnp.bfloat16)
    return pl.pallas_call(
        scatter_kernel,
        out_shape=(jax.ShapeDtypeStruct(BLOCK[0], jnp.bfloat16), jax.ShapeDtypeStruct(BLOCK[2], jnp.float32),
                   jax.ShapeDtypeStruct(grad.shape, grad.dtype)),
        in_specs=[any_space, vmem, any_space], out_specs=(any_space, vmem, any_space),
        scratch_shapes=[
            low(16, *BLOCK[0]), low(16, *BLOCK[0]), low(40, *part_shape(SCATTER_CUTS, 0, 0)), low(35, *part_shape(SCATTER_CUTS, 0, None)),
            *[pltpu.VMEM((5,) + BLOCK[2], jnp.float32)] * 2, dma((5,)), dma((5,)), dma((2,)), *scatter_sems()],
        compiler_params=pltpu.CompilerParams(collective_id=1, has_side_effects=True, vmem_limit_bytes=48 * 2**20),
        name="scatter_terms",
    )(terms, gains, grad)


SLOTS, D, HD, PAIRS = 512, 768, 64, 6
WIDE_PAIRS = 3
TILES_IN, TILES_OUT = 7, 5
EPSILON = 1e-06
LOG2E = 1.4426950408889634
SCALE = 0.125 * LOG2E
APART = 256.0
F32, BF16 = jnp.float32, jnp.bfloat16
ACROSS, DOWN = ((1,), (1,)), ((0,), (0,))


def dot(a, b, dims=((1,), (0,))):
    return lax.dot_general(a, b, (dims, ((), ())), preferred_element_type=F32)


def split(value):
    high = value.astype(BF16)
    return high, (value - high.astype(F32)).astype(BF16)


def head_means(value, spread, exact=True):
    high, low = split(value)
    means = dot(high, spread)
    return means + dot(low, spread) if exact else means


def gelu_and_slope(x):
    t = 1.0 / (1.0 + (0.3275911 * 0.7071067811865476) * jnp.abs(x))
    bell = jnp.exp2((-0.5 * LOG2E) * (x * x))
    poly = t * (0.127414796 + t * (-0.142248368 + t * (0.7107068705 + t * (-0.7265760135 + t * 0.5307027145))))
    tail = poly * bell
    phi = jnp.where(x >= 0, 1.0 - tail, tail)
    return x * phi, phi + (0.3989422804014327 * x) * bell


def lanes(index, width):
    return pl.ds(index * width if isinstance(index, int) else pl.multiple_of(index * width, width), width)


FIRST_OUT, SECOND_IN, SECOND_OUT, SECOND_BACK, LAST_OUT, LAST_BACK, LAST_HEADS, LAST_PROJECT, STEPS = 7, 12, 19, 24, 31, 36, 40, 41, 44
LAST_TILE = 2


def up_first(index):
    return (index + 3) % TILES_IN


def clip(index, high):
    return jnp.clip(index, 0, high)


def last_back(t):
    return up_first(jnp.where(t < LAST_HEADS, clip(t - LAST_BACK, 3), 4 + clip(t - LAST_PROJECT, 2)))


def in_tile(t):
    layer = ((t >= FIRST_OUT) & (t < LAST_OUT)).astype(jnp.int32)
    forward = jnp.where(t < FIRST_OUT, t, clip(t - SECOND_IN, 6))
    backward = jnp.where(t < LAST_OUT, up_first(clip(t - SECOND_BACK, 6)), last_back(t))
    return layer, jnp.where(t < SECOND_OUT, forward, backward)


def has_tile(t):
    return (t < LAST_HEADS) | (t >= LAST_PROJECT)


def tile_slot(t):
    return (t - (LAST_PROJECT - LAST_HEADS) * (t >= LAST_PROJECT)) % 2


def uses_in(t):
    forward = (t < FIRST_OUT) | ((t >= SECOND_IN) & (t < SECOND_OUT))
    return forward | ((t >= SECOND_BACK) & (t < LAST_OUT)) | ((t >= LAST_BACK) & has_tile(t))


def out_tile(t):
    layer = ((t >= SECOND_IN) & (t < SECOND_BACK)).astype(jnp.int32)
    tile = jnp.where(t < SECOND_IN, clip(t - FIRST_OUT, 4), jnp.where(t < SECOND_BACK, clip(t - SECOND_OUT, 4), clip(t - LAST_OUT, 4)))
    return layer, tile


def in_terms(t):
    late = t >= LAST_BACK
    return 1 - late.astype(jnp.int32), jnp.where(late, last_back(t), up_first(clip(t - SECOND_BACK, 6)))


def gains_of(rows, width, start, count, columns):
    lane, column = lax.broadcasted_iota(jnp.int32, (128, columns), 0), lax.broadcasted_iota(jnp.int32, (128, columns), 1)
    place = column % (count * width)
    picked = dot(rows, jnp.where(lane == start + place % count, 1.0, 0.0).astype(BF16))
    row = lax.broadcasted_iota(jnp.int32, picked.shape, 0)
    owner = (lax.broadcasted_iota(jnp.int32, picked.shape, 1) % (count * width)) // count
    return jnp.sum(jnp.where(row == owner * BLOCK[2][0], picked, 0.0), 0, keepdims=True)


def compute_kernel(trading, counts, *refs):
    if trading:
        own, refs = refs[:3], refs[3:]
    else:
        (full_in, full_out, full_gains), refs, own = refs[:3], refs[3:], None
    (inputs, cotangent, augq_ref, augk_ref, spread_ref, section_out, grad_ref, grad_low, grad_land, totals_ref, terms_in_ref, terms_out), refs = (
        refs[:12], refs[12:])
    (tiles, tile_sem, ln_ref, qg_ref, kg_ref, hidden, saved, scale, slope, combined, dy, dproj, acc, dq, dk, do, dhigh, dlow, terms_tile,
     terms_sem, entry_sem, gain_ref), refs = (refs[:22], refs[22:]) if not trading else (refs[3:25], refs[:3] + refs[25:])
    sems, swap, scatter_refs = None, (), None
    if trading:
        (full_in, full_out, own_out, full_gains), sems, swap, scatter_refs = refs[:4], refs[4:14], refs[14:17], refs[17:]
    normed, q, k, v, rq, rk, linv = [Saved(saved, which) for which in range(7)]
    t = pl.program_id(0)
    layer = in_tile(t)[0]
    project = (t < FIRST_OUT) | ((t >= SECOND_IN) & (t < SECOND_OUT))
    project_back = ((t >= SECOND_BACK) & (t < LAST_OUT)) | ((t >= LAST_BACK) & has_tile(t))
    output = (t >= FIRST_OUT) & (t < SECOND_IN)
    output_both = (t >= SECOND_OUT) & (t < SECOND_BACK)
    back = (t >= LAST_OUT) & (t < LAST_BACK)
    heads_now = (t == SECOND_BACK + 4) | ((t >= LAST_HEADS) & (t < LAST_PROJECT))
    layer = jnp.where(output, 0, layer)
    tile = jnp.where(project | project_back, in_tile(t)[1], out_tile(t)[1])
    section, trade = lax.axis_index("section"), None
    if swap:
        trade = Trade(section, section_out, hidden, dy, grad_land, *swap)
    spread = spread_ref[...]
    weights = Weights(Place() if trading else None, own, (full_in, full_out, full_gains), tiles, tile_sem, sems)
    weights.step(t)
    w_ref = tiles.at[tile_slot(t)]

    def thirds(body):
        for part in range(WIDE_PAIRS):
            body(pl.ds(256 * part, 256))

    def by_rows(body):
        for index in range(SLOTS // 128):
            body(pl.ds(index * 128, 128))

    @pl.when(t == 0)
    def _():
        entries = [pltpu.make_async_copy(inputs.at[section, 0], hidden.at[0], entry_sem.at[0]),
                   pltpu.make_async_copy(cotangent.at[section, 0], dy, entry_sem.at[1])]
        for entry in entries:
            entry.start()
        for entry in entries:
            entry.wait()
        gain_ref[...] = jnp.zeros_like(gain_ref)
        starts = (0, counts[0], counts[0] + counts[1])
        for which in range(2):
            rows = full_gains[which]
            for target, start, count, columns in zip((ln_ref, qg_ref, kg_ref), starts, counts, (D, 256, 256)):
                target[which] = gains_of(rows, D // counts[0], start, count, columns)

    def low_lanes():
        return lax.broadcasted_iota(jnp.int32, (SLOTS, 128), 1) < HD

    def fold_gains():
        for which in range(2):
            parts = [[gain_ref[which, row : row + 1, 128 * part : 128 * (part + 1)] for part in range(PAIRS)] for row in range(3)]
            sums = [functools.reduce(jnp.add, row) for row in parts[1:]]
            sums = [total + pltpu.roll(total, HD, 1) for total in sums]
            for part in range(PAIRS):
                totals_ref[8 * which + part : 8 * which + part + 1, :] = parts[0][part]
            first = lax.broadcasted_iota(jnp.int32, (1, 128), 1) < HD
            totals_ref[8 * which + 6 : 8 * which + 7, :] = jnp.where(first, *sums)
            totals_ref[8 * which + 7 : 8 * which + 8, :] = jnp.zeros((1, 128), F32)

    @pl.when(project & (tile == 0))
    def _():
        def body(rows):
            h = hidden[layer, rows, :].astype(F32)
            centred = h - jnp.mean(h, -1, keepdims=True)
            root = lax.rsqrt(jnp.mean(centred * centred, -1, keepdims=True) + EPSILON)
            scale[layer, rows, :] = jnp.broadcast_to(root, (128, 128))
            normed[layer, rows, :] = (centred * root * ln_ref[layer]).astype(BF16)
        by_rows(body)

    @pl.when(project)
    def _():
        def projected(columns):
            return dot(normed[layer, :, :], w_ref[:, columns])

        def heads(low_ref, root_ref, gain, factor):
            @thirds
            def _(columns):
                x = projected(columns)
                centred = x - head_means(x, spread)
                root = lax.rsqrt(head_means(centred * centred, spread, False) + EPSILON)
                root_ref[layer, :, columns] = root.astype(BF16)
                low_ref[layer, :, columns] = (centred * root * (gain * factor)).astype(BF16)

        pl.when(tile == 0)(lambda: heads(q, rq, qg_ref[layer], SCALE))
        pl.when(tile == 1)(lambda: heads(k, rk, kg_ref[layer], 1.0))

        @pl.when(tile == 2)
        def _():
            v[layer, :, :] = projected(slice(None)).astype(BF16)
            low = low_lanes()
            augq, augk = augq_ref[...], augk_ref[...]
            ones = jnp.ones((SLOTS, 128), BF16)

            def pair(index):
                part = lanes(index, 128)
                qp, kp, vp = q[layer, :, part], k[layer, :, part], v[layer, :, part]
                results = []
                for head in (0, 1):
                    mine = low if head == 0 else ~low
                    scores = dot(jnp.where(mine, qp, augq), jnp.where(mine, kp, augk), ACROSS)
                    results.append(dot(jnp.exp2(scores).astype(BF16), jnp.where(mine, vp, ones)))
                inverse = 1.0 / pltpu.roll(jnp.where(low, results[1], results[0]), HD, 1)
                linv[layer, :, part] = inverse.astype(BF16)
                combined[layer, 0, :, part] = (jnp.where(low, results[0], results[1]) * inverse).astype(BF16)
            for index in range(PAIRS):
                pair(index)

        @pl.when(tile > 2)
        def _():
            @thirds
            def _(columns):
                value, rise = gelu_and_slope(projected(columns))
                slope[layer, tile - 3, :, columns] = rise.astype(BF16)
                combined[layer, tile - 2, :, columns] = value.astype(BF16)

    @pl.when(output | output_both)
    def _():
        dq[...] = jnp.where(tile == 0, hidden[layer].astype(F32), dq[...]) + dot(combined[layer, tile], w_ref[...])

        @pl.when(tile == TILES_OUT - 1)
        def _():
            result = dq[...].astype(BF16)
            hidden[layer + 1] = result
            if trade:
                trade.give_output(layer)
            else:
                section_out[layer] = result

    @pl.when(output_both | back)
    def _():
        made = jnp.where(t < LAST_OUT, t - SECOND_OUT, TILES_OUT + t - LAST_OUT)
        pl.when(made >= 2)(lambda: terms_copy(terms_out, terms_tile, terms_sem, made % 2, 0, 0).wait())

        def grads(columns):
            return dot(dy[...], w_ref[columns, :], ACROSS)

        def terms():
            terms_tile[made % 2] = dot(combined[layer, tile], dy[...], DOWN).astype(BF16)

        @pl.when(tile == 0)
        def _():
            terms()

            @thirds
            def _(columns):
                grad, inverse = grads(columns), linv[layer, :, columns].astype(F32)
                do[:, columns] = (grad * inverse).astype(BF16)
                total = head_means(grad * combined[layer, 0, :, columns].astype(F32), spread) * (inverse * -HD)
                for half in (0, 128):
                    part = pl.ds(columns.start + half, 128)
                    high, low = split(pltpu.roll(total[:, half : half + 128], HD, 1))
                    dhigh[:, part] = high
                    dlow[:, part] = low

        @pl.when(tile > 0)
        def _():
            terms()

            @thirds
            def _(columns):
                dproj[tile + 2, :, columns] = (grads(columns) * slope[layer, tile - 1, :, columns].astype(F32)).astype(BF16)

        terms_copy(terms_out, terms_tile, terms_sem, made % 2, layer, tile).start()
        if not trading:
            pl.when(t == LAST_BACK - 1)(lambda: terms_settled(terms_out, terms_tile, terms_sem))

    @pl.when(heads_now)
    def _():
        low = low_lanes()
        spot = lax.broadcasted_iota(jnp.int32, (SLOTS, 128), 1) % HD
        first = spot == 0
        augv = jnp.where(spot < 2, 1.0, 0.0).astype(BF16)
        augq, augk = augq_ref[...], augk_ref[...]
        none = jnp.zeros((SLOTS, 128), BF16)

        def pair(index):
            part = lanes(index, 128)
            qp, kp, vp, dop = q[layer, :, part], k[layer, :, part], v[layer, :, part], do[:, part]
            augd = jnp.where(first, dhigh[:, part], dlow[:, part])
            sums = [None, None, None]
            for head in (0, 1):
                mine = low if head == 0 else ~low
                e = jnp.exp2(dot(jnp.where(mine, kp, augk), jnp.where(mine, qp, augq), ACROSS))
                dp = dot(jnp.where(mine, vp, augv), jnp.where(mine, dop, augd), ACROSS)
                ds = (e * dp).astype(BF16)
                parts = (dot(ds, jnp.where(mine, kp, none), DOWN), dot(ds, jnp.where(mine, qp, none)),
                         dot(e.astype(BF16), jnp.where(mine, dop, none)))
                sums = [part_sum if total is None else total + part_sum for total, part_sum in zip(sums, parts)]
            dq[:, part] = sums[0] * 0.125
            dk[:, part] = sums[1] * (1.0 / LOG2E)
            dproj[2, :, part] = sums[2].astype(BF16)
        for index in range(PAIRS):
            pair(index)

    @pl.when(project_back & (tile == 0))
    def _():
        for which, grads, low_ref, root_ref, gain, factor in ((0, dq, q, rq, qg_ref, SCALE), (1, dk, k, rk, kg_ref, 1.0)):
            @thirds
            def _(columns):
                grad, gains = grads[:, columns], gain[layer]
                xhat = low_ref[layer, :, columns].astype(F32) * (1.0 / (gains * factor))
                scaled = grad * gains
                mean = head_means(scaled, spread, False)
                along = head_means(scaled * xhat, spread, False)
                dproj[which, :, columns] = (root_ref[layer, :, columns].astype(F32) * (scaled - mean - xhat * along)).astype(BF16)
                gain_ref[layer, which + 1 : which + 2, columns] += jnp.sum(grad * xhat, 0, keepdims=True)

    @pl.when(project_back)
    def _():
        acc[...] = jnp.where(tile == up_first(0), 0.0, acc[...]) + dot(dproj[tile], w_ref[...], ACROSS)
        terms_in_ref[...] = dot(normed[layer, :, :], dproj[tile], DOWN).astype(BF16)

        @pl.when(tile == LAST_TILE)
        def _():
            gains = ln_ref[layer]

            def body(rows):
                grad = acc[rows, :]
                xhat = normed[layer, rows, :].astype(F32) * (1.0 / gains)
                scaled = grad * gains
                mean = jnp.mean(scaled, -1, keepdims=True)
                along = jnp.mean(scaled * xhat, -1, keepdims=True)
                total = dy[rows, :].astype(F32) + scale[layer, rows, :1] * (scaled - mean - xhat * along)
                low = total.astype(BF16)
                if trade:
                    pl.when(layer == section)(lambda: grad_ref.__setitem__((rows, slice(None)), total))
                else:
                    grad_ref[layer, rows, :] = total
                pl.when(layer == 1)(lambda: dy.__setitem__((rows, slice(None)), low))
                pl.when(layer == 0)(lambda: grad_low.__setitem__((rows, slice(None)), low))
                gain_ref[layer, 0:1, :] += jnp.sum(grad * xhat, 0, keepdims=True)
            by_rows(body)
            if trade:
                pl.when(layer == 1)(trade.give_grad)
                pl.when(layer == 0)(trade.finish)
            pl.when(layer == 0)(fold_gains)

    if trading:
        pl.when(t >= LAST_BACK - 1)(
            lambda: outer_scatter(t, terms_out, terms_tile, terms_sem, own_out, combined, slope, saved, *scatter_refs))


class Saved:
    def __init__(self, ref, which):
        self.ref, self.which = ref, which

    def __getitem__(self, index):
        return self.ref[(index[0], self.which) + index[1:]]

    def __setitem__(self, index, value):
        self.ref[(index[0], self.which) + index[1:]] = value


def terms_copy(terms_out, terms_tile, terms_sem, slot, layer, tile):
    target = terms_out.at[layer, pl.ds(pl.multiple_of(tile * D, D), D), :]
    return pltpu.make_async_copy(terms_tile.at[slot], target, terms_sem.at[slot])


def terms_settled(terms_out, terms_tile, terms_sem):
    for slot in range(2):
        terms_copy(terms_out, terms_tile, terms_sem, slot, 0, 0).wait()


def outer_scatter(t, terms_out, terms_tile, terms_sem, own_out, combined, slope, saved, rest_land, ready_sem, *sems):
    place = Place()
    rows = BLOCK[1][0]

    def half(number):
        return pl.ds(pl.multiple_of((number % 2) * rows, 16), rows)

    def held(number):
        return combined.at[number // 10, (number // 2) % 5, half(number)]

    def core_land(number):
        return slope.at[number // 8, (number // 2) % 4, half(number)]

    def land(colour, slot):
        piece = colour * 20 + slot
        return saved.at[1, piece // 5, pl.ds(pl.multiple_of((piece % 5) * 96, 16), 96)]

    scatter = Scatter(place, 1, terms_out, held, core_land, land, lambda slot: rest_land.at[slot], sems[:7])

    @pl.when(t == LAST_BACK - 1)
    def _():
        terms_settled(terms_out, terms_tile, terms_sem)
        greet(place, ready_sem)
        scatter.begin()

    first, count = 0, 0
    for slot, steps in enumerate(OUTER_ORDER):
        here = (t == LAST_BACK - 1 + slot).astype(jnp.int32)
        first += here * sum(map(len, OUTER_ORDER[:slot]))
        count += here * len(steps)
    scatter.run([step for steps in OUTER_ORDER for step in steps], first, count)
    pl.when(t == STEPS - 1)(lambda: scatter.finish(own_out, sems[7]))


class Trade:
    def __init__(self, section, section_out, hidden, dy, grad_land, own_sem, send_sem, recv_sem):
        self.section, self.section_out, self.hidden, self.dy, self.grad_land = section, section_out, hidden, dy, grad_land
        self.own_sem, self.send_sem, self.recv_sem = own_sem, send_sem, recv_sem
        self.pair = (1 - section, lax.axis_index("wide"))

    def kept(self):
        return pltpu.make_async_copy(self.hidden.at[self.section + 1], self.section_out.at[self.section], self.own_sem)

    def copy(self, source, target, index):
        return pltpu.make_async_remote_copy(
            src_ref=source, dst_ref=target, send_sem=self.send_sem.at[index], recv_sem=self.recv_sem.at[index],
            device_id=self.pair, device_id_type=MESH)

    def given(self):
        return self.copy(self.hidden.at[2 - self.section], self.section_out.at[self.section], 0)

    def grad(self):
        return self.copy(self.dy, self.grad_land, 1)

    def give_output(self, layer):
        pl.when(layer == self.section)(lambda: self.kept().start())
        pl.when(layer != self.section)(lambda: self.given().start())

    def give_grad(self):
        pl.when(self.section == 0)(lambda: self.grad().start())

    def finish(self):
        self.kept().wait()
        self.given().wait_send()
        self.copy(self.hidden.at[2 - self.section], self.section_out.at[1 - self.section], 0).wait_recv()
        pl.when(self.section == 0)(lambda: self.grad().wait_send())
        pl.when(self.section == 1)(lambda: self.grad().wait_recv())


def both_layers(trading, counts, weights, gains, inputs, cotangent, augq, augk, spread):
    square = (SLOTS, D)

    def whole(*dims):
        return pl.BlockSpec(dims, lambda t: (0,) * len(dims))

    low, wide = (lambda *dims: pltpu.VMEM(dims, BF16)), (lambda *dims: pltpu.VMEM(dims, F32))
    any_space, dma = pl.BlockSpec(memory_space=pl.ANY), pltpu.SemaphoreType.DMA
    full = [jax.ShapeDtypeStruct(dims, BF16) for dims in ((2, D, TILES_IN * D), (2, TILES_OUT * D, D))]
    if trading:
        in_specs, operands = [any_space] * 3, (*weights, gains)
        out_specs, more_specs = [any_space, whole(*square), whole(*square), any_space], [any_space] * 3
        sems = [dma((5, 3, 16)), dma((3, 16)), dma((3, 16))] * 3 + [dma((3,))]
        extra = [low(2, 16 * BLOCK[2][0], 128)] + sems + [dma(()), dma((2,)), dma((2,))]
        extra += [low(35, *part_shape(SCATTER_CUTS, 1, None)), pltpu.SemaphoreType.REGULAR] + scatter_sems()
        grad_shape, more = square, full + [jax.ShapeDtypeStruct(BLOCK[1], BF16)]
        params = dict(collective_id=2, has_side_effects=True)
    else:
        in_specs, operands = [any_space] * 2 + [whole(*gains.shape)], (*weights, gains)
        out_specs, more_specs = [whole(2, *square), whole(2, *square), whole(*square), whole(*square)], []
        grad_shape, extra, more, params = (2,) + square, [], [], {}
    return pl.pallas_call(
        functools.partial(compute_kernel, trading, counts),
        grid=(STEPS,),
        in_specs=in_specs + [any_space, any_space, whole(SLOTS, 128), whole(SLOTS, 128), whole(256, 256)],
        out_specs=out_specs + [
            whole(16, 128), pl.BlockSpec((None, D, D), lambda t: (in_terms(t)[0], 0, in_terms(t)[1])), any_space,
        ] + more_specs,
        scratch_shapes=[
            low(2, D, D), dma((2,)), wide(2, 1, D), wide(2, 1, 256), wide(2, 1, 256),
            low(3, *square), low(2, 8, *square), wide(2, SLOTS, 128), low(2, 4, *square), low(2, 5, *square), low(*square), low(7, *square),
            wide(*square), wide(*square), wide(*square), low(*square), low(*square), low(*square), low(2, D, D), dma((2,)), dma((2,)),
            wide(2, 8, D),
        ] + extra,
        out_shape=[
            jax.ShapeDtypeStruct((2,) + square, BF16), jax.ShapeDtypeStruct(grad_shape, F32), jax.ShapeDtypeStruct(square, BF16),
            jax.ShapeDtypeStruct(square, BF16), jax.ShapeDtypeStruct((16, 128), F32), *full,
        ] + more,
        compiler_params=pltpu.CompilerParams(vmem_limit_bytes=63 * 2**20, **params),
        name="both_layers",
    )(*operands, inputs, cotangent, augq, augk, spread)


def augment(image_id, token_size):
    lane = jnp.arange(128)[None, :] % HD
    size = jnp.log2(token_size.astype(F32))[:, None]
    high = size.astype(BF16).astype(F32)
    same = image_id[:, None] == lane - 2
    q = jnp.where((lane < 2) | (lane == 5) | same, 1.0, 0.0)
    k = jnp.where(lane == 0, high, jnp.where(lane == 1, size - high, jnp.where(lane == 5, -APART, jnp.where(same, APART, 0.0))))
    return q.astype(BF16), k.astype(BF16)


def spread_matrix():
    head = jnp.arange(256) // HD
    return ((head[:, None] == head[None, :]) / HD).astype(BF16)


def gather_all(piece, axis):
    return lax.all_gather(lax.all_gather(piece, "wide", axis=axis, tiled=True), "section", axis=0, tiled=True)


def scatter_all(terms, axis):
    own = lax.psum_scatter(terms, "section", scatter_dimension=0, tiled=True)
    return lax.psum_scatter(own, "wide", scatter_dimension=axis, tiled=True)


def on_device(inputs, cotangent, token_size, image_id, w_in, w_out, ln_gain, q_gain, k_gain):
    section, wide = lax.axis_index("section"), lax.axis_index("wide")
    width = lax.axis_size("wide")
    blocks_fit = width == 16 and w_in.shape[1:] == BLOCK[0] and w_out.shape[1:] == BLOCK[1]
    ends = [0]
    for gain in (ln_gain, q_gain, k_gain):
        ends.append(ends[-1] + gain.shape[1])
    own_gains = jnp.concatenate([ln_gain, q_gain, k_gain], 1)
    gains = jnp.pad(own_gains, ((0, BLOCK[2][0] - 1), (0, BLOCK[2][1] - ends[3])))
    weights = (w_in[0], w_out[0])
    if not blocks_fit:
        weights = (gather_all(w_in, 1), gather_all(w_out, 1))
        gains = gather_all(gains[None], 1)
    augq, augk = augment(image_id[section, 0], token_size[section, 0])
    outs, grads, grad_low, grad_land, totals, terms_in, terms_out, *more = both_layers(
        blocks_fit, tuple(gain.shape[1] for gain in (ln_gain, q_gain, k_gain)), weights, gains, inputs,
        cotangent, augq, augk, spread_matrix())
    swap = [(0, 1), (1, 0)]

    def both_micro(pair):
        mine = lax.dynamic_index_in_dim(pair, section, 0, False)
        other = lax.dynamic_index_in_dim(pair, 1 - section, 0, False).astype(BF16)
        other = lax.ppermute(other, "section", swap).astype(mine.dtype)
        return jnp.where(section == 0, jnp.stack([mine, other]), jnp.stack([other, mine]))[None, :, None]

    places = (0, D, D + HD, D + 2 * HD)
    if blocks_fit:
        own_in, totals, last_land = scatter_terms(terms_in, totals, grad_low)
        other = jnp.where(section == 0, last_land, grad_land).astype(F32)
        is_own = (jnp.arange(2) == section)[:, None, None]
        grads = jnp.where(is_own, grads[None], other[None])[None, :, None]
        outs = outs[None, :, None]
        own_in, own_out = own_in[None].astype(F32), more[2][None].astype(F32)
    else:
        own_in = scatter_all(terms_in, 1).astype(F32)
        own_out = scatter_all(terms_out, 1).astype(F32)
        totals = lax.psum(totals, ("section", "wide"))
        outs, grads = both_micro(outs), both_micro(grads)
    mine = lax.dynamic_index_in_dim(totals.reshape(2, 1024), section, 0, False)
    gain_grads = [
        lax.dynamic_slice_in_dim(mine[low:high], wide * gain.shape[1], gain.shape[1])[None]
        for low, high, gain in zip(places, places[1:], (ln_gain, q_gain, k_gain))
    ]
    return (outs, grads, own_in, own_out, *gain_grads)


def solution(mesh):
    return jax.shard_map(
        on_device,
        mesh=mesh,
        in_specs=(
            P(None, "wide", None, None),
            P(None, "wide", None, None),
            P(None, "wide", None),
            P(None, "wide", None),
            P("section", "wide", None),
            P("section", "wide", None),
            P("section", "wide"),
            P("section", "wide"),
            P("section", "wide"),
        ),
        out_specs=(
            P("section", None, "wide", None, None),
            P("section", None, "wide", None, None),
            P("section", "wide", None),
            P("section", "wide", None),
            P("section", "wide"),
            P("section", "wide"),
            P("section", "wide"),
        ),
        check_vma=False,
    )
```
